32 devices in a mesh: seq: 8 (over z, y), head: 4 (over x, core).
Axes of the slice: x: 2, y: 2, z: 4, core: 2. Of those that a mesh axis runs over, the one named last changes fastest.
Arguments:
- tokens: float32 [4, 2048, 1536], P(None, 'seq'), may hold values from -6 to 6
- teacher: float32 [4, 2048, 1536], P(None, 'seq', 'head'), may hold values from -6 to 6
- document_start: int32 [4, 2048], P(None, 'seq'), may hold values from 0 to 2047, as said below
- valid_mask: int32 [4, 2048], replicated, may hold values from 0 to 1, as said below
- input_gain: float32 [1536], replicated, may hold values from 0.5 to 1.5
- gate_weight: bfloat16 [1536, 3072], P(None, 'head'), may hold values from -0.15625 to 0.15625
- value_weight: bfloat16 [1536, 3072], P(None, 'head'), may hold values from -0.15625 to 0.15625
- keyquery_weight: bfloat16 [1536, 256], replicated, may hold values from -0.15625 to 0.15625
- step_weight: bfloat16 [1536, 48], P(None, 'head'), may hold values from -0.15625 to 0.15625
- value_conv_weight: float32 [4, 3072], P(None, 'head'), may hold values from -3 to 3
- value_conv_bias: float32 [3072], P('head'), may hold values from -3 to 3
- keyquery_conv_weight: float32 [4, 256], replicated, may hold values from -3 to 3
- keyquery_conv_bias: float32 [256], replicated, may hold values from -3 to 3
- step_bias: float32 [48], P('head'), may hold values from -9 to -5
- rate_log: float32 [48], P('head'), may hold values from -1 to 1.5
- skip_gain: float32 [48], P('head'), may hold values from 0.5 to 1.5
- norm_gain: float32 [3072], P('head'), may hold values from 0.5 to 1.5
- out_weight: bfloat16 [3072, 1536], P('head'), may hold values from -0.109375 to 0.109375
Outputs:
- output: float32 [4, 2048, 1536], P(None, 'seq', 'head')
- loss_value: float32 [], replicated
- tokens_grad: float32 [4, 2048, 1536], P(None, 'seq', 'head')
- input_gain_grad: float32 [1536], P('head')
- gate_weight_grad: float32 [1536, 3072], P('seq', 'head')
- value_weight_grad: float32 [1536, 3072], P('seq', 'head')
- keyquery_weight_grad: float32 [1536, 256], P('seq')
- step_weight_grad: float32 [1536, 48], P('seq', 'head')
- value_conv_weight_grad: float32 [4, 3072], P(None, 'head')
- value_conv_bias_grad: float32 [3072], P('head')
- keyquery_conv_weight_grad: float32 [4, 256], replicated
- keyquery_conv_bias_grad: float32 [256], replicated
- step_bias_grad: float32 [48], P('head')
- rate_log_grad: float32 [48], P('head')
- skip_gain_grad: float32 [48], P('head')
- norm_gain_grad: float32 [3072], P('head')
- out_weight_grad: float32 [3072, 1536], P('head', 'seq')
The draws below stay inside these ranges and needn't reach their ends.
Inputs may be any that keep to these rules, and one draw needn't show every extreme that they name: document_start[b, t] is the first position of the document that holds position t of sequence b: document_start[b, 0] = 0, it never falls along t and document_start[b, t] <= t. In every draw one sequence is a single document of all 2048 positions, and in every other sequence the last position begins a document of its own. `valid_mask`: the last position of every sequence is valid.
All inputs are finite; a program needn't handle non-finite values.
Results may differ from the reference program's by a relative error of at most 0.0081.
Values may be sent and summed in bfloat16 or wider, within the bound.
A program may use at most 192 MiB of HBM per device.

```python
import jax
import jax.numpy as jnp
from jax import lax

D = 1536
NHEADS = 48
HEADDIM = 64
STATE = 128
DI = 3072
SEQS = 4
SEG = 256
SEQ_LEN = 2048


def draw_document_start(key, part):
    key = jax.random.fold_in(key, 11)
    roll_key, whole_key = jax.random.split(key)
    rolls = jax.random.randint(roll_key, (SEQS, SEQ_LEN), 0, 2 * SEG)
    single = jax.random.randint(whole_key, (), 0, SEQS)
    positions = jnp.arange(SEQ_LEN, dtype=jnp.int32)
    sequence_ids = jnp.arange(SEQS, dtype=jnp.int32)
    opened = (rolls == 0) | (positions[None, :] == SEQ_LEN - 1)
    flagged = opened & (positions[None, :] > 0) & (sequence_ids[:, None] != single)
    marks = jnp.where(flagged, positions[None, :], 0)
    return lax.cummax(marks, axis=1).astype(jnp.int32)


def draw_valid_mask(key, part):
    key = jax.random.fold_in(key, 23)
    rolls = jax.random.randint(key, (SEQS, SEQ_LEN), 0, 4 * SEQ_LEN)
    positions = jnp.arange(SEQ_LEN, dtype=jnp.int32)
    chosen = (rolls < SEQ_LEN + 2 * positions[None, :]) | (positions[None, :] == SEQ_LEN - 1)
    return chosen.astype(jnp.int32)


def block_levels(own_key, dims, shards, least, top_value):
    level = 1.0
    for dim, blocks in shards:
        steps = jax.random.uniform(jax.random.fold_in(jax.random.fold_in(own_key, 6), dim), (blocks,), jnp.float32, least / len(shards), top_value / len(shards))
        level = level * jnp.repeat(jnp.exp(steps), dims[dim] // blocks).reshape((-1,) + (1,) * (len(dims) - 1 - dim))
    return level


def centred(own_key, dims, spread, limit, cuts=(), kind=jnp.bfloat16):
    level = block_levels(own_key, dims, cuts, -0.22, 0.18) if cuts else 1.0
    array = jax.random.normal(own_key, dims, jnp.float32) * spread * level
    return jnp.minimum(jnp.maximum(array, -limit), limit).astype(kind)


def setup_inputs(seed: int = 0) -> dict:
    key_list = jax.random.split(jax.random.key(seed), 19)
    tokens = centred(key_list[0], (SEQS, SEQ_LEN, D), 1.0, 6.0, ((1, 8),), jnp.float32)
    teacher = centred(key_list[1], (SEQS, SEQ_LEN, D), 1.0, 6.0, ((1, 8), (2, 4)), jnp.float32)
    document_start = draw_document_start(jax.random.fold_in(key_list[18], 71), 0)
    valid_mask = draw_valid_mask(jax.random.fold_in(key_list[18], 71), 0)
    input_gain = jnp.clip(1.0 + 0.1 * jax.random.normal(key_list[4], (D,), jnp.float32), 0.5, 1.5)
    gate_weight = centred(key_list[5], (D, DI), D ** -0.5, 0.15625, ((1, 4),))
    value_weight = centred(key_list[6], (D, DI), D ** -0.5, 0.15625, ((1, 4),))
    keyquery_weight = centred(key_list[7], (D, 2 * STATE), D ** -0.5, 0.15625)
    step_weight = centred(key_list[8], (D, NHEADS), D ** -0.5, 0.15625, ((1, 4),))
    value_conv_weight = centred(key_list[9], (4, DI), 4 ** -0.5, 3.0, ((1, 4),), jnp.float32)
    value_conv_bias = centred(key_list[10], (DI,), 0.5, 3.0, ((0, 4),), jnp.float32)
    keyquery_conv_weight = centred(key_list[11], (4, 2 * STATE), 4 ** -0.5, 3.0, (), jnp.float32)
    keyquery_conv_bias = centred(key_list[12], (2 * STATE,), 0.5, 3.0, (), jnp.float32)
    step_bias = jnp.clip(-9.0 + 4.0 * jax.random.uniform(key_list[13], (NHEADS,), jnp.float32) ** block_levels(key_list[13], (NHEADS,), ((0, 4),), -0.2, 0.2), -9.0, -5.0)
    rate_log = jnp.clip(-1.0 + 2.5 * jax.random.uniform(key_list[14], (NHEADS,), jnp.float32) ** block_levels(key_list[14], (NHEADS,), ((0, 4),), -0.2, 0.2), -1.0, 1.5)
    skip_gain = jnp.clip(0.5 + 1.0 * jax.random.uniform(key_list[15], (NHEADS,), jnp.float32) ** block_levels(key_list[15], (NHEADS,), ((0, 4),), -0.2, 0.2), 0.5, 1.5)
    norm_gain = jnp.clip(1.0 + 0.1 * jax.random.normal(key_list[16], (DI,), jnp.float32), 0.5, 1.5)
    out_weight = centred(key_list[17], (DI, D), DI ** -0.5, 0.109375, ((0, 4),))
    return {"tokens": tokens, "teacher": teacher, "document_start": document_start, "valid_mask": valid_mask, "input_gain": input_gain, "gate_weight": gate_weight, "value_weight": value_weight, "keyquery_weight": keyquery_weight, "step_weight": step_weight, "value_conv_weight": value_conv_weight, "value_conv_bias": value_conv_bias, "keyquery_conv_weight": keyquery_conv_weight, "keyquery_conv_bias": keyquery_conv_bias, "step_bias": step_bias, "rate_log": rate_log, "skip_gain": skip_gain, "norm_gain": norm_gain, "out_weight": out_weight}


norm_eps = 1e-05
highest = lax.Precision.HIGHEST

@jax.custom_vjp
def low(v):
    return lax.optimization_barrier(v.astype(jnp.bfloat16)).astype(jnp.float32)

@jax.custom_vjp
def low_back(v):
    return v

def low_keep(v):
    return (low(v), None)

def low_pass(kept, grad):
    return (grad,)

def back_keep(v):
    return (v, None)

def back_low(kept, grad):
    return (low(grad),)
low.defvjp(low_keep, low_pass)
low_back.defvjp(back_keep, back_low)

def project(left, right):
    return jnp.dot(left, right, precision=highest)

def causal_conv(inputs, weight, conv_bias, document_start):
    length = inputs.shape[1]
    positions = jnp.arange(length, dtype=jnp.int32)
    summed = conv_bias + weight[0] * inputs
    for lag_index in range(1, weight.shape[0]):
        shifted = jnp.pad(inputs, ((0, 0), (lag_index, 0), (0, 0)))[:, :length]
        usable = (positions[None, :] - lag_index >= document_start).astype(jnp.float32)
        summed = summed + weight[lag_index] * shifted * usable[:, :, None]
    return summed

def block_step(carried, pieces):
    heads_block, steps_block, rates_block, keys_block, query_block, docs_block, begin_at = pieces
    positions = begin_at + jnp.arange(SEG, dtype=jnp.int32)
    cumulative = jnp.cumsum(rates_block, axis=1)
    linked = (positions[None, None, :] >= docs_block[:, :, None]) & (positions[None, None, :] <= positions[None, :, None])
    linked_heads = linked[:, :, :, None]
    difference = cumulative[:, :, None, :] - cumulative[:, None, :, :]
    decay_mat = jnp.where(linked_heads, jnp.exp(jnp.where(linked_heads, difference, 0.0)), 0.0)
    scores = jnp.einsum('btn,bun->btu', query_block, keys_block, precision=highest)
    mixing = decay_mat * scores[:, :, :, None] * steps_block[:, None, :, :]
    outputs = jnp.einsum('btuh,buhp->bthp', mixing, heads_block, precision=highest)
    kept_mask = (docs_block < begin_at).astype(jnp.float32)
    entering = jnp.exp(cumulative) * kept_mask[:, :, None]
    outputs = outputs + entering[:, :, :, None] * jnp.einsum('btn,bhpn->bthp', query_block, carried, precision=highest)
    trailing = (positions[None, :] >= docs_block[:, -1:]).astype(jnp.float32)
    weights_end = jnp.exp(cumulative[:, -1:, :] - cumulative) * trailing[:, :, None] * steps_block
    passed = jnp.exp(cumulative[:, -1, :]) * kept_mask[:, -1:]
    carried = passed[:, :, None, None] * carried + jnp.einsum('buh,buhp,bun->bhpn', weights_end, heads_block, keys_block, precision=highest)
    return (carried, outputs)

def state_space(heads_input, steps, rates, keys_input, queries, document_start):
    sequence_count = steps.shape[0]
    length = steps.shape[1]
    blocks = length // SEG

    def to_blocks(value):
        return jnp.moveaxis(value.reshape((sequence_count, blocks, SEG) + value.shape[2:]), 1, 0)
    begins = (jnp.arange(blocks, dtype=jnp.int32) * SEG).astype(jnp.int32)
    start_state = jnp.zeros((sequence_count, NHEADS, HEADDIM, STATE), jnp.float32)
    final_state, outputs = lax.scan(jax.checkpoint(block_step), start_state, (to_blocks(heads_input), to_blocks(steps), to_blocks(rates), to_blocks(keys_input), to_blocks(queries), to_blocks(document_start), begins))
    return jnp.moveaxis(outputs, 0, 1).reshape(sequence_count, length, NHEADS, HEADDIM)

def reference(tokens, teacher, document_start, valid_mask, input_gain, gate_weight, value_weight, keyquery_weight, step_weight, value_conv_weight, value_conv_bias, keyquery_conv_weight, keyquery_conv_bias, step_bias, rate_log, skip_gain, norm_gain, out_weight):
    mask_float = valid_mask.astype(jnp.float32)
    valid_count = jnp.sum(mask_float)

    def layer(tokens, input_gain, gate_weight, value_weight, keyquery_weight, step_weight, value_conv_weight, value_conv_bias, keyquery_conv_weight, keyquery_conv_bias, step_bias, rate_log, skip_gain, norm_gain, out_weight):
        mean_square = lax.optimization_barrier(jnp.mean(tokens * tokens, axis=-1, keepdims=True))
        normed = low(tokens * lax.rsqrt(mean_square + norm_eps) * input_gain)
        gate_linear = low_back(project(normed, gate_weight))
        values_linear = low(low_back(project(normed, value_weight)))
        keyquery_linear = low(low_back(project(normed, keyquery_weight)))
        steps_linear = low_back(project(normed, step_weight))
        values_conv = jax.nn.silu(causal_conv(values_linear, value_conv_weight, value_conv_bias, document_start))
        keyquery_conv = jax.nn.silu(causal_conv(keyquery_linear, keyquery_conv_weight, keyquery_conv_bias, document_start))
        keys_input = keyquery_conv[..., :STATE]
        queries = keyquery_conv[..., STATE:]
        steps = jax.nn.softplus(steps_linear + step_bias)
        rates = steps * -jnp.exp(rate_log)
        heads_input = values_conv.reshape(SEQS, SEQ_LEN, NHEADS, HEADDIM)
        mixed_heads = state_space(heads_input, steps, rates, keys_input, queries, document_start) + skip_gain[:, None] * heads_input
        mixed_flat = mixed_heads.reshape(SEQS, SEQ_LEN, NHEADS * HEADDIM)
        gated_out = mixed_flat * jax.nn.silu(gate_linear)
        row_scale = lax.rsqrt(lax.optimization_barrier(jnp.mean(gated_out * gated_out, axis=-1, keepdims=True)) + norm_eps)
        normed_out = low(gated_out * row_scale * norm_gain)
        branch = low_back(project(normed_out, out_weight))
        output = tokens + branch
        difference = output - teacher
        loss_value = jnp.sum(mask_float[:, :, None] * difference * difference) / (D * valid_count)
        return (loss_value, output)
    loss_value, pullback, output = jax.vjp(layer, tokens, input_gain, gate_weight.astype(jnp.float32), value_weight.astype(jnp.float32), keyquery_weight.astype(jnp.float32), step_weight.astype(jnp.float32), value_conv_weight, value_conv_bias, keyquery_conv_weight, keyquery_conv_bias, step_bias, rate_log, skip_gain, norm_gain, out_weight.astype(jnp.float32), has_aux=True)
    grads = pullback(jnp.ones((), jnp.float32))
    return (output, loss_value, grads[0], grads[1], grads[2], grads[3], grads[4], grads[5], grads[6], grads[7], grads[8], grads[9], grads[10], grads[11], grads[12], grads[13], grads[14])
```

```python
import functools

import jax
import jax.numpy as jnp
from jax import lax
from jax.experimental import pallas as pl
from jax.experimental.pallas import tpu as pltpu
from jax.sharding import PartitionSpec as P

D = 1536
NHEADS = 48
HEADDIM = 64
STATE = 128
LANES = 128
VMEM_LIMIT = 56 << 20

norm_eps = 1e-05
highest = lax.Precision.HIGHEST
MESH = pl.DeviceIdType.MESH
f32 = jnp.float32
bf16 = jnp.bfloat16
NT = (((1,), (1,)), ((), ()))
TN = (((0,), (0,)), ((), ()))

in_vmem = pl.BlockSpec(memory_space=pltpu.VMEM)
in_smem = pl.BlockSpec(memory_space=pltpu.SMEM)


def params(cid):
    return pltpu.CompilerParams(
        collective_id=cid, has_side_effects=True, vmem_limit_bytes=VMEM_LIMIT
    )


def remote(src, dst, send, recv, target):
    return pltpu.make_async_remote_copy(
        src_ref=src,
        dst_ref=dst,
        send_sem=send,
        recv_sem=recv,
        device_id=target,
        device_id_type=MESH,
    )


def loop(count, fn):
    lax.fori_loop(0, count, lambda i, c: (fn(i), c)[1], 0)


def dot_nt(a, b, precision=None):
    return lax.dot_general(a, b, NT, precision=precision, preferred_element_type=f32)


def dot_tn(a, b, precision=None):
    return lax.dot_general(a, b, TN, precision=precision, preferred_element_type=f32)


def chain_kernel(
    reverse, group, decay_ref, local_ref, out_ref, held, outgoing, send_sem, recv_sem
):
    n = lax.axis_size("seq")
    place = lax.axis_index("seq")
    head = lax.axis_index("head")
    ahead = n - 1 - place if reverse else place
    by = -1 if reverse else 1
    chunks, rows = held.shape[0], held.shape[1]
    barrier = pltpu.get_barrier_semaphore()

    @pl.when(ahead > 0)
    def _():
        pl.semaphore_signal(barrier, inc=1, device_id=(place - by, head), device_id_type=MESH)

    @pl.when(ahead < n - 1)
    def _():
        pl.semaphore_wait(barrier, 1)

    def copy(c):
        return remote(
            outgoing.at[c], held.at[c], send_sem.at[c], recv_sem.at[c], (place + by, head)
        )

    def step(c):
        @pl.when(ahead > 0)
        def _():
            copy(c).wait_recv()

        @pl.when(ahead == 0)
        def _():
            held[c] = jnp.zeros(held.shape[1:], bf16)

        for g in range(group):
            part = pl.ds(g * HEADDIM, HEADDIM)
            inner = pl.ds(pl.multiple_of(c * rows + g * HEADDIM, HEADDIM), HEADDIM)
            state = held[c, part].astype(f32)
            outgoing[c, part] = (decay_ref[c * group + g] * state + local_ref[inner]).astype(bf16)

        @pl.when(ahead < n - 1)
        def _():
            copy(c).start()

        out_ref[pl.ds(pl.multiple_of(c * rows, rows), rows)] = held[c]

    loop(chunks, step)

    @pl.when(ahead < n - 1)
    def _():
        loop(chunks, lambda c: copy(c).wait_send())


def chain(decay, local, reverse, cid):
    total = local.shape[0] * local.shape[1]
    group = next(g for g in (3, 2, 1) if decay.shape[1] % g == 0)
    rows = group * HEADDIM
    chunks = total // rows
    out = pl.pallas_call(
        functools.partial(chain_kernel, reverse, group),
        out_shape=jax.ShapeDtypeStruct((total, STATE), bf16),
        in_specs=[in_smem, in_vmem],
        out_specs=in_vmem,
        scratch_shapes=[
            pltpu.VMEM((chunks, rows, STATE), bf16),
            pltpu.VMEM((chunks, rows, STATE), bf16),
            pltpu.SemaphoreType.DMA((chunks,)),
            pltpu.SemaphoreType.DMA((chunks,)),
        ],
        compiler_params=params(cid),
        name="chain_back" if reverse else "chain_forward",
    )(decay.reshape(-1), local.reshape(total, STATE))
    return out.reshape(local.shape)


def ring_place(n, index):
    odd, half = lax.rem(index, 2), lax.div(index, 2)
    return half * (1 - odd) + (n - 1 - half) * odd


def ring_index(n, spot):
    late = lax.div(2 * spot, n)
    return 2 * spot * (1 - late) + (2 * (n - 1 - spot) + 1) * late


def ring_kernel(n, count, cuts, *refs):
    parts, outs = refs[:count], refs[count : 2 * count]
    held, sems = refs[2 * count : 4 * count], refs[4 * count :]
    place = lax.axis_index("seq")
    head = lax.axis_index("head")
    spot = ring_place(n, place)
    after = (ring_index(n, lax.rem(spot + 1, n)), head)
    before = (ring_index(n, lax.rem(spot + n - 1, n)), head)
    barrier = pltpu.get_barrier_semaphore()
    for target in (after, before):
        pl.semaphore_signal(barrier, inc=1, device_id=target, device_id_type=MESH)
    pl.semaphore_wait(barrier, 2)

    streams = []
    for i in range(count):
        width = parts[i].shape[1]
        for way in range(2):
            columns = pl.ds(0, cuts[i]) if way == 0 else pl.ds(cuts[i], width - cuts[i])
            streams.append((parts[i], outs[i], held[2 * i + way], columns, way))
    send_sem, recv_sem = sems

    def piece(i, step):
        part, _, _, columns, way = streams[i]
        shift = -1 - step if way == 0 else 1 + step
        rows = part.shape[0] // n
        index = ring_index(n, lax.rem(spot + shift + 2 * n, n))
        return part.at[pl.ds(pl.multiple_of(index * rows, rows), rows), columns]

    def copy(i, step, src):
        slots, way = streams[i][2], streams[i][4]
        return remote(
            src,
            slots.at[step],
            send_sem.at[i, step],
            recv_sem.at[i, step],
            after if way == 0 else before,
        )

    for i in range(len(streams)):
        copy(i, 0, piece(i, 0)).start()

    def one(step):
        for i in range(len(streams)):
            slots = streams[i][2]
            copy(i, step, slots.at[step]).wait_recv()
            slots[step] = (slots[step].astype(f32) + piece(i, step + 1)[...].astype(f32)).astype(
                slots.dtype
            )
            copy(i, step + 1, slots.at[step]).start()

    loop(n - 2, one)
    for i in range(len(streams)):
        _, out, slots, columns, _ = streams[i]
        copy(i, n - 2, slots.at[n - 2]).wait_recv()
        out[:, columns] = slots[n - 2].astype(f32) + piece(i, n - 1)[...].astype(f32)
    for i in range(len(streams)):
        copy(i, 0, piece(i, 0)).wait_send()
        loop(n - 2, lambda step, i=i: copy(i, step + 1, streams[i][2].at[step]).wait_send())


def ring_sums(parts, cid):
    n = lax.axis_size("seq")
    cuts = [p.shape[1] // LANES // 2 * LANES for p in parts]
    rows = [p.shape[0] // n for p in parts]
    held = []
    for p, cut, r in zip(parts, cuts, rows):
        held += [
            pltpu.VMEM((n - 1, r, cut), p.dtype),
            pltpu.VMEM((n - 1, r, p.shape[1] - cut), p.dtype),
        ]
    count = len(parts)
    return pl.pallas_call(
        functools.partial(ring_kernel, n, count, cuts),
        out_shape=[jax.ShapeDtypeStruct((r, p.shape[1]), f32) for p, r in zip(parts, rows)],
        in_specs=[in_vmem] * count,
        out_specs=[in_vmem] * count,
        scratch_shapes=held
        + [
            pltpu.SemaphoreType.DMA((2 * count, n - 1)),
            pltpu.SemaphoreType.DMA((2 * count, n - 1)),
        ],
        compiler_params=params(cid),
        name="ring_sums",
    )(*parts)


class Group:
    def __init__(self, n):
        self.n = n
        self.chips = n // 2
        self.seq = lax.axis_index("seq")
        self.me = lax.axis_index("head")
        self.chip = lax.div(self.me, 2)
        self.core = lax.rem(self.me, 2)
        self.mate = self.me + 1 - 2 * self.core

    def at(self, head):
        return (self.seq, head)

    def chip_after(self, k):
        return lax.rem(self.chip + k, self.chips)

    def chip_before(self, k):
        return lax.rem(self.chip + self.chips - k, self.chips)

    def peer(self, k):
        return 2 * self.chip_after(k) + self.core

    def other(self, k):
        return lax.rem(self.me + k, self.n)

    def greet(self):
        barrier = pltpu.get_barrier_semaphore()
        for k in range(1, self.n):
            pl.semaphore_signal(
                barrier, inc=1, device_id=self.at(self.other(k)), device_id_type=MESH
            )
        pl.semaphore_wait(barrier, self.n - 1)


def share(group, source, table, send_sem, recv_sem):
    for k in range(1, group.n):
        remote(
            source,
            table.at[group.me],
            send_sem.at[k - 1],
            recv_sem.at[group.me],
            group.at(group.other(k)),
        ).start()


def shared(group, source, table, send_sem, recv_sem):
    for k in range(1, group.n):
        sender = group.other(k)
        copy = remote(
            source, table.at[sender], send_sem.at[k - 1], recv_sem.at[sender], group.at(sender)
        )
        copy.wait_send()
        copy.wait_recv()


def row_tile(chunk):
    return pl.ds(pl.multiple_of(chunk * LANES, LANES), LANES)


def as_column(row, width):
    tile = jnp.broadcast_to(row, (LANES, LANES)).T
    return jnp.concatenate([tile] * (-(-width // LANES)), axis=1)[:, :width]


def as_row(values):
    ones = jnp.ones((8, values.shape[1]), f32)
    return dot_nt(ones, values, highest)[:1]


def scatter_phases(group, chunks, part, mate_in, chip_out, chip_in, sems):
    mate_send, mate_recv, chip_send, chip_recv = sems

    def mate_copy(c, x):
        return remote(
            part.at[2 * x + 1 - group.core, row_tile(c)],
            mate_in.at[x, row_tile(c)],
            mate_send.at[x, c],
            mate_recv.at[x, c],
            group.at(group.mate),
        )

    def chip_copy(c, k):
        return remote(
            chip_out.at[k - 1, row_tile(c)],
            chip_in.at[k - 1, row_tile(c)],
            chip_send.at[k - 1, c],
            chip_recv.at[k - 1, c],
            group.at(group.peer(k)),
        )

    def start_mate(c):
        for x in range(group.chips):
            mate_copy(c, x).start()

    def start_chip(c):
        for x in range(group.chips):
            mate_copy(c, x).wait_recv()
        for k in range(1, group.chips):
            x = group.chip_after(k)
            both = part[2 * x + group.core, row_tile(c)].astype(f32) + mate_in[
                x, row_tile(c)
            ].astype(f32)
            chip_out[k - 1, row_tile(c)] = both.astype(bf16)
            chip_copy(c, k).start()

    def total(c):
        value = part[group.me, row_tile(c)].astype(f32) + mate_in[
            group.chip, row_tile(c)
        ].astype(f32)
        for k in range(1, group.chips):
            chip_copy(c, k).wait_recv()
            value = value + chip_in[k - 1, row_tile(c)].astype(f32)
        return value

    def finish(c):
        for x in range(group.chips):
            mate_copy(c, x).wait_send()
        for k in range(1, group.chips):
            chip_copy(c, k).wait_send()

    return start_mate, start_chip, total, finish


def out_kernel(
    n,
    gated_ref,
    weight_ref,
    square_ref,
    tokens_ref,
    teacher_ref,
    mask_ref,
    output_ref,
    grad_ref,
    rowdot_ref,
    squared_ref,
    loss_ref,
    part,
    mate_in,
    chip_out,
    chip_in,
    gathered,
    squares,
    dots,
    dot_out,
    mate_send,
    mate_recv,
    chip_send,
    chip_recv,
    gm_send,
    gm_recv,
    gc_send,
    gc_recv,
    gf_send,
    gf_recv,
    sq_send,
    sq_recv,
    rd_send,
    rd_recv,
):
    group = Group(n)
    group.greet()
    chunks = gated_ref.shape[0] // LANES
    width = tokens_ref.shape[1]
    share(group, square_ref, squares, sq_send, sq_recv)
    start_mate, start_chip, total, finish = scatter_phases(
        group, chunks, part, mate_in, chip_out, chip_in, (mate_send, mate_recv, chip_send, chip_recv)
    )

    def product(c):
        rows = gated_ref[row_tile(c)]
        for j in range(n):
            block = (
                weight_ref[:, j * width : (j + 1) * width] if len(weight_ref.shape) == 2 else weight_ref[j]
            )
            part[j, row_tile(c)] = jnp.dot(rows, block, preferred_element_type=f32).astype(bf16)
        start_mate(c)

    loop(chunks, product)
    loop(chunks, start_chip)
    shared(group, square_ref, squares, sq_send, sq_recv)
    squares[group.me] = square_ref[...]
    loss_ref[...] = jnp.zeros_like(loss_ref)

    def to_mate(c):
        block = gathered.at[group.me, row_tile(c)]
        return remote(block, block, gm_send.at[c], gm_recv.at[c], group.at(group.mate))

    def to_chip(c, k):
        block = gathered.at[group.me, row_tile(c)]
        return remote(
            block, block, gc_send.at[k - 1, c], gc_recv.at[k - 1, c], group.at(group.peer(k))
        )

    def forward(c, k):
        block = gathered.at[2 * group.chip_before(k) + group.core, row_tile(c)]
        return remote(
            block, block, gf_send.at[k - 1, c], gf_recv.at[k - 1, c], group.at(group.mate)
        )

    def rest(c):
        squared = squares[0, pl.ds(c, 1)]
        for j in range(1, n):
            squared = squared + squares[j, pl.ds(c, 1)]
        squared_ref[pl.ds(c, 1)] = squared
        scale = lax.rsqrt(squared * (1.0 / (NHEADS * HEADDIM)) + norm_eps)
        branch = total(c) * as_column(scale, width)
        output = tokens_ref[row_tile(c)] + branch
        output_ref[row_tile(c)] = output
        difference = output - teacher_ref[row_tile(c)]
        weighted = difference * as_column(mask_ref[pl.ds(c, 1)], width)
        low = weighted.astype(bf16)
        gathered[group.me, row_tile(c)] = low
        to_mate(c).start()
        for k in range(1, group.chips):
            to_chip(c, k).start()
        loss_ref[...] += jnp.sum(weighted * difference, axis=0, keepdims=True)
        dot_out[pl.ds(c, 1)] = as_row(low.astype(f32) * branch)

    loop(chunks, rest)
    share(group, dot_out, dots, rd_send, rd_recv)

    def pass_on(c):
        for k in range(1, group.chips):
            to_chip(c, k).wait_recv()
            forward(c, k).start()

    loop(chunks, pass_on)

    def end(c):
        to_mate(c).wait()
        for k in range(1, group.chips):
            to_chip(c, k).wait_send()
            forward(c, k).wait()
        finish(c)
        for j in range(n):
            grad_ref[j, row_tile(c)] = gathered[j, row_tile(c)]

    loop(chunks, end)
    shared(group, dot_out, dots, rd_send, rd_recv)
    row_sum = dot_out[...]
    for k in range(1, n):
        row_sum = row_sum + dots[group.other(k)]
    rowdot_ref[...] = row_sum


def scatter_scratch(n, rows, width):
    chips, chunks = n // 2, rows // LANES
    dma = pltpu.SemaphoreType.DMA
    return [
        pltpu.VMEM((n, rows, width), bf16),
        pltpu.VMEM((chips, rows, width), bf16),
        pltpu.VMEM((chips - 1, rows, width), bf16),
        pltpu.VMEM((chips - 1, rows, width), bf16),
    ], [dma((chips, chunks)), dma((chips, chunks)), dma((chips - 1, chunks)), dma((chips - 1, chunks))]


def blocked(weight, n):
    width = weight.shape[1] // n
    if width % LANES == 0:
        return weight
    return jnp.moveaxis(weight.reshape(weight.shape[0], n, width), 1, 0)


def out_phase(gated, weight, square_rows, tokens, teacher, mask_rows, cid):
    n = lax.axis_size("head")
    rows, width = tokens.shape
    chips, chunks = n // 2, rows // LANES
    buffers, sems = scatter_scratch(n, rows, width)
    dma = pltpu.SemaphoreType.DMA
    return pl.pallas_call(
        functools.partial(out_kernel, n),
        out_shape=[
            jax.ShapeDtypeStruct((rows, width), f32),
            jax.ShapeDtypeStruct((n, rows, width), bf16),
            jax.ShapeDtypeStruct((chunks, LANES), f32),
            jax.ShapeDtypeStruct((chunks, LANES), f32),
            jax.ShapeDtypeStruct((1, width), f32),
        ],
        in_specs=[in_vmem] * 6,
        out_specs=[in_vmem] * 5,
        scratch_shapes=buffers
        + [
            pltpu.VMEM((n, rows, width), bf16),
            pltpu.VMEM((n, chunks, LANES), f32),
            pltpu.VMEM((n, chunks, LANES), f32),
            pltpu.VMEM((chunks, LANES), f32),
        ]
        + sems
        + [
            dma((chunks,)),
            dma((chunks,)),
            dma((chips - 1, chunks)),
            dma((chips - 1, chunks)),
            dma((chips - 1, chunks)),
            dma((chips - 1, chunks)),
            dma((n - 1,)),
            dma((n,)),
            dma((n - 1,)),
            dma((n,)),
        ],
        compiler_params=params(cid),
        name="out_phase",
    )(gated, blocked(weight, n), square_rows, tokens, teacher, mask_rows)


def in_kernel(
    n,
    count,
    *refs,
):
    grads, weights = refs[:count], refs[count : 2 * count]
    (
        normed_ref,
        tokens_ref,
        output_ref,
        teacher_ref,
        gain_ref,
        mask_ref,
        inverse_ref,
        out_ref,
        columns_ref,
        part,
        mate_in,
        chip_out,
        chip_in,
        dots,
        dot_out,
        mate_send,
        mate_recv,
        chip_send,
        chip_recv,
        rd_send,
        rd_recv,
    ) = refs[2 * count :]
    group = Group(n)
    group.greet()
    chunks = tokens_ref.shape[0] // LANES
    width = tokens_ref.shape[1]
    start_mate, start_chip, total, finish = scatter_phases(
        group, chunks, part, mate_in, chip_out, chip_in, (mate_send, mate_recv, chip_send, chip_recv)
    )
    columns_ref[...] = jnp.zeros_like(columns_ref)

    def product(c):
        row_sum = jnp.zeros((1, LANES), f32)
        for j in range(n):
            place = slice(j * width, (j + 1) * width)
            value = jnp.zeros((LANES, width), f32)
            for g, w in zip(grads, weights):
                value = value + dot_nt(g[row_tile(c)], w[place])
            part[j, row_tile(c)] = value.astype(bf16)
            product_n = value * normed_ref[row_tile(c), place].astype(f32)
            columns_ref[:, place] += jnp.sum(product_n, axis=0, keepdims=True)
            row_sum = row_sum + as_row(product_n)
        dot_out[pl.ds(c, 1)] = row_sum
        start_mate(c)

    loop(chunks, product)
    share(group, dot_out, dots, rd_send, rd_recv)
    loop(chunks, start_chip)
    shared(group, dot_out, dots, rd_send, rd_recv)
    dots[group.me] = dot_out[...]

    def rest(c):
        row_sum = dots[0, pl.ds(c, 1)]
        for j in range(1, n):
            row_sum = row_sum + dots[j, pl.ds(c, 1)]
        inverse = inverse_ref[pl.ds(c, 1)]
        tokens = tokens_ref[row_tile(c)]
        out_grad = (output_ref[row_tile(c)] - teacher_ref[row_tile(c)]) * as_column(
            mask_ref[pl.ds(c, 1)], width
        )
        out_ref[row_tile(c)] = (
            out_grad
            + as_column(inverse, width) * gain_ref[...] * total(c)
            - tokens * as_column(inverse * inverse * row_sum * (1.0 / D), width)
        )

    loop(chunks, rest)
    loop(chunks, finish)


def in_phase(grads, weights, normed, tokens, output, teacher, gain, mask_rows, inverse_rows, cid):
    n = lax.axis_size("head")
    rows, width = tokens.shape
    chunks = rows // LANES
    buffers, sems = scatter_scratch(n, rows, width)
    dma = pltpu.SemaphoreType.DMA
    return pl.pallas_call(
        functools.partial(in_kernel, n, len(grads)),
        out_shape=[
            jax.ShapeDtypeStruct((rows, width), f32),
            jax.ShapeDtypeStruct((1, D), f32),
        ],
        in_specs=[in_vmem] * (2 * len(grads) + 7),
        out_specs=[in_vmem] * 2,
        scratch_shapes=buffers
        + [pltpu.VMEM((n, chunks, LANES), f32), pltpu.VMEM((chunks, LANES), f32)]
        + sems
        + [dma((n - 1,)), dma((n,))],
        compiler_params=params(cid),
        name="in_phase",
    )(*grads, *weights, normed, tokens, output, teacher, gain, mask_rows, inverse_rows)


def small_kernel(axis, n, source_ref, out_ref, table, send_sem, recv_sem):
    place = lax.axis_index(axis)
    fixed = lax.axis_index("seq" if axis == "head" else "head")

    def at(index):
        return (fixed, index) if axis == "head" else (index, fixed)

    barrier = pltpu.get_barrier_semaphore()
    for k in range(1, n):
        pl.semaphore_signal(
            barrier, inc=1, device_id=at(lax.rem(place + k, n)), device_id_type=MESH
        )
    pl.semaphore_wait(barrier, n - 1)

    def copy(k, sender, target):
        return remote(
            source_ref, table.at[sender], send_sem.at[k], recv_sem.at[sender], at(target)
        )

    for k in range(1, n):
        copy(k - 1, place, lax.rem(place + k, n)).start()
    for k in range(1, n):
        sender = lax.rem(place + k, n)
        copy(k - 1, sender, sender).wait()
    table[place] = source_ref[...]
    value = table[0]
    for k in range(1, n):
        value = value + table[k]
    out_ref[...] = value


def small_sum(source, axis, cid):
    n = lax.axis_size(axis)
    return pl.pallas_call(
        functools.partial(small_kernel, axis, n),
        out_shape=jax.ShapeDtypeStruct(source.shape, f32),
        in_specs=[in_vmem],
        out_specs=in_vmem,
        scratch_shapes=[
            pltpu.VMEM((n,) + source.shape, f32),
            pltpu.SemaphoreType.DMA((n - 1,)),
            pltpu.SemaphoreType.DMA((n,)),
        ],
        compiler_params=params(cid),
        name="small_sum_" + axis,
    )(source)


def packed(arrays):
    flat = jnp.concatenate([a.reshape(-1) for a in arrays])
    size = -(-flat.shape[0] // 1024) * 1024
    return jnp.pad(flat, (0, size - flat.shape[0])).reshape(-1, LANES)


def unpacked(value, arrays):
    flat, at, found = value.reshape(-1), 0, []
    for a in arrays:
        found.append(flat[at : at + a.size].reshape(a.shape))
        at += a.size
    return found


def passed_along(x, axis, by):
    count = lax.axis_size(axis)
    pairs = [(i, i + by) for i in range(count) if 0 <= i + by < count]
    return lax.ppermute(x, axis, pairs)


def silu_slope(linear):
    sigmoid_value = jax.nn.sigmoid(linear)
    return sigmoid_value * (1.0 + linear * (1.0 - sigmoid_value))


def body(
    tokens,
    teacher,
    document_start,
    valid_mask,
    input_gain,
    gate_weight,
    value_weight,
    keyquery_weight,
    step_weight,
    value_conv_weight,
    value_conv_bias,
    keyquery_conv_weight,
    keyquery_conv_bias,
    step_bias,
    rate_log,
    skip_gain,
    norm_gain,
    out_weight,
):
    head_index = lax.axis_index("head")
    sequence_index = lax.axis_index("seq")
    sequence_count = tokens.shape[0]
    shard_length = tokens.shape[1]
    rows = sequence_count * shard_length
    local_heads = skip_gain.shape[0]
    local_inner = local_heads * HEADDIM
    inner_total = NHEADS * HEADDIM
    column_count = D // lax.axis_size("head")
    column_start = head_index * column_count
    shard_begin = sequence_index * shard_length
    positions = shard_begin + jnp.arange(shard_length, dtype=jnp.int32)
    valid_count = jnp.sum(valid_mask.astype(f32))
    local_mask = lax.dynamic_slice_in_dim(valid_mask, shard_begin, shard_length, 1).astype(f32)
    mask_rows = (local_mask * (2.0 / (D * valid_count))).reshape(-1, LANES)
    inverse_root = lax.rsqrt(jnp.mean(tokens * tokens, axis=-1, keepdims=True) + norm_eps)
    normed = (tokens * inverse_root * input_gain).astype(bf16)
    values_linear = jnp.dot(normed, value_weight, preferred_element_type=f32).astype(bf16)
    keyquery_linear = jnp.dot(normed, keyquery_weight, preferred_element_type=f32).astype(bf16)
    conv_input = jnp.concatenate([values_linear, keyquery_linear], axis=-1)
    conv_lags = value_conv_weight.shape[0]
    previous = passed_along(conv_input[:, shard_length - (conv_lags - 1) :], "seq", 1)
    gate_linear = jnp.dot(normed, gate_weight, preferred_element_type=f32)
    steps_linear = jnp.dot(normed, step_weight, preferred_element_type=f32)
    extended = jnp.concatenate([previous, conv_input], axis=1).astype(f32)
    conv_weight = jnp.concatenate([value_conv_weight, keyquery_conv_weight], axis=1)
    conv_offset = jnp.concatenate([value_conv_bias, keyquery_conv_bias], axis=0)
    usable = []
    windows = []
    conv_linear = conv_offset + jnp.zeros_like(extended[:, :shard_length])
    for lag_index in range(conv_lags):
        usable.append((positions[None, :] - lag_index >= document_start).astype(f32)[:, :, None])
        windows.append(
            extended[:, conv_lags - 1 - lag_index : conv_lags - 1 - lag_index + shard_length]
        )
        conv_linear = conv_linear + conv_weight[lag_index] * windows[lag_index] * usable[lag_index]
    conv_out = jax.nn.silu(conv_linear)
    keys_input = conv_out[..., local_inner : local_inner + STATE]
    queries = conv_out[..., local_inner + STATE :]
    heads_input = conv_out[..., :local_inner].reshape(
        sequence_count, shard_length, local_heads, HEADDIM
    )
    steps = jax.nn.softplus(steps_linear + step_bias)
    decay_rate = -jnp.exp(rate_log)
    rates = steps * decay_rate
    cumulative = jnp.transpose(jnp.cumsum(rates, axis=1), (0, 2, 1))
    steps_heads = jnp.transpose(steps, (0, 2, 1))
    linked = (positions[None, None, :] >= document_start[:, :, None]) & (
        positions[None, None, :] <= positions[None, :, None]
    )
    linked_heads = linked[:, None]
    decay_mat = jnp.where(
        linked_heads,
        jnp.exp(
            jnp.where(linked_heads, cumulative[:, :, :, None] - cumulative[:, :, None, :], 0.0)
        ),
        0.0,
    )
    scores = jnp.einsum("btn,bun->btu", queries, keys_input, precision=highest)
    mixing = decay_mat * scores[:, None] * steps_heads[:, :, None, :]
    local_out = jnp.einsum("bhtu,buhp->bthp", mixing, heads_input, precision=highest)
    kept_mask = (document_start < shard_begin).astype(f32)
    entering = jnp.exp(cumulative) * kept_mask[:, None, :]
    trailing = (positions[None, :] >= document_start[:, -1:]).astype(f32)
    end_decay = jnp.exp(cumulative[:, :, -1:] - cumulative) * trailing[:, None, :]
    weights_end = end_decay * steps_heads
    state_local = jnp.einsum(
        "bhu,buhp,bun->bhpn", weights_end, heads_input, keys_input, precision=highest
    )
    passed = jnp.exp(cumulative[:, :, -1]) * kept_mask[:, -1:]
    folded = (sequence_count, local_inner, STATE)
    unfolded = (sequence_count, local_heads, HEADDIM, STATE)
    state_in = chain(passed, state_local.reshape(folded), False, 1).reshape(unfolded).astype(f32)
    projected = jnp.einsum("btn,bhpn->bthp", queries, state_in, precision=highest)
    entering_rows = jnp.transpose(entering, (0, 2, 1))
    mixed_heads = (
        local_out + entering_rows[..., None] * projected + skip_gain[:, None] * heads_input
    )
    mixed_flat = mixed_heads.reshape(rows, local_inner)
    gate_flat = gate_linear.reshape(rows, local_inner)
    gate_act = jax.nn.silu(gate_flat)
    gated_out = mixed_flat * gate_act
    square_rows = jnp.sum(gated_out * gated_out, axis=-1).reshape(-1, LANES)
    gained = (gated_out * norm_gain).astype(bf16)
    token_cols = lax.dynamic_slice_in_dim(tokens, column_start, column_count, 2).reshape(rows, -1)
    teacher_rows = teacher.reshape(rows, column_count)
    output, piece_blocks, rowdot, square_total, loss_cols = out_phase(
        gained, out_weight, square_rows, token_cols, teacher_rows, mask_rows, 2
    )
    piece_cols = jnp.moveaxis(piece_blocks, 0, 1).reshape(rows, D)
    row_scale = lax.rsqrt(square_total / inner_total + norm_eps).reshape(rows, 1)
    row_dot = rowdot.reshape(rows, 1)
    normed_out = (gated_out * row_scale * norm_gain).astype(bf16)
    column_grad = dot_tn(piece_cols, normed_out).astype(bf16)
    grad_rows = dot_nt(piece_cols, out_weight)
    gain_out_grad = jnp.sum(grad_rows * gated_out * row_scale, axis=0)
    gated_grad = row_scale * norm_gain * grad_rows - gated_out * (
        row_scale**2 * row_dot / inner_total
    )
    mixed_grad = gated_grad * gate_act
    gate_grad = (gated_grad * mixed_flat * silu_slope(gate_flat)).astype(bf16)
    heads_grad = mixed_grad.reshape(sequence_count, shard_length, local_heads, HEADDIM)
    skip_gain_grad = jnp.einsum("bthp,bthp->h", heads_grad, heads_input, precision=highest)
    state_local_grad = jnp.einsum(
        "bht,bthp,btn->bhpn", entering, heads_grad, queries, precision=highest
    )
    end_grad = (
        chain(passed, state_local_grad.reshape(folded), True, 3).reshape(unfolded).astype(f32)
    )
    pairwise = jnp.einsum("bthp,buhp->bhtu", heads_grad, heads_input, precision=highest)
    heads_input_grad = skip_gain[:, None] * heads_grad
    heads_input_grad = heads_input_grad + jnp.einsum(
        "bhtu,bthp->buhp", mixing, heads_grad, precision=highest
    )
    heads_input_grad = heads_input_grad + jnp.einsum(
        "bhu,bhpn,bun->buhp", weights_end, end_grad, keys_input, precision=highest
    )
    weighted = pairwise * decay_mat
    scores_grad = jnp.einsum("bhtu,bhu->btu", weighted, steps_heads, precision=highest)
    steps_grad = jnp.einsum("bhtu,btu->bhu", weighted, scores, precision=highest)
    cum_terms = weighted * scores[:, None] * steps_heads[:, :, None, :]
    cum_grad = jnp.sum(cum_terms, axis=-1) - jnp.sum(cum_terms, axis=-2)
    queries_grad = jnp.einsum("btu,bun->btn", scores_grad, keys_input, precision=highest)
    queries_grad = queries_grad + jnp.einsum(
        "bht,bthp,bhpn->btn", entering, heads_grad, state_in, precision=highest
    )
    keys_grad = jnp.einsum("btu,btn->bun", scores_grad, queries, precision=highest)
    keys_grad = keys_grad + jnp.einsum(
        "bhu,bhpn,buhp->bun", weights_end, end_grad, heads_input, precision=highest
    )
    entering_grad = jnp.einsum("bthp,bthp->bht", heads_grad, projected, precision=highest)
    cum_grad = cum_grad + entering_grad * entering
    passed_grad = jnp.einsum("bhpn,bhpn->bh", end_grad, state_in, precision=highest)
    end_term = jnp.einsum(
        "bhpn,buhp,bun->bhu", end_grad, heads_input, keys_input, precision=highest
    )
    steps_grad = steps_grad + end_term * end_decay
    end_mix = end_term * weights_end
    cum_grad = cum_grad - end_mix
    last_term = passed_grad * passed + jnp.sum(end_mix, axis=-1)
    last_slot = (jnp.arange(shard_length, dtype=jnp.int32) == shard_length - 1).astype(f32)
    cum_grad = cum_grad + last_term[:, :, None] * last_slot
    rates_grad = jnp.flip(jnp.cumsum(jnp.flip(cum_grad, axis=-1), axis=-1), axis=-1)
    steps_grad = steps_grad + rates_grad * decay_rate[None, :, None]
    rate_log_grad = jnp.sum(rates_grad * steps_heads, axis=(0, 2)) * decay_rate
    steps_linear_grad = jnp.transpose(steps_grad, (0, 2, 1)) * jax.nn.sigmoid(
        steps_linear + step_bias
    )
    step_bias_grad = jnp.sum(steps_linear_grad, axis=(0, 1))
    conv_out_grad = jnp.concatenate(
        [
            heads_input_grad.reshape(sequence_count, shard_length, local_inner),
            keys_grad,
            queries_grad,
        ],
        axis=-1,
    )
    conv_linear_grad = conv_out_grad * silu_slope(conv_linear)
    conv_offset_grad = jnp.sum(conv_linear_grad, axis=(0, 1))
    conv_channels = conv_linear_grad.shape[2]
    weight_rows = []
    conv_input_grad = conv_weight[0] * conv_linear_grad * usable[0]
    edge_grad = jnp.zeros((sequence_count, conv_lags - 1, conv_channels), f32)
    for lag_index in range(conv_lags):
        masked = conv_linear_grad * usable[lag_index]
        weight_rows.append(jnp.sum(masked * windows[lag_index], axis=(0, 1)))
        if lag_index > 0:
            tail_zeros = jnp.zeros((sequence_count, lag_index, conv_channels), f32)
            conv_input_grad = conv_input_grad + conv_weight[lag_index] * jnp.concatenate(
                [masked[:, lag_index:], tail_zeros], axis=1
            )
            head_zeros = jnp.zeros((sequence_count, conv_lags - 1 - lag_index, conv_channels), f32)
            edge_grad = edge_grad + jnp.concatenate(
                [head_zeros, conv_weight[lag_index] * masked[:, :lag_index]], axis=1
            )
    conv_weight_grad = jnp.stack(weight_rows, axis=0)
    incoming = passed_along(edge_grad, "seq", -1)
    lead_zeros = jnp.zeros((sequence_count, shard_length - (conv_lags - 1), conv_channels), f32)
    conv_input_grad = conv_input_grad + jnp.concatenate([lead_zeros, incoming], axis=1)
    step_pad = ((0, 0), (0, LANES - local_heads))
    values_grad = conv_input_grad[..., :local_inner].astype(bf16).reshape(rows, local_inner)
    narrow_grad = jnp.concatenate(
        [
            conv_input_grad[..., local_inner:].reshape(rows, 2 * STATE),
            jnp.pad(steps_linear_grad.reshape(rows, local_heads), step_pad),
        ],
        axis=-1,
    ).astype(bf16)
    narrow_weight = jnp.concatenate([keyquery_weight, jnp.pad(step_weight, step_pad)], axis=-1)
    normed = normed.reshape(rows, D)
    gain_cols = lax.dynamic_slice_in_dim(input_gain, column_start, column_count, 0)
    tokens_grad, gain_columns = in_phase(
        (gate_grad, values_grad, narrow_grad),
        (gate_weight, value_weight, narrow_weight),
        normed,
        token_cols,
        output,
        teacher_rows,
        gain_cols[None],
        mask_rows,
        inverse_root.reshape(-1, LANES),
        4,
    )
    gate_part = dot_tn(normed, gate_grad).astype(bf16)
    value_part = dot_tn(normed, values_grad).astype(bf16)
    narrow_part = dot_tn(normed, narrow_grad)
    out_total, gate_total, value_total, narrow_total = ring_sums(
        (column_grad, gate_part, value_part, narrow_part), 5
    )
    group_parts = [
        narrow_total[:, : 2 * STATE],
        conv_weight_grad[:, local_inner:],
        conv_offset_grad[local_inner:],
        gain_columns,
        jnp.sum(loss_cols)[None],
    ]
    (
        keyquery_total,
        keyquery_conv_part,
        keyquery_offset_part,
        gain_columns,
        loss_part,
    ) = unpacked(small_sum(packed(group_parts), "head", 6), group_parts)
    line_parts = [
        conv_weight_grad[:, :local_inner],
        conv_offset_grad[:local_inner],
        keyquery_conv_part,
        keyquery_offset_part,
        step_bias_grad,
        rate_log_grad,
        skip_gain_grad,
        gain_out_grad,
        lax.dynamic_slice_in_dim(gain_columns.reshape(-1), column_start, column_count, 0),
        loss_part,
    ]
    (
        value_conv_total,
        value_offset_total,
        keyquery_conv_total,
        keyquery_offset_total,
        step_bias_total,
        rate_log_total,
        skip_gain_total,
        norm_gain_total,
        input_gain_total,
        loss_total,
    ) = unpacked(small_sum(packed(line_parts), "seq", 7), line_parts)
    return (
        output.reshape(sequence_count, shard_length, column_count),
        loss_total[0] * 0.5,
        tokens_grad.reshape(sequence_count, shard_length, column_count),
        input_gain_total / gain_cols,
        gate_total,
        value_total,
        keyquery_total,
        narrow_total[:, 2 * STATE : 2 * STATE + local_heads],
        value_conv_total,
        value_offset_total,
        keyquery_conv_total,
        keyquery_offset_total,
        step_bias_total,
        rate_log_total,
        skip_gain_total,
        norm_gain_total,
        out_total.T,
    )


def solution(mesh):
    placed = (
        P(None, "seq", None),
        P(None, "seq", "head"),
        P(None, "seq"),
        P(),
        P(),
        P(None, "head"),
        P(None, "head"),
        P(),
        P(None, "head"),
        P(None, "head"),
        P("head"),
        P(),
        P(),
        P("head"),
        P("head"),
        P("head"),
        P("head"),
        P("head", None),
    )
    return jax.shard_map(
        body,
        mesh=mesh,
        in_specs=placed,
        out_specs=(
            P(None, "seq", "head"),
            P(),
            P(None, "seq", "head"),
            P("head"),
            P("seq", "head"),
            P("seq", "head"),
            P("seq", None),
            P("seq", "head"),
            P(None, "head"),
            P("head"),
            P(),
            P(),
            P("head"),
            P("head"),
            P("head"),
            P("head"),
            P("head", "seq"),
        ),
        check_vma=False,
    )
```

```python
import functools

import jax
import jax.numpy as jnp
from jax import lax
from jax.experimental import pallas as pl
from jax.experimental.pallas import tpu as pltpu
from jax.sharding import PartitionSpec as P

D = 1536
NHEADS = 48
HEADDIM = 64
STATE = 128
LANES = 128
VMEM_LIMIT = 56 << 20

norm_eps = 1e-05
highest = lax.Precision.HIGHEST
MESH = pl.DeviceIdType.MESH
f32 = jnp.float32
bf16 = jnp.bfloat16
NT = (((1,), (1,)), ((), ()))
TN = (((0,), (0,)), ((), ()))

in_vmem = pl.BlockSpec(memory_space=pltpu.VMEM)
in_smem = pl.BlockSpec(memory_space=pltpu.SMEM)


def params(cid):
    return pltpu.CompilerParams(
        collective_id=cid, has_side_effects=True, vmem_limit_bytes=VMEM_LIMIT
    )


def remote(src, dst, send, recv, target):
    return pltpu.make_async_remote_copy(
        src_ref=src,
        dst_ref=dst,
        send_sem=send,
        recv_sem=recv,
        device_id=target,
        device_id_type=MESH,
    )


def loop(count, fn):
    lax.fori_loop(0, count, lambda i, c: (fn(i), c)[1], 0)


def dot_nt(a, b, precision=None):
    return lax.dot_general(a, b, NT, precision=precision, preferred_element_type=f32)


def dot_tn(a, b, precision=None):
    return lax.dot_general(a, b, TN, precision=precision, preferred_element_type=f32)


def ring_place(n, index):
    odd, half = lax.rem(index, 2), lax.div(index, 2)
    return half * (1 - odd) + (n - 1 - half) * odd


def ring_index(n, spot):
    late = lax.div(2 * spot, n)
    return 2 * spot * (1 - late) + (2 * (n - 1 - spot) + 1) * late


def ring_kernel(n, count, cuts, *refs):
    parts, outs = refs[:count], refs[count : 2 * count]
    held, sems = refs[2 * count : 4 * count], refs[4 * count :]
    place = lax.axis_index("seq")
    head = lax.axis_index("head")
    spot = ring_place(n, place)
    after = (ring_index(n, lax.rem(spot + 1, n)), head)
    before = (ring_index(n, lax.rem(spot + n - 1, n)), head)
    barrier = pltpu.get_barrier_semaphore()
    for target in (after, before):
        pl.semaphore_signal(barrier, inc=1, device_id=target, device_id_type=MESH)
    pl.semaphore_wait(barrier, 2)

    streams = []
    for i in range(count):
        width = parts[i].shape[1]
        for way in range(2):
            columns = pl.ds(0, cuts[i]) if way == 0 else pl.ds(cuts[i], width - cuts[i])
            streams.append((parts[i], outs[i], held[2 * i + way], columns, way))
    send_sem, recv_sem = sems

    def piece(i, step):
        part, _, _, columns, way = streams[i]
        shift = -1 - step if way == 0 else 1 + step
        rows = part.shape[0] // n
        index = ring_index(n, lax.rem(spot + shift + 2 * n, n))
        return part.at[pl.ds(pl.multiple_of(index * rows, rows), rows), columns]

    def copy(i, step, src):
        slots, way = streams[i][2], streams[i][4]
        return remote(
            src,
            slots.at[step],
            send_sem.at[i, step],
            recv_sem.at[i, step],
            after if way == 0 else before,
        )

    for i in range(len(streams)):
        copy(i, 0, piece(i, 0)).start()

    def one(step):
        for i in range(len(streams)):
            slots = streams[i][2]
            copy(i, step, slots.at[step]).wait_recv()
            slots[step] = (slots[step].astype(f32) + piece(i, step + 1)[...].astype(f32)).astype(
                slots.dtype
            )
            copy(i, step + 1, slots.at[step]).start()

    loop(n - 2, one)
    for i in range(len(streams)):
        _, out, slots, columns, _ = streams[i]
        copy(i, n - 2, slots.at[n - 2]).wait_recv()
        out[:, columns] = slots[n - 2].astype(f32) + piece(i, n - 1)[...].astype(f32)
    for i in range(len(streams)):
        copy(i, 0, piece(i, 0)).wait_send()
        loop(n - 2, lambda step, i=i: copy(i, step + 1, streams[i][2].at[step]).wait_send())


def ring_sums(parts, cid):
    n = lax.axis_size("seq")
    cuts = [p.shape[1] // LANES // 2 * LANES for p in parts]
    rows = [p.shape[0] // n for p in parts]
    held = []
    for p, cut, r in zip(parts, cuts, rows):
        held += [
            pltpu.VMEM((n - 1, r, cut), p.dtype),
            pltpu.VMEM((n - 1, r, p.shape[1] - cut), p.dtype),
        ]
    count = len(parts)
    return pl.pallas_call(
        functools.partial(ring_kernel, n, count, cuts),
        out_shape=[jax.ShapeDtypeStruct((r, p.shape[1]), f32) for p, r in zip(parts, rows)],
        in_specs=[in_vmem] * count,
        out_specs=[in_vmem] * count,
        scratch_shapes=held
        + [
            pltpu.SemaphoreType.DMA((2 * count, n - 1)),
            pltpu.SemaphoreType.DMA((2 * count, n - 1)),
        ],
        compiler_params=params(cid),
        name="ring_sums",
    )(*parts)


class Group:
    def __init__(self, n):
        self.n = n
        self.chips = n // 2
        self.seq = lax.axis_index("seq")
        self.me = lax.axis_index("head")
        self.chip = lax.div(self.me, 2)
        self.core = lax.rem(self.me, 2)
        self.mate = self.me + 1 - 2 * self.core

    def at(self, head):
        return (self.seq, head)

    def chip_after(self, k):
        return lax.rem(self.chip + k, self.chips)

    def chip_before(self, k):
        return lax.rem(self.chip + self.chips - k, self.chips)

    def peer(self, k):
        return 2 * self.chip_after(k) + self.core

    def other(self, k):
        return lax.rem(self.me + k, self.n)

    def greet(self):
        barrier = pltpu.get_barrier_semaphore()
        for k in range(1, self.n):
            pl.semaphore_signal(
                barrier, inc=1, device_id=self.at(self.other(k)), device_id_type=MESH
            )
        pl.semaphore_wait(barrier, self.n - 1)


def share(group, source, table, send_sem, recv_sem):
    for k in range(1, group.n):
        remote(
            source,
            table.at[group.me],
            send_sem.at[k - 1],
            recv_sem.at[group.me],
            group.at(group.other(k)),
        ).start()


def shared(group, source, table, send_sem, recv_sem):
    for k in range(1, group.n):
        sender = group.other(k)
        copy = remote(
            source, table.at[sender], send_sem.at[k - 1], recv_sem.at[sender], group.at(sender)
        )
        copy.wait_send()
        copy.wait_recv()


def row_tile(chunk):
    return pl.ds(pl.multiple_of(chunk * LANES, LANES), LANES)


def as_column(row, width):
    tile = jnp.broadcast_to(row, (LANES, LANES)).T
    return jnp.concatenate([tile] * (-(-width // LANES)), axis=1)[:, :width]


def as_row(values):
    return rows_of(values)


def scatter_phases(group, chunks, part, mate_in, chip_out, chip_in, sems):
    mate_send, mate_recv, chip_send, chip_recv = sems

    def mate_copy(c, x):
        return remote(
            part.at[2 * x + 1 - group.core, row_tile(c)],
            mate_in.at[x, row_tile(c)],
            mate_send.at[x, c],
            mate_recv.at[x, c],
            group.at(group.mate),
        )

    def chip_copy(c, k):
        return remote(
            chip_out.at[k - 1, row_tile(c)],
            chip_in.at[k - 1, row_tile(c)],
            chip_send.at[k - 1, c],
            chip_recv.at[k - 1, c],
            group.at(group.peer(k)),
        )

    def start_mate(c):
        for x in range(group.chips):
            mate_copy(c, x).start()

    def start_chip(c):
        for x in range(group.chips):
            mate_copy(c, x).wait_recv()
        for k in range(1, group.chips):
            x = group.chip_after(k)
            both = part[2 * x + group.core, row_tile(c)].astype(f32) + mate_in[
                x, row_tile(c)
            ].astype(f32)
            chip_out[k - 1, row_tile(c)] = both.astype(bf16)
            chip_copy(c, k).start()

    def total(c):
        value = part[group.me, row_tile(c)].astype(f32) + mate_in[
            group.chip, row_tile(c)
        ].astype(f32)
        for k in range(1, group.chips):
            chip_copy(c, k).wait_recv()
            value = value + chip_in[k - 1, row_tile(c)].astype(f32)
        return value

    def finish(c):
        for x in range(group.chips):
            mate_copy(c, x).wait_send()
        for k in range(1, group.chips):
            chip_copy(c, k).wait_send()

    return start_mate, start_chip, total, finish


def out_kernel(
    n,
    gated_ref,
    weight_ref,
    square_ref,
    tokens_ref,
    teacher_ref,
    mask_ref,
    output_ref,
    grad_ref,
    rowdot_ref,
    squared_ref,
    loss_ref,
    part,
    mate_in,
    chip_out,
    chip_in,
    gathered,
    squares,
    dots,
    dot_out,
    mate_send,
    mate_recv,
    chip_send,
    chip_recv,
    gm_send,
    gm_recv,
    gc_send,
    gc_recv,
    gf_send,
    gf_recv,
    sq_send,
    sq_recv,
    rd_send,
    rd_recv,
):
    group = Group(n)
    group.greet()
    chunks = gated_ref.shape[0] // LANES
    width = tokens_ref.shape[1]
    share(group, square_ref, squares, sq_send, sq_recv)
    start_mate, start_chip, total, finish = scatter_phases(
        group, chunks, part, mate_in, chip_out, chip_in, (mate_send, mate_recv, chip_send, chip_recv)
    )

    def product(c):
        rows = gated_ref[row_tile(c)]
        for j in range(n):
            block = (
                weight_ref[:, j * width : (j + 1) * width] if len(weight_ref.shape) == 2 else weight_ref[j]
            )
            part[j, row_tile(c)] = jnp.dot(rows, block, preferred_element_type=f32).astype(bf16)
        start_mate(c)

    loop(chunks, product)
    loop(chunks, start_chip)
    shared(group, square_ref, squares, sq_send, sq_recv)
    squares[group.me] = square_ref[...]
    loss_ref[...] = jnp.zeros_like(loss_ref)

    def to_mate(c):
        block = gathered.at[group.me, row_tile(c)]
        return remote(block, block, gm_send.at[c], gm_recv.at[c], group.at(group.mate))

    def to_chip(c, k):
        block = gathered.at[group.me, row_tile(c)]
        return remote(
            block, block, gc_send.at[k - 1, c], gc_recv.at[k - 1, c], group.at(group.peer(k))
        )

    def forward(c, k):
        block = gathered.at[2 * group.chip_before(k) + group.core, row_tile(c)]
        return remote(
            block, block, gf_send.at[k - 1, c], gf_recv.at[k - 1, c], group.at(group.mate)
        )

    def rest(c):
        squared = squares[0, pl.ds(c, 1)]
        for j in range(1, n):
            squared = squared + squares[j, pl.ds(c, 1)]
        squared_ref[pl.ds(c, 1)] = squared
        scale = lax.rsqrt(squared * (1.0 / (NHEADS * HEADDIM)) + norm_eps)
        branch = total(c) * as_column(scale, width)
        output = tokens_ref[row_tile(c)] + branch
        output_ref[row_tile(c)] = output
        difference = output - teacher_ref[row_tile(c)]
        weighted = difference * as_column(mask_ref[pl.ds(c, 1)], width)
        low = weighted.astype(bf16)
        gathered[group.me, row_tile(c)] = low
        to_mate(c).start()
        for k in range(1, group.chips):
            to_chip(c, k).start()
        loss_ref[...] += jnp.sum(weighted * difference, axis=0, keepdims=True)
        dot_out[pl.ds(c, 1)] = as_row(low.astype(f32) * branch)

    loop(chunks, rest)
    share(group, dot_out, dots, rd_send, rd_recv)

    def pass_on(c):
        for k in range(1, group.chips):
            to_chip(c, k).wait_recv()
            forward(c, k).start()

    loop(chunks, pass_on)

    def end(c):
        to_mate(c).wait()
        for k in range(1, group.chips):
            to_chip(c, k).wait_send()
            forward(c, k).wait()
        finish(c)
        for j in range(n):
            grad_ref[j, row_tile(c)] = gathered[j, row_tile(c)]

    loop(chunks, end)
    shared(group, dot_out, dots, rd_send, rd_recv)
    row_sum = dot_out[...]
    for k in range(1, n):
        row_sum = row_sum + dots[group.other(k)]
    rowdot_ref[...] = row_sum


def scatter_scratch(n, rows, width):
    chips, chunks = n // 2, rows // LANES
    dma = pltpu.SemaphoreType.DMA
    return [
        pltpu.VMEM((n, rows, width), bf16),
        pltpu.VMEM((chips, rows, width), bf16),
        pltpu.VMEM((chips - 1, rows, width), bf16),
        pltpu.VMEM((chips - 1, rows, width), bf16),
    ], [dma((chips, chunks)), dma((chips, chunks)), dma((chips - 1, chunks)), dma((chips - 1, chunks))]


def blocked(weight, n):
    width = weight.shape[1] // n
    if width % LANES == 0:
        return weight
    return jnp.moveaxis(weight.reshape(weight.shape[0], n, width), 1, 0)


def out_phase(gated, weight, square_rows, tokens, teacher, mask_rows, cid):
    n = lax.axis_size("head")
    rows, width = tokens.shape
    chips, chunks = n // 2, rows // LANES
    buffers, sems = scatter_scratch(n, rows, width)
    dma = pltpu.SemaphoreType.DMA
    return pl.pallas_call(
        functools.partial(out_kernel, n),
        out_shape=[
            jax.ShapeDtypeStruct((rows, width), f32),
            jax.ShapeDtypeStruct((n, rows, width), bf16),
            jax.ShapeDtypeStruct((chunks, LANES), f32),
            jax.ShapeDtypeStruct((chunks, LANES), f32),
            jax.ShapeDtypeStruct((1, width), f32),
        ],
        in_specs=[in_vmem] * 6,
        out_specs=[in_vmem] * 5,
        scratch_shapes=buffers
        + [
            pltpu.VMEM((n, rows, width), bf16),
            pltpu.VMEM((n, chunks, LANES), f32),
            pltpu.VMEM((n, chunks, LANES), f32),
            pltpu.VMEM((chunks, LANES), f32),
        ]
        + sems
        + [
            dma((chunks,)),
            dma((chunks,)),
            dma((chips - 1, chunks)),
            dma((chips - 1, chunks)),
            dma((chips - 1, chunks)),
            dma((chips - 1, chunks)),
            dma((n - 1,)),
            dma((n,)),
            dma((n - 1,)),
            dma((n,)),
        ],
        compiler_params=params(cid),
        name="out_phase",
    )(gated, blocked(weight, n), square_rows, tokens, teacher, mask_rows)


def in_kernel(
    n,
    count,
    *refs,
):
    grads, weights = refs[:count], refs[count : 2 * count]
    (
        normed_ref,
        tokens_ref,
        output_ref,
        teacher_ref,
        gain_ref,
        mask_ref,
        inverse_ref,
        out_ref,
        columns_ref,
        part,
        mate_in,
        chip_out,
        chip_in,
        dots,
        dot_out,
        mate_send,
        mate_recv,
        chip_send,
        chip_recv,
        rd_send,
        rd_recv,
    ) = refs[2 * count :]
    group = Group(n)
    group.greet()
    chunks = tokens_ref.shape[0] // LANES
    width = tokens_ref.shape[1]
    start_mate, start_chip, total, finish = scatter_phases(
        group, chunks, part, mate_in, chip_out, chip_in, (mate_send, mate_recv, chip_send, chip_recv)
    )
    columns_ref[...] = jnp.zeros_like(columns_ref)

    def product(c):
        row_sum = jnp.zeros((1, LANES), f32)
        for j in range(n):
            place = slice(j * width, (j + 1) * width)
            value = jnp.zeros((LANES, width), f32)
            for g, w in zip(grads, weights):
                value = value + dot_nt(g[row_tile(c)], w[place])
            part[j, row_tile(c)] = value.astype(bf16)
            product_n = value * normed_ref[row_tile(c), place].astype(f32)
            columns_ref[:, place] += jnp.sum(product_n, axis=0, keepdims=True)
            row_sum = row_sum + as_row(product_n)
        dot_out[pl.ds(c, 1)] = row_sum
        start_mate(c)

    loop(chunks, product)
    share(group, dot_out, dots, rd_send, rd_recv)
    loop(chunks, start_chip)
    shared(group, dot_out, dots, rd_send, rd_recv)
    dots[group.me] = dot_out[...]

    def rest(c):
        row_sum = dots[0, pl.ds(c, 1)]
        for j in range(1, n):
            row_sum = row_sum + dots[j, pl.ds(c, 1)]
        inverse = inverse_ref[pl.ds(c, 1)]
        tokens = tokens_ref[row_tile(c)]
        out_grad = (output_ref[row_tile(c)] - teacher_ref[row_tile(c)]) * as_column(
            mask_ref[pl.ds(c, 1)], width
        )
        out_ref[row_tile(c)] = (
            out_grad
            + as_column(inverse, width) * gain_ref[...] * total(c)
            - tokens * as_column(inverse * inverse * row_sum * (1.0 / D), width)
        )

    loop(chunks, rest)
    loop(chunks, finish)


def in_phase(grads, weights, normed, tokens, output, teacher, gain, mask_rows, inverse_rows, cid):
    n = lax.axis_size("head")
    rows, width = tokens.shape
    chunks = rows // LANES
    buffers, sems = scatter_scratch(n, rows, width)
    dma = pltpu.SemaphoreType.DMA
    return pl.pallas_call(
        functools.partial(in_kernel, n, len(grads)),
        out_shape=[
            jax.ShapeDtypeStruct((rows, width), f32),
            jax.ShapeDtypeStruct((1, D), f32),
        ],
        in_specs=[in_vmem] * (2 * len(grads) + 7),
        out_specs=[in_vmem] * 2,
        scratch_shapes=buffers
        + [pltpu.VMEM((n, chunks, LANES), f32), pltpu.VMEM((chunks, LANES), f32)]
        + sems
        + [dma((n - 1,)), dma((n,))],
        compiler_params=params(cid),
        name="in_phase",
    )(*grads, *weights, normed, tokens, output, teacher, gain, mask_rows, inverse_rows)


def small_kernel(axis, n, source_ref, out_ref, table, send_sem, recv_sem):
    place = lax.axis_index(axis)
    fixed = lax.axis_index("seq" if axis == "head" else "head")

    def at(index):
        return (fixed, index) if axis == "head" else (index, fixed)

    barrier = pltpu.get_barrier_semaphore()
    for k in range(1, n):
        pl.semaphore_signal(
            barrier, inc=1, device_id=at(lax.rem(place + k, n)), device_id_type=MESH
        )
    pl.semaphore_wait(barrier, n - 1)

    def copy(k, sender, target):
        return remote(
            source_ref, table.at[sender], send_sem.at[k], recv_sem.at[sender], at(target)
        )

    for k in range(1, n):
        copy(k - 1, place, lax.rem(place + k, n)).start()
    for k in range(1, n):
        sender = lax.rem(place + k, n)
        copy(k - 1, sender, sender).wait()
    table[place] = source_ref[...]
    value = table[0]
    for k in range(1, n):
        value = value + table[k]
    out_ref[...] = value


def small_sum(source, axis, cid):
    n = lax.axis_size(axis)
    return pl.pallas_call(
        functools.partial(small_kernel, axis, n),
        out_shape=jax.ShapeDtypeStruct(source.shape, f32),
        in_specs=[in_vmem],
        out_specs=in_vmem,
        scratch_shapes=[
            pltpu.VMEM((n,) + source.shape, f32),
            pltpu.SemaphoreType.DMA((n - 1,)),
            pltpu.SemaphoreType.DMA((n,)),
        ],
        compiler_params=params(cid),
        name="small_sum_" + axis,
    )(source)


def packed(arrays):
    flat = jnp.concatenate([a.reshape(-1) for a in arrays])
    size = -(-flat.shape[0] // 1024) * 1024
    return jnp.pad(flat, (0, size - flat.shape[0])).reshape(-1, LANES)


def unpacked(value, arrays):
    flat, at, found = value.reshape(-1), 0, []
    for a in arrays:
        found.append(flat[at : at + a.size].reshape(a.shape))
        at += a.size
    return found


def blocks(width, size=256):
    return [(at, min(size, width - at)) for at in range(0, width, size)]


def fold_lanes(values):
    rows, width = values.shape
    if width % LANES:
        fill = jnp.zeros((rows, LANES - width % LANES), values.dtype)
        values = jnp.concatenate([values, fill], axis=1)
    total = values[:, :LANES]
    for at in range(LANES, width, LANES):
        total = total + values[:, at : at + LANES]
    return total


def rows_of(values):
    return jnp.sum(fold_lanes(values).T, axis=0, keepdims=True)


def head_spread(channels):
    row = lax.broadcasted_iota(jnp.int32, (LANES, channels), 0)
    head = lax.broadcasted_iota(jnp.int32, (LANES, channels), 1) // HEADDIM
    return ((row % 16 == head) & (row < 48)).astype(f32).astype(bf16)


def head_gather(channels):
    head = lax.broadcasted_iota(jnp.int32, (channels, LANES), 0) // HEADDIM
    return (lax.broadcasted_iota(jnp.int32, (channels, LANES), 1) == head).astype(f32).astype(bf16)


def spread(values, marks):
    lane = lax.broadcasted_iota(jnp.int32, values.shape, 1)
    values = jnp.where(lane < 16, values, 0.0)
    high = values.astype(bf16).astype(f32)
    left = values - high
    middle = left.astype(bf16).astype(f32)
    low = (left - middle).astype(bf16).astype(f32)
    three = high + pltpu.roll(middle, 16, 1) + pltpu.roll(low, 32, 1)
    return jnp.dot(three.astype(bf16), marks, preferred_element_type=f32)


def gather_heads(values, marks):
    high = values.astype(bf16)
    low = (values - high.astype(f32)).astype(bf16)
    return jnp.dot(high, marks, preferred_element_type=f32) + jnp.dot(
        low, marks, preferred_element_type=f32
    )


def softplus(x):
    y = jnp.exp(-jnp.abs(x))
    small = y * (1.0 - y * (1.0 / 2 - y * (1.0 / 3 - y * (1.0 / 4 - y * (1.0 / 5)))))
    return jnp.maximum(x, 0.0) + jnp.where(y < 0.03, small, jnp.log(1.0 + y))


def position_masks(docs_row, begin):
    length = docs_row.shape[1]
    column = jnp.broadcast_to(docs_row, (LANES, length)).T
    place = begin + lax.broadcasted_iota(jnp.int32, (length, LANES), 0).astype(f32)
    return column, place


def front_kernel(
    heads,
    tokens_hbm,
    gain_ref,
    value_hbm,
    keyquery_hbm,
    step_ref,
    gate_hbm,
    docs_ref,
    vectors_ref,
    value_conv_ref,
    value_offset_ref,
    keyquery_conv_ref,
    keyquery_offset_ref,
    norm_gain_ref,
    normed_out,
    linear_out,
    conv_out,
    gate_out,
    mixed_out,
    gained_out,
    halo_out,
    state_out,
    steps_out,
    cumulative_out,
    linear_steps_out,
    square_out,
    inverse_out,
    tokens,
    value_weight,
    keyquery_weight,
    gate_weight,
    normed,
    linear,
    conv,
    gate,
    mixed,
    gained,
    tail,
    halo,
    extended,
    heads_in,
    keys,
    queries,
    scores,
    mask_bias,
    locals_,
    held,
    outgoing,
    passed,
    entering,
    load_sem,
    token_sem,
    store_sem,
    halo_sem,
    chain_send,
    chain_recv,
):
    n = lax.axis_size("seq")
    place = lax.axis_index("seq")
    head = lax.axis_index("head")
    count, length, _ = tokens.shape
    channels = value_weight.shape[1]
    both = channels + 2 * STATE
    lags = value_conv_ref.shape[0]
    begin = (place * length).astype(f32)
    chunk_rows = STATE // 4
    chunks = count * 4

    loads = [
        pltpu.make_async_copy(value_hbm, value_weight, load_sem.at[0]),
        pltpu.make_async_copy(keyquery_hbm, keyquery_weight, load_sem.at[1]),
        pltpu.make_async_copy(gate_hbm, gate_weight, load_sem.at[2]),
    ]

    def token_load(b):
        return pltpu.make_async_copy(tokens_hbm.at[b], tokens.at[b], token_sem.at[b])

    for b in range(count):
        token_load(b).start()
        if b == 0:
            loads[0].start()
            loads[1].start()
    loads[2].start()

    stores = [
        (normed, normed_out),
        (linear, linear_out),
        (conv, conv_out),
        (gate, gate_out),
        (mixed, mixed_out),
        (gained, gained_out),
    ]

    def store(i, b):
        source, target = stores[i]
        return pltpu.make_async_copy(source.at[b], target.at[b], store_sem.at[i, b])

    barrier = pltpu.get_barrier_semaphore()

    @pl.when(place > 0)
    def _():
        pl.semaphore_signal(barrier, inc=1, device_id=(place - 1, head), device_id_type=MESH)

    @pl.when(place < n - 1)
    def _():
        pl.semaphore_signal(barrier, inc=1, device_id=(place + 1, head), device_id_type=MESH)

    def norm(b):
        token_load(b).wait()
        x = tokens[b]
        inverse = lax.rsqrt(jnp.mean(x * x, axis=-1, keepdims=True) + norm_eps)
        normed[b] = (x * inverse * gain_ref[...]).astype(bf16)
        inverse_out[pl.ds(b, 1)] = jnp.broadcast_to(inverse, (length, LANES)).T[:1]
        store(0, b).start()

    loop(count, norm)
    loads[0].wait()
    loads[1].wait()

    last = jnp.concatenate([normed[b, length - 16 :] for b in range(count)], axis=0)
    for at, width in blocks(channels):
        tail[:, at : at + width] = jnp.dot(
            last, value_weight[:, at : at + width], preferred_element_type=f32
        ).astype(bf16)
    tail[:, channels:] = jnp.dot(last, keyquery_weight[...], preferred_element_type=f32).astype(bf16)
    pl.semaphore_wait(barrier, (place > 0).astype(jnp.int32) + (place < n - 1).astype(jnp.int32))
    halo_copy = remote(tail, halo, halo_sem.at[0], halo_sem.at[1], (place + 1, head))

    @pl.when(place < n - 1)
    def _():
        halo_copy.start()

    def project(b):
        rows = normed[b]
        for at, width in blocks(channels):
            linear[b, :, at : at + width] = jnp.dot(
                rows, value_weight[:, at : at + width], preferred_element_type=f32
            ).astype(bf16)
        linear[b, :, channels:] = jnp.dot(
            rows, keyquery_weight[...], preferred_element_type=f32
        ).astype(bf16)
        linear_steps_out[b] = jnp.dot(rows, step_ref[...], preferred_element_type=f32)
        store(1, b).start()

    loop(count, project)

    @pl.when(place > 0)
    def _():
        halo_copy.wait_recv()

    @pl.when(place == 0)
    def _():
        halo[...] = jnp.zeros_like(halo)

    halo_out[...] = halo[...]
    marks = head_spread(channels)
    step_bias = vectors_ref[0:1]
    decay_rate = -jnp.exp(vectors_ref[1:2])
    skip = spread(vectors_ref[...], marks)[2:3]
    triangle = (
        lax.broadcasted_iota(jnp.int32, (length, length), 0)
        >= lax.broadcasted_iota(jnp.int32, (length, length), 1)
    ).astype(f32)

    def states(b):
        column, spot = position_masks(docs_ref[pl.ds(b, 1)].astype(f32), begin)
        extended[0:16] = halo[pl.ds(pl.multiple_of(b * 16, 16), 16)].astype(f32)
        extended[16:] = linear[b].astype(f32)
        usable = [None] + [(spot - lag >= column).astype(f32) for lag in range(1, lags)]
        for at in range(0, both, LANES):
            if at < channels:
                weight, offset, place_at = value_conv_ref, value_offset_ref, at
            else:
                weight, offset, place_at = keyquery_conv_ref, keyquery_offset_ref, at - channels
            lanes = slice(place_at, place_at + LANES)
            value = offset[:, lanes] + weight[0:1, lanes] * extended[16:, at : at + LANES]
            for lag in range(1, lags):
                value = value + weight[lag : lag + 1, lanes] * (
                    extended[16 - lag : 16 - lag + length, at : at + LANES] * usable[lag]
                )
            conv[b, :, at : at + LANES] = value
            active = value * jax.nn.sigmoid(value)
            if at < channels:
                heads_in[b, :, at : at + LANES] = active
            elif at < channels + STATE:
                keys[b] = active.astype(bf16)
            else:
                queries[b] = active.astype(bf16)
        store(2, b).start()
        steps = softplus(linear_steps_out[b] + step_bias)
        cumulative = jnp.dot(
            triangle, steps * decay_rate, precision=highest, preferred_element_type=f32
        )
        steps_out[b] = steps
        cumulative_out[b] = cumulative
        kept = (column < begin).astype(f32)
        trailing = (spot >= column[length - 1 :]).astype(f32)
        entering[b] = jnp.exp(cumulative) * kept
        end_weight = jnp.exp(cumulative[length - 1 :] - cumulative) * trailing * steps
        weighted = (heads_in[b] * spread(end_weight, marks)).astype(bf16)
        locals_[b] = dot_tn(keys[b], weighted)
        last_entering = entering[b, length - 8 :]
        passed[b] = spread(last_entering, marks)

    loop(count, states)

    def chain_copy(c):
        part = (lax.div(c, 4), pl.ds(pl.multiple_of(lax.rem(c, 4) * chunk_rows, chunk_rows), chunk_rows))
        return remote(
            outgoing.at[part], held.at[part], chain_send.at[c], chain_recv.at[c], (place + 1, head)
        )

    def chain_step(c):
        b = lax.div(c, 4)
        rows = pl.ds(pl.multiple_of(lax.rem(c, 4) * chunk_rows, chunk_rows), chunk_rows)

        @pl.when(place > 0)
        def _():
            chain_copy(c).wait_recv()

        @pl.when(place == 0)
        def _():
            held[b, rows] = jnp.zeros((chunk_rows, channels), bf16)

        outgoing[b, rows] = (
            passed[b, 7:8] * held[b, rows].astype(f32) + locals_[b, rows]
        ).astype(bf16)

        @pl.when(place < n - 1)
        def _():
            chain_copy(c).start()

    pairs = channels // LANES
    lag_slots = 5
    slots = chunks + lag_slots * (n - 1)

    def chain_slot(i):
        c = i - lag_slots * place

        @pl.when((c >= 0) & (c < chunks))
        def _():
            chain_step(c)

    first_half = lax.broadcasted_iota(jnp.int32, (length, LANES), 1) < HEADDIM
    loads[2].wait()

    def inside(b):
        column, spot = position_masks(docs_ref[pl.ds(b, 1)].astype(f32), begin)
        wide = jnp.concatenate([column] * (length // LANES), axis=1)
        t = begin + lax.broadcasted_iota(jnp.int32, (length, length), 0).astype(f32)
        u = begin + lax.broadcasted_iota(jnp.int32, (length, length), 1).astype(f32)
        mask_bias[...] = jnp.where((u >= wide) & (u <= t), 0.0, -1e30)
        scores[...] = dot_nt(queries[b], keys[b])
        cumulative = cumulative_out[b]
        across = cumulative.T
        spread_steps = spread(steps_out[b], marks)
        for pair in range(pairs):
            lanes = slice(pair * LANES, (pair + 1) * LANES)
            scaled = heads_in[b, :, lanes] * spread_steps[:, lanes]
            value = jnp.zeros((length, LANES), f32)
            for half in range(2):
                h = 2 * pair + half
                decay = jnp.exp(cumulative[:, h : h + 1] - across[h : h + 1] + mask_bias[...])
                mixing = (decay * scores[...]).astype(bf16)
                mine = jnp.where(first_half if half == 0 else ~first_half, scaled, 0.0).astype(bf16)
                value = value + jnp.dot(mixing, mine, preferred_element_type=f32)
            mixed[b, :, lanes] = value
            chain_slot(b * (pairs + 1) + pair)
        rows = normed[b]
        for at, width in blocks(channels):
            gate[b, :, at : at + width] = jnp.dot(
                rows, gate_weight[:, at : at + width], preferred_element_type=f32
            )
        store(3, b).start()
        chain_slot(b * (pairs + 1) + pairs)

    loop(count, inside)
    done = count * (pairs + 1)
    if slots > done:
        loop(slots - done, lambda i: chain_slot(i + done))

    def close(b):
        state_out[b] = held[b]
        projected = jnp.dot(queries[b], held[b], preferred_element_type=f32)
        value = mixed[b] + spread(entering[b], marks) * projected + skip * heads_in[b]
        mixed[b] = value
        store(4, b).start()
        linear_gate = gate[b]
        gated = value * (linear_gate * jax.nn.sigmoid(linear_gate))
        gained[b] = (gated * norm_gain_ref[...]).astype(bf16)
        store(5, b).start()
        square_out[pl.ds(b, 1)] = rows_of(gated * gated)

    loop(count, close)

    @pl.when(place < n - 1)
    def _():
        halo_copy.wait_send()
        loop(chunks, lambda c: chain_copy(c).wait_send())

    for i in range(len(stores)):
        loop(count, lambda b, i=i: store(i, b).wait())


def front(tokens, gain, value_weight, keyquery_weight, step_weight, gate_weight, docs, vectors, conv, norm_gain, cid):
    count, length, _ = tokens.shape
    channels = value_weight.shape[1]
    heads = channels // HEADDIM
    both = channels + 2 * STATE
    chunks = count * 4
    dma = pltpu.SemaphoreType.DMA
    hbm = pl.BlockSpec(memory_space=pl.ANY)
    shape = jax.ShapeDtypeStruct
    big = [
        ((count, length, D), bf16),
        ((count, length, both), bf16),
        ((count, length, both), f32),
        ((count, length, channels), f32),
        ((count, length, channels), f32),
        ((count, length, channels), bf16),
    ]
    small = [
        ((count * 16, both), bf16),
        ((count, STATE, channels), bf16),
        ((count, length, LANES), f32),
        ((count, length, LANES), f32),
        ((count, length, LANES), f32),
        ((count, length), f32),
        ((count, length), f32),
    ]
    return pl.pallas_call(
        functools.partial(front_kernel, heads),
        out_shape=[shape(*s) for s in big + small],
        in_specs=[hbm, in_vmem, hbm, hbm, in_vmem, hbm] + [in_vmem] * 7,
        out_specs=[hbm] * len(big) + [in_vmem] * len(small),
        scratch_shapes=[
            pltpu.VMEM((count, length, D), f32),
            pltpu.VMEM((D, channels), bf16),
            pltpu.VMEM((D, 2 * STATE), bf16),
            pltpu.VMEM((D, channels), bf16),
        ]
        + [pltpu.VMEM(*s) for s in big]
        + [
            pltpu.VMEM((count * 16, both), bf16),
            pltpu.VMEM((count * 16, both), bf16),
            pltpu.VMEM((length + 16, both), f32),
            pltpu.VMEM((count, length, channels), f32),
            pltpu.VMEM((count, length, STATE), bf16),
            pltpu.VMEM((count, length, STATE), bf16),
            pltpu.VMEM((length, length), f32),
            pltpu.VMEM((length, length), f32),
            pltpu.VMEM((count, STATE, channels), f32),
            pltpu.VMEM((count, STATE, channels), bf16),
            pltpu.VMEM((count, STATE, channels), bf16),
            pltpu.VMEM((count, 8, channels), f32),
            pltpu.VMEM((count, length, LANES), f32),
            dma((3,)),
            dma((count,)),
            dma((len(big), count)),
            dma((2,)),
            dma((chunks,)),
            dma((chunks,)),
        ],
        compiler_params=params(cid),
        name="front",
    )(tokens, gain, value_weight, keyquery_weight, step_weight, gate_weight, docs, vectors, *conv, norm_gain)


def back_kernel(
    pieces_hbm,
    weight_hbm,
    gate_hbm,
    mixed_hbm,
    conv_hbm,
    linear_hbm,
    halo_ref,
    state_ref,
    steps_ref,
    cumulative_ref,
    linear_steps_ref,
    square_ref,
    rowdot_ref,
    docs_ref,
    vectors_ref,
    value_conv_ref,
    keyquery_conv_ref,
    norm_gain_ref,
    normed_out_out,
    gate_grad_out,
    values_grad_out,
    narrow_out,
    conv_grad_out,
    vector_grad_out,
    gain_grad_out,
    pieces,
    weight,
    gate,
    mixed,
    conv,
    linear,
    normed_out,
    gate_grad,
    values_grad,
    narrow,
    heads_in,
    heads_grad,
    keys,
    queries,
    scores,
    scores_grad,
    mask_bias,
    inner,
    narrow_grad,
    locals_,
    held,
    outgoing,
    passed,
    extended,
    spread_grad,
    usable_rows,
    edge,
    edge_in,
    tails,
    load_sem,
    row_sem,
    store_sem,
    edge_send,
    edge_recv,
    chain_send,
    chain_recv,
):
    n = lax.axis_size("seq")
    place = lax.axis_index("seq")
    head = lax.axis_index("head")
    ahead = n - 1 - place
    count, length, channels = gate.shape
    both = channels + 2 * STATE
    lags = value_conv_ref.shape[0]
    begin = (place * length).astype(f32)
    chunk_rows = STATE // 4
    chunks = count * 4
    groups, width = pieces.shape[0], pieces.shape[2]
    inner_total = NHEADS * HEADDIM

    loads = [
        pltpu.make_async_copy(weight_hbm, weight, load_sem.at[0]),
        pltpu.make_async_copy(pieces_hbm, pieces, load_sem.at[1]),
    ]
    for copy in loads:
        copy.start()
    row_arrays = [(gate_hbm, gate), (mixed_hbm, mixed), (conv_hbm, conv), (linear_hbm, linear)]

    def row_load(i, b):
        source, target = row_arrays[i]
        return pltpu.make_async_copy(source.at[b], target.at[b], row_sem.at[i, b])

    for b in range(count):
        for i in range(3):
            row_load(i, b).start()
    for b in range(count):
        row_load(3, b).start()

    stores = [
        (normed_out, normed_out_out),
        (gate_grad, gate_grad_out),
        (values_grad, values_grad_out),
        (narrow, narrow_out),
    ]

    def store(i, b):
        source, target = stores[i]
        return pltpu.make_async_copy(source.at[b], target.at[b], store_sem.at[i, b])

    barrier = pltpu.get_barrier_semaphore()

    @pl.when(place > 0)
    def _():
        pl.semaphore_signal(barrier, inc=1, device_id=(place - 1, head), device_id_type=MESH)

    @pl.when(place < n - 1)
    def _():
        pl.semaphore_signal(barrier, inc=1, device_id=(place + 1, head), device_id_type=MESH)

    marks = head_spread(channels)
    collect = head_gather(channels)
    step_bias = vectors_ref[0:1]
    decay_rate = -jnp.exp(vectors_ref[1:2])
    skip = spread(vectors_ref[...], marks)[2:3]
    gain_grad_out[...] = jnp.zeros_like(gain_grad_out)
    vector_grad_out[...] = jnp.zeros_like(vector_grad_out)
    conv_grad_out[...] = jnp.zeros_like(conv_grad_out)
    for copy in loads:
        copy.wait()

    def row_column(ref, b):
        per = length // LANES
        row = jnp.concatenate([ref[pl.ds(b * per + i, 1)] for i in range(per)], axis=1)
        return jnp.broadcast_to(row, (LANES, length)).T

    def widened(column, size):
        return jnp.concatenate([column] * (size // LANES), axis=1)

    def gated_norm(b):
        for i in range(3):
            row_load(i, b).wait()
        scale = lax.rsqrt(row_column(square_ref, b) * (1.0 / inner_total) + norm_eps)
        pull = scale * scale * row_column(rowdot_ref, b) * (1.0 / inner_total)
        column, _ = position_masks(docs_ref[pl.ds(b, 1)].astype(f32), begin)
        entering = spread(
            jnp.exp(cumulative_ref[b]) * (column < begin).astype(f32), marks
        )
        passed[b] = entering[length - 8 :]
        for at, size in blocks(channels):
            lanes = slice(at, at + size)
            grad_rows = jnp.zeros((length, size), f32)
            for j in range(groups):
                block = (
                    weight[lanes, j * width : (j + 1) * width]
                    if len(weight.shape) == 2
                    else weight[j, lanes]
                )
                grad_rows = grad_rows + dot_nt(pieces[j, pl.ds(pl.multiple_of(b * length, length), length)], block)
            linear_gate = gate[b, :, lanes]
            sigmoid_value = jax.nn.sigmoid(linear_gate)
            active = linear_gate * sigmoid_value
            value = mixed[b, :, lanes]
            gated = value * active
            norm_gain = norm_gain_ref[:, lanes]
            scaled = gated * widened(scale, size)
            normed_out[b, :, lanes] = (scaled * norm_gain).astype(bf16)
            gain_grad_out[:, lanes] += jnp.sum(grad_rows * scaled, axis=0, keepdims=True)
            gated_grad = widened(scale, size) * norm_gain * grad_rows - gated * widened(pull, size)
            heads_grad[b, :, lanes] = gated_grad * active
            slope = sigmoid_value * (1.0 + linear_gate * (1.0 - sigmoid_value))
            gate_grad[b, :, lanes] = (gated_grad * value * slope).astype(bf16)
            values = conv[b, :, lanes]
            heads_in[b, :, lanes] = values * jax.nn.sigmoid(values)
        store(0, b).start()
        store(1, b).start()
        values = conv[b, :, channels : channels + STATE]
        keys[b] = (values * jax.nn.sigmoid(values)).astype(bf16)
        values = conv[b, :, channels + STATE :]
        queries[b] = (values * jax.nn.sigmoid(values)).astype(bf16)
        locals_[b] = dot_tn(queries[b], (heads_grad[b] * entering).astype(bf16))

    loop(count, gated_norm)
    pl.semaphore_wait(barrier, (place > 0).astype(jnp.int32) + (place < n - 1).astype(jnp.int32))

    def chain_copy(c):
        part = (lax.div(c, 4), pl.ds(pl.multiple_of(lax.rem(c, 4) * chunk_rows, chunk_rows), chunk_rows))
        return remote(
            outgoing.at[part], held.at[part], chain_send.at[c], chain_recv.at[c], (place - 1, head)
        )

    def chain_step(c):
        b = lax.div(c, 4)
        rows = pl.ds(pl.multiple_of(lax.rem(c, 4) * chunk_rows, chunk_rows), chunk_rows)

        @pl.when(ahead > 0)
        def _():
            chain_copy(c).wait_recv()

        @pl.when(ahead == 0)
        def _():
            held[b, rows] = jnp.zeros((chunk_rows, channels), bf16)

        outgoing[b, rows] = (
            passed[b, 7:8] * held[b, rows].astype(f32) + locals_[b, rows]
        ).astype(bf16)

        @pl.when(place > 0)
        def _():
            chain_copy(c).start()

    pairs = channels // LANES
    lag_slots = 4

    def chain_slot(i):
        c = i - lag_slots * ahead

        @pl.when((c >= 0) & (c < chunks))
        def _():
            chain_step(c)

    first_half = lax.broadcasted_iota(jnp.int32, (length, LANES), 1) < HEADDIM

    def inside(b):
        docs_row = docs_ref[pl.ds(b, 1)].astype(f32)
        u = begin + lax.broadcasted_iota(jnp.int32, (length, length), 0).astype(f32)
        t = begin + lax.broadcasted_iota(jnp.int32, (length, length), 1).astype(f32)
        mask_bias[...] = jnp.where((u >= docs_row) & (u <= t), 0.0, -1e30)
        scores[...] = dot_nt(keys[b], queries[b])
        scores_grad[...] = jnp.zeros_like(scores_grad)
        cumulative = cumulative_ref[b]
        across = cumulative.T
        spread_steps = spread(steps_ref[b], marks)
        for pair in range(pairs):
            lanes = slice(pair * LANES, (pair + 1) * LANES)
            scaled = heads_in[b, :, lanes] * spread_steps[:, lanes]
            grads = heads_grad[b, :, lanes]
            low_grads = grads.astype(bf16)
            value = jnp.zeros((length, LANES), f32)
            for half in range(2):
                h = 2 * pair + half
                mine = first_half if half == 0 else ~first_half
                decay = jnp.exp(across[h : h + 1] - cumulative[:, h : h + 1] + mask_bias[...])
                mixing = (decay * scores[...]).astype(bf16)
                value = value + jnp.dot(
                    mixing, jnp.where(mine, grads, 0.0).astype(bf16), preferred_element_type=f32
                )
                pairwise = dot_nt(jnp.where(mine, scaled, 0.0).astype(bf16), low_grads)
                scores_grad[...] += decay * pairwise
            inner[b, :, lanes] = value
            chain_slot(b * (pairs + 1) + pair)
        low = scores_grad[...].astype(bf16)
        narrow_grad[b, :, :STATE] = jnp.dot(low, queries[b], preferred_element_type=f32)
        narrow_grad[b, :, STATE:] = dot_tn(low, keys[b])
        chain_slot(b * (pairs + 1) + pairs)

    loop(count, inside)
    done = count * (pairs + 1)
    extended[0:16] = jnp.zeros((16, both), f32)
    spread_grad[0:16] = jnp.zeros((16, both), f32)
    spread_grad[16 + length :] = jnp.zeros((16, both), f32)
    usable_rows[...] = jnp.zeros_like(usable_rows)
    upper = (
        lax.broadcasted_iota(jnp.int32, (length, length), 0)
        <= lax.broadcasted_iota(jnp.int32, (length, length), 1)
    ).astype(f32)
    last_row = lax.broadcasted_iota(jnp.int32, (length, LANES), 0) == length - 1

    def edge_copy(b):
        return remote(edge.at[b], edge_in.at[b], edge_send.at[b], edge_recv.at[b], (place - 1, head))

    def close(b):
        need = lag_slots * ahead + 4 * (b + 1)
        start = jnp.maximum(done, lag_slots * ahead + 4 * b)
        lax.fori_loop(start, jnp.maximum(start, need), lambda i, x: (chain_slot(i), x)[1], 0)
        column, spot = position_masks(docs_ref[pl.ds(b, 1)].astype(f32), begin)
        cumulative = cumulative_ref[b]
        steps = steps_ref[b]
        kept = (column < begin).astype(f32)
        trailing = (spot >= column[length - 1 :]).astype(f32)
        entering = jnp.exp(cumulative) * kept
        end_decay = jnp.exp(cumulative[length - 1 :] - cumulative) * trailing
        end_weight = end_decay * steps
        end_grad = held[b]
        x = heads_in[b]
        dy = heads_grad[b]
        grown = jnp.dot(keys[b], end_grad, preferred_element_type=f32)
        spread_end = spread(end_weight, marks)
        narrow_grad[b, :, :STATE] += dot_nt((x * spread_end).astype(bf16), end_grad)
        narrow_grad[b, :, STATE:] += dot_nt(
            (dy * spread(entering, marks)).astype(bf16), state_ref[b]
        )
        grad = skip * dy + spread(steps, marks) * inner[b] + spread_end * grown
        dot_out = gather_heads(dy * (mixed[b] - skip * x), collect)
        dot_inner = gather_heads(x * inner[b], collect)
        dot_end = gather_heads(x * grown, collect)
        dot_skip = gather_heads(dy * x, collect)
        through = jnp.sum(
            end_grad.astype(f32) * state_ref[b].astype(f32), axis=0, keepdims=True
        )
        passed_grad = gather_heads(jnp.broadcast_to(through, (8, channels)), collect)[:1]
        end_mix = dot_end * end_weight
        last_term = passed_grad * entering[length - 1 :] + jnp.sum(end_mix, axis=0, keepdims=True)
        cum_grad = dot_out - steps * dot_inner - end_mix + jnp.where(last_row, last_term, 0.0)
        rates_grad = jnp.dot(upper, cum_grad, precision=highest, preferred_element_type=f32)
        steps_grad = dot_inner + end_decay * dot_end + rates_grad * decay_rate
        linear_grad = steps_grad * jax.nn.sigmoid(linear_steps_ref[b] + step_bias)
        narrow[b, :, 2 * STATE :] = linear_grad.astype(bf16)
        vector_grad_out[0:1] += jnp.sum(linear_grad, axis=0, keepdims=True)
        vector_grad_out[1:2] += jnp.sum(rates_grad * steps, axis=0, keepdims=True) * decay_rate
        vector_grad_out[2:3] += jnp.sum(dot_skip, axis=0, keepdims=True)

        row_load(3, b).wait()
        extended[0:16] = halo_ref[pl.ds(pl.multiple_of(b * 16, 16), 16)].astype(f32)
        extended[16:] = linear[b].astype(f32)
        middle = slice(16, 16 + length)
        for lag in range(1, lags):
            usable_rows[lag - 1, middle] = (spot - lag >= column).astype(f32)
        for at in range(0, both, LANES):
            lanes = slice(at, at + LANES)
            values = conv[b, :, lanes]
            sigmoid_value = jax.nn.sigmoid(values)
            slope = sigmoid_value * (1.0 + values * (1.0 - sigmoid_value))
            if at < channels:
                out_grad = grad[:, lanes]
                taps, tap = value_conv_ref, lanes
            else:
                place_at = at - channels
                out_grad = narrow_grad[b, :, place_at : place_at + LANES]
                taps, tap = keyquery_conv_ref, slice(place_at, place_at + LANES)
            local = out_grad * slope
            spread_grad[middle, lanes] = local
            input_grad = taps[0:1, tap] * local
            edges = jnp.zeros((8, LANES), f32)
            conv_grad_out[0:1, lanes] += jnp.sum(local * extended[middle, lanes], axis=0, keepdims=True)
            conv_grad_out[lags : lags + 1, lanes] += jnp.sum(local, axis=0, keepdims=True)
            for lag in range(1, lags):
                mask = usable_rows[lag - 1, middle]
                conv_grad_out[lag : lag + 1, lanes] += jnp.sum(
                    local * mask * extended[16 - lag : 16 - lag + length, lanes],
                    axis=0,
                    keepdims=True,
                )
                later = slice(16 + lag, 16 + lag + length)
                input_grad = input_grad + taps[lag : lag + 1, tap] * (
                    spread_grad[later, lanes] * usable_rows[lag - 1, later]
                )
                first = slice(8 + lag, 16 + lag)
                edges = edges + taps[lag : lag + 1, tap] * (
                    spread_grad[first, lanes] * usable_rows[lag - 1, first]
                )
            edge[b, :, lanes] = edges
            tails[b, :, lanes] = input_grad[length - 16 :]
            if at < channels:
                values_grad[b, :, lanes] = input_grad.astype(bf16)
            else:
                narrow[b, :, tap] = input_grad.astype(bf16)

        @pl.when(place > 0)
        def _():
            edge_copy(b).start()

    loop(count, close)

    def finish(b):
        @pl.when(place < n - 1)
        def _():
            edge_copy(b).wait_recv()
            last = slice(length - 16, length)
            tails[b, 8:] = tails[b, 8:] + edge_in[b]
            values_grad[b, last] = tails[b, :, :channels].astype(bf16)
            narrow[b, last, : 2 * STATE] = tails[b, :, channels:].astype(bf16)

        store(2, b).start()
        store(3, b).start()

    loop(count, finish)

    @pl.when(place > 0)
    def _():
        loop(count, lambda b: edge_copy(b).wait_send())
        loop(chunks, lambda c: chain_copy(c).wait_send())

    for i in range(len(stores)):
        loop(count, lambda b, i=i: store(i, b).wait())


def back(
    pieces,
    weight,
    gate,
    mixed,
    conv,
    linear,
    halo,
    state_in,
    steps,
    cumulative,
    linear_steps,
    square_rows,
    rowdot,
    docs,
    vectors,
    value_conv_weight,
    keyquery_conv_weight,
    norm_gain,
    cid,
):
    count, length, channels = gate.shape
    both = channels + 2 * STATE
    lags = value_conv_weight.shape[0]
    weight = blocked(weight, pieces.shape[0])
    chunks = count * 4
    dma = pltpu.SemaphoreType.DMA
    hbm = pl.BlockSpec(memory_space=pl.ANY)
    shape = jax.ShapeDtypeStruct
    vmem = pltpu.VMEM
    big = [
        ((count, length, channels), bf16),
        ((count, length, channels), bf16),
        ((count, length, channels), bf16),
        ((count, length, 2 * STATE + LANES), bf16),
    ]
    small = [((8, both), f32), ((8, LANES), f32), ((1, channels), f32)]
    return pl.pallas_call(
        back_kernel,
        out_shape=[shape(*s) for s in big + small],
        in_specs=[hbm] * 6 + [in_vmem] * 12,
        out_specs=[hbm] * len(big) + [in_vmem] * len(small),
        scratch_shapes=[
            vmem(pieces.shape, bf16),
            vmem(weight.shape, bf16),
            vmem(gate.shape, f32),
            vmem(mixed.shape, f32),
            vmem(conv.shape, f32),
            vmem(linear.shape, bf16),
        ]
        + [vmem(*s) for s in big]
        + [
            vmem((count, length, channels), f32),
            vmem((count, length, channels), f32),
            vmem((count, length, STATE), bf16),
            vmem((count, length, STATE), bf16),
            vmem((length, length), f32),
            vmem((length, length), f32),
            vmem((length, length), f32),
            vmem((count, length, channels), f32),
            vmem((count, length, 2 * STATE), f32),
            vmem((count, STATE, channels), f32),
            vmem((count, STATE, channels), bf16),
            vmem((count, STATE, channels), bf16),
            vmem((count, 8, channels), f32),
            vmem((length + 16, both), f32),
            vmem((length + 32, both), f32),
            vmem((lags - 1, length + 32, LANES), f32),
            vmem((count, 8, both), f32),
            vmem((count, 8, both), f32),
            vmem((count, 16, both), f32),
            dma((2,)),
            dma((4, count)),
            dma((len(big), count)),
            dma((count,)),
            dma((count,)),
            dma((chunks,)),
            dma((chunks,)),
        ],
        compiler_params=params(cid),
        name="back",
    )(
        pieces,
        weight,
        gate,
        mixed,
        conv,
        linear,
        halo,
        state_in,
        steps,
        cumulative,
        linear_steps,
        square_rows,
        rowdot,
        docs,
        vectors,
        value_conv_weight,
        keyquery_conv_weight,
        norm_gain,
    )


def body(
    tokens,
    teacher,
    document_start,
    valid_mask,
    input_gain,
    gate_weight,
    value_weight,
    keyquery_weight,
    step_weight,
    value_conv_weight,
    value_conv_bias,
    keyquery_conv_weight,
    keyquery_conv_bias,
    step_bias,
    rate_log,
    skip_gain,
    norm_gain,
    out_weight,
):
    head_index = lax.axis_index("head")
    sequence_index = lax.axis_index("seq")
    sequence_count = tokens.shape[0]
    shard_length = tokens.shape[1]
    rows = sequence_count * shard_length
    local_heads = skip_gain.shape[0]
    local_inner = local_heads * HEADDIM
    column_count = D // lax.axis_size("head")
    column_start = head_index * column_count
    shard_begin = sequence_index * shard_length
    valid_count = jnp.sum(valid_mask.astype(f32))
    local_mask = lax.dynamic_slice_in_dim(valid_mask, shard_begin, shard_length, 1).astype(f32)
    mask_rows = (local_mask * (2.0 / (D * valid_count))).reshape(-1, LANES)
    step_pad = ((0, 0), (0, LANES - local_heads))
    vectors = jnp.pad(
        jnp.stack([step_bias, rate_log, skip_gain]), ((0, 5), (0, LANES - local_heads))
    )
    (
        normed,
        linear,
        conv_linear,
        gate_linear,
        mixed,
        gained,
        halo,
        state_in,
        steps,
        cumulative,
        steps_linear,
        square_rows,
        inverse_rows,
    ) = front(
        tokens,
        input_gain[None],
        value_weight,
        keyquery_weight,
        jnp.pad(step_weight, step_pad),
        gate_weight,
        document_start,
        vectors,
        (
            value_conv_weight,
            value_conv_bias[None],
            keyquery_conv_weight,
            keyquery_conv_bias[None],
        ),
        norm_gain[None],
        1,
    )
    conv_lags = value_conv_weight.shape[0]
    square_rows = square_rows.reshape(-1, LANES)
    gained = gained.reshape(rows, local_inner)
    token_cols = lax.dynamic_slice_in_dim(tokens, column_start, column_count, 2).reshape(rows, -1)
    teacher_rows = teacher.reshape(rows, column_count)
    output, piece_blocks, rowdot, square_total, loss_cols = out_phase(
        gained, out_weight, square_rows, token_cols, teacher_rows, mask_rows, 2
    )
    (
        normed_out,
        gate_grad,
        values_grad,
        narrow_grad,
        conv_grad,
        vector_grad,
        gain_out_grad,
    ) = back(
        piece_blocks,
        out_weight,
        gate_linear,
        mixed,
        conv_linear,
        linear,
        halo,
        state_in,
        steps,
        cumulative,
        steps_linear,
        square_total,
        rowdot,
        document_start,
        vectors,
        value_conv_weight,
        keyquery_conv_weight,
        norm_gain[None],
        3,
    )
    gate_grad = gate_grad.reshape(rows, local_inner)
    values_grad = values_grad.reshape(rows, local_inner)
    narrow_grad = narrow_grad.reshape(rows, -1)
    piece_cols = jnp.moveaxis(piece_blocks, 0, 1).reshape(rows, D)
    column_grad = dot_tn(piece_cols, normed_out.reshape(rows, local_inner)).astype(bf16)
    narrow_weight = jnp.concatenate([keyquery_weight, jnp.pad(step_weight, step_pad)], axis=-1)
    normed = normed.reshape(rows, D)
    gain_cols = lax.dynamic_slice_in_dim(input_gain, column_start, column_count, 0)
    tokens_grad, gain_columns = in_phase(
        (gate_grad, values_grad, narrow_grad),
        (gate_weight, value_weight, narrow_weight),
        normed,
        token_cols,
        output,
        teacher_rows,
        gain_cols[None],
        mask_rows,
        inverse_rows.reshape(-1, LANES),
        4,
    )
    gate_part = dot_tn(normed, gate_grad).astype(bf16)
    value_part = dot_tn(normed, values_grad).astype(bf16)
    narrow_part = dot_tn(normed, narrow_grad)
    out_total, gate_total, value_total, narrow_total = ring_sums(
        (column_grad, gate_part, value_part, narrow_part), 5
    )
    group_parts = [
        narrow_total[:, : 2 * STATE],
        conv_grad[:conv_lags, local_inner:],
        conv_grad[conv_lags, local_inner:],
        gain_columns,
        jnp.sum(loss_cols)[None],
    ]
    (
        keyquery_total,
        keyquery_conv_part,
        keyquery_offset_part,
        gain_columns,
        loss_part,
    ) = unpacked(small_sum(packed(group_parts), "head", 6), group_parts)
    line_parts = [
        conv_grad[:conv_lags, :local_inner],
        conv_grad[conv_lags, :local_inner],
        keyquery_conv_part,
        keyquery_offset_part,
        vector_grad[0, :local_heads],
        vector_grad[1, :local_heads],
        vector_grad[2, :local_heads],
        gain_out_grad[0],
        lax.dynamic_slice_in_dim(gain_columns.reshape(-1), column_start, column_count, 0),
        loss_part,
    ]
    (
        value_conv_total,
        value_offset_total,
        keyquery_conv_total,
        keyquery_offset_total,
        step_bias_total,
        rate_log_total,
        skip_gain_total,
        norm_gain_total,
        input_gain_total,
        loss_total,
    ) = unpacked(small_sum(packed(line_parts), "seq", 7), line_parts)
    return (
        output.reshape(sequence_count, shard_length, column_count),
        loss_total[0] * 0.5,
        tokens_grad.reshape(sequence_count, shard_length, column_count),
        input_gain_total / gain_cols,
        gate_total,
        value_total,
        keyquery_total,
        narrow_total[:, 2 * STATE : 2 * STATE + local_heads],
        value_conv_total,
        value_offset_total,
        keyquery_conv_total,
        keyquery_offset_total,
        step_bias_total,
        rate_log_total,
        skip_gain_total,
        norm_gain_total,
        out_total.T,
    )


def solution(mesh):
    placed = (
        P(None, "seq", None),
        P(None, "seq", "head"),
        P(None, "seq"),
        P(),
        P(),
        P(None, "head"),
        P(None, "head"),
        P(),
        P(None, "head"),
        P(None, "head"),
        P("head"),
        P(),
        P(),
        P("head"),
        P("head"),
        P("head"),
        P("head"),
        P("head", None),
    )
    return jax.shard_map(
        body,
        mesh=mesh,
        in_specs=placed,
        out_specs=(
            P(None, "seq", "head"),
            P(),
            P(None, "seq", "head"),
            P("head"),
            P("seq", "head"),
            P("seq", "head"),
            P("seq", None),
            P("seq", "head"),
            P(None, "head"),
            P("head"),
            P(),
            P(),
            P("head"),
            P("head"),
            P("head"),
            P("head"),
            P("head", "seq"),
        ),
        check_vma=False,
    )
```

```python
import functools

import jax
import jax.numpy as jnp
from jax import lax
from jax.experimental import pallas as pl
from jax.experimental.pallas import tpu as pltpu
from jax.sharding import PartitionSpec as P

D = 1536
NHEADS = 48
HEADDIM = 64
STATE = 128
LANES = 128
VMEM_LIMIT = 56 << 20

norm_eps = 1e-05
highest = lax.Precision.HIGHEST
MESH = pl.DeviceIdType.MESH
f32 = jnp.float32
bf16 = jnp.bfloat16
NT = (((1,), (1,)), ((), ()))
TN = (((0,), (0,)), ((), ()))

in_vmem = pl.BlockSpec(memory_space=pltpu.VMEM)
in_smem = pl.BlockSpec(memory_space=pltpu.SMEM)


def params(cid):
    return pltpu.CompilerParams(
        collective_id=cid, has_side_effects=True, vmem_limit_bytes=VMEM_LIMIT
    )


def remote(src, dst, send, recv, target):
    return pltpu.make_async_remote_copy(
        src_ref=src,
        dst_ref=dst,
        send_sem=send,
        recv_sem=recv,
        device_id=target,
        device_id_type=MESH,
    )


def loop(count, fn):
    lax.fori_loop(0, count, lambda i, c: (fn(i), c)[1], 0)


def dot_nt(a, b, precision=None):
    return lax.dot_general(a, b, NT, precision=precision, preferred_element_type=f32)


def dot_tn(a, b, precision=None):
    return lax.dot_general(a, b, TN, precision=precision, preferred_element_type=f32)


def ring_place(n, index):
    odd, half = lax.rem(index, 2), lax.div(index, 2)
    return half * (1 - odd) + (n - 1 - half) * odd


def ring_index(n, spot):
    late = lax.div(2 * spot, n)
    return 2 * spot * (1 - late) + (2 * (n - 1 - spot) + 1) * late


class Group:
    def __init__(self, n):
        self.n = n
        self.chips = n // 2
        self.seq = lax.axis_index("seq")
        self.me = lax.axis_index("head")
        self.chip = lax.div(self.me, 2)
        self.core = lax.rem(self.me, 2)
        self.mate = self.me + 1 - 2 * self.core

    def at(self, head):
        return (self.seq, head)

    def chip_after(self, k):
        return lax.rem(self.chip + k, self.chips)

    def chip_before(self, k):
        return lax.rem(self.chip + self.chips - k, self.chips)

    def peer(self, k):
        return 2 * self.chip_after(k) + self.core

    def other(self, k):
        return lax.rem(self.me + k, self.n)

    def greet(self):
        barrier = pltpu.get_barrier_semaphore()
        for k in range(1, self.n):
            pl.semaphore_signal(
                barrier, inc=1, device_id=self.at(self.other(k)), device_id_type=MESH
            )
        pl.semaphore_wait(barrier, self.n - 1)


def share(group, source, table, send_sem, recv_sem):
    for k in range(1, group.n):
        remote(
            source,
            table.at[group.me],
            send_sem.at[k - 1],
            recv_sem.at[group.me],
            group.at(group.other(k)),
        ).start()


def shared(group, source, table, send_sem, recv_sem):
    for k in range(1, group.n):
        sender = group.other(k)
        copy = remote(
            source, table.at[sender], send_sem.at[k - 1], recv_sem.at[sender], group.at(sender)
        )
        copy.wait_send()
        copy.wait_recv()


def row_tile(chunk):
    return pl.ds(pl.multiple_of(chunk * LANES, LANES), LANES)


def as_column(row, width):
    tile = jnp.broadcast_to(row, (LANES, row.shape[1])).T
    return jnp.concatenate([tile] * (-(-width // LANES)), axis=1)[:, :width]


def scatter_phases(group, row_block, part, mate_in, chip_out, chip_in, sems):
    mate_send, mate_recv, chip_send, chip_recv = sems

    def mate_copy(c, x):
        return remote(
            part.at[2 * x + 1 - group.core, row_block(c)],
            mate_in.at[x, row_block(c)],
            mate_send.at[x, c],
            mate_recv.at[x, c],
            group.at(group.mate),
        )

    def chip_copy(c, k):
        return remote(
            chip_out.at[k - 1, row_block(c)],
            chip_in.at[k - 1, row_block(c)],
            chip_send.at[k - 1, c],
            chip_recv.at[k - 1, c],
            group.at(group.peer(k)),
        )

    def start_mate(c):
        for x in range(group.chips):
            mate_copy(c, x).start()

    def start_chip(c):
        for x in range(group.chips):
            mate_copy(c, x).wait_recv()
        for k in range(1, group.chips):
            x = group.chip_after(k)
            both = part[2 * x + group.core, row_block(c)].astype(f32) + mate_in[
                x, row_block(c)
            ].astype(f32)
            chip_out[k - 1, row_block(c)] = both.astype(bf16)
            chip_copy(c, k).start()

    def total(c):
        value = part[group.me, row_block(c)].astype(f32) + mate_in[
            group.chip, row_block(c)
        ].astype(f32)
        for k in range(1, group.chips):
            chip_copy(c, k).wait_recv()
            value = value + chip_in[k - 1, row_block(c)].astype(f32)
        return value

    def finish(c):
        for x in range(group.chips):
            mate_copy(c, x).wait_send()
        for k in range(1, group.chips):
            chip_copy(c, k).wait_send()

    return start_mate, start_chip, total, finish


def out_kernel(
    n,
    gated_ref,
    weight_ref,
    square_ref,
    tokens_hbm,
    teacher_hbm,
    mask_ref,
    output_ref,
    grad_ref,
    rowdot_ref,
    squared_ref,
    loss_ref,
    tokens_out,
    tokens_ref,
    teacher_ref,
    part,
    mate_in,
    chip_out,
    chip_in,
    gathered,
    squares,
    dots,
    dot_out,
    mate_send,
    mate_recv,
    chip_send,
    chip_recv,
    gm_send,
    gm_recv,
    gc_send,
    gc_recv,
    gf_send,
    gf_recv,
    sq_send,
    sq_recv,
    rd_send,
    rd_recv,
    load_sem,
):
    group = Group(n)
    count, length, width = tokens_ref.shape
    if tokens_hbm.shape[2] == width:
        token_columns = tokens_hbm
    else:
        start = pl.multiple_of(group.me * width, LANES)
        token_columns = tokens_hbm.at[:, :, pl.ds(start, width)]
    token_load = pltpu.make_async_copy(token_columns, tokens_ref, load_sem.at[0])
    token_load.start()
    teacher_load = pltpu.make_async_copy(teacher_hbm, teacher_ref, load_sem.at[1])
    teacher_load.start()
    group.greet()
    chunks = gated_ref.shape[0] // LANES
    per = length // LANES

    def rows_in(c):
        return lax.div(c, per), pl.ds(pl.multiple_of(lax.rem(c, per) * LANES, LANES), LANES)

    share(group, square_ref, squares, sq_send, sq_recv)
    start_mate, start_chip, total, finish = scatter_phases(
        group, row_tile, part, mate_in, chip_out, chip_in, (mate_send, mate_recv, chip_send, chip_recv)
    )

    def product(c):
        rows = gated_ref[row_tile(c)]
        for j in range(n):
            block = (
                weight_ref[:, j * width : (j + 1) * width] if len(weight_ref.shape) == 2 else weight_ref[j]
            )
            part[j, row_tile(c)] = jnp.dot(rows, block, preferred_element_type=f32).astype(bf16)
        start_mate(c)

    loop(chunks, product)
    loop(chunks, start_chip)
    shared(group, square_ref, squares, sq_send, sq_recv)
    squares[group.me] = square_ref[...]
    loss_ref[...] = jnp.zeros_like(loss_ref)

    def to_mate(c):
        block = gathered.at[group.me, row_tile(c)]
        return remote(block, block, gm_send.at[c], gm_recv.at[c], group.at(group.mate))

    def to_chip(c, k):
        block = gathered.at[group.me, row_tile(c)]
        return remote(
            block, block, gc_send.at[k - 1, c], gc_recv.at[k - 1, c], group.at(group.peer(k))
        )

    def forward(c, k):
        block = gathered.at[2 * group.chip_before(k) + group.core, row_tile(c)]
        return remote(
            block, block, gf_send.at[k - 1, c], gf_recv.at[k - 1, c], group.at(group.mate)
        )

    token_load.wait()
    teacher_load.wait()
    token_store = pltpu.make_async_copy(tokens_ref, tokens_out, load_sem.at[0])
    token_store.start()

    def rest(c):
        squared = squares[0, pl.ds(c, 1)]
        for j in range(1, n):
            squared = squared + squares[j, pl.ds(c, 1)]
        squared_ref[pl.ds(c, 1)] = squared
        scale = lax.rsqrt(squared * (1.0 / (NHEADS * HEADDIM)) + norm_eps)
        branch = total(c) * as_column(scale, width)
        output = tokens_ref[rows_in(c)] + branch
        output_ref[row_tile(c)] = output
        difference = output - teacher_ref[rows_in(c)]
        weighted = difference * as_column(mask_ref[pl.ds(c, 1)], width)
        low = weighted.astype(bf16)
        gathered[group.me, row_tile(c)] = low
        to_mate(c).start()
        for k in range(1, group.chips):
            to_chip(c, k).start()
        loss_ref[...] += jnp.sum(weighted * difference, axis=0, keepdims=True)
        dot_out[pl.ds(c, 1)] = rows_of(low.astype(f32) * branch)

    loop(chunks, rest)
    share(group, dot_out, dots, rd_send, rd_recv)

    def pass_on(c):
        for k in range(1, group.chips):
            to_chip(c, k).wait_recv()
            forward(c, k).start()

    loop(chunks, pass_on)

    def end(c):
        to_mate(c).wait()
        for k in range(1, group.chips):
            to_chip(c, k).wait_send()
            forward(c, k).wait()
        finish(c)
        for j in range(n):
            grad_ref[j, row_tile(c)] = gathered[j, row_tile(c)]

    loop(chunks, end)
    shared(group, dot_out, dots, rd_send, rd_recv)
    row_sum = dot_out[...]
    for k in range(1, n):
        row_sum = row_sum + dots[group.other(k)]
    rowdot_ref[...] = row_sum
    token_store.wait()


def scatter_scratch(n, rows, width, chunks):
    chips = n // 2
    dma = pltpu.SemaphoreType.DMA
    return [
        pltpu.VMEM((n, rows, width), bf16),
        pltpu.VMEM((chips, rows, width), bf16),
        pltpu.VMEM((chips - 1, rows, width), bf16),
        pltpu.VMEM((chips - 1, rows, width), bf16),
    ], [dma((chips, chunks)), dma((chips, chunks)), dma((chips - 1, chunks)), dma((chips - 1, chunks))]


def blocked(weight, n):
    width = weight.shape[1] // n
    if width % LANES == 0:
        return weight
    return jnp.moveaxis(weight.reshape(weight.shape[0], n, width), 1, 0)


def out_phase(gated, weight, square_rows, tokens, teacher, mask_rows, cid):
    n = lax.axis_size("head")
    count, length, width = teacher.shape
    rows = count * length
    chips, chunks = n // 2, rows // LANES
    if width % LANES:
        tokens = lax.dynamic_slice_in_dim(tokens, lax.axis_index("head") * width, width, 2)
    buffers, sems = scatter_scratch(n, rows, width, chunks)
    dma = pltpu.SemaphoreType.DMA
    hbm = pl.BlockSpec(memory_space=pl.ANY)
    return pl.pallas_call(
        functools.partial(out_kernel, n),
        out_shape=[
            jax.ShapeDtypeStruct((rows, width), f32),
            jax.ShapeDtypeStruct((n, rows, width), bf16),
            jax.ShapeDtypeStruct((chunks, LANES), f32),
            jax.ShapeDtypeStruct((chunks, LANES), f32),
            jax.ShapeDtypeStruct((1, width), f32),
            jax.ShapeDtypeStruct((count, length, width), f32),
        ],
        in_specs=[in_vmem] * 3 + [hbm] * 2 + [in_vmem],
        out_specs=[in_vmem] * 5 + [hbm],
        scratch_shapes=[pltpu.VMEM((count, length, width), f32)] * 2
        + buffers
        + [
            pltpu.VMEM((n, rows, width), bf16),
            pltpu.VMEM((n, chunks, LANES), f32),
            pltpu.VMEM((n, chunks, LANES), f32),
            pltpu.VMEM((chunks, LANES), f32),
        ]
        + sems
        + [
            dma((chunks,)),
            dma((chunks,)),
            dma((chips - 1, chunks)),
            dma((chips - 1, chunks)),
            dma((chips - 1, chunks)),
            dma((chips - 1, chunks)),
            dma((n - 1,)),
            dma((n,)),
            dma((n - 1,)),
            dma((n,)),
            dma((2,)),
        ],
        compiler_params=params(cid),
        name="out_phase",
    )(gated, blocked(weight, n), square_rows, tokens, teacher, mask_rows)


def blocks(width, size=256):
    return [(at, min(size, width - at)) for at in range(0, width, size)]


def fold_lanes(values):
    rows, width = values.shape
    if width % LANES:
        fill = jnp.zeros((rows, LANES - width % LANES), values.dtype)
        values = jnp.concatenate([values, fill], axis=1)
    total = values[:, :LANES]
    for at in range(LANES, width, LANES):
        total = total + values[:, at : at + LANES]
    return total


def rows_of(values):
    return jnp.sum(fold_lanes(values).T, axis=0, keepdims=True)


def head_spread(channels):
    row = lax.broadcasted_iota(jnp.int32, (LANES, channels), 0)
    head = lax.broadcasted_iota(jnp.int32, (LANES, channels), 1) // HEADDIM
    return ((row % 16 == head) & (row < 48)).astype(f32).astype(bf16)


def head_gather(channels):
    head = lax.broadcasted_iota(jnp.int32, (channels, LANES), 0) // HEADDIM
    return (lax.broadcasted_iota(jnp.int32, (channels, LANES), 1) == head).astype(f32).astype(bf16)


def spread(values, marks):
    lane = lax.broadcasted_iota(jnp.int32, values.shape, 1)
    values = jnp.where(lane < 16, values, 0.0)
    high = values.astype(bf16).astype(f32)
    left = values - high
    middle = left.astype(bf16).astype(f32)
    low = (left - middle).astype(bf16).astype(f32)
    three = high + pltpu.roll(middle, 16, 1) + pltpu.roll(low, 32, 1)
    return jnp.dot(three.astype(bf16), marks, preferred_element_type=f32)


def gather_heads(values, marks):
    high = values.astype(bf16)
    low = (values - high.astype(f32)).astype(bf16)
    return jnp.dot(high, marks, preferred_element_type=f32) + jnp.dot(
        low, marks, preferred_element_type=f32
    )


def softplus(x):
    y = jnp.exp(-jnp.abs(x))
    small = y * (1.0 - y * (1.0 / 2 - y * (1.0 / 3 - y * (1.0 / 4 - y * (1.0 / 5)))))
    return jnp.maximum(x, 0.0) + jnp.where(y < 0.03, small, jnp.log(1.0 + y))


def lane_row(ref):
    row = ref[...][None, :]
    return jnp.concatenate([row, jnp.zeros((1, LANES - row.shape[1]), f32)], axis=1)


def long_row(ref, b, length):
    per = length // LANES
    return jnp.concatenate([ref[pl.ds(b * per + i, 1)] for i in range(per)], axis=1)


def spread_row(row, marks):
    return spread(jnp.broadcast_to(row, (8, LANES)), marks)[:1]


def position_masks(docs_row, begin):
    length = docs_row.shape[1]
    column = jnp.broadcast_to(docs_row, (LANES, length)).T
    place = begin + lax.broadcasted_iota(jnp.int32, (length, LANES), 0).astype(f32)
    return column, place


def front_kernel(
    heads,
    tokens_hbm,
    gain_ref,
    value_hbm,
    keyquery_hbm,
    step_ref,
    gate_hbm,
    docs_ref,
    step_bias_ref,
    rate_log_ref,
    skip_ref,
    value_conv_ref,
    value_offset_ref,
    keyquery_conv_ref,
    keyquery_offset_ref,
    norm_gain_ref,
    normed_out,
    linear_out,
    conv_out,
    gate_out,
    mixed_out,
    gained_out,
    halo_out,
    state_out,
    steps_out,
    cumulative_out,
    linear_steps_out,
    square_out,
    inverse_out,
    tokens,
    value_weight,
    keyquery_weight,
    gate_weight,
    normed,
    linear,
    conv,
    gate,
    mixed,
    gained,
    tail,
    halo,
    extended,
    heads_in,
    keys,
    queries,
    scores,
    mask_bias,
    locals_,
    held,
    outgoing,
    passed,
    entering,
    load_sem,
    token_sem,
    store_sem,
    halo_sem,
    chain_send,
    chain_recv,
):
    n = lax.axis_size("seq")
    place = lax.axis_index("seq")
    head = lax.axis_index("head")
    count, length, _ = tokens.shape
    channels = value_weight.shape[1]
    both = channels + 2 * STATE
    lags = value_conv_ref.shape[0]
    begin = (place * length).astype(f32)
    chunk_rows = STATE // 4
    chunks = count * 4

    loads = [
        pltpu.make_async_copy(value_hbm, value_weight, load_sem.at[0]),
        pltpu.make_async_copy(keyquery_hbm, keyquery_weight, load_sem.at[1]),
        pltpu.make_async_copy(gate_hbm, gate_weight, load_sem.at[2]),
    ]

    def token_load(b):
        return pltpu.make_async_copy(tokens_hbm.at[b], tokens.at[b], token_sem.at[b])

    for b in range(count):
        token_load(b).start()
        if b == 0:
            loads[0].start()
            loads[1].start()
    loads[2].start()

    stores = [
        (normed, normed_out),
        (linear, linear_out),
        (conv, conv_out),
        (gate, gate_out),
        (mixed, mixed_out),
        (gained, gained_out),
    ]

    def store(i, b):
        source, target = stores[i]
        return pltpu.make_async_copy(source.at[b], target.at[b], store_sem.at[i, b])

    barrier = pltpu.get_barrier_semaphore()

    @pl.when(place > 0)
    def _():
        pl.semaphore_signal(barrier, inc=1, device_id=(place - 1, head), device_id_type=MESH)

    @pl.when(place < n - 1)
    def _():
        pl.semaphore_signal(barrier, inc=1, device_id=(place + 1, head), device_id_type=MESH)

    def norm(b):
        token_load(b).wait()
        x = tokens[b]
        inverse = lax.rsqrt(jnp.mean(x * x, axis=-1, keepdims=True) + norm_eps)
        normed[b] = (x * inverse * gain_ref[...][None, :]).astype(bf16)
        inverse_out[pl.ds(b, 1)] = jnp.broadcast_to(inverse, (length, LANES)).T[:1]
        store(0, b).start()

    loop(count, norm)
    loads[0].wait()
    loads[1].wait()

    last = jnp.concatenate([normed[b, length - 16 :] for b in range(count)], axis=0)
    for at, width in blocks(channels):
        tail[:, at : at + width] = jnp.dot(
            last, value_weight[:, at : at + width], preferred_element_type=f32
        ).astype(bf16)
    tail[:, channels:] = jnp.dot(last, keyquery_weight[...], preferred_element_type=f32).astype(bf16)
    pl.semaphore_wait(barrier, (place > 0).astype(jnp.int32) + (place < n - 1).astype(jnp.int32))
    halo_copy = remote(tail, halo, halo_sem.at[0], halo_sem.at[1], (place + 1, head))

    @pl.when(place < n - 1)
    def _():
        halo_copy.start()

    def project(b):
        rows = normed[b]
        for at, width in blocks(channels):
            linear[b, :, at : at + width] = jnp.dot(
                rows, value_weight[:, at : at + width], preferred_element_type=f32
            ).astype(bf16)
        linear[b, :, channels:] = jnp.dot(
            rows, keyquery_weight[...], preferred_element_type=f32
        ).astype(bf16)
        narrow_steps = dot_nt(rows, step_ref[...])
        linear_steps_out[b] = jnp.concatenate(
            [narrow_steps, jnp.zeros((length, LANES - heads), f32)], axis=1
        )
        store(1, b).start()

    loop(count, project)

    @pl.when(place > 0)
    def _():
        halo_copy.wait_recv()

    @pl.when(place == 0)
    def _():
        halo[...] = jnp.zeros_like(halo)

    halo_out[...] = halo[...]
    marks = head_spread(channels)
    step_bias = lane_row(step_bias_ref)
    decay_rate = -jnp.exp(lane_row(rate_log_ref))
    skip = spread_row(lane_row(skip_ref), marks)
    triangle = (
        lax.broadcasted_iota(jnp.int32, (length, length), 0)
        >= lax.broadcasted_iota(jnp.int32, (length, length), 1)
    ).astype(f32)

    def states(b):
        column, spot = position_masks(docs_ref[pl.ds(b, 1)].astype(f32), begin)
        extended[0:16] = halo[pl.ds(pl.multiple_of(b * 16, 16), 16)].astype(f32)
        extended[16:] = linear[b].astype(f32)
        usable = [None] + [(spot - lag >= column).astype(f32) for lag in range(1, lags)]
        for at in range(0, both, LANES):
            if at < channels:
                weight, offset, place_at = value_conv_ref, value_offset_ref, at
            else:
                weight, offset, place_at = keyquery_conv_ref, keyquery_offset_ref, at - channels
            lanes = slice(place_at, place_at + LANES)
            value = offset[lanes][None, :] + weight[0:1, lanes] * extended[16:, at : at + LANES]
            for lag in range(1, lags):
                value = value + weight[lag : lag + 1, lanes] * (
                    extended[16 - lag : 16 - lag + length, at : at + LANES] * usable[lag]
                )
            conv[b, :, at : at + LANES] = value
            active = value * jax.nn.sigmoid(value)
            if at < channels:
                heads_in[b, :, at : at + LANES] = active
            elif at < channels + STATE:
                keys[b] = active.astype(bf16)
            else:
                queries[b] = active.astype(bf16)
        store(2, b).start()
        steps = softplus(linear_steps_out[b] + step_bias)
        cumulative = jnp.dot(
            triangle, steps * decay_rate, precision=highest, preferred_element_type=f32
        )
        steps_out[b] = steps
        cumulative_out[b] = cumulative
        kept = (column < begin).astype(f32)
        trailing = (spot >= column[length - 1 :]).astype(f32)
        entering[b] = jnp.exp(cumulative) * kept
        end_weight = jnp.exp(cumulative[length - 1 :] - cumulative) * trailing * steps
        weighted = (heads_in[b] * spread(end_weight, marks)).astype(bf16)
        locals_[b] = dot_tn(keys[b], weighted)
        last_entering = entering[b, length - 8 :]
        passed[b] = spread(last_entering, marks)

    loop(count, states)

    def chain_copy(c):
        part = (lax.div(c, 4), pl.ds(pl.multiple_of(lax.rem(c, 4) * chunk_rows, chunk_rows), chunk_rows))
        return remote(
            outgoing.at[part], held.at[part], chain_send.at[c], chain_recv.at[c], (place + 1, head)
        )

    def chain_step(c):
        b = lax.div(c, 4)
        rows = pl.ds(pl.multiple_of(lax.rem(c, 4) * chunk_rows, chunk_rows), chunk_rows)

        @pl.when(place > 0)
        def _():
            chain_copy(c).wait_recv()

        @pl.when(place == 0)
        def _():
            held[b, rows] = jnp.zeros((chunk_rows, channels), bf16)

        outgoing[b, rows] = (
            passed[b, 7:8] * held[b, rows].astype(f32) + locals_[b, rows]
        ).astype(bf16)

        @pl.when(place < n - 1)
        def _():
            chain_copy(c).start()

    pairs = channels // LANES
    lag_slots = 5
    slots = chunks + lag_slots * (n - 1)

    def chain_slot(i):
        c = i - lag_slots * place

        @pl.when((c >= 0) & (c < chunks))
        def _():
            chain_step(c)

    first_half = lax.broadcasted_iota(jnp.int32, (length, LANES), 1) < HEADDIM
    loads[2].wait()

    def inside(b):
        column, spot = position_masks(docs_ref[pl.ds(b, 1)].astype(f32), begin)
        wide = jnp.concatenate([column] * (length // LANES), axis=1)
        t = begin + lax.broadcasted_iota(jnp.int32, (length, length), 0).astype(f32)
        u = begin + lax.broadcasted_iota(jnp.int32, (length, length), 1).astype(f32)
        mask_bias[...] = jnp.where((u >= wide) & (u <= t), 0.0, -1e30)
        scores[...] = dot_nt(queries[b], keys[b])
        cumulative = cumulative_out[b]
        across = cumulative.T
        spread_steps = spread(steps_out[b], marks)
        for pair in range(pairs):
            lanes = slice(pair * LANES, (pair + 1) * LANES)
            scaled = heads_in[b, :, lanes] * spread_steps[:, lanes]
            value = jnp.zeros((length, LANES), f32)
            for half in range(2):
                h = 2 * pair + half
                decay = jnp.exp(cumulative[:, h : h + 1] - across[h : h + 1] + mask_bias[...])
                mixing = (decay * scores[...]).astype(bf16)
                mine = jnp.where(first_half if half == 0 else ~first_half, scaled, 0.0).astype(bf16)
                value = value + jnp.dot(mixing, mine, preferred_element_type=f32)
            mixed[b, :, lanes] = value
            chain_slot(b * (pairs + 1) + pair)
        rows = normed[b]
        for at, width in blocks(channels):
            gate[b, :, at : at + width] = jnp.dot(
                rows, gate_weight[:, at : at + width], preferred_element_type=f32
            )
        store(3, b).start()
        chain_slot(b * (pairs + 1) + pairs)

    loop(count, inside)
    done = count * (pairs + 1)
    if slots > done:
        loop(slots - done, lambda i: chain_slot(i + done))

    def close(b):
        state_out[b] = held[b]
        projected = jnp.dot(queries[b], held[b], preferred_element_type=f32)
        value = mixed[b] + spread(entering[b], marks) * projected + skip * heads_in[b]
        mixed[b] = value
        store(4, b).start()
        linear_gate = gate[b]
        gated = value * (linear_gate * jax.nn.sigmoid(linear_gate))
        gained[b] = (gated * norm_gain_ref[...][None, :]).astype(bf16)
        store(5, b).start()
        squared = rows_of(gated * gated)
        for i in range(length // LANES):
            square_out[pl.ds(b * (length // LANES) + i, 1)] = squared[
                :, i * LANES : (i + 1) * LANES
            ]

    loop(count, close)

    @pl.when(place < n - 1)
    def _():
        halo_copy.wait_send()
        loop(chunks, lambda c: chain_copy(c).wait_send())

    for i in range(len(stores)):
        loop(count, lambda b, i=i: store(i, b).wait())


def front(tokens, gain, value_weight, keyquery_weight, step_weight, gate_weight, docs, vectors, conv, norm_gain, cid):
    count, length, _ = tokens.shape
    channels = value_weight.shape[1]
    heads = channels // HEADDIM
    both = channels + 2 * STATE
    chunks = count * 4
    dma = pltpu.SemaphoreType.DMA
    hbm = pl.BlockSpec(memory_space=pl.ANY)
    shape = jax.ShapeDtypeStruct
    big = [
        ((count, length, D), bf16),
        ((count, length, both), bf16),
        ((count, length, both), f32),
        ((count, length, channels), f32),
        ((count, length, channels), f32),
        ((count, length, channels), bf16),
    ]
    small = [
        ((count * 16, both), bf16),
        ((count, STATE, channels), bf16),
        ((count, length, LANES), f32),
        ((count, length, LANES), f32),
        ((count, length, LANES), f32),
        ((count * length // LANES, LANES), f32),
        ((count, length), f32),
    ]
    return pl.pallas_call(
        functools.partial(front_kernel, heads),
        out_shape=[shape(*s) for s in big + small],
        in_specs=[hbm, in_vmem, hbm, hbm, in_vmem, hbm] + [in_vmem] * 9,
        out_specs=[hbm] * len(big) + [in_vmem] * len(small),
        scratch_shapes=[
            pltpu.VMEM((count, length, D), f32),
            pltpu.VMEM((D, channels), bf16),
            pltpu.VMEM((D, 2 * STATE), bf16),
            pltpu.VMEM((D, channels), bf16),
        ]
        + [pltpu.VMEM(*s) for s in big]
        + [
            pltpu.VMEM((count * 16, both), bf16),
            pltpu.VMEM((count * 16, both), bf16),
            pltpu.VMEM((length + 16, both), f32),
            pltpu.VMEM((count, length, channels), f32),
            pltpu.VMEM((count, length, STATE), bf16),
            pltpu.VMEM((count, length, STATE), bf16),
            pltpu.VMEM((length, length), f32),
            pltpu.VMEM((length, length), f32),
            pltpu.VMEM((count, STATE, channels), f32),
            pltpu.VMEM((count, STATE, channels), bf16),
            pltpu.VMEM((count, STATE, channels), bf16),
            pltpu.VMEM((count, 8, channels), f32),
            pltpu.VMEM((count, length, LANES), f32),
            dma((3,)),
            dma((count,)),
            dma((len(big), count)),
            dma((2,)),
            dma((chunks,)),
            dma((chunks,)),
        ],
        compiler_params=params(cid),
        name="front",
    )(tokens, gain, value_weight, keyquery_weight, step_weight, gate_weight, docs, *vectors, *conv, norm_gain)


def back_kernel(
    pieces_hbm,
    weight_hbm,
    gate_hbm,
    mixed_hbm,
    conv_hbm,
    linear_hbm,
    halo_ref,
    state_ref,
    steps_ref,
    cumulative_ref,
    linear_steps_ref,
    square_ref,
    rowdot_ref,
    docs_ref,
    step_bias_ref,
    rate_log_ref,
    skip_ref,
    value_conv_ref,
    keyquery_conv_ref,
    norm_gain_ref,
    normed_out_out,
    gate_grad_out,
    values_grad_out,
    narrow_out,
    conv_grad_out,
    vector_grad_out,
    gain_grad_out,
    pieces,
    weight,
    gate,
    mixed,
    conv,
    linear,
    normed_out,
    gate_grad,
    values_grad,
    narrow,
    heads_in,
    heads_grad,
    keys,
    queries,
    scores,
    scores_grad,
    mask_bias,
    inner,
    narrow_grad,
    locals_,
    held,
    outgoing,
    passed,
    extended,
    spread_grad,
    usable_rows,
    edge,
    edge_in,
    tails,
    load_sem,
    row_sem,
    store_sem,
    edge_send,
    edge_recv,
    chain_send,
    chain_recv,
):
    n = lax.axis_size("seq")
    place = lax.axis_index("seq")
    head = lax.axis_index("head")
    ahead = n - 1 - place
    count, length, channels = gate.shape
    both = channels + 2 * STATE
    lags = value_conv_ref.shape[0]
    begin = (place * length).astype(f32)
    chunk_rows = STATE // 4
    chunks = count * 4
    groups, width = pieces.shape[0], pieces.shape[2]
    inner_total = NHEADS * HEADDIM

    loads = [
        pltpu.make_async_copy(weight_hbm, weight, load_sem.at[0]),
        pltpu.make_async_copy(pieces_hbm, pieces, load_sem.at[1]),
    ]
    for copy in loads:
        copy.start()
    row_arrays = [(gate_hbm, gate), (mixed_hbm, mixed), (conv_hbm, conv), (linear_hbm, linear)]

    def row_load(i, b):
        source, target = row_arrays[i]
        return pltpu.make_async_copy(source.at[b], target.at[b], row_sem.at[i, b])

    for b in range(count):
        for i in range(3):
            row_load(i, b).start()
    for b in range(count):
        row_load(3, b).start()

    stores = [
        (normed_out, normed_out_out),
        (gate_grad, gate_grad_out),
        (values_grad, values_grad_out),
        (narrow, narrow_out),
    ]

    def store(i, b):
        source, target = stores[i]
        return pltpu.make_async_copy(source.at[b], target.at[b], store_sem.at[i, b])

    barrier = pltpu.get_barrier_semaphore()

    @pl.when(place > 0)
    def _():
        pl.semaphore_signal(barrier, inc=1, device_id=(place - 1, head), device_id_type=MESH)

    @pl.when(place < n - 1)
    def _():
        pl.semaphore_signal(barrier, inc=1, device_id=(place + 1, head), device_id_type=MESH)

    marks = head_spread(channels)
    collect = head_gather(channels)
    step_bias = lane_row(step_bias_ref)
    decay_rate = -jnp.exp(lane_row(rate_log_ref))
    skip = spread_row(lane_row(skip_ref), marks)
    gain_grad_out[...] = jnp.zeros_like(gain_grad_out)
    vector_grad_out[...] = jnp.zeros_like(vector_grad_out)
    conv_grad_out[...] = jnp.zeros_like(conv_grad_out)
    for copy in loads:
        copy.wait()

    def row_column(ref, b):
        return jnp.broadcast_to(long_row(ref, b, length), (LANES, length)).T

    def widened(column, size):
        return jnp.concatenate([column] * (size // LANES), axis=1)

    def gated_norm(b):
        for i in range(3):
            row_load(i, b).wait()
        scale = lax.rsqrt(row_column(square_ref, b) * (1.0 / inner_total) + norm_eps)
        pull = scale * scale * row_column(rowdot_ref, b) * (1.0 / inner_total)
        column, _ = position_masks(docs_ref[pl.ds(b, 1)].astype(f32), begin)
        entering = spread(
            jnp.exp(cumulative_ref[b]) * (column < begin).astype(f32), marks
        )
        passed[b] = entering[length - 8 :]
        for at, size in blocks(channels):
            lanes = slice(at, at + size)
            grad_rows = jnp.zeros((length, size), f32)
            for j in range(groups):
                block = (
                    weight[lanes, j * width : (j + 1) * width]
                    if len(weight.shape) == 2
                    else weight[j, lanes]
                )
                grad_rows = grad_rows + dot_nt(pieces[j, pl.ds(pl.multiple_of(b * length, length), length)], block)
            linear_gate = gate[b, :, lanes]
            sigmoid_value = jax.nn.sigmoid(linear_gate)
            active = linear_gate * sigmoid_value
            value = mixed[b, :, lanes]
            gated = value * active
            norm_gain = norm_gain_ref[lanes][None, :]
            scaled = gated * widened(scale, size)
            normed_out[b, :, lanes] = (scaled * norm_gain).astype(bf16)
            gain_grad_out[:, lanes] += jnp.sum(grad_rows * scaled, axis=0, keepdims=True)
            gated_grad = widened(scale, size) * norm_gain * grad_rows - gated * widened(pull, size)
            heads_grad[b, :, lanes] = gated_grad * active
            slope = sigmoid_value * (1.0 + linear_gate * (1.0 - sigmoid_value))
            gate_grad[b, :, lanes] = (gated_grad * value * slope).astype(bf16)
            values = conv[b, :, lanes]
            heads_in[b, :, lanes] = values * jax.nn.sigmoid(values)
        store(0, b).start()
        store(1, b).start()
        values = conv[b, :, channels : channels + STATE]
        keys[b] = (values * jax.nn.sigmoid(values)).astype(bf16)
        values = conv[b, :, channels + STATE :]
        queries[b] = (values * jax.nn.sigmoid(values)).astype(bf16)
        locals_[b] = dot_tn(queries[b], (heads_grad[b] * entering).astype(bf16))

    loop(count, gated_norm)
    pl.semaphore_wait(barrier, (place > 0).astype(jnp.int32) + (place < n - 1).astype(jnp.int32))

    def chain_copy(c):
        part = (lax.div(c, 4), pl.ds(pl.multiple_of(lax.rem(c, 4) * chunk_rows, chunk_rows), chunk_rows))
        return remote(
            outgoing.at[part], held.at[part], chain_send.at[c], chain_recv.at[c], (place - 1, head)
        )

    def chain_step(c):
        b = lax.div(c, 4)
        rows = pl.ds(pl.multiple_of(lax.rem(c, 4) * chunk_rows, chunk_rows), chunk_rows)

        @pl.when(ahead > 0)
        def _():
            chain_copy(c).wait_recv()

        @pl.when(ahead == 0)
        def _():
            held[b, rows] = jnp.zeros((chunk_rows, channels), bf16)

        outgoing[b, rows] = (
            passed[b, 7:8] * held[b, rows].astype(f32) + locals_[b, rows]
        ).astype(bf16)

        @pl.when(place > 0)
        def _():
            chain_copy(c).start()

    pairs = channels // LANES
    lag_slots = 4

    def chain_slot(i):
        c = i - lag_slots * ahead

        @pl.when((c >= 0) & (c < chunks))
        def _():
            chain_step(c)

    first_half = lax.broadcasted_iota(jnp.int32, (length, LANES), 1) < HEADDIM

    def inside(b):
        docs_row = docs_ref[pl.ds(b, 1)].astype(f32)
        u = begin + lax.broadcasted_iota(jnp.int32, (length, length), 0).astype(f32)
        t = begin + lax.broadcasted_iota(jnp.int32, (length, length), 1).astype(f32)
        mask_bias[...] = jnp.where((u >= docs_row) & (u <= t), 0.0, -1e30)
        scores[...] = dot_nt(keys[b], queries[b])
        scores_grad[...] = jnp.zeros_like(scores_grad)
        cumulative = cumulative_ref[b]
        across = cumulative.T
        spread_steps = spread(steps_ref[b], marks)
        for pair in range(pairs):
            lanes = slice(pair * LANES, (pair + 1) * LANES)
            scaled = heads_in[b, :, lanes] * spread_steps[:, lanes]
            grads = heads_grad[b, :, lanes]
            low_grads = grads.astype(bf16)
            value = jnp.zeros((length, LANES), f32)
            for half in range(2):
                h = 2 * pair + half
                mine = first_half if half == 0 else ~first_half
                decay = jnp.exp(across[h : h + 1] - cumulative[:, h : h + 1] + mask_bias[...])
                mixing = (decay * scores[...]).astype(bf16)
                value = value + jnp.dot(
                    mixing, jnp.where(mine, grads, 0.0).astype(bf16), preferred_element_type=f32
                )
                pairwise = dot_nt(jnp.where(mine, scaled, 0.0).astype(bf16), low_grads)
                scores_grad[...] += decay * pairwise
            inner[b, :, lanes] = value
            chain_slot(b * (pairs + 1) + pair)
        low = scores_grad[...].astype(bf16)
        narrow_grad[b, :, :STATE] = jnp.dot(low, queries[b], preferred_element_type=f32)
        narrow_grad[b, :, STATE:] = dot_tn(low, keys[b])
        chain_slot(b * (pairs + 1) + pairs)

    loop(count, inside)
    done = count * (pairs + 1)
    extended[0:16] = jnp.zeros((16, both), f32)
    spread_grad[0:16] = jnp.zeros((16, both), f32)
    spread_grad[16 + length :] = jnp.zeros((16, both), f32)
    usable_rows[...] = jnp.zeros_like(usable_rows)
    upper = (
        lax.broadcasted_iota(jnp.int32, (length, length), 0)
        <= lax.broadcasted_iota(jnp.int32, (length, length), 1)
    ).astype(f32)
    last_row = lax.broadcasted_iota(jnp.int32, (length, LANES), 0) == length - 1

    def edge_copy(b):
        return remote(edge.at[b], edge_in.at[b], edge_send.at[b], edge_recv.at[b], (place - 1, head))

    def close(b):
        need = lag_slots * ahead + 4 * (b + 1)
        start = jnp.maximum(done, lag_slots * ahead + 4 * b)
        lax.fori_loop(start, jnp.maximum(start, need), lambda i, x: (chain_slot(i), x)[1], 0)
        column, spot = position_masks(docs_ref[pl.ds(b, 1)].astype(f32), begin)
        cumulative = cumulative_ref[b]
        steps = steps_ref[b]
        kept = (column < begin).astype(f32)
        trailing = (spot >= column[length - 1 :]).astype(f32)
        entering = jnp.exp(cumulative) * kept
        end_decay = jnp.exp(cumulative[length - 1 :] - cumulative) * trailing
        end_weight = end_decay * steps
        end_grad = held[b]
        x = heads_in[b]
        dy = heads_grad[b]
        grown = jnp.dot(keys[b], end_grad, preferred_element_type=f32)
        spread_end = spread(end_weight, marks)
        narrow_grad[b, :, :STATE] += dot_nt((x * spread_end).astype(bf16), end_grad)
        narrow_grad[b, :, STATE:] += dot_nt(
            (dy * spread(entering, marks)).astype(bf16), state_ref[b]
        )
        grad = skip * dy + spread(steps, marks) * inner[b] + spread_end * grown
        dot_out = gather_heads(dy * (mixed[b] - skip * x), collect)
        dot_inner = gather_heads(x * inner[b], collect)
        dot_end = gather_heads(x * grown, collect)
        dot_skip = gather_heads(dy * x, collect)
        through = jnp.sum(
            end_grad.astype(f32) * state_ref[b].astype(f32), axis=0, keepdims=True
        )
        passed_grad = gather_heads(jnp.broadcast_to(through, (8, channels)), collect)[:1]
        end_mix = dot_end * end_weight
        last_term = passed_grad * entering[length - 1 :] + jnp.sum(end_mix, axis=0, keepdims=True)
        cum_grad = dot_out - steps * dot_inner - end_mix + jnp.where(last_row, last_term, 0.0)
        rates_grad = jnp.dot(upper, cum_grad, precision=highest, preferred_element_type=f32)
        steps_grad = dot_inner + end_decay * dot_end + rates_grad * decay_rate
        linear_grad = steps_grad * jax.nn.sigmoid(linear_steps_ref[b] + step_bias)
        narrow[b, :, 2 * STATE :] = linear_grad.astype(bf16)
        vector_grad_out[0:1] += jnp.sum(linear_grad, axis=0, keepdims=True)
        vector_grad_out[1:2] += jnp.sum(rates_grad * steps, axis=0, keepdims=True) * decay_rate
        vector_grad_out[2:3] += jnp.sum(dot_skip, axis=0, keepdims=True)

        row_load(3, b).wait()
        extended[0:16] = halo_ref[pl.ds(pl.multiple_of(b * 16, 16), 16)].astype(f32)
        extended[16:] = linear[b].astype(f32)
        middle = slice(16, 16 + length)
        for lag in range(1, lags):
            usable_rows[lag - 1, middle] = (spot - lag >= column).astype(f32)
        for at in range(0, both, LANES):
            lanes = slice(at, at + LANES)
            values = conv[b, :, lanes]
            sigmoid_value = jax.nn.sigmoid(values)
            slope = sigmoid_value * (1.0 + values * (1.0 - sigmoid_value))
            if at < channels:
                out_grad = grad[:, lanes]
                taps, tap = value_conv_ref, lanes
            else:
                place_at = at - channels
                out_grad = narrow_grad[b, :, place_at : place_at + LANES]
                taps, tap = keyquery_conv_ref, slice(place_at, place_at + LANES)
            local = out_grad * slope
            spread_grad[middle, lanes] = local
            input_grad = taps[0:1, tap] * local
            edges = jnp.zeros((8, LANES), f32)
            conv_grad_out[0:1, lanes] += jnp.sum(local * extended[middle, lanes], axis=0, keepdims=True)
            conv_grad_out[lags : lags + 1, lanes] += jnp.sum(local, axis=0, keepdims=True)
            for lag in range(1, lags):
                mask = usable_rows[lag - 1, middle]
                conv_grad_out[lag : lag + 1, lanes] += jnp.sum(
                    local * mask * extended[16 - lag : 16 - lag + length, lanes],
                    axis=0,
                    keepdims=True,
                )
                later = slice(16 + lag, 16 + lag + length)
                input_grad = input_grad + taps[lag : lag + 1, tap] * (
                    spread_grad[later, lanes] * usable_rows[lag - 1, later]
                )
                first = slice(8 + lag, 16 + lag)
                edges = edges + taps[lag : lag + 1, tap] * (
                    spread_grad[first, lanes] * usable_rows[lag - 1, first]
                )
            edge[b, :, lanes] = edges
            tails[b, :, lanes] = input_grad[length - 16 :]
            if at < channels:
                values_grad[b, :, lanes] = input_grad.astype(bf16)
            else:
                narrow[b, :, tap] = input_grad.astype(bf16)

        @pl.when(place > 0)
        def _():
            edge_copy(b).start()

    loop(count, close)

    def finish(b):
        @pl.when(place < n - 1)
        def _():
            edge_copy(b).wait_recv()
            last = slice(length - 16, length)
            tails[b, 8:] = tails[b, 8:] + edge_in[b]
            values_grad[b, last] = tails[b, :, :channels].astype(bf16)
            narrow[b, last, : 2 * STATE] = tails[b, :, channels:].astype(bf16)

        store(2, b).start()
        store(3, b).start()

    loop(count, finish)

    @pl.when(place > 0)
    def _():
        loop(count, lambda b: edge_copy(b).wait_send())
        loop(chunks, lambda c: chain_copy(c).wait_send())

    for i in range(len(stores)):
        loop(count, lambda b, i=i: store(i, b).wait())


def back(
    pieces,
    weight,
    gate,
    mixed,
    conv,
    linear,
    halo,
    state_in,
    steps,
    cumulative,
    linear_steps,
    square_rows,
    rowdot,
    docs,
    vectors,
    value_conv_weight,
    keyquery_conv_weight,
    norm_gain,
    cid,
):
    count, length, channels = gate.shape
    both = channels + 2 * STATE
    lags = value_conv_weight.shape[0]
    weight = blocked(weight, pieces.shape[0])
    chunks = count * 4
    dma = pltpu.SemaphoreType.DMA
    hbm = pl.BlockSpec(memory_space=pl.ANY)
    shape = jax.ShapeDtypeStruct
    vmem = pltpu.VMEM
    big = [
        ((count, length, channels), bf16),
        ((count, length, channels), bf16),
        ((count, length, channels), bf16),
        ((count, length, 2 * STATE + LANES), bf16),
    ]
    small = [((8, both), f32), ((8, LANES), f32), ((1, channels), f32)]
    return pl.pallas_call(
        back_kernel,
        out_shape=[shape(*s) for s in big + small],
        in_specs=[hbm] * 6 + [in_vmem] * 14,
        out_specs=[hbm] * len(big) + [in_vmem] * len(small),
        scratch_shapes=[
            vmem(pieces.shape, bf16),
            vmem(weight.shape, bf16),
            vmem(gate.shape, f32),
            vmem(mixed.shape, f32),
            vmem(conv.shape, f32),
            vmem(linear.shape, bf16),
        ]
        + [vmem(*s) for s in big]
        + [
            vmem((count, length, channels), f32),
            vmem((count, length, channels), f32),
            vmem((count, length, STATE), bf16),
            vmem((count, length, STATE), bf16),
            vmem((length, length), f32),
            vmem((length, length), f32),
            vmem((length, length), f32),
            vmem((count, length, channels), f32),
            vmem((count, length, 2 * STATE), f32),
            vmem((count, STATE, channels), f32),
            vmem((count, STATE, channels), bf16),
            vmem((count, STATE, channels), bf16),
            vmem((count, 8, channels), f32),
            vmem((length + 16, both), f32),
            vmem((length + 32, both), f32),
            vmem((lags - 1, length + 32, LANES), f32),
            vmem((count, 8, both), f32),
            vmem((count, 8, both), f32),
            vmem((count, 16, both), f32),
            dma((2,)),
            dma((4, count)),
            dma((len(big), count)),
            dma((count,)),
            dma((count,)),
            dma((chunks,)),
            dma((chunks,)),
        ],
        compiler_params=params(cid),
        name="back",
    )(
        pieces,
        weight,
        gate,
        mixed,
        conv,
        linear,
        halo,
        state_in,
        steps,
        cumulative,
        linear_steps,
        square_rows,
        rowdot,
        docs,
        *vectors,
        value_conv_weight,
        keyquery_conv_weight,
        norm_gain,
    )


class Ring:
    def __init__(self, streams, send_sem, recv_sem):
        self.n = lax.axis_size("seq")
        self.streams, self.send_sem, self.recv_sem = streams, send_sem, recv_sem
        head = lax.axis_index("head")
        self.spot = ring_place(self.n, lax.axis_index("seq"))
        self.after = (ring_index(self.n, lax.rem(self.spot + 1, self.n)), head)
        self.before = (ring_index(self.n, lax.rem(self.spot + self.n - 1, self.n)), head)

    def piece(self, i, step):
        part, _, columns, way = self.streams[i]
        shift = -1 - step if way == 0 else 1 + step
        rows = part.shape[0] // self.n
        index = ring_index(self.n, lax.rem(self.spot + shift + 2 * self.n, self.n))
        return part.at[pl.ds(pl.multiple_of(index * rows, rows), rows), columns]

    def copy(self, i, step, source):
        slots, way = self.streams[i][1], self.streams[i][3]
        return remote(
            source,
            slots.at[step],
            self.send_sem.at[i, step],
            self.recv_sem.at[i, step],
            self.after if way == 0 else self.before,
        )

    def start(self, i):
        self.copy(i, 0, self.piece(i, 0)).start()

    def pass_on(self, i, step):
        slots = self.streams[i][1]
        self.copy(i, step, slots.at[step]).wait_recv()
        total = slots[step].astype(f32) + self.piece(i, step + 1)[...].astype(f32)
        slots[step] = total.astype(slots.dtype)
        self.copy(i, step + 1, slots.at[step]).start()

    def last(self, i):
        slots, step = self.streams[i][1], self.n - 2
        self.copy(i, step, slots.at[step]).wait_recv()
        return slots[step].astype(f32) + self.piece(i, step + 1)[...].astype(f32)

    def finish(self, i):
        slots = self.streams[i][1]
        self.copy(i, 0, self.piece(i, 0)).wait_send()
        loop(self.n - 2, lambda step: self.copy(i, step + 1, slots.at[step]).wait_send())


def ring_streams(part, slots):
    cut, width = slots[0].shape[2], part.shape[1]
    return [(part, slots[0], pl.ds(0, cut), 0), (part, slots[1], pl.ds(cut, width - cut), 1)]


def ring_slots(n, rows, width, kind):
    cut = width // LANES // 2 * LANES
    return [pltpu.VMEM((n - 1, rows, cut), kind), pltpu.VMEM((n - 1, rows, width - cut), kind)]


class Doubling:
    def __init__(self, axis, current, table, send_sem, recv_sem):
        self.axis, self.current, self.table = axis, current, table
        self.send_sem, self.recv_sem = send_sem, recv_sem
        self.stages = table.shape[0]

    def copy(self, stage):
        bit = 1 << stage
        mine = lax.axis_index(self.axis)
        other = mine + bit - 2 * bit * lax.rem(lax.div(mine, bit), 2)
        if self.axis == "head":
            target = (lax.axis_index("seq"), other)
        else:
            target = (other, lax.axis_index("head"))
        return remote(
            self.current,
            self.table.at[stage],
            self.send_sem.at[stage],
            self.recv_sem.at[stage],
            target,
        )

    def start(self, stage):
        self.copy(stage).start()

    def finish(self, stage):
        self.copy(stage).wait()
        self.current[...] = self.current[...] + self.table[stage]


def stages_of(n):
    return n.bit_length() - 1


def tile_place(index, width):
    per = width // LANES
    return index // per, slice(index % per * LANES, index % per * LANES + LANES)


class Tiles:
    def __init__(self, ref):
        self.ref, self.index = ref, 0

    def put(self, row):
        for at in range(0, row.shape[1], LANES):
            r, lanes = tile_place(self.index, self.ref.shape[1])
            self.ref[r : r + 1, lanes] = row[:, at : at + LANES]
            self.index += 1

    def take(self, width):
        found = []
        for _ in range(width // LANES):
            r, lanes = tile_place(self.index, self.ref.shape[1])
            found.append(self.ref[r : r + 1, lanes])
            self.index += 1
        return jnp.concatenate(found, axis=1)


def tail_kernel(
    heads,
    normed_hbm,
    values_grad_hbm,
    narrow_hbm,
    gate_grad_hbm,
    pieces_hbm,
    normed_out_hbm,
    value_weight_hbm,
    gate_weight_hbm,
    keyquery_weight_hbm,
    step_weight_ref,
    tokens_ref,
    output_ref,
    teacher_ref,
    gain_ref,
    mask_ref,
    inverse_ref,
    conv_grad_ref,
    vector_grad_ref,
    gain_grad_ref,
    loss_cols_ref,
    tokens_grad_out,
    value_out,
    gate_out,
    out_out,
    keyquery_out,
    step_out,
    value_conv_out,
    value_offset_out,
    keyquery_conv_out,
    keyquery_offset_out,
    step_bias_out,
    rate_log_out,
    skip_out,
    norm_gain_out,
    input_gain_out,
    loss_out,
    normed,
    values_grad,
    narrow,
    gate_grad,
    pieces,
    normed_out,
    value_weight,
    gate_weight,
    keyquery_weight,
    value_part,
    gate_part,
    out_part,
    keyquery_part,
    vs0,
    vs1,
    gs0,
    gs1,
    os0,
    os1,
    ks0,
    ks1,
    step_whole,
    step_part,
    step_table,
    keyquery_sum,
    keyquery_table,
    group_sum,
    group_table,
    line_sum,
    line_table,
    columns,
    part,
    mate_in,
    chip_out,
    chip_in,
    dots,
    dot_out,
    load_sem,
    ring_send,
    ring_recv,
    step_send,
    step_recv,
    kq_send,
    kq_recv,
    group_send,
    group_recv,
    line_send,
    line_recv,
    mate_send,
    mate_recv,
    chip_send,
    chip_recv,
    rd_send,
    rd_recv,
):
    heads_n = lax.axis_size("head")
    n = lax.axis_size("seq")
    place = lax.axis_index("seq")
    count, length, width = tokens_ref.shape
    rows = count * length
    channels = value_part.shape[1]
    both = channels + 2 * STATE
    lags = value_conv_out.shape[0]
    group = Group(heads_n)
    loads = [
        pltpu.make_async_copy(source, target, load_sem.at[i])
        for i, (source, target) in enumerate(
            [
                (normed_hbm, normed),
                (values_grad_hbm, values_grad),
                (narrow_hbm, narrow),
                (value_weight_hbm, value_weight),
                (gate_grad_hbm, gate_grad),
                (gate_weight_hbm, gate_weight),
                (keyquery_weight_hbm, keyquery_weight),
                (pieces_hbm, pieces),
                (normed_out_hbm, normed_out),
            ]
        )
    ]
    for copy in loads:
        copy.start()
    barrier = pltpu.get_barrier_semaphore()
    for k in range(1, heads_n):
        pl.semaphore_signal(
            barrier, inc=1, device_id=group.at(group.other(k)), device_id_type=MESH
        )
    for k in range(1, n):
        pl.semaphore_signal(
            barrier, inc=1, device_id=(lax.rem(place + k, n), group.me), device_id_type=MESH
        )
    pl.semaphore_wait(barrier, heads_n + n - 2)

    ring = Ring(
        ring_streams(value_part, (vs0, vs1))
        + ring_streams(keyquery_part, (ks0, ks1))
        + ring_streams(gate_part, (gs0, gs1))
        + ring_streams(out_part, (os0, os1)),
        ring_send,
        ring_recv,
    )
    streams = range(len(ring.streams))
    group_total = Doubling("head", group_sum, group_table, group_send, group_recv)
    line_total = Doubling("seq", line_sum, line_table, line_send, line_recv)
    keyquery_total = Doubling("head", keyquery_sum, keyquery_table, kq_send, kq_recv)

    for i in (0, 1, 2):
        loads[i].wait()

    def weight_block(target, grads):
        def one(i):
            block = pl.ds(pl.multiple_of(i * 256, 256), 256)
            target[block] = dot_tn(normed[:, block], grads[...]).astype(target.dtype)

        loop(D // 256, one)

    weight_block(value_part, values_grad)
    ring.start(0)
    ring.start(1)
    weight_block(keyquery_part, narrow.at[:, : 2 * STATE])
    ring.start(2)
    ring.start(3)
    loads[4].wait()
    weight_block(gate_part, gate_grad)
    ring.start(4)
    ring.start(5)
    loads[7].wait()
    loads[8].wait()
    for j in range(heads_n):
        out_part[j * width : (j + 1) * width] = dot_tn(pieces[j], normed_out[...]).astype(bf16)
    ring.start(6)
    ring.start(7)

    step_rows = D // n
    for at, size in blocks(D):
        step_whole[:, at : at + size] = dot_tn(narrow[:, 2 * STATE :], normed[:, at : at + size])
    step_part[...] = jnp.zeros_like(step_part)
    for s in range(n):
        step_part[s, :, :step_rows] = step_whole[:16, s * step_rows : (s + 1) * step_rows]

    def step_copy(k, index, sender):
        return remote(
            step_part.at[index],
            step_table.at[sender],
            step_send.at[k - 1],
            step_recv.at[sender],
            (index, group.me),
        )

    for k in range(1, n):
        step_copy(k, lax.rem(place + k, n), place).start()

    for i in (3, 5, 6):
        loads[i].wait()
    columns[...] = jnp.zeros_like(columns)

    def own_columns(row):
        mine = jnp.zeros((1, width), f32)
        for j in range(heads_n):
            mine = mine + jnp.where(group.me == j, row[:, j * width : (j + 1) * width], 0.0)
        return mine

    gain = own_columns(gain_ref[...][None, :])

    def row_block(c):
        return pl.ds(pl.multiple_of(c * length, length), length)

    start_mate, start_chip, total, finish = scatter_phases(
        group, row_block, part, mate_in, chip_out, chip_in, (mate_send, mate_recv, chip_send, chip_recv)
    )

    def product(c):
        row_sum = jnp.zeros((length, LANES), f32)
        for j in range(heads_n):
            lanes = slice(j * width, (j + 1) * width)
            value = dot_nt(gate_grad[row_block(c)], gate_weight[lanes])
            value = value + dot_nt(values_grad[row_block(c)], value_weight[lanes])
            value = value + dot_nt(narrow[row_block(c), : 2 * STATE], keyquery_weight[lanes])
            value = value + jnp.dot(
                narrow[row_block(c), 2 * STATE : 2 * STATE + heads],
                step_weight_ref[:, lanes],
                preferred_element_type=f32,
            )
            part[j, row_block(c)] = value.astype(bf16)
            scaled = value * normed[row_block(c), lanes].astype(f32)
            columns[:, lanes] += jnp.sum(scaled, axis=0, keepdims=True)
            row_sum = row_sum + fold_lanes(scaled)
        dot_out[pl.ds(c, 1)] = jnp.sum(row_sum.T, axis=0, keepdims=True)
        start_mate(c)

        @pl.when(c > 0)
        def _():
            start_chip(c - 1)

        @pl.when(c < n - 2)
        def _():
            for i in streams:
                ring.pass_on(i, c)

    loop(count, product)
    start_chip(count - 1)
    share(group, dot_out, dots, rd_send, rd_recv)

    tiles = Tiles(group_sum)
    group_sum[...] = jnp.zeros_like(group_sum)
    for lag in range(lags + 1):
        tiles.put(conv_grad_ref[lag : lag + 1, channels:])
    tiles.put(columns[...])
    tiles.put(fold_lanes(loss_cols_ref[...]))
    for stage in range(group_total.stages):
        group_total.start(stage)
        group_total.finish(stage)

    tiles, summed = Tiles(line_sum), Tiles(group_sum)
    line_sum[...] = jnp.zeros_like(line_sum)
    for lag in range(lags + 1):
        tiles.put(conv_grad_ref[lag : lag + 1, :channels])
        tiles.put(summed.take(2 * STATE))
    tiles.put(gain_grad_ref[...])
    for i in range(3):
        tiles.put(vector_grad_ref[i : i + 1])
    tiles.put(summed.take(D))
    tiles.put(summed.take(LANES))
    shared(group, dot_out, dots, rd_send, rd_recv)
    dots[group.me] = dot_out[...]

    def rest(c):
        row_sum = dots[0, pl.ds(c, 1)]
        for j in range(1, heads_n):
            row_sum = row_sum + dots[j, pl.ds(c, 1)]
        inverse = inverse_ref[pl.ds(c, 1)]
        tokens = tokens_ref[c]
        out_grad = (output_ref[row_block(c)] - teacher_ref[c]) * as_column(
            long_row(mask_ref, c, length), width
        )
        tokens_grad_out[row_block(c)] = (
            out_grad
            + as_column(inverse, width) * gain * total(c)
            - tokens * as_column(inverse * inverse * row_sum * (1.0 / D), width)
        )

        @pl.when(count + c < n - 2)
        def _():
            for i in streams:
                ring.pass_on(i, count + c)

    loop(count, rest)
    more = n - 2 - 2 * count
    if more > 0:

        def further(s):
            for i in streams:
                ring.pass_on(i, 2 * count + s)

        loop(more, further)
    for stage in range(line_total.stages):
        line_total.start(stage)
        line_total.finish(stage)
    loop(count, finish)

    cut = ks0.shape[2]
    keyquery_sum[:, :cut] = ring.last(2)
    keyquery_sum[:, cut:] = ring.last(3)
    for stage in range(keyquery_total.stages):
        keyquery_total.start(stage)
        keyquery_total.finish(stage)
    keyquery_out[...] = keyquery_sum[...]

    cut = vs0.shape[2]
    value_out[:, :cut] = ring.last(0)
    value_out[:, cut:] = ring.last(1)
    gate_out[:, :cut] = ring.last(4)
    gate_out[:, cut:] = ring.last(5)
    out_out[:, :cut] = ring.last(6)
    out_out[:, cut:] = ring.last(7)

    for k in range(1, n):
        sender = lax.rem(place + k, n)
        copy = step_copy(k, sender, sender)
        copy.wait_send()
        copy.wait_recv()
    step_table[place] = step_part[place]
    step_sum = step_table[0]
    for s in range(1, n):
        step_sum = step_sum + step_table[s]
    step_out[...] = step_sum[:heads, :step_rows]

    tiles = Tiles(line_sum)
    for lag in range(lags + 1):
        own_row, shared_row = tiles.take(channels), tiles.take(2 * STATE)
        if lag < lags:
            value_conv_out[lag : lag + 1] = own_row
            keyquery_conv_out[lag : lag + 1] = shared_row
        else:
            value_offset_out[...] = own_row[0]
            keyquery_offset_out[...] = shared_row[0]
    norm_gain_out[...] = tiles.take(channels)[0]
    for target in (step_bias_out, rate_log_out, skip_out):
        target[...] = tiles.take(LANES)[0, :heads]
    input_gain_out[...] = (own_columns(tiles.take(D)) / gain)[0]
    loss_out[...] = 0.5 * jnp.sum(tiles.take(LANES), axis=1, keepdims=True)[0]
    for i in streams:
        ring.finish(i)


def tail(
    normed,
    values_grad,
    narrow,
    gate_grad,
    pieces,
    normed_out,
    value_weight,
    gate_weight,
    keyquery_weight,
    step_weight,
    tokens,
    output,
    teacher,
    gain,
    mask_rows,
    inverse_rows,
    conv_grad,
    vector_grad,
    gain_grad,
    loss_cols,
    lags,
    cid,
):
    heads_n, n = lax.axis_size("head"), lax.axis_size("seq")
    count, length, width = tokens.shape
    rows = count * length
    channels = value_weight.shape[1]
    heads = channels // HEADDIM
    both = channels + 2 * STATE
    own = D // n
    step_lanes = -(-own // LANES) * LANES
    buffers, sems = scatter_scratch(heads_n, rows, width, count)
    shape, vmem, dma = jax.ShapeDtypeStruct, pltpu.VMEM, pltpu.SemaphoreType.DMA
    hbm = pl.BlockSpec(memory_space=pl.ANY)
    group_tiles = (lags + 1) * 2 * STATE // LANES + D // LANES + 1
    line_tiles = (lags + 1) * both // LANES + channels // LANES + 3 + D // LANES + 1
    group_shape = (-(-group_tiles * LANES // (8 * 512)) * 8, 512)
    line_shape = (-(-line_tiles * LANES // (8 * both)) * 8, both)
    head_stages, line_stages = stages_of(heads_n), stages_of(n)
    outs = [
        (rows, width),
        (own, channels),
        (own, channels),
        (own, channels),
        (own, 2 * STATE),
        (heads, own),
        (lags, channels),
        (channels,),
        (lags, 2 * STATE),
        (2 * STATE,),
        (heads,),
        (heads,),
        (heads,),
        (channels,),
        (width,),
        (1,),
    ]
    slots = ring_slots(n, own, channels, bf16)
    return pl.pallas_call(
        functools.partial(tail_kernel, heads),
        out_shape=[shape(s, f32) for s in outs],
        in_specs=[hbm] * 9 + [in_vmem] * 11,
        out_specs=[in_vmem] * len(outs),
        scratch_shapes=[
            vmem(a.shape, a.dtype)
            for a in (
                normed,
                values_grad,
                narrow,
                gate_grad,
                pieces,
                normed_out,
                value_weight,
                gate_weight,
                keyquery_weight,
            )
        ]
        + [
            vmem((D, channels), bf16),
            vmem((D, channels), bf16),
            vmem((D, channels), bf16),
            vmem((D, 2 * STATE), f32),
        ]
        + slots * 3
        + ring_slots(n, own, 2 * STATE, f32)
        + [
            vmem((LANES, D), f32),
            vmem((n, 16, step_lanes), f32),
            vmem((n, 16, step_lanes), f32),
            vmem((own, 2 * STATE), f32),
            vmem((head_stages, own, 2 * STATE), f32),
            vmem(group_shape, f32),
            vmem((head_stages,) + group_shape, f32),
            vmem(line_shape, f32),
            vmem((line_stages,) + line_shape, f32),
            vmem((1, D), f32),
        ]
        + buffers
        + [vmem((heads_n, count, length), f32), vmem((count, length), f32)]
        + [
            dma((9,)),
            dma((8, n - 1)),
            dma((8, n - 1)),
            dma((n - 1,)),
            dma((n,)),
            dma((head_stages,)),
            dma((head_stages,)),
            dma((head_stages,)),
            dma((head_stages,)),
            dma((line_stages,)),
            dma((line_stages,)),
        ]
        + sems
        + [dma((heads_n - 1,)), dma((heads_n,))],
        compiler_params=params(cid),
        name="tail",
    )(
        normed,
        values_grad,
        narrow,
        gate_grad,
        pieces,
        normed_out,
        value_weight,
        gate_weight,
        keyquery_weight,
        step_weight,
        tokens,
        output,
        teacher,
        gain,
        mask_rows,
        inverse_rows,
        conv_grad,
        vector_grad,
        gain_grad,
        loss_cols,
    )


def deliver_kernel(count, *refs):
    for source, target in zip(refs[:count], refs[count:]):
        target[...] = source[...]


def deliver(arrays):
    return pl.pallas_call(
        functools.partial(deliver_kernel, len(arrays)),
        out_shape=[jax.ShapeDtypeStruct(a.shape, a.dtype) for a in arrays],
        in_specs=[in_vmem] * len(arrays),
        out_specs=[in_vmem] * len(arrays),
        compiler_params=pltpu.CompilerParams(vmem_limit_bytes=VMEM_LIMIT),
        name="deliver",
    )(*arrays)


def body(
    tokens,
    teacher,
    document_start,
    valid_mask,
    input_gain,
    gate_weight,
    value_weight,
    keyquery_weight,
    step_weight,
    value_conv_weight,
    value_conv_bias,
    keyquery_conv_weight,
    keyquery_conv_bias,
    step_bias,
    rate_log,
    skip_gain,
    norm_gain,
    out_weight,
):
    sequence_index = lax.axis_index("seq")
    count, length, _ = tokens.shape
    channels = gate_weight.shape[1]
    width = teacher.shape[2]
    rows = count * length
    lags = value_conv_weight.shape[0]
    valid_count = jnp.sum(valid_mask.astype(f32))
    local_mask = lax.dynamic_slice_in_dim(valid_mask, sequence_index * length, length, 1)
    mask_rows = (local_mask.astype(f32) * (2.0 / (D * valid_count))).reshape(-1, LANES)
    vectors = (step_bias, rate_log, skip_gain)
    (
        normed,
        linear,
        conv_linear,
        gate_linear,
        mixed,
        gained,
        halo,
        state_in,
        steps,
        cumulative,
        steps_linear,
        square_rows,
        inverse_rows,
    ) = front(
        tokens,
        input_gain,
        value_weight,
        keyquery_weight,
        step_weight.T,
        gate_weight,
        document_start,
        vectors,
        (value_conv_weight, value_conv_bias, keyquery_conv_weight, keyquery_conv_bias),
        norm_gain,
        1,
    )
    output, pieces, rowdot, square_total, loss_cols, token_cols = out_phase(
        gained.reshape(rows, channels), out_weight, square_rows, tokens, teacher, mask_rows, 2
    )
    (
        normed_out,
        gate_grad,
        values_grad,
        narrow_grad,
        conv_grad,
        vector_grad,
        gain_grad,
    ) = back(
        pieces,
        out_weight,
        gate_linear,
        mixed,
        conv_linear,
        linear,
        halo,
        state_in,
        steps,
        cumulative,
        steps_linear,
        square_total,
        rowdot,
        document_start,
        vectors,
        value_conv_weight,
        keyquery_conv_weight,
        norm_gain,
        3,
    )
    (
        tokens_grad,
        value_total,
        gate_total,
        out_total,
        keyquery_total,
        step_total,
        value_conv_total,
        value_offset_total,
        keyquery_conv_total,
        keyquery_offset_total,
        step_bias_total,
        rate_log_total,
        skip_total,
        norm_gain_total,
        input_gain_total,
        loss_total,
    ) = tail(
        normed.reshape(rows, D),
        values_grad.reshape(rows, channels),
        narrow_grad.reshape(rows, -1),
        gate_grad.reshape(rows, channels),
        pieces,
        normed_out.reshape(rows, channels),
        value_weight,
        gate_weight,
        keyquery_weight,
        step_weight.T,
        token_cols,
        output,
        teacher,
        input_gain,
        mask_rows,
        inverse_rows,
        conv_grad,
        vector_grad,
        gain_grad,
        loss_cols,
        lags,
        4,
    )
    results = deliver(
        (
            output.reshape(count, length, width),
            loss_total,
            tokens_grad.reshape(count, length, width),
            input_gain_total,
            gate_total,
            value_total,
            keyquery_total,
            step_total,
            value_conv_total,
            value_offset_total,
            keyquery_conv_total,
            keyquery_offset_total,
            step_bias_total,
            rate_log_total,
            skip_total,
            norm_gain_total,
            out_total,
        )
    )
    return (
        results[0],
        results[1].reshape(()),
        *results[2:7],
        results[7].T,
        *results[8:16],
        results[16].T,
    )


def solution(mesh):
    placed = (
        P(None, "seq", None),
        P(None, "seq", "head"),
        P(None, "seq"),
        P(),
        P(),
        P(None, "head"),
        P(None, "head"),
        P(),
        P(None, "head"),
        P(None, "head"),
        P("head"),
        P(),
        P(),
        P("head"),
        P("head"),
        P("head"),
        P("head"),
        P("head", None),
    )
    return jax.shard_map(
        body,
        mesh=mesh,
        in_specs=placed,
        out_specs=(
            P(None, "seq", "head"),
            P(),
            P(None, "seq", "head"),
            P("head"),
            P("seq", "head"),
            P("seq", "head"),
            P("seq", None),
            P("seq", "head"),
            P(None, "head"),
            P("head"),
            P(),
            P(),
            P("head"),
            P("head"),
            P("head"),
            P("head"),
            P("head", "seq"),
        ),
        check_vma=False,
    )
```

```python
import functools

import jax
import jax.numpy as jnp
from jax import lax
from jax.experimental import pallas as pl
from jax.experimental.pallas import tpu as pltpu
from jax.sharding import PartitionSpec as P

D = 1536
NHEADS = 48
HEADDIM = 64
STATE = 128
LANES = 128
VMEM_LIMIT = 60 << 20

norm_eps = 1e-05
highest = lax.Precision.HIGHEST
MESH = pl.DeviceIdType.MESH
f32 = jnp.float32
bf16 = jnp.bfloat16
NT = (((1,), (1,)), ((), ()))
TN = (((0,), (0,)), ((), ()))

in_vmem = pl.BlockSpec(memory_space=pltpu.VMEM)
in_smem = pl.BlockSpec(memory_space=pltpu.SMEM)


def params(cid):
    return pltpu.CompilerParams(
        collective_id=cid, has_side_effects=True, vmem_limit_bytes=VMEM_LIMIT
    )


def remote(src, dst, send, recv, target):
    return pltpu.make_async_remote_copy(
        src_ref=src,
        dst_ref=dst,
        send_sem=send,
        recv_sem=recv,
        device_id=target,
        device_id_type=MESH,
    )


def loop(count, fn):
    lax.fori_loop(0, count, lambda i, c: (fn(i), c)[1], 0)


def dot_nt(a, b, precision=None):
    return lax.dot_general(a, b, NT, precision=precision, preferred_element_type=f32)


def dot_tn(a, b, precision=None):
    return lax.dot_general(a, b, TN, precision=precision, preferred_element_type=f32)


def ring_place(n, index):
    odd, half = lax.rem(index, 2), lax.div(index, 2)
    return half * (1 - odd) + (n - 1 - half) * odd


def ring_index(n, spot):
    late = lax.div(2 * spot, n)
    return 2 * spot * (1 - late) + (2 * (n - 1 - spot) + 1) * late


class Ring:
    def __init__(self, streams, send_sem, recv_sem):
        self.n = lax.axis_size("seq")
        self.streams, self.send_sem, self.recv_sem = streams, send_sem, recv_sem
        head = lax.axis_index("head")
        self.spot = ring_place(self.n, lax.axis_index("seq"))
        self.after = (ring_index(self.n, lax.rem(self.spot + 1, self.n)), head)
        self.before = (ring_index(self.n, lax.rem(self.spot + self.n - 1, self.n)), head)

    def piece(self, i, step):
        part, _, columns, way = self.streams[i]
        shift = -1 - step if way == 0 else 1 + step
        rows = part.shape[0] // self.n
        index = ring_index(self.n, lax.rem(self.spot + shift + 2 * self.n, self.n))
        return part.at[pl.ds(pl.multiple_of(index * rows, rows), rows), columns]

    def copy(self, i, step, source):
        slots, way = self.streams[i][1], self.streams[i][3]
        return remote(
            source,
            slots.at[step],
            self.send_sem.at[i, step],
            self.recv_sem.at[i, step],
            self.after if way == 0 else self.before,
        )

    def start(self, i):
        self.copy(i, 0, self.piece(i, 0)).start()

    def pass_on(self, i, step):
        slots = self.streams[i][1]
        self.copy(i, step, slots.at[step]).wait_recv()
        total = slots[step].astype(f32) + self.piece(i, step + 1)[...].astype(f32)
        slots[step] = total.astype(slots.dtype)
        self.copy(i, step + 1, slots.at[step]).start()

    def last(self, i):
        slots, step = self.streams[i][1], self.n - 2
        self.copy(i, step, slots.at[step]).wait_recv()
        return slots[step].astype(f32) + self.piece(i, step + 1)[...].astype(f32)

    def finish(self, i):
        slots = self.streams[i][1]
        self.copy(i, 0, self.piece(i, 0)).wait_send()
        loop(self.n - 2, lambda step: self.copy(i, step + 1, slots.at[step]).wait_send())


def ring_streams(part, slots):
    cut, width = slots[0].shape[2], part.shape[1]
    return [(part, slots[0], pl.ds(0, cut), 0), (part, slots[1], pl.ds(cut, width - cut), 1)]


def ring_slots(n, rows, width, kind):
    cut = width // LANES // 2 * LANES
    return [pltpu.VMEM((n - 1, rows, cut), kind), pltpu.VMEM((n - 1, rows, width - cut), kind)]


class PairChain:
    def __init__(self, ahead, by, local, passed, buffers, send_sem, recv_sem):
        self.n = lax.axis_size("seq")
        self.place, self.head = lax.axis_index("seq"), lax.axis_index("head")
        self.by, self.pair, self.second = by, lax.div(ahead, 2), lax.rem(ahead, 2)
        self.local, self.passed = local, passed
        (
            self.state,
            self.offer_a,
            self.offer_b,
            self.offered_a,
            self.offered_b,
            self.inflow,
            self.through,
            self.next_a,
            self.next_b,
        ) = buffers
        self.send_sem, self.recv_sem = send_sem, recv_sem
        self.cut = self.inflow.shape[2]
        self.count, _, channels = self.state.shape
        self.low, self.high = pl.ds(0, self.cut), pl.ds(self.cut, channels - self.cut)
        self.all_rows = pl.ds(0, STATE)

    def copy(self, kind, b, source, target, ahead):
        return remote(
            source,
            target,
            self.send_sem.at[kind, b],
            self.recv_sem.at[kind, b],
            (self.place + self.by * ahead, self.head),
        )

    def greet(self, barrier):
        mate = self.place + self.by * (1 - 2 * self.second)
        before, after = self.pair > 0, self.pair < self.n // 2 - 1
        pl.semaphore_signal(barrier, inc=1, device_id=(mate, self.head), device_id_type=MESH)
        for there, step in ((before, -2), (after, 2)):

            @pl.when(there)
            def _():
                pl.semaphore_signal(
                    barrier,
                    inc=1,
                    device_id=(self.place + self.by * step, self.head),
                    device_id_type=MESH,
                )

        return 1 + before.astype(jnp.int32) + after.astype(jnp.int32)

    def offering(self, b, second):
        if second:
            return self.copy(0, b, self.offer_b.at[b], self.offered_b.at[b], -1)
        return self.copy(0, b, self.offer_a.at[b], self.offered_a.at[b], 1)

    def handing(self, b, second):
        if second:
            return self.copy(
                1, b, self.inflow.at[b], self.state.at[b, self.all_rows, self.low], -1
            )
        return self.copy(1, b, self.through.at[b], self.state.at[b, self.all_rows, self.high], 1)

    def passing(self, b, second):
        if second:
            return self.copy(2, b, self.next_a.at[b], self.inflow.at[b], 2)
        return self.copy(2, b, self.next_b.at[b], self.state.at[b, self.all_rows, self.high], 2)

    def offer(self, b):
        for second in (False, True):

            @pl.when(self.second == int(second))
            def _():
                lanes = self.high if second else self.low
                buffer = self.offer_b if second else self.offer_a
                buffer[b, :STATE] = self.local[b, :, lanes].astype(bf16)
                decay = self.passed[b, 7:8, lanes]
                high = decay.astype(bf16).astype(f32)
                row = lax.broadcasted_iota(jnp.int32, (16, decay.shape[1]), 0)
                rows = jnp.where(row == 0, high, jnp.where(row == 1, decay - high, 0.0))
                buffer[b, STATE:] = rows.astype(bf16)
                self.offering(b, second).start()

    def pass_on(self, b):
        more = self.pair < self.n // 2 - 1

        @pl.when(self.second == 0)
        def _():
            self.offering(b, True).wait_recv()

            @pl.when(self.pair > 0)
            def _():
                self.passing(b, False).wait_recv()

            @pl.when(self.pair == 0)
            def _():
                self.state[b, :, self.high] = jnp.zeros(self.next_b.shape[1:], bf16)

            state = self.state[b, :, self.high].astype(f32)
            value = self.passed[b, 7:8, self.high] * state + self.local[b, :, self.high]
            self.through[b] = value.astype(bf16)
            self.handing(b, False).start()

            @pl.when(more)
            def _():
                decay = self.offered_b[b, STATE:].astype(f32)
                decay = decay[0:1] + decay[1:2]
                self.next_b[b] = (
                    decay * value + self.offered_b[b, :STATE].astype(f32)
                ).astype(bf16)
                self.passing(b, False).start()

        @pl.when(self.second == 1)
        def _():
            self.offering(b, False).wait_recv()

            @pl.when(self.pair > 0)
            def _():
                self.passing(b, True).wait_recv()

            @pl.when(self.pair == 0)
            def _():
                self.inflow[b] = jnp.zeros(self.inflow.shape[1:], bf16)

            self.handing(b, True).start()
            decay = self.offered_a[b, STATE:].astype(f32)
            decay = decay[0:1] + decay[1:2]
            value = decay * self.inflow[b].astype(f32) + self.offered_a[b, :STATE].astype(f32)
            self.state[b, :, self.low] = value.astype(bf16)

            @pl.when(more)
            def _():
                self.next_a[b] = (
                    self.passed[b, 7:8, self.low] * value + self.local[b, :, self.low]
                ).astype(bf16)
                self.passing(b, True).start()

    def ready(self, b):
        for second in (False, True):

            @pl.when(self.second == int(second))
            def _():
                self.handing(b, not second).wait_recv()

    def slot(self, i, first, lag):
        turn = i - first - lag * self.pair

        @pl.when((turn >= 0) & (turn < 4 * self.count) & (lax.rem(turn + 4 * self.n, 4) == 0))
        def _():
            self.pass_on(lax.div(turn, 4))

    def slots(self, first, lag):
        return first + 4 * (self.count - 1) + 1 + lag * (self.n // 2 - 1)

    def finish(self):
        for second in (False, True):

            @pl.when(self.second == int(second))
            def _():
                def one(b):
                    self.offering(b, second).wait_send()
                    self.handing(b, second).wait_send()

                    @pl.when(self.pair < self.n // 2 - 1)
                    def _():
                        self.passing(b, second).wait_send()

                loop(self.count, one)


def chain_buffers(count, channels):
    cut = channels // LANES // 2 * LANES
    rest = channels - cut
    shapes = [
        (STATE, channels),
        (STATE + 16, cut),
        (STATE + 16, rest),
        (STATE + 16, cut),
        (STATE + 16, rest),
        (STATE, cut),
        (STATE, rest),
        (STATE, cut),
        (STATE, rest),
    ]
    return [pltpu.VMEM((count,) + s, bf16) for s in shapes]


class Group:
    def __init__(self, n):
        self.n = n
        self.chips = n // 2
        self.seq = lax.axis_index("seq")
        self.me = lax.axis_index("head")
        self.chip = lax.div(self.me, 2)
        self.core = lax.rem(self.me, 2)
        self.mate = self.me + 1 - 2 * self.core

    def at(self, head):
        return (self.seq, head)

    def chip_after(self, k):
        return lax.rem(self.chip + k, self.chips)

    def chip_before(self, k):
        return lax.rem(self.chip + self.chips - k, self.chips)

    def peer(self, k):
        return 2 * self.chip_after(k) + self.core

    def other(self, k):
        return lax.rem(self.me + k, self.n)

    def greet(self):
        barrier = pltpu.get_barrier_semaphore()
        for k in range(1, self.n):
            pl.semaphore_signal(
                barrier, inc=1, device_id=self.at(self.other(k)), device_id_type=MESH
            )
        pl.semaphore_wait(barrier, self.n - 1)


def share(group, source, table, send_sem, recv_sem):
    for k in range(1, group.n):
        remote(
            source,
            table.at[group.me],
            send_sem.at[k - 1],
            recv_sem.at[group.me],
            group.at(group.other(k)),
        ).start()


def shared(group, source, table, send_sem, recv_sem):
    for k in range(1, group.n):
        sender = group.other(k)
        copy = remote(
            source, table.at[sender], send_sem.at[k - 1], recv_sem.at[sender], group.at(sender)
        )
        copy.wait_send()
        copy.wait_recv()


def row_tile(chunk):
    return pl.ds(pl.multiple_of(chunk * LANES, LANES), LANES)


def as_column(row, width):
    tile = jnp.broadcast_to(row, (LANES, row.shape[1])).T
    return jnp.concatenate([tile] * (-(-width // LANES)), axis=1)[:, :width]


def scatter_phases(group, row_block, part, mate_in, chip_out, chip_in, sems):
    mate_send, mate_recv, chip_send, chip_recv = sems

    def mate_copy(c, x):
        return remote(
            part.at[2 * x + 1 - group.core, row_block(c)],
            mate_in.at[x, row_block(c)],
            mate_send.at[x, c],
            mate_recv.at[x, c],
            group.at(group.mate),
        )

    def chip_copy(c, k):
        return remote(
            chip_out.at[k - 1, row_block(c)],
            chip_in.at[k - 1, row_block(c)],
            chip_send.at[k - 1, c],
            chip_recv.at[k - 1, c],
            group.at(group.peer(k)),
        )

    def start_mate(c):
        for x in range(group.chips):
            mate_copy(c, x).start()

    def start_chip(c):
        for x in range(group.chips):
            mate_copy(c, x).wait_recv()
        for k in range(1, group.chips):
            x = group.chip_after(k)
            both = part[2 * x + group.core, row_block(c)].astype(f32) + mate_in[
                x, row_block(c)
            ].astype(f32)
            chip_out[k - 1, row_block(c)] = both.astype(bf16)
            chip_copy(c, k).start()

    def total(c):
        value = part[group.me, row_block(c)].astype(f32) + mate_in[
            group.chip, row_block(c)
        ].astype(f32)
        for k in range(1, group.chips):
            chip_copy(c, k).wait_recv()
            value = value + chip_in[k - 1, row_block(c)].astype(f32)
        return value

    def finish(c):
        for x in range(group.chips):
            mate_copy(c, x).wait_send()
        for k in range(1, group.chips):
            chip_copy(c, k).wait_send()

    return start_mate, start_chip, total, finish


def out_kernel(
    n,
    gated_ref,
    weight_ref,
    square_ref,
    tokens_hbm,
    teacher_hbm,
    mask_ref,
    output_ref,
    grad_ref,
    rowdot_ref,
    squared_ref,
    loss_ref,
    tokens_out,
    tokens_ref,
    teacher_ref,
    part,
    mate_in,
    chip_out,
    chip_in,
    gathered,
    squares,
    dots,
    dot_out,
    mate_send,
    mate_recv,
    chip_send,
    chip_recv,
    gm_send,
    gm_recv,
    gc_send,
    gc_recv,
    gf_send,
    gf_recv,
    sq_send,
    sq_recv,
    rd_send,
    rd_recv,
    load_sem,
):
    group = Group(n)
    count, length, width = tokens_ref.shape
    if tokens_hbm.shape[2] == width:
        token_columns = tokens_hbm
    else:
        start = pl.multiple_of(group.me * width, LANES)
        token_columns = tokens_hbm.at[:, :, pl.ds(start, width)]
    token_load = pltpu.make_async_copy(token_columns, tokens_ref, load_sem.at[0])
    token_load.start()
    teacher_load = pltpu.make_async_copy(teacher_hbm, teacher_ref, load_sem.at[1])
    teacher_load.start()
    group.greet()
    chunks = gated_ref.shape[0] // LANES
    per = length // LANES

    def rows_in(c):
        return lax.div(c, per), pl.ds(pl.multiple_of(lax.rem(c, per) * LANES, LANES), LANES)

    share(group, square_ref, squares, sq_send, sq_recv)
    start_mate, start_chip, total, finish = scatter_phases(
        group, row_tile, part, mate_in, chip_out, chip_in, (mate_send, mate_recv, chip_send, chip_recv)
    )

    def product(c):
        rows = gated_ref[row_tile(c)]
        for j in range(n):
            block = (
                weight_ref[:, j * width : (j + 1) * width] if len(weight_ref.shape) == 2 else weight_ref[j]
            )
            part[j, row_tile(c)] = jnp.dot(rows, block, preferred_element_type=f32).astype(bf16)
        start_mate(c)

    loop(chunks, product)
    loop(chunks, start_chip)
    shared(group, square_ref, squares, sq_send, sq_recv)
    squares[group.me] = square_ref[...]
    loss_ref[...] = jnp.zeros_like(loss_ref)

    def to_mate(c):
        block = gathered.at[group.me, row_tile(c)]
        return remote(block, block, gm_send.at[c], gm_recv.at[c], group.at(group.mate))

    def to_chip(c, k):
        block = gathered.at[group.me, row_tile(c)]
        return remote(
            block, block, gc_send.at[k - 1, c], gc_recv.at[k - 1, c], group.at(group.peer(k))
        )

    def forward(c, k):
        block = gathered.at[2 * group.chip_before(k) + group.core, row_tile(c)]
        return remote(
            block, block, gf_send.at[k - 1, c], gf_recv.at[k - 1, c], group.at(group.mate)
        )

    token_load.wait()
    teacher_load.wait()
    token_store = pltpu.make_async_copy(tokens_ref, tokens_out, load_sem.at[0])
    token_store.start()

    def rest(c):
        squared = squares[0, pl.ds(c, 1)]
        for j in range(1, n):
            squared = squared + squares[j, pl.ds(c, 1)]
        squared_ref[pl.ds(c, 1)] = squared
        scale = lax.rsqrt(squared * (1.0 / (NHEADS * HEADDIM)) + norm_eps)
        branch = total(c) * as_column(scale, width)
        output = tokens_ref[rows_in(c)] + branch
        output_ref[row_tile(c)] = output
        difference = output - teacher_ref[rows_in(c)]
        weighted = difference * as_column(mask_ref[pl.ds(c, 1)], width)
        low = weighted.astype(bf16)
        gathered[group.me, row_tile(c)] = low
        to_mate(c).start()
        for k in range(1, group.chips):
            to_chip(c, k).start()
        loss_ref[...] += jnp.sum(weighted * difference, axis=0, keepdims=True)
        dot_out[pl.ds(c, 1)] = rows_of(low.astype(f32) * branch)

    loop(chunks, rest)
    share(group, dot_out, dots, rd_send, rd_recv)

    def pass_on(c):
        for k in range(1, group.chips):
            to_chip(c, k).wait_recv()
            forward(c, k).start()

    loop(chunks, pass_on)

    def end(c):
        to_mate(c).wait()
        for k in range(1, group.chips):
            to_chip(c, k).wait_send()
            forward(c, k).wait()
        finish(c)
        for j in range(n):
            grad_ref[j, row_tile(c)] = gathered[j, row_tile(c)]

    loop(chunks, end)
    shared(group, dot_out, dots, rd_send, rd_recv)
    row_sum = dot_out[...]
    for k in range(1, n):
        row_sum = row_sum + dots[group.other(k)]
    rowdot_ref[...] = row_sum
    token_store.wait()


def scatter_scratch(n, rows, width, chunks):
    chips = n // 2
    dma = pltpu.SemaphoreType.DMA
    return [
        pltpu.VMEM((n, rows, width), bf16),
        pltpu.VMEM((chips, rows, width), bf16),
        pltpu.VMEM((chips - 1, rows, width), bf16),
        pltpu.VMEM((chips - 1, rows, width), bf16),
    ], [dma((chips, chunks)), dma((chips, chunks)), dma((chips - 1, chunks)), dma((chips - 1, chunks))]


def blocked(weight, n):
    width = weight.shape[1] // n
    if width % LANES == 0:
        return weight
    return jnp.moveaxis(weight.reshape(weight.shape[0], n, width), 1, 0)


def out_phase(gated, weight, square_rows, tokens, teacher, mask_rows, cid):
    n = lax.axis_size("head")
    count, length, width = teacher.shape
    rows = count * length
    chips, chunks = n // 2, rows // LANES
    if width % LANES:
        tokens = lax.dynamic_slice_in_dim(tokens, lax.axis_index("head") * width, width, 2)
    buffers, sems = scatter_scratch(n, rows, width, chunks)
    dma = pltpu.SemaphoreType.DMA
    hbm = pl.BlockSpec(memory_space=pl.ANY)
    return pl.pallas_call(
        functools.partial(out_kernel, n),
        out_shape=[
            jax.ShapeDtypeStruct((rows, width), f32),
            jax.ShapeDtypeStruct((n, rows, width), bf16),
            jax.ShapeDtypeStruct((chunks, LANES), f32),
            jax.ShapeDtypeStruct((chunks, LANES), f32),
            jax.ShapeDtypeStruct((1, width), f32),
            jax.ShapeDtypeStruct((count, length, width), f32),
        ],
        in_specs=[in_vmem] * 3 + [hbm] * 2 + [in_vmem],
        out_specs=[in_vmem] * 5 + [hbm],
        scratch_shapes=[pltpu.VMEM((count, length, width), f32)] * 2
        + buffers
        + [
            pltpu.VMEM((n, rows, width), bf16),
            pltpu.VMEM((n, chunks, LANES), f32),
            pltpu.VMEM((n, chunks, LANES), f32),
            pltpu.VMEM((chunks, LANES), f32),
        ]
        + sems
        + [
            dma((chunks,)),
            dma((chunks,)),
            dma((chips - 1, chunks)),
            dma((chips - 1, chunks)),
            dma((chips - 1, chunks)),
            dma((chips - 1, chunks)),
            dma((n - 1,)),
            dma((n,)),
            dma((n - 1,)),
            dma((n,)),
            dma((2,)),
        ],
        compiler_params=params(cid),
        name="out_phase",
    )(gated, blocked(weight, n), square_rows, tokens, teacher, mask_rows)


def blocks(width, size=256):
    return [(at, min(size, width - at)) for at in range(0, width, size)]


def fold_lanes(values):
    rows, width = values.shape
    if width % LANES:
        fill = jnp.zeros((rows, LANES - width % LANES), values.dtype)
        values = jnp.concatenate([values, fill], axis=1)
    total = values[:, :LANES]
    for at in range(LANES, width, LANES):
        total = total + values[:, at : at + LANES]
    return total


def rows_of(values):
    return jnp.sum(fold_lanes(values).T, axis=0, keepdims=True)


def head_spread(channels):
    row = lax.broadcasted_iota(jnp.int32, (LANES, channels), 0)
    head = lax.broadcasted_iota(jnp.int32, (LANES, channels), 1) // HEADDIM
    return ((row % 16 == head) & (row < 48)).astype(f32).astype(bf16)


def head_gather(channels):
    head = lax.broadcasted_iota(jnp.int32, (channels, LANES), 0) // HEADDIM
    return (lax.broadcasted_iota(jnp.int32, (channels, LANES), 1) == head).astype(f32).astype(bf16)


def spread(values, marks):
    lane = lax.broadcasted_iota(jnp.int32, values.shape, 1)
    values = jnp.where(lane < 16, values, 0.0)
    high = values.astype(bf16).astype(f32)
    left = values - high
    middle = left.astype(bf16).astype(f32)
    low = (left - middle).astype(bf16).astype(f32)
    three = high + pltpu.roll(middle, 16, 1) + pltpu.roll(low, 32, 1)
    return jnp.dot(three.astype(bf16), marks, preferred_element_type=f32)


def gather_heads(values, marks):
    high = values.astype(bf16)
    low = (values - high.astype(f32)).astype(bf16)
    return jnp.dot(high, marks, preferred_element_type=f32) + jnp.dot(
        low, marks, preferred_element_type=f32
    )


def softplus(x):
    y = jnp.exp(-jnp.abs(x))
    small = y * (1.0 - y * (1.0 / 2 - y * (1.0 / 3 - y * (1.0 / 4 - y * (1.0 / 5)))))
    return jnp.maximum(x, 0.0) + jnp.where(y < 0.03, small, jnp.log(1.0 + y))


def lane_row(ref):
    row = ref[...][None, :]
    return jnp.concatenate([row, jnp.zeros((1, LANES - row.shape[1]), f32)], axis=1)


def long_row(ref, b, length):
    per = length // LANES
    return jnp.concatenate([ref[pl.ds(b * per + i, 1)] for i in range(per)], axis=1)


def spread_row(row, marks):
    return spread(jnp.broadcast_to(row, (8, LANES)), marks)[:1]


def position_masks(docs_row, begin):
    length = docs_row.shape[1]
    column = jnp.broadcast_to(docs_row, (LANES, length)).T
    place = begin + lax.broadcasted_iota(jnp.int32, (length, LANES), 0).astype(f32)
    return column, place


def front_kernel(
    heads,
    tokens_hbm,
    gain_ref,
    value_hbm,
    keyquery_hbm,
    step_ref,
    gate_hbm,
    docs_ref,
    step_bias_ref,
    rate_log_ref,
    skip_ref,
    value_conv_ref,
    value_offset_ref,
    keyquery_conv_ref,
    keyquery_offset_ref,
    norm_gain_ref,
    normed_out,
    linear_out,
    conv_out,
    gate_out,
    mixed_out,
    gained_out,
    halo_out,
    state_out,
    steps_out,
    cumulative_out,
    linear_steps_out,
    square_out,
    inverse_out,
    tokens,
    last_tokens,
    value_weight,
    keyquery_weight,
    gate_weight,
    normed,
    linear,
    conv,
    gate,
    mixed,
    gained,
    tail,
    halo,
    extended,
    heads_in,
    keys,
    queries,
    scores,
    mask_bias,
    locals_,
    state,
    offer_a,
    offer_b,
    offered_a,
    offered_b,
    inflow,
    through,
    next_a,
    next_b,
    passed,
    entering,
    load_sem,
    last_sem,
    token_sem,
    store_sem,
    halo_sem,
    chain_send,
    chain_recv,
):
    n = lax.axis_size("seq")
    place = lax.axis_index("seq")
    head = lax.axis_index("head")
    count, length, _ = tokens.shape
    channels = value_weight.shape[1]
    both = channels + 2 * STATE
    lags = value_conv_ref.shape[0]
    begin = (place * length).astype(f32)

    loads = [
        pltpu.make_async_copy(value_hbm, value_weight, load_sem.at[0]),
        pltpu.make_async_copy(keyquery_hbm, keyquery_weight, load_sem.at[1]),
        pltpu.make_async_copy(gate_hbm, gate_weight, load_sem.at[2]),
    ]

    def token_load(b):
        return pltpu.make_async_copy(tokens_hbm.at[b], tokens.at[b], token_sem.at[b])

    def last_load(b):
        return pltpu.make_async_copy(
            tokens_hbm.at[b, length - 16 :], last_tokens.at[b], last_sem.at[b]
        )

    for b in range(count):
        last_load(b).start()
    loads[0].start()
    loads[1].start()
    for b in range(count):
        token_load(b).start()
    loads[2].start()

    stores = [
        (normed, normed_out),
        (linear, linear_out),
        (conv, conv_out),
        (gate, gate_out),
        (mixed, mixed_out),
        (gained, gained_out),
    ]

    def store(i, b):
        source, target = stores[i]
        return pltpu.make_async_copy(source.at[b], target.at[b], store_sem.at[i, b])

    barrier = pltpu.get_barrier_semaphore()

    chain = PairChain(
        place,
        1,
        locals_,
        passed,
        (
            state,
            offer_a,
            offer_b,
            offered_a,
            offered_b,
            inflow,
            through,
            next_a,
            next_b,
        ),
        chain_send,
        chain_recv,
    )
    expected = chain.greet(barrier)

    @pl.when(place > 0)
    def _():
        pl.semaphore_signal(barrier, inc=1, device_id=(place - 1, head), device_id_type=MESH)

    @pl.when(place < n - 1)
    def _():
        pl.semaphore_signal(barrier, inc=1, device_id=(place + 1, head), device_id_type=MESH)

    expected = expected + (place > 0).astype(jnp.int32) + (place < n - 1).astype(jnp.int32)

    def normalized(x):
        inverse = lax.rsqrt(jnp.mean(x * x, axis=-1, keepdims=True) + norm_eps)
        return inverse, (x * inverse * gain_ref[...][None, :]).astype(bf16)

    for b in range(count):
        last_load(b).wait()
    last = jnp.concatenate([normalized(last_tokens[b])[1] for b in range(count)], axis=0)
    loads[0].wait()
    loads[1].wait()
    for at, width in blocks(channels):
        tail[:, at : at + width] = jnp.dot(
            last, value_weight[:, at : at + width], preferred_element_type=f32
        ).astype(bf16)
    tail[:, channels:] = jnp.dot(last, keyquery_weight[...], preferred_element_type=f32).astype(bf16)
    pl.semaphore_wait(barrier, expected)
    halo_copy = remote(tail, halo, halo_sem.at[0], halo_sem.at[1], (place + 1, head))

    @pl.when(place < n - 1)
    def _():
        halo_copy.start()

    marks = head_spread(channels)
    step_bias = lane_row(step_bias_ref)
    decay_rate = -jnp.exp(lane_row(rate_log_ref))
    skip = spread_row(lane_row(skip_ref), marks)
    triangle = (
        lax.broadcasted_iota(jnp.int32, (length, length), 0)
        >= lax.broadcasted_iota(jnp.int32, (length, length), 1)
    ).astype(f32)

    def norm(b):
        token_load(b).wait()
        inverse, rows = normalized(tokens[b])
        normed[b] = rows
        inverse_out[pl.ds(b, 1)] = jnp.broadcast_to(inverse, (length, LANES)).T[:1]
        store(0, b).start()

    def project_values(b):
        rows = normed[b]
        for at, width in blocks(channels):
            linear[b, :, at : at + width] = jnp.dot(
                rows, value_weight[:, at : at + width], preferred_element_type=f32
            ).astype(bf16)

    def project_rest(b):
        rows = normed[b]
        linear[b, :, channels:] = jnp.dot(
            rows, keyquery_weight[...], preferred_element_type=f32
        ).astype(bf16)
        narrow_steps = dot_nt(rows, step_ref[...])
        linear_steps_out[b] = jnp.concatenate(
            [narrow_steps, jnp.zeros((length, LANES - heads), f32)], axis=1
        )
        store(1, b).start()

    def states(b):
        @pl.when((b == 0) & (place > 0))
        def _():
            halo_copy.wait_recv()

        @pl.when((b == 0) & (place == 0))
        def _():
            halo[...] = jnp.zeros_like(halo)

        column, spot = position_masks(docs_ref[pl.ds(b, 1)].astype(f32), begin)
        extended[0:16] = halo[pl.ds(pl.multiple_of(b * 16, 16), 16)].astype(f32)
        extended[16:] = linear[b].astype(f32)
        usable = [None] + [(spot - lag >= column).astype(f32) for lag in range(1, lags)]
        for at in range(0, both, LANES):
            if at < channels:
                weight, offset, place_at = value_conv_ref, value_offset_ref, at
            else:
                weight, offset, place_at = keyquery_conv_ref, keyquery_offset_ref, at - channels
            lanes = slice(place_at, place_at + LANES)
            value = offset[lanes][None, :] + weight[0:1, lanes] * extended[16:, at : at + LANES]
            for lag in range(1, lags):
                value = value + weight[lag : lag + 1, lanes] * (
                    extended[16 - lag : 16 - lag + length, at : at + LANES] * usable[lag]
                )
            conv[b, :, at : at + LANES] = value
            active = value * jax.nn.sigmoid(value)
            if at < channels:
                heads_in[b, :, at : at + LANES] = active
            elif at < channels + STATE:
                keys[b] = active.astype(bf16)
            else:
                queries[b] = active.astype(bf16)
        store(2, b).start()
        steps = softplus(linear_steps_out[b] + step_bias)
        cumulative = jnp.dot(
            triangle, steps * decay_rate, precision=highest, preferred_element_type=f32
        )
        steps_out[b] = steps
        cumulative_out[b] = cumulative
        kept = (column < begin).astype(f32)
        trailing = (spot >= column[length - 1 :]).astype(f32)
        entering[b] = jnp.exp(cumulative) * kept
        end_weight = jnp.exp(cumulative[length - 1 :] - cumulative) * trailing * steps
        weighted = (heads_in[b] * spread(end_weight, marks)).astype(bf16)
        locals_[b] = dot_tn(keys[b], weighted)
        last_entering = entering[b, length - 8 :]
        passed[b] = spread(last_entering, marks)

    pairs = channels // LANES
    first_slot, lag_slots = 7, 6

    def chain_slot(i):
        chain.slot(i, first_slot, lag_slots)

    def begin_sequence(b):
        for k, unit in enumerate((norm, project_values, project_rest, states)):
            unit(b)
            if unit is states:
                chain.offer(b)
            chain_slot(4 * b + k)

    loop(count, begin_sequence)
    halo_out[...] = halo[...]
    first_half = lax.broadcasted_iota(jnp.int32, (length, LANES), 1) < HEADDIM
    loads[2].wait()

    def inside(b):
        column, spot = position_masks(docs_ref[pl.ds(b, 1)].astype(f32), begin)
        wide = jnp.concatenate([column] * (length // LANES), axis=1)
        t = begin + lax.broadcasted_iota(jnp.int32, (length, length), 0).astype(f32)
        u = begin + lax.broadcasted_iota(jnp.int32, (length, length), 1).astype(f32)
        mask_bias[...] = jnp.where((u >= wide) & (u <= t), 0.0, -1e30)
        scores[...] = dot_nt(queries[b], keys[b])
        cumulative = cumulative_out[b]
        across = cumulative.T
        spread_steps = spread(steps_out[b], marks)
        for pair in range(pairs):
            lanes = slice(pair * LANES, (pair + 1) * LANES)
            scaled = heads_in[b, :, lanes] * spread_steps[:, lanes]
            value = jnp.zeros((length, LANES), f32)
            for half in range(2):
                h = 2 * pair + half
                decay = jnp.exp(cumulative[:, h : h + 1] - across[h : h + 1] + mask_bias[...])
                mixing = (decay * scores[...]).astype(bf16)
                mine = jnp.where(first_half if half == 0 else ~first_half, scaled, 0.0).astype(bf16)
                value = value + jnp.dot(mixing, mine, preferred_element_type=f32)
            mixed[b, :, lanes] = value
            chain_slot(4 * count + b * (pairs + 1) + pair)
        rows = normed[b]
        for at, width in blocks(channels):
            gate[b, :, at : at + width] = jnp.dot(
                rows, gate_weight[:, at : at + width], preferred_element_type=f32
            )
        store(3, b).start()
        chain_slot(4 * count + b * (pairs + 1) + pairs)

    loop(count, inside)
    done = count * (pairs + 5)
    slots = chain.slots(first_slot, lag_slots)
    if slots > done:
        loop(slots - done, lambda i: chain_slot(i + done))

    def close(b):
        chain.ready(b)
        state_out[b] = state[b]
        projected = jnp.dot(queries[b], state[b], preferred_element_type=f32)
        value = mixed[b] + spread(entering[b], marks) * projected + skip * heads_in[b]
        mixed[b] = value
        store(4, b).start()
        linear_gate = gate[b]
        gated = value * (linear_gate * jax.nn.sigmoid(linear_gate))
        gained[b] = (gated * norm_gain_ref[...][None, :]).astype(bf16)
        store(5, b).start()
        squared = rows_of(gated * gated)
        for i in range(length // LANES):
            square_out[pl.ds(b * (length // LANES) + i, 1)] = squared[
                :, i * LANES : (i + 1) * LANES
            ]

    loop(count, close)

    @pl.when(place < n - 1)
    def _():
        halo_copy.wait_send()

    chain.finish()

    for i in range(len(stores)):
        loop(count, lambda b, i=i: store(i, b).wait())


def front(tokens, gain, value_weight, keyquery_weight, step_weight, gate_weight, docs, vectors, conv, norm_gain, cid):
    count, length, _ = tokens.shape
    channels = value_weight.shape[1]
    heads = channels // HEADDIM
    both = channels + 2 * STATE
    dma = pltpu.SemaphoreType.DMA
    hbm = pl.BlockSpec(memory_space=pl.ANY)
    shape = jax.ShapeDtypeStruct
    big = [
        ((count, length, D), bf16),
        ((count, length, both), bf16),
        ((count, length, both), f32),
        ((count, length, channels), f32),
        ((count, length, channels), f32),
        ((count, length, channels), bf16),
    ]
    small = [
        ((count * 16, both), bf16),
        ((count, STATE, channels), bf16),
        ((count, length, LANES), f32),
        ((count, length, LANES), f32),
        ((count, length, LANES), f32),
        ((count * length // LANES, LANES), f32),
        ((count, length), f32),
    ]
    return pl.pallas_call(
        functools.partial(front_kernel, heads),
        out_shape=[shape(*s) for s in big + small],
        in_specs=[hbm, in_vmem, hbm, hbm, in_vmem, hbm] + [in_vmem] * 9,
        out_specs=[hbm] * len(big) + [in_vmem] * len(small),
        scratch_shapes=[
            pltpu.VMEM((count, length, D), f32),
            pltpu.VMEM((count, 16, D), f32),
            pltpu.VMEM((D, channels), bf16),
            pltpu.VMEM((D, 2 * STATE), bf16),
            pltpu.VMEM((D, channels), bf16),
        ]
        + [pltpu.VMEM(*s) for s in big]
        + [
            pltpu.VMEM((count * 16, both), bf16),
            pltpu.VMEM((count * 16, both), bf16),
            pltpu.VMEM((length + 16, both), f32),
            pltpu.VMEM((count, length, channels), f32),
            pltpu.VMEM((count, length, STATE), bf16),
            pltpu.VMEM((count, length, STATE), bf16),
            pltpu.VMEM((length, length), f32),
            pltpu.VMEM((length, length), f32),
            pltpu.VMEM((count, STATE, channels), f32),
        ]
        + chain_buffers(count, channels)
        + [
            pltpu.VMEM((count, 8, channels), f32),
            pltpu.VMEM((count, length, LANES), f32),
            dma((3,)),
            dma((count,)),
            dma((count,)),
            dma((len(big), count)),
            dma((2,)),
            dma((3, count)),
            dma((3, count)),
        ],
        compiler_params=params(cid),
        name="front",
    )(tokens, gain, value_weight, keyquery_weight, step_weight, gate_weight, docs, *vectors, *conv, norm_gain)


def back_kernel(
    pieces_hbm,
    weight_hbm,
    gate_hbm,
    mixed_hbm,
    conv_hbm,
    linear_hbm,
    normed_hbm,
    halo_ref,
    state_ref,
    steps_ref,
    cumulative_ref,
    linear_steps_ref,
    square_ref,
    rowdot_ref,
    docs_ref,
    step_bias_ref,
    rate_log_ref,
    skip_ref,
    value_conv_ref,
    keyquery_conv_ref,
    norm_gain_ref,
    gate_grad_out,
    values_grad_out,
    narrow_out,
    conv_grad_out,
    vector_grad_out,
    gain_grad_out,
    out_total,
    gate_total,
    pieces,
    weight,
    gate,
    mixed,
    conv,
    linear,
    normed,
    normed_out,
    gate_grad,
    values_grad,
    narrow,
    out_part,
    gate_part,
    os0,
    os1,
    gs0,
    gs1,
    heads_in,
    heads_grad,
    keys,
    queries,
    scores,
    scores_grad,
    mask_bias,
    narrow_grad,
    locals_,
    state,
    offer_a,
    offer_b,
    offered_a,
    offered_b,
    inflow,
    through,
    next_a,
    next_b,
    passed,
    extended,
    spread_grad,
    usable_rows,
    edge,
    edge_in,
    tails,
    load_sem,
    row_sem,
    store_sem,
    edge_send,
    edge_recv,
    chain_send,
    chain_recv,
    ring_send,
    ring_recv,
):
    n = lax.axis_size("seq")
    place = lax.axis_index("seq")
    head = lax.axis_index("head")
    ahead = n - 1 - place
    count, length, channels = gate.shape
    both = channels + 2 * STATE
    lags = value_conv_ref.shape[0]
    begin = (place * length).astype(f32)
    groups, width = pieces.shape[0], pieces.shape[2]
    inner_total = NHEADS * HEADDIM

    loads = [
        pltpu.make_async_copy(weight_hbm, weight, load_sem.at[0]),
        pltpu.make_async_copy(pieces_hbm, pieces, load_sem.at[1]),
        pltpu.make_async_copy(normed_hbm, normed, load_sem.at[2]),
    ]
    loads[0].start()
    loads[1].start()
    row_arrays = [(gate_hbm, gate), (mixed_hbm, mixed), (conv_hbm, conv), (linear_hbm, linear)]

    def row_load(i, b):
        source, target = row_arrays[i]
        return pltpu.make_async_copy(source.at[b], target.at[b], row_sem.at[i, b])

    for b in range(count):
        for i in range(3):
            row_load(i, b).start()
    loads[2].start()
    for b in range(count):
        row_load(3, b).start()
    inner = gate

    stores = [
        (gate_grad, gate_grad_out),
        (values_grad, values_grad_out),
        (narrow, narrow_out),
    ]

    def store(i, b):
        source, target = stores[i]
        return pltpu.make_async_copy(source.at[b], target.at[b], store_sem.at[i, b])

    barrier = pltpu.get_barrier_semaphore()

    @pl.when(place > 0)
    def _():
        pl.semaphore_signal(barrier, inc=1, device_id=(place - 1, head), device_id_type=MESH)

    @pl.when(place < n - 1)
    def _():
        pl.semaphore_signal(barrier, inc=1, device_id=(place + 1, head), device_id_type=MESH)

    chain = PairChain(
        ahead,
        -1,
        locals_,
        passed,
        (
            state,
            offer_a,
            offer_b,
            offered_a,
            offered_b,
            inflow,
            through,
            next_a,
            next_b,
        ),
        chain_send,
        chain_recv,
    )
    expected = chain.greet(barrier)
    spot_here = ring_place(n, place)
    for step in (1, n - 1):
        neighbour = ring_index(n, lax.rem(spot_here + step, n))
        pl.semaphore_signal(barrier, inc=1, device_id=(neighbour, head), device_id_type=MESH)

    marks = head_spread(channels)
    collect = head_gather(channels)
    step_bias = lane_row(step_bias_ref)
    decay_rate = -jnp.exp(lane_row(rate_log_ref))
    skip = spread_row(lane_row(skip_ref), marks)
    gain_grad_out[...] = jnp.zeros_like(gain_grad_out)
    vector_grad_out[...] = jnp.zeros_like(vector_grad_out)
    conv_grad_out[...] = jnp.zeros_like(conv_grad_out)
    loads[0].wait()
    loads[1].wait()
    ring = Ring(
        ring_streams(out_part, (os0, os1)) + ring_streams(gate_part, (gs0, gs1)),
        ring_send,
        ring_recv,
    )
    ring_steps = n - 2

    def pass_on(first, step):
        @pl.when((step >= 0) & (step < ring_steps))
        def _():
            ring.pass_on(first, step)
            ring.pass_on(first + 1, step)

    def row_column(ref, b):
        return jnp.broadcast_to(long_row(ref, b, length), (LANES, length)).T

    def widened(column, size):
        return jnp.concatenate([column] * (size // LANES), axis=1)

    pl.semaphore_wait(
        barrier,
        expected + 2 + (place > 0).astype(jnp.int32) + (place < n - 1).astype(jnp.int32),
    )

    pairs = channels // LANES
    first_slot, lag_slots = 7, 6

    def chain_slot(i):
        chain.slot(i, first_slot, lag_slots)

    def gated_norm(b):
        for i in range(3):
            row_load(i, b).wait()
        scale = lax.rsqrt(row_column(square_ref, b) * (1.0 / inner_total) + norm_eps)
        pull = scale * scale * row_column(rowdot_ref, b) * (1.0 / inner_total)
        column, _ = position_masks(docs_ref[pl.ds(b, 1)].astype(f32), begin)
        entering = spread(
            jnp.exp(cumulative_ref[b]) * (column < begin).astype(f32), marks
        )
        passed[b] = entering[length - 8 :]
        column_blocks = blocks(channels)
        for k, (at, size) in enumerate(column_blocks):
            lanes = slice(at, at + size)
            grad_rows = jnp.zeros((length, size), f32)
            for j in range(groups):
                block = (
                    weight[lanes, j * width : (j + 1) * width]
                    if len(weight.shape) == 2
                    else weight[j, lanes]
                )
                grad_rows = grad_rows + dot_nt(pieces[j, pl.ds(pl.multiple_of(b * length, length), length)], block)
            linear_gate = gate[b, :, lanes]
            sigmoid_value = jax.nn.sigmoid(linear_gate)
            active = linear_gate * sigmoid_value
            value = mixed[b, :, lanes]
            gated = value * active
            norm_gain = norm_gain_ref[lanes][None, :]
            scaled = gated * widened(scale, size)
            normed_out[b, :, lanes] = (scaled * norm_gain).astype(bf16)
            gain_grad_out[:, lanes] += jnp.sum(grad_rows * scaled, axis=0, keepdims=True)
            gated_grad = widened(scale, size) * norm_gain * grad_rows - gated * widened(pull, size)
            heads_grad[b, :, lanes] = gated_grad * active
            slope = sigmoid_value * (1.0 + linear_gate * (1.0 - sigmoid_value))
            gate_grad[b, :, lanes] = (gated_grad * value * slope).astype(bf16)
            values = conv[b, :, lanes]
            heads_in[b, :, lanes] = values * jax.nn.sigmoid(values)
            chain_slot(4 * b + k)
        store(0, b).start()
        values = conv[b, :, channels : channels + STATE]
        keys[b] = (values * jax.nn.sigmoid(values)).astype(bf16)
        values = conv[b, :, channels + STATE :]
        queries[b] = (values * jax.nn.sigmoid(values)).astype(bf16)
        locals_[b] = dot_tn(queries[b], (heads_grad[b] * entering).astype(bf16))
        chain.offer(b)
        for k in range(len(column_blocks), 4):
            chain_slot(4 * b + k)

    loop(count, gated_norm)

    slot = 4 * count
    for j in range(groups):
        grads = jnp.concatenate([normed_out[b] for b in range(count)], axis=0)
        out_part[j * width : (j + 1) * width] = dot_tn(pieces[j], grads).astype(bf16)
        chain_slot(slot + j)
    slot += groups
    ring.start(0)
    ring.start(1)
    loads[2].wait()
    gate_blocks = D // 256

    def gate_block(i):
        block = pl.ds(pl.multiple_of(i * 256, 256), 256)
        rows = jnp.concatenate([normed[b, :, block] for b in range(count)], axis=0)
        grads = jnp.concatenate([gate_grad[b] for b in range(count)], axis=0)
        gate_part[block] = dot_tn(rows, grads).astype(bf16)
        chain_slot(slot + i)

    loop(gate_blocks, gate_block)
    slot += gate_blocks
    ring.start(2)
    ring.start(3)

    first_half = lax.broadcasted_iota(jnp.int32, (length, LANES), 1) < HEADDIM

    def inside(b):
        docs_row = docs_ref[pl.ds(b, 1)].astype(f32)
        u = begin + lax.broadcasted_iota(jnp.int32, (length, length), 0).astype(f32)
        t = begin + lax.broadcasted_iota(jnp.int32, (length, length), 1).astype(f32)
        mask_bias[...] = jnp.where((u >= docs_row) & (u <= t), 0.0, -1e30)
        scores[...] = dot_nt(keys[b], queries[b])
        scores_grad[...] = jnp.zeros_like(scores_grad)
        cumulative = cumulative_ref[b]
        across = cumulative.T
        spread_steps = spread(steps_ref[b], marks)
        for pair in range(pairs):
            lanes = slice(pair * LANES, (pair + 1) * LANES)
            scaled = heads_in[b, :, lanes] * spread_steps[:, lanes]
            grads = heads_grad[b, :, lanes]
            low_grads = grads.astype(bf16)
            value = jnp.zeros((length, LANES), f32)
            for half in range(2):
                h = 2 * pair + half
                mine = first_half if half == 0 else ~first_half
                decay = jnp.exp(across[h : h + 1] - cumulative[:, h : h + 1] + mask_bias[...])
                mixing = (decay * scores[...]).astype(bf16)
                value = value + jnp.dot(
                    mixing, jnp.where(mine, grads, 0.0).astype(bf16), preferred_element_type=f32
                )
                pairwise = dot_nt(jnp.where(mine, scaled, 0.0).astype(bf16), low_grads)
                scores_grad[...] += decay * pairwise
            inner[b, :, lanes] = value
            chain_slot(slot + b * (pairs + 1) + pair)
            if pair == 1:
                pass_on(0, b)
            if pair == pairs - 2:
                pass_on(2, b)
        low = scores_grad[...].astype(bf16)
        narrow_grad[b, :, :STATE] = jnp.dot(low, queries[b], preferred_element_type=f32)
        narrow_grad[b, :, STATE:] = dot_tn(low, keys[b])
        chain_slot(slot + b * (pairs + 1) + pairs)

    loop(count, inside)
    done = slot + count * (pairs + 1)
    slots = chain.slots(first_slot, lag_slots)
    if slots > done:
        loop(slots - done, lambda i: chain_slot(i + done))
    extended[0:16] = jnp.zeros((16, both), f32)
    spread_grad[0:16] = jnp.zeros((16, both), f32)
    spread_grad[16 + length :] = jnp.zeros((16, both), f32)
    usable_rows[...] = jnp.zeros_like(usable_rows)
    upper = (
        lax.broadcasted_iota(jnp.int32, (length, length), 0)
        <= lax.broadcasted_iota(jnp.int32, (length, length), 1)
    ).astype(f32)
    last_row = lax.broadcasted_iota(jnp.int32, (length, LANES), 0) == length - 1

    def edge_copy(b):
        return remote(edge.at[b], edge_in.at[b], edge_send.at[b], edge_recv.at[b], (place - 1, head))

    def close(b):
        pass_on(0, count + b)
        column, spot = position_masks(docs_ref[pl.ds(b, 1)].astype(f32), begin)
        cumulative = cumulative_ref[b]
        steps = steps_ref[b]
        kept = (column < begin).astype(f32)
        trailing = (spot >= column[length - 1 :]).astype(f32)
        entering = jnp.exp(cumulative) * kept
        end_decay = jnp.exp(cumulative[length - 1 :] - cumulative) * trailing
        end_weight = end_decay * steps
        chain.ready(b)
        end_grad = state[b]
        x = heads_in[b]
        dy = heads_grad[b]
        grown = jnp.dot(keys[b], end_grad, preferred_element_type=f32)
        spread_end = spread(end_weight, marks)
        narrow_grad[b, :, :STATE] += dot_nt((x * spread_end).astype(bf16), end_grad)
        narrow_grad[b, :, STATE:] += dot_nt(
            (dy * spread(entering, marks)).astype(bf16), state_ref[b]
        )
        grad = skip * dy + spread(steps, marks) * inner[b] + spread_end * grown
        dot_out = gather_heads(dy * (mixed[b] - skip * x), collect)
        dot_inner = gather_heads(x * inner[b], collect)
        dot_end = gather_heads(x * grown, collect)
        dot_skip = gather_heads(dy * x, collect)
        through = jnp.sum(
            end_grad.astype(f32) * state_ref[b].astype(f32), axis=0, keepdims=True
        )
        passed_grad = gather_heads(jnp.broadcast_to(through, (8, channels)), collect)[:1]
        end_mix = dot_end * end_weight
        last_term = passed_grad * entering[length - 1 :] + jnp.sum(end_mix, axis=0, keepdims=True)
        cum_grad = dot_out - steps * dot_inner - end_mix + jnp.where(last_row, last_term, 0.0)
        rates_grad = jnp.dot(upper, cum_grad, precision=highest, preferred_element_type=f32)
        steps_grad = dot_inner + end_decay * dot_end + rates_grad * decay_rate
        linear_grad = steps_grad * jax.nn.sigmoid(linear_steps_ref[b] + step_bias)
        narrow[b, :, 2 * STATE :] = linear_grad.astype(bf16)
        vector_grad_out[0:1] += jnp.sum(linear_grad, axis=0, keepdims=True)
        vector_grad_out[1:2] += jnp.sum(rates_grad * steps, axis=0, keepdims=True) * decay_rate
        vector_grad_out[2:3] += jnp.sum(dot_skip, axis=0, keepdims=True)

        pass_on(2, count + b)
        row_load(3, b).wait()
        extended[0:16] = halo_ref[pl.ds(pl.multiple_of(b * 16, 16), 16)].astype(f32)
        extended[16:] = linear[b].astype(f32)
        middle = slice(16, 16 + length)
        for lag in range(1, lags):
            usable_rows[lag - 1, middle] = (spot - lag >= column).astype(f32)
        for at in range(0, both, LANES):
            lanes = slice(at, at + LANES)
            values = conv[b, :, lanes]
            sigmoid_value = jax.nn.sigmoid(values)
            slope = sigmoid_value * (1.0 + values * (1.0 - sigmoid_value))
            if at < channels:
                out_grad = grad[:, lanes]
                taps, tap = value_conv_ref, lanes
            else:
                place_at = at - channels
                out_grad = narrow_grad[b, :, place_at : place_at + LANES]
                taps, tap = keyquery_conv_ref, slice(place_at, place_at + LANES)
            local = out_grad * slope
            spread_grad[middle, lanes] = local
            input_grad = taps[0:1, tap] * local
            edges = jnp.zeros((8, LANES), f32)
            conv_grad_out[0:1, lanes] += jnp.sum(local * extended[middle, lanes], axis=0, keepdims=True)
            conv_grad_out[lags : lags + 1, lanes] += jnp.sum(local, axis=0, keepdims=True)
            for lag in range(1, lags):
                mask = usable_rows[lag - 1, middle]
                conv_grad_out[lag : lag + 1, lanes] += jnp.sum(
                    local * mask * extended[16 - lag : 16 - lag + length, lanes],
                    axis=0,
                    keepdims=True,
                )
                later = slice(16 + lag, 16 + lag + length)
                input_grad = input_grad + taps[lag : lag + 1, tap] * (
                    spread_grad[later, lanes] * usable_rows[lag - 1, later]
                )
                first = slice(8 + lag, 16 + lag)
                edges = edges + taps[lag : lag + 1, tap] * (
                    spread_grad[first, lanes] * usable_rows[lag - 1, first]
                )
            edge[b, :, lanes] = edges
            tails[b, :, lanes] = input_grad[length - 16 :]
            if at < channels:
                values_grad[b, :, lanes] = input_grad.astype(bf16)
            else:
                narrow[b, :, tap] = input_grad.astype(bf16)

        @pl.when(place > 0)
        def _():
            edge_copy(b).start()

    loop(count, close)

    def finish(b):
        @pl.when(place < n - 1)
        def _():
            edge_copy(b).wait_recv()
            last = slice(length - 16, length)
            tails[b, 8:] = tails[b, 8:] + edge_in[b]
            values_grad[b, last] = tails[b, :, :channels].astype(bf16)
            narrow[b, last, : 2 * STATE] = tails[b, :, channels:].astype(bf16)

        store(1, b).start()
        store(2, b).start()

    loop(count, finish)

    if ring_steps > 2 * count:

        def further(s):
            pass_on(0, 2 * count + s)
            pass_on(2, 2 * count + s)

        loop(ring_steps - 2 * count, further)
    cut = os0.shape[2]
    out_total[:, :cut] = ring.last(0)
    out_total[:, cut:] = ring.last(1)
    gate_total[:, :cut] = ring.last(2)
    gate_total[:, cut:] = ring.last(3)
    for i in range(4):
        ring.finish(i)

    @pl.when(place > 0)
    def _():
        loop(count, lambda b: edge_copy(b).wait_send())

    chain.finish()

    for i in range(len(stores)):
        loop(count, lambda b, i=i: store(i, b).wait())


def back(
    pieces,
    weight,
    gate,
    mixed,
    conv,
    linear,
    normed,
    halo,
    state_in,
    steps,
    cumulative,
    linear_steps,
    square_rows,
    rowdot,
    docs,
    vectors,
    value_conv_weight,
    keyquery_conv_weight,
    norm_gain,
    cid,
):
    count, length, channels = gate.shape
    both = channels + 2 * STATE
    lags = value_conv_weight.shape[0]
    weight = blocked(weight, pieces.shape[0])
    dma = pltpu.SemaphoreType.DMA
    hbm = pl.BlockSpec(memory_space=pl.ANY)
    shape = jax.ShapeDtypeStruct
    vmem = pltpu.VMEM
    n = lax.axis_size("seq")
    own = D // n
    big = [
        ((count, length, channels), bf16),
        ((count, length, channels), bf16),
        ((count, length, 2 * STATE + LANES), bf16),
    ]
    small = [
        ((8, both), f32),
        ((8, LANES), f32),
        ((1, channels), f32),
        ((own, channels), f32),
        ((own, channels), f32),
    ]
    return pl.pallas_call(
        back_kernel,
        out_shape=[shape(*s) for s in big + small],
        in_specs=[hbm] * 7 + [in_vmem] * 14,
        out_specs=[hbm] * len(big) + [in_vmem] * len(small),
        scratch_shapes=[
            vmem(pieces.shape, bf16),
            vmem(weight.shape, bf16),
            vmem(gate.shape, f32),
            vmem(mixed.shape, f32),
            vmem(conv.shape, f32),
            vmem(linear.shape, bf16),
            vmem(normed.shape, bf16),
            vmem((count, length, channels), bf16),
        ]
        + [vmem(*s) for s in big]
        + [vmem((D, channels), bf16), vmem((D, channels), bf16)]
        + ring_slots(n, own, channels, bf16) * 2
        + [
            vmem((count, length, channels), f32),
            vmem((count, length, channels), f32),
            vmem((count, length, STATE), bf16),
            vmem((count, length, STATE), bf16),
            vmem((length, length), f32),
            vmem((length, length), f32),
            vmem((length, length), f32),
            vmem((count, length, 2 * STATE), f32),
            vmem((count, STATE, channels), f32),
        ]
        + chain_buffers(count, channels)
        + [
            vmem((count, 8, channels), f32),
            vmem((length + 16, both), f32),
            vmem((length + 32, both), f32),
            vmem((lags - 1, length + 32, LANES), f32),
            vmem((count, 8, both), f32),
            vmem((count, 8, both), f32),
            vmem((count, 16, both), f32),
            dma((3,)),
            dma((4, count)),
            dma((len(big), count)),
            dma((count,)),
            dma((count,)),
            dma((3, count)),
            dma((3, count)),
            dma((4, n - 1)),
            dma((4, n - 1)),
        ],
        compiler_params=params(cid),
        name="back",
    )(
        pieces,
        weight,
        gate,
        mixed,
        conv,
        linear,
        normed,
        halo,
        state_in,
        steps,
        cumulative,
        linear_steps,
        square_rows,
        rowdot,
        docs,
        *vectors,
        value_conv_weight,
        keyquery_conv_weight,
        norm_gain,
    )


class Doubling:
    def __init__(self, axis, current, table, send_sem, recv_sem):
        self.axis, self.current, self.table = axis, current, table
        self.send_sem, self.recv_sem = send_sem, recv_sem
        self.stages = table.shape[0]

    def copy(self, stage):
        bit = 1 << stage
        mine = lax.axis_index(self.axis)
        other = mine + bit - 2 * bit * lax.rem(lax.div(mine, bit), 2)
        if self.axis == "head":
            target = (lax.axis_index("seq"), other)
        else:
            target = (other, lax.axis_index("head"))
        return remote(
            self.current,
            self.table.at[stage],
            self.send_sem.at[stage],
            self.recv_sem.at[stage],
            target,
        )

    def start(self, stage):
        self.copy(stage).start()

    def finish(self, stage):
        self.copy(stage).wait()
        self.current[...] = self.current[...] + self.table[stage]


def stages_of(n):
    return n.bit_length() - 1


def tile_place(index, width):
    per = width // LANES
    return index // per, slice(index % per * LANES, index % per * LANES + LANES)


class Tiles:
    def __init__(self, ref):
        self.ref, self.index = ref, 0

    def put(self, row):
        for at in range(0, row.shape[1], LANES):
            r, lanes = tile_place(self.index, self.ref.shape[1])
            self.ref[r : r + 1, lanes] = row[:, at : at + LANES]
            self.index += 1

    def take(self, width):
        found = []
        for _ in range(width // LANES):
            r, lanes = tile_place(self.index, self.ref.shape[1])
            found.append(self.ref[r : r + 1, lanes])
            self.index += 1
        return jnp.concatenate(found, axis=1)


def tail_kernel(
    heads,
    normed_hbm,
    values_grad_hbm,
    narrow_hbm,
    gate_grad_hbm,
    value_weight_hbm,
    gate_weight_hbm,
    keyquery_weight_hbm,
    step_weight_ref,
    tokens_ref,
    output_ref,
    teacher_ref,
    gain_ref,
    mask_ref,
    inverse_ref,
    conv_grad_ref,
    vector_grad_ref,
    gain_grad_ref,
    loss_cols_ref,
    tokens_grad_out,
    value_out,
    keyquery_out,
    step_out,
    value_conv_out,
    value_offset_out,
    keyquery_conv_out,
    keyquery_offset_out,
    step_bias_out,
    rate_log_out,
    skip_out,
    norm_gain_out,
    input_gain_out,
    loss_out,
    normed,
    values_grad,
    narrow,
    gate_grad,
    value_weight,
    gate_weight,
    keyquery_weight,
    value_part,
    keyquery_part,
    vs0,
    vs1,
    ks0,
    ks1,
    step_whole,
    step_part,
    step_table,
    keyquery_sum,
    keyquery_table,
    group_sum,
    group_table,
    line_sum,
    line_table,
    columns,
    part,
    mate_in,
    chip_out,
    chip_in,
    dots,
    dot_out,
    load_sem,
    ring_send,
    ring_recv,
    step_send,
    step_recv,
    kq_send,
    kq_recv,
    group_send,
    group_recv,
    line_send,
    line_recv,
    mate_send,
    mate_recv,
    chip_send,
    chip_recv,
    rd_send,
    rd_recv,
):
    heads_n = lax.axis_size("head")
    n = lax.axis_size("seq")
    place = lax.axis_index("seq")
    count, length, width = tokens_ref.shape
    rows = count * length
    channels = value_part.shape[1]
    both = channels + 2 * STATE
    lags = value_conv_out.shape[0]
    group = Group(heads_n)
    loads = [
        pltpu.make_async_copy(source, target, load_sem.at[i])
        for i, (source, target) in enumerate(
            [
                (normed_hbm, normed),
                (values_grad_hbm, values_grad),
                (narrow_hbm, narrow),
                (value_weight_hbm, value_weight),
                (gate_grad_hbm, gate_grad),
                (gate_weight_hbm, gate_weight),
                (keyquery_weight_hbm, keyquery_weight),
            ]
        )
    ]
    for copy in loads:
        copy.start()
    barrier = pltpu.get_barrier_semaphore()
    for k in range(1, heads_n):
        pl.semaphore_signal(
            barrier, inc=1, device_id=group.at(group.other(k)), device_id_type=MESH
        )
    for k in range(1, n):
        pl.semaphore_signal(
            barrier, inc=1, device_id=(lax.rem(place + k, n), group.me), device_id_type=MESH
        )
    pl.semaphore_wait(barrier, heads_n + n - 2)

    ring = Ring(
        ring_streams(value_part, (vs0, vs1))
        + ring_streams(keyquery_part, (ks0, ks1)),
        ring_send,
        ring_recv,
    )
    streams = range(len(ring.streams))
    group_total = Doubling("head", group_sum, group_table, group_send, group_recv)
    line_total = Doubling("seq", line_sum, line_table, line_send, line_recv)
    keyquery_total = Doubling("head", keyquery_sum, keyquery_table, kq_send, kq_recv)

    for i in (0, 1, 2):
        loads[i].wait()

    def weight_block(target, grads):
        def one(i):
            block = pl.ds(pl.multiple_of(i * 256, 256), 256)
            target[block] = dot_tn(normed[:, block], grads[...]).astype(target.dtype)

        loop(D // 256, one)

    weight_block(value_part, values_grad)
    ring.start(0)
    ring.start(1)
    weight_block(keyquery_part, narrow.at[:, : 2 * STATE])
    ring.start(2)
    ring.start(3)
    step_rows = D // n
    for at, size in blocks(D):
        step_whole[:, at : at + size] = dot_tn(narrow[:, 2 * STATE :], normed[:, at : at + size])
    step_part[...] = jnp.zeros_like(step_part)
    for s in range(n):
        step_part[s, :, :step_rows] = step_whole[:16, s * step_rows : (s + 1) * step_rows]

    def step_copy(k, index, sender):
        return remote(
            step_part.at[index],
            step_table.at[sender],
            step_send.at[k - 1],
            step_recv.at[sender],
            (index, group.me),
        )

    for k in range(1, n):
        step_copy(k, lax.rem(place + k, n), place).start()

    for i in (3, 4, 5, 6):
        loads[i].wait()
    columns[...] = jnp.zeros_like(columns)

    def own_columns(row):
        mine = jnp.zeros((1, width), f32)
        for j in range(heads_n):
            mine = mine + jnp.where(group.me == j, row[:, j * width : (j + 1) * width], 0.0)
        return mine

    gain = own_columns(gain_ref[...][None, :])

    def row_block(c):
        return pl.ds(pl.multiple_of(c * length, length), length)

    start_mate, start_chip, total, finish = scatter_phases(
        group, row_block, part, mate_in, chip_out, chip_in, (mate_send, mate_recv, chip_send, chip_recv)
    )

    def product(c):
        row_sum = jnp.zeros((length, LANES), f32)
        for j in range(heads_n):
            lanes = slice(j * width, (j + 1) * width)
            value = dot_nt(gate_grad[row_block(c)], gate_weight[lanes])
            value = value + dot_nt(values_grad[row_block(c)], value_weight[lanes])
            value = value + dot_nt(narrow[row_block(c), : 2 * STATE], keyquery_weight[lanes])
            value = value + jnp.dot(
                narrow[row_block(c), 2 * STATE : 2 * STATE + heads],
                step_weight_ref[:, lanes],
                preferred_element_type=f32,
            )
            part[j, row_block(c)] = value.astype(bf16)
            scaled = value * normed[row_block(c), lanes].astype(f32)
            columns[:, lanes] += jnp.sum(scaled, axis=0, keepdims=True)
            row_sum = row_sum + fold_lanes(scaled)
        dot_out[pl.ds(c, 1)] = jnp.sum(row_sum.T, axis=0, keepdims=True)
        start_mate(c)

        @pl.when(c > 0)
        def _():
            start_chip(c - 1)

        @pl.when(c < n - 2)
        def _():
            for i in streams:
                ring.pass_on(i, c)

    loop(count, product)
    start_chip(count - 1)
    share(group, dot_out, dots, rd_send, rd_recv)

    tiles = Tiles(group_sum)
    group_sum[...] = jnp.zeros_like(group_sum)
    for lag in range(lags + 1):
        tiles.put(conv_grad_ref[lag : lag + 1, channels:])
    tiles.put(columns[...])
    tiles.put(fold_lanes(loss_cols_ref[...]))
    for stage in range(group_total.stages):
        group_total.start(stage)
        group_total.finish(stage)

    tiles, summed = Tiles(line_sum), Tiles(group_sum)
    line_sum[...] = jnp.zeros_like(line_sum)
    for lag in range(lags + 1):
        tiles.put(conv_grad_ref[lag : lag + 1, :channels])
        tiles.put(summed.take(2 * STATE))
    tiles.put(gain_grad_ref[...])
    for i in range(3):
        tiles.put(vector_grad_ref[i : i + 1])
    tiles.put(summed.take(D))
    tiles.put(summed.take(LANES))
    shared(group, dot_out, dots, rd_send, rd_recv)
    dots[group.me] = dot_out[...]

    def rest(c):
        row_sum = dots[0, pl.ds(c, 1)]
        for j in range(1, heads_n):
            row_sum = row_sum + dots[j, pl.ds(c, 1)]
        inverse = inverse_ref[pl.ds(c, 1)]
        tokens = tokens_ref[c]
        out_grad = (output_ref[row_block(c)] - teacher_ref[c]) * as_column(
            long_row(mask_ref, c, length), width
        )
        tokens_grad_out[row_block(c)] = (
            out_grad
            + as_column(inverse, width) * gain * total(c)
            - tokens * as_column(inverse * inverse * row_sum * (1.0 / D), width)
        )

        @pl.when(count + c < n - 2)
        def _():
            for i in streams:
                ring.pass_on(i, count + c)

    loop(count, rest)
    more = n - 2 - 2 * count
    if more > 0:

        def further(s):
            for i in streams:
                ring.pass_on(i, 2 * count + s)

        loop(more, further)
    for stage in range(line_total.stages):
        line_total.start(stage)
        line_total.finish(stage)
    loop(count, finish)

    cut = ks0.shape[2]
    keyquery_sum[:, :cut] = ring.last(2)
    keyquery_sum[:, cut:] = ring.last(3)
    for stage in range(keyquery_total.stages):
        keyquery_total.start(stage)
        keyquery_total.finish(stage)
    keyquery_out[...] = keyquery_sum[...]

    cut = vs0.shape[2]
    value_out[:, :cut] = ring.last(0)
    value_out[:, cut:] = ring.last(1)

    for k in range(1, n):
        sender = lax.rem(place + k, n)
        copy = step_copy(k, sender, sender)
        copy.wait_send()
        copy.wait_recv()
    step_table[place] = step_part[place]
    step_sum = step_table[0]
    for s in range(1, n):
        step_sum = step_sum + step_table[s]
    step_out[...] = step_sum[:heads, :step_rows]

    tiles = Tiles(line_sum)
    for lag in range(lags + 1):
        own_row, shared_row = tiles.take(channels), tiles.take(2 * STATE)
        if lag < lags:
            value_conv_out[lag : lag + 1] = own_row
            keyquery_conv_out[lag : lag + 1] = shared_row
        else:
            value_offset_out[...] = own_row[0]
            keyquery_offset_out[...] = shared_row[0]
    norm_gain_out[...] = tiles.take(channels)[0]
    for target in (step_bias_out, rate_log_out, skip_out):
        target[...] = tiles.take(LANES)[0, :heads]
    input_gain_out[...] = (own_columns(tiles.take(D)) / gain)[0]
    loss_out[...] = 0.5 * jnp.sum(tiles.take(LANES), axis=1, keepdims=True)[0]
    for i in streams:
        ring.finish(i)


def tail(
    normed,
    values_grad,
    narrow,
    gate_grad,
    value_weight,
    gate_weight,
    keyquery_weight,
    step_weight,
    tokens,
    output,
    teacher,
    gain,
    mask_rows,
    inverse_rows,
    conv_grad,
    vector_grad,
    gain_grad,
    loss_cols,
    lags,
    cid,
):
    heads_n, n = lax.axis_size("head"), lax.axis_size("seq")
    count, length, width = tokens.shape
    rows = count * length
    channels = value_weight.shape[1]
    heads = channels // HEADDIM
    both = channels + 2 * STATE
    own = D // n
    step_lanes = -(-own // LANES) * LANES
    buffers, sems = scatter_scratch(heads_n, rows, width, count)
    shape, vmem, dma = jax.ShapeDtypeStruct, pltpu.VMEM, pltpu.SemaphoreType.DMA
    hbm = pl.BlockSpec(memory_space=pl.ANY)
    group_tiles = (lags + 1) * 2 * STATE // LANES + D // LANES + 1
    line_tiles = (lags + 1) * both // LANES + channels // LANES + 3 + D // LANES + 1
    group_shape = (-(-group_tiles * LANES // (8 * 512)) * 8, 512)
    line_shape = (-(-line_tiles * LANES // (8 * both)) * 8, both)
    head_stages, line_stages = stages_of(heads_n), stages_of(n)
    outs = [
        (rows, width),
        (own, channels),
        (own, 2 * STATE),
        (heads, own),
        (lags, channels),
        (channels,),
        (lags, 2 * STATE),
        (2 * STATE,),
        (heads,),
        (heads,),
        (heads,),
        (channels,),
        (width,),
        (1,),
    ]
    slots = ring_slots(n, own, channels, bf16)
    return pl.pallas_call(
        functools.partial(tail_kernel, heads),
        out_shape=[shape(s, f32) for s in outs],
        in_specs=[hbm] * 7 + [in_vmem] * 11,
        out_specs=[in_vmem] * len(outs),
        scratch_shapes=[
            vmem(a.shape, a.dtype)
            for a in (
                normed,
                values_grad,
                narrow,
                gate_grad,
                value_weight,
                gate_weight,
                keyquery_weight,
            )
        ]
        + [
            vmem((D, channels), bf16),
            vmem((D, 2 * STATE), f32),
        ]
        + slots
        + ring_slots(n, own, 2 * STATE, f32)
        + [
            vmem((LANES, D), f32),
            vmem((n, 16, step_lanes), f32),
            vmem((n, 16, step_lanes), f32),
            vmem((own, 2 * STATE), f32),
            vmem((head_stages, own, 2 * STATE), f32),
            vmem(group_shape, f32),
            vmem((head_stages,) + group_shape, f32),
            vmem(line_shape, f32),
            vmem((line_stages,) + line_shape, f32),
            vmem((1, D), f32),
        ]
        + buffers
        + [vmem((heads_n, count, length), f32), vmem((count, length), f32)]
        + [
            dma((7,)),
            dma((4, n - 1)),
            dma((4, n - 1)),
            dma((n - 1,)),
            dma((n,)),
            dma((head_stages,)),
            dma((head_stages,)),
            dma((head_stages,)),
            dma((head_stages,)),
            dma((line_stages,)),
            dma((line_stages,)),
        ]
        + sems
        + [dma((heads_n - 1,)), dma((heads_n,))],
        compiler_params=params(cid),
        name="tail",
    )(
        normed,
        values_grad,
        narrow,
        gate_grad,
        value_weight,
        gate_weight,
        keyquery_weight,
        step_weight,
        tokens,
        output,
        teacher,
        gain,
        mask_rows,
        inverse_rows,
        conv_grad,
        vector_grad,
        gain_grad,
        loss_cols,
    )


def deliver_kernel(count, *refs):
    for source, target in zip(refs[:count], refs[count:]):
        target[...] = source[...]


def deliver(arrays):
    return pl.pallas_call(
        functools.partial(deliver_kernel, len(arrays)),
        out_shape=[jax.ShapeDtypeStruct(a.shape, a.dtype) for a in arrays],
        in_specs=[in_vmem] * len(arrays),
        out_specs=[in_vmem] * len(arrays),
        compiler_params=pltpu.CompilerParams(vmem_limit_bytes=VMEM_LIMIT),
        name="deliver",
    )(*arrays)


def body(
    tokens,
    teacher,
    document_start,
    valid_mask,
    input_gain,
    gate_weight,
    value_weight,
    keyquery_weight,
    step_weight,
    value_conv_weight,
    value_conv_bias,
    keyquery_conv_weight,
    keyquery_conv_bias,
    step_bias,
    rate_log,
    skip_gain,
    norm_gain,
    out_weight,
):
    sequence_index = lax.axis_index("seq")
    count, length, _ = tokens.shape
    channels = gate_weight.shape[1]
    width = teacher.shape[2]
    rows = count * length
    lags = value_conv_weight.shape[0]
    valid_count = jnp.sum(valid_mask.astype(f32))
    local_mask = lax.dynamic_slice_in_dim(valid_mask, sequence_index * length, length, 1)
    mask_rows = (local_mask.astype(f32) * (2.0 / (D * valid_count))).reshape(-1, LANES)
    vectors = (step_bias, rate_log, skip_gain)
    (
        normed,
        linear,
        conv_linear,
        gate_linear,
        mixed,
        gained,
        halo,
        state_in,
        steps,
        cumulative,
        steps_linear,
        square_rows,
        inverse_rows,
    ) = front(
        tokens,
        input_gain,
        value_weight,
        keyquery_weight,
        step_weight.T,
        gate_weight,
        document_start,
        vectors,
        (value_conv_weight, value_conv_bias, keyquery_conv_weight, keyquery_conv_bias),
        norm_gain,
        1,
    )
    output, pieces, rowdot, square_total, loss_cols, token_cols = out_phase(
        gained.reshape(rows, channels), out_weight, square_rows, tokens, teacher, mask_rows, 2
    )
    (
        gate_grad,
        values_grad,
        narrow_grad,
        conv_grad,
        vector_grad,
        gain_grad,
        out_total,
        gate_total,
    ) = back(
        pieces,
        out_weight,
        gate_linear,
        mixed,
        conv_linear,
        linear,
        normed,
        halo,
        state_in,
        steps,
        cumulative,
        steps_linear,
        square_total,
        rowdot,
        document_start,
        vectors,
        value_conv_weight,
        keyquery_conv_weight,
        norm_gain,
        3,
    )
    (
        tokens_grad,
        value_total,
        keyquery_total,
        step_total,
        value_conv_total,
        value_offset_total,
        keyquery_conv_total,
        keyquery_offset_total,
        step_bias_total,
        rate_log_total,
        skip_total,
        norm_gain_total,
        input_gain_total,
        loss_total,
    ) = tail(
        normed.reshape(rows, D),
        values_grad.reshape(rows, channels),
        narrow_grad.reshape(rows, -1),
        gate_grad.reshape(rows, channels),
        value_weight,
        gate_weight,
        keyquery_weight,
        step_weight.T,
        token_cols,
        output,
        teacher,
        input_gain,
        mask_rows,
        inverse_rows,
        conv_grad,
        vector_grad,
        gain_grad,
        loss_cols,
        lags,
        4,
    )
    results = deliver(
        (
            output.reshape(count, length, width),
            loss_total,
            tokens_grad.reshape(count, length, width),
            input_gain_total,
            gate_total,
            value_total,
            keyquery_total,
            step_total,
            value_conv_total,
            value_offset_total,
            keyquery_conv_total,
            keyquery_offset_total,
            step_bias_total,
            rate_log_total,
            skip_total,
            norm_gain_total,
            out_total,
        )
    )
    return (
        results[0],
        results[1].reshape(()),
        *results[2:7],
        results[7].T,
        *results[8:16],
        results[16].T,
    )


def solution(mesh):
    placed = (
        P(None, "seq", None),
        P(None, "seq", "head"),
        P(None, "seq"),
        P(),
        P(),
        P(None, "head"),
        P(None, "head"),
        P(),
        P(None, "head"),
        P(None, "head"),
        P("head"),
        P(),
        P(),
        P("head"),
        P("head"),
        P("head"),
        P("head"),
        P("head", None),
    )
    return jax.shard_map(
        body,
        mesh=mesh,
        in_specs=placed,
        out_specs=(
            P(None, "seq", "head"),
            P(),
            P(None, "seq", "head"),
            P("head"),
            P("seq", "head"),
            P("seq", "head"),
            P("seq", None),
            P("seq", "head"),
            P(None, "head"),
            P("head"),
            P(),
            P(),
            P("head"),
            P("head"),
            P("head"),
            P("head"),
            P("head", "seq"),
        ),
        check_vma=False,
    )
```

```python
import functools
import types

import jax
import jax.numpy as jnp
from jax import lax
from jax.experimental import pallas as pl
from jax.experimental.pallas import tpu as pltpu
from jax.sharding import PartitionSpec as P

D = 1536
NHEADS = 48
HEADDIM = 64
STATE = 128
LANES = 128
VMEM_LIMIT = 62 << 20

norm_eps = 1e-05
highest = lax.Precision.HIGHEST
MESH = pl.DeviceIdType.MESH
f32 = jnp.float32
bf16 = jnp.bfloat16
NT = (((1,), (1,)), ((), ()))
TN = (((0,), (0,)), ((), ()))

in_vmem = pl.BlockSpec(memory_space=pltpu.VMEM)
in_smem = pl.BlockSpec(memory_space=pltpu.SMEM)


def params(cid):
    return pltpu.CompilerParams(
        collective_id=cid, has_side_effects=True, vmem_limit_bytes=VMEM_LIMIT
    )


def remote(src, dst, send, recv, target):
    return pltpu.make_async_remote_copy(
        src_ref=src,
        dst_ref=dst,
        send_sem=send,
        recv_sem=recv,
        device_id=target,
        device_id_type=MESH,
    )


def loop(count, fn):
    lax.fori_loop(0, count, lambda i, c: (fn(i), c)[1], 0)


def dot_nt(a, b, precision=None):
    return lax.dot_general(a, b, NT, precision=precision, preferred_element_type=f32)


def dot_tn(a, b, precision=None):
    return lax.dot_general(a, b, TN, precision=precision, preferred_element_type=f32)


def ring_place(n, index):
    odd, half = lax.rem(index, 2), lax.div(index, 2)
    return half * (1 - odd) + (n - 1 - half) * odd


def ring_index(n, spot):
    late = lax.div(2 * spot, n)
    return 2 * spot * (1 - late) + (2 * (n - 1 - spot) + 1) * late


class Ring:
    def __init__(self, send_sem, recv_sem):
        self.n = lax.axis_size("seq")
        self.streams, self.send_sem, self.recv_sem = [], send_sem, recv_sem
        head = lax.axis_index("head")
        self.spot = ring_place(self.n, lax.axis_index("seq"))
        self.after = (ring_index(self.n, lax.rem(self.spot + 1, self.n)), head)
        self.before = (ring_index(self.n, lax.rem(self.spot + self.n - 1, self.n)), head)

    def add(self, part, slots, by_rows=False, first=0):
        rows, width = part.shape[0] // self.n, part.shape[1]
        cut = slots[0].shape[1] if by_rows else slots[0].shape[2]
        if by_rows:
            halves = tuple(((first + way * cut, cut), (0, width)) for way in range(2))
        else:
            halves = (((0, rows), (0, cut)), ((0, rows), (cut, width - cut)))
        for way in range(2):
            lines, columns = halves[way]
            self.streams.append((part, slots[way], lines, pl.ds(*columns), way))

    def piece(self, i, step):
        part, _, (first, count), columns, way = self.streams[i]
        shift = -1 - step if way == 0 else 1 + step
        rows = part.shape[0] // self.n
        index = ring_index(self.n, lax.rem(self.spot + shift + 2 * self.n, self.n))
        return part.at[pl.ds(pl.multiple_of(index * rows + first, 8), count), columns]

    def copy(self, i, step, source):
        slots, way = self.streams[i][1], self.streams[i][4]
        return remote(
            source,
            slots.at[step],
            self.send_sem.at[i, step],
            self.recv_sem.at[i, step],
            self.after if way == 0 else self.before,
        )

    def start(self, i):
        self.copy(i, 0, self.piece(i, 0)).start()

    def pass_on(self, i, step):
        slots = self.streams[i][1]
        self.copy(i, step, slots.at[step]).wait_recv()
        total = slots[step].astype(f32) + self.piece(i, step + 1)[...].astype(f32)
        slots[step] = total.astype(slots.dtype)
        self.copy(i, step + 1, slots.at[step]).start()

    def last(self, i):
        slots, step = self.streams[i][1], self.n - 2
        self.copy(i, step, slots.at[step]).wait_recv()
        return slots[step].astype(f32) + self.piece(i, step + 1)[...].astype(f32)

    def finish(self, i):
        slots = self.streams[i][1]
        self.copy(i, 0, self.piece(i, 0)).wait_send()
        loop(self.n - 2, lambda step: self.copy(i, step + 1, slots.at[step]).wait_send())


def ring_slots(n, rows, width, kind):
    cut = width // LANES // 2 * LANES
    return [pltpu.VMEM((n - 1, rows, cut), kind), pltpu.VMEM((n - 1, rows, width - cut), kind)]


def step_at(table, here):
    found, here = jnp.int32(-1), jnp.asarray(here, jnp.int32)
    for place, step in table:
        found = found + (step + 1) * (here == place).astype(jnp.int32)
    return found


def sequence_at(table, here, pair):
    found, here = jnp.int32(-1), jnp.asarray(here, jnp.int32)
    for place, owner, b in table:
        found = found + (b + 1) * ((here == place) & (pair == owner)).astype(jnp.int32)
    return found


class PairChain:
    def __init__(self, ahead, by, local, passed, buffers, send_sem, recv_sem):
        self.n = lax.axis_size("seq")
        self.place, self.head = lax.axis_index("seq"), lax.axis_index("head")
        self.by, self.pair, self.second = by, lax.div(ahead, 2), lax.rem(ahead, 2)
        self.local, self.passed = local, passed
        self.state, self.offers, self.offered, self.hand, self.following = buffers
        self.send_sem, self.recv_sem = send_sem, recv_sem
        self.count, _, channels = self.state.shape
        cut = channels // LANES // 2 * LANES
        self.sizes = (channels - cut, cut)
        self.lanes = (pl.ds(cut, channels - cut), pl.ds(0, cut))

    def copy(self, kind, b, source, target, ahead):
        return remote(
            source,
            target,
            self.send_sem.at[kind, b],
            self.recv_sem.at[kind, b],
            (self.place + self.by * ahead, self.head),
        )

    def within(self, buffer, b, second):
        return buffer.at[b, pl.ds(0, buffer.shape[1]), pl.ds(0, self.sizes[second])]

    def offering(self, b, second):
        other = 1 - second
        return self.copy(
            0,
            b,
            self.within(self.offers, b, other),
            self.within(self.offered, b, other),
            1 - 2 * second,
        )

    def handing(self, b, second):
        target = self.state.at[b, pl.ds(0, STATE), self.lanes[second]]
        return self.copy(1, b, self.within(self.hand, b, second), target, 1 - 2 * second)

    def passing(self, b, second):
        if second:
            target = self.within(self.hand, b, second)
        else:
            target = self.state.at[b, pl.ds(0, STATE), self.lanes[second]]
        return self.copy(2, b, self.within(self.following, b, second), target, 2)

    def offer(self, b):
        for second in range(2):

            @pl.when(self.second == second)
            def _():
                other = 1 - second
                lanes, size = self.lanes[other], self.sizes[other]
                self.offers[b, :STATE, :size] = self.local[b, :, lanes].astype(bf16)
                decay = self.passed[b, 7:8, lanes]
                high = decay.astype(bf16).astype(f32)
                row = lax.broadcasted_iota(jnp.int32, (16, size), 0)
                rows = jnp.where(row == 0, high, jnp.where(row == 1, decay - high, 0.0))
                self.offers[b, STATE:, :size] = rows.astype(bf16)
                self.offering(b, second).start()

    def pass_on(self, b):
        more = self.pair < self.n // 2 - 1
        for second in range(2):

            @pl.when(self.second == second)
            def _():
                lanes, size = self.lanes[second], self.sizes[second]
                self.offering(b, 1 - second).wait_recv()

                @pl.when(self.pair > 0)
                def _():
                    self.passing(b, second).wait_recv()

                @pl.when(self.pair == 0)
                def _():
                    zeros = jnp.zeros((STATE, size), bf16)
                    if second:
                        self.hand[b, :, :size] = zeros
                    else:
                        self.state[b, :, lanes] = zeros

                own_decay, own = self.passed[b, 7:8, lanes], self.local[b, :, lanes]
                decay = self.offered[b, STATE:, :size].astype(f32)
                decay = decay[0:1] + decay[1:2]
                offered = self.offered[b, :STATE, :size].astype(f32)
                if second:
                    self.handing(b, second).start()
                    value = decay * self.hand[b, :, :size].astype(f32) + offered
                    self.state[b, :, lanes] = value.astype(bf16)
                    following = own_decay * value + own
                else:
                    value = own_decay * self.state[b, :, lanes].astype(f32) + own
                    self.hand[b, :, :size] = value.astype(bf16)
                    self.handing(b, second).start()
                    following = decay * value + offered

                @pl.when(more)
                def _():
                    self.following[b, :, :size] = following.astype(bf16)
                    self.passing(b, second).start()

    def ready(self, b):
        for second in range(2):

            @pl.when(self.second == second)
            def _():
                self.handing(b, 1 - second).wait_recv()

    def turn(self, here, table):
        b = sequence_at(table, here, self.pair)

        @pl.when(b >= 0)
        def _():
            self.pass_on(b)

    def rest(self, table):
        held = {(pair, b) for _, pair, b in table}
        for pair in range(self.n // 2):
            for b in range(self.count):
                if (pair, b) not in held:

                    @pl.when(self.pair == pair)
                    def _():
                        self.pass_on(b)

    def finish(self):
        for second in range(2):

            @pl.when(self.second == second)
            def _():
                def one(b):
                    self.offering(b, second).wait_send()
                    self.handing(b, second).wait_send()

                    @pl.when(self.pair < self.n // 2 - 1)
                    def _():
                        self.passing(b, second).wait_send()

                loop(self.count, one)


def chain_buffers(count, channels):
    wide = channels - channels // LANES // 2 * LANES
    shapes = [(STATE, channels), (STATE + 16, wide), (STATE + 16, wide), (STATE, wide), (STATE, wide)]
    return [pltpu.VMEM((count,) + s, bf16) for s in shapes]


class Group:
    def __init__(self, n):
        self.n = n
        self.chips = n // 2
        self.seq = lax.axis_index("seq")
        self.me = lax.axis_index("head")
        self.chip = lax.div(self.me, 2)
        self.core = lax.rem(self.me, 2)
        self.mate = self.me + 1 - 2 * self.core

    def at(self, head):
        return (self.seq, head)

    def chip_after(self, k):
        return lax.rem(self.chip + k, self.chips)

    def chip_before(self, k):
        return lax.rem(self.chip + self.chips - k, self.chips)

    def peer(self, k):
        return 2 * self.chip_after(k) + self.core

    def other(self, k):
        return lax.rem(self.me + k, self.n)

    def greet(self):
        barrier = pltpu.get_barrier_semaphore()
        for k in range(1, self.n):
            pl.semaphore_signal(
                barrier, inc=1, device_id=self.at(self.other(k)), device_id_type=MESH
            )
        pl.semaphore_wait(barrier, self.n - 1)


def share(group, source, table, send_sem, recv_sem):
    for k in range(1, group.n):
        remote(
            source,
            table.at[group.me],
            send_sem.at[k - 1],
            recv_sem.at[group.me],
            group.at(group.other(k)),
        ).start()


def shared(group, source, table, send_sem, recv_sem):
    for k in range(1, group.n):
        sender = group.other(k)
        copy = remote(
            source, table.at[sender], send_sem.at[k - 1], recv_sem.at[sender], group.at(sender)
        )
        copy.wait_send()
        copy.wait_recv()


def row_tile(chunk):
    return pl.ds(pl.multiple_of(chunk * LANES, LANES), LANES)


def as_column(row, width):
    tile = jnp.broadcast_to(row, (LANES, row.shape[1])).T
    return jnp.concatenate([tile] * (-(-width // LANES)), axis=1)[:, :width]


def scatter_phases(group, row_block, part, mate_in, chip_out, chip_in, sems):
    mate_send, mate_recv, chip_send, chip_recv = sems

    def mate_copy(c, x):
        return remote(
            part.at[2 * x + 1 - group.core, row_block(c)],
            mate_in.at[x, row_block(c)],
            mate_send.at[x, c],
            mate_recv.at[x, c],
            group.at(group.mate),
        )

    def chip_copy(c, k):
        return remote(
            chip_out.at[k - 1, row_block(c)],
            chip_in.at[k - 1, row_block(c)],
            chip_send.at[k - 1, c],
            chip_recv.at[k - 1, c],
            group.at(group.peer(k)),
        )

    def start_mate(c):
        for x in range(group.chips):
            mate_copy(c, x).start()

    def start_chip(c):
        for x in range(group.chips):
            mate_copy(c, x).wait_recv()
        for k in range(1, group.chips):
            x = group.chip_after(k)
            both = part[2 * x + group.core, row_block(c)].astype(f32) + mate_in[
                x, row_block(c)
            ].astype(f32)
            chip_out[k - 1, row_block(c)] = both.astype(bf16)
            chip_copy(c, k).start()

    def total(c):
        value = part[group.me, row_block(c)].astype(f32) + mate_in[
            group.chip, row_block(c)
        ].astype(f32)
        for k in range(1, group.chips):
            chip_copy(c, k).wait_recv()
            value = value + chip_in[k - 1, row_block(c)].astype(f32)
        return value

    def finish(c):
        for x in range(group.chips):
            mate_copy(c, x).wait_send()
        for k in range(1, group.chips):
            chip_copy(c, k).wait_send()

    return start_mate, start_chip, total, finish


def out_kernel(
    n,
    gated_ref,
    weight_ref,
    square_ref,
    tokens_hbm,
    teacher_hbm,
    mask_ref,
    output_ref,
    grad_ref,
    rowdot_ref,
    squared_ref,
    loss_ref,
    tokens_out,
    tokens_ref,
    teacher_ref,
    part,
    mate_in,
    chip_out,
    chip_in,
    gathered,
    squares,
    dots,
    dot_out,
    mate_send,
    mate_recv,
    chip_send,
    chip_recv,
    gm_send,
    gm_recv,
    gc_send,
    gc_recv,
    gf_send,
    gf_recv,
    sq_send,
    sq_recv,
    rd_send,
    rd_recv,
    load_sem,
):
    group = Group(n)
    count, length, width = tokens_ref.shape
    if tokens_hbm.shape[2] == width:
        token_columns = tokens_hbm
    else:
        start = pl.multiple_of(group.me * width, LANES)
        token_columns = tokens_hbm.at[:, :, pl.ds(start, width)]
    token_load = pltpu.make_async_copy(token_columns, tokens_ref, load_sem.at[0])
    token_load.start()
    teacher_load = pltpu.make_async_copy(teacher_hbm, teacher_ref, load_sem.at[1])
    teacher_load.start()
    group.greet()
    chunks = gated_ref.shape[0] // LANES
    per = length // LANES

    def rows_in(c):
        return lax.div(c, per), pl.ds(pl.multiple_of(lax.rem(c, per) * LANES, LANES), LANES)

    share(group, square_ref, squares, sq_send, sq_recv)
    start_mate, start_chip, total, finish = scatter_phases(
        group, row_tile, part, mate_in, chip_out, chip_in, (mate_send, mate_recv, chip_send, chip_recv)
    )

    def product(c):
        rows = gated_ref[row_tile(c)]
        for j in range(n):
            block = (
                weight_ref[:, j * width : (j + 1) * width] if len(weight_ref.shape) == 2 else weight_ref[j]
            )
            part[j, row_tile(c)] = jnp.dot(rows, block, preferred_element_type=f32).astype(bf16)
        start_mate(c)

    loop(chunks, product)
    loop(chunks, start_chip)
    shared(group, square_ref, squares, sq_send, sq_recv)
    squares[group.me] = square_ref[...]
    loss_ref[...] = jnp.zeros_like(loss_ref)

    def to_mate(c):
        block = gathered.at[group.me, row_tile(c)]
        return remote(block, block, gm_send.at[c], gm_recv.at[c], group.at(group.mate))

    def to_chip(c, k):
        block = gathered.at[group.me, row_tile(c)]
        return remote(
            block, block, gc_send.at[k - 1, c], gc_recv.at[k - 1, c], group.at(group.peer(k))
        )

    def forward(c, k):
        block = gathered.at[2 * group.chip_before(k) + group.core, row_tile(c)]
        return remote(
            block, block, gf_send.at[k - 1, c], gf_recv.at[k - 1, c], group.at(group.mate)
        )

    token_load.wait()
    teacher_load.wait()
    token_store = pltpu.make_async_copy(tokens_ref, tokens_out, load_sem.at[0])
    token_store.start()

    def rest(c):
        squared = squares[0, pl.ds(c, 1)]
        for j in range(1, n):
            squared = squared + squares[j, pl.ds(c, 1)]
        squared_ref[pl.ds(c, 1)] = squared
        scale = lax.rsqrt(squared * (1.0 / (NHEADS * HEADDIM)) + norm_eps)
        branch = total(c) * as_column(scale, width)
        output = tokens_ref[rows_in(c)] + branch
        output_ref[row_tile(c)] = output
        difference = output - teacher_ref[rows_in(c)]
        weighted = difference * as_column(mask_ref[pl.ds(c, 1)], width)
        low = weighted.astype(bf16)
        gathered[group.me, row_tile(c)] = low
        to_mate(c).start()
        for k in range(1, group.chips):
            to_chip(c, k).start()
        loss_ref[...] += jnp.sum(weighted * difference, axis=0, keepdims=True)
        dot_out[pl.ds(c, 1)] = rows_of(low.astype(f32) * branch)

    loop(chunks, rest)
    share(group, dot_out, dots, rd_send, rd_recv)

    def pass_on(c):
        for k in range(1, group.chips):
            to_chip(c, k).wait_recv()
            forward(c, k).start()

    loop(chunks, pass_on)

    def end(c):
        to_mate(c).wait()
        for k in range(1, group.chips):
            to_chip(c, k).wait_send()
            forward(c, k).wait()
        finish(c)
        for j in range(n):
            grad_ref[j, row_tile(c)] = gathered[j, row_tile(c)]

    loop(chunks, end)
    shared(group, dot_out, dots, rd_send, rd_recv)
    row_sum = dot_out[...]
    for k in range(1, n):
        row_sum = row_sum + dots[group.other(k)]
    rowdot_ref[...] = row_sum
    token_store.wait()


def scatter_scratch(n, rows, width, chunks):
    chips = n // 2
    dma = pltpu.SemaphoreType.DMA
    return [
        pltpu.VMEM((n, rows, width), bf16),
        pltpu.VMEM((chips, rows, width), bf16),
        pltpu.VMEM((chips - 1, rows, width), bf16),
        pltpu.VMEM((chips - 1, rows, width), bf16),
    ], [dma((chips, chunks)), dma((chips, chunks)), dma((chips - 1, chunks)), dma((chips - 1, chunks))]


def blocked(weight, n):
    width = weight.shape[1] // n
    if width % LANES == 0:
        return weight
    return jnp.moveaxis(weight.reshape(weight.shape[0], n, width), 1, 0)


def out_phase(gated, weight, square_rows, tokens, teacher, mask_rows, cid):
    n = lax.axis_size("head")
    count, length, width = teacher.shape
    rows = count * length
    chips, chunks = n // 2, rows // LANES
    if width % LANES:
        tokens = lax.dynamic_slice_in_dim(tokens, lax.axis_index("head") * width, width, 2)
    buffers, sems = scatter_scratch(n, rows, width, chunks)
    dma = pltpu.SemaphoreType.DMA
    hbm = pl.BlockSpec(memory_space=pl.ANY)
    return pl.pallas_call(
        functools.partial(out_kernel, n),
        out_shape=[
            jax.ShapeDtypeStruct((rows, width), f32),
            jax.ShapeDtypeStruct((n, rows, width), bf16),
            jax.ShapeDtypeStruct((chunks, LANES), f32),
            jax.ShapeDtypeStruct((chunks, LANES), f32),
            jax.ShapeDtypeStruct((1, width), f32),
            jax.ShapeDtypeStruct((count, length, width), f32),
        ],
        in_specs=[in_vmem] * 3 + [hbm] * 2 + [in_vmem],
        out_specs=[in_vmem] * 5 + [hbm],
        scratch_shapes=[pltpu.VMEM((count, length, width), f32)] * 2
        + buffers
        + [
            pltpu.VMEM((n, rows, width), bf16),
            pltpu.VMEM((n, chunks, LANES), f32),
            pltpu.VMEM((n, chunks, LANES), f32),
            pltpu.VMEM((chunks, LANES), f32),
        ]
        + sems
        + [
            dma((chunks,)),
            dma((chunks,)),
            dma((chips - 1, chunks)),
            dma((chips - 1, chunks)),
            dma((chips - 1, chunks)),
            dma((chips - 1, chunks)),
            dma((n - 1,)),
            dma((n,)),
            dma((n - 1,)),
            dma((n,)),
            dma((2,)),
        ],
        compiler_params=params(cid),
        name="out_phase",
    )(gated, blocked(weight, n), square_rows, tokens, teacher, mask_rows)


def blocks(width, size=256):
    return [(at, min(size, width - at)) for at in range(0, width, size)]


def fold_lanes(values):
    rows, width = values.shape
    if width % LANES:
        fill = jnp.zeros((rows, LANES - width % LANES), values.dtype)
        values = jnp.concatenate([values, fill], axis=1)
    total = values[:, :LANES]
    for at in range(LANES, width, LANES):
        total = total + values[:, at : at + LANES]
    return total


def rows_of(values):
    return jnp.sum(fold_lanes(values).T, axis=0, keepdims=True)


def head_spread(channels):
    row = lax.broadcasted_iota(jnp.int32, (LANES, channels), 0)
    head = lax.broadcasted_iota(jnp.int32, (LANES, channels), 1) // HEADDIM
    return ((row % 16 == head) & (row < 48)).astype(f32).astype(bf16)


def head_gather(channels):
    head = lax.broadcasted_iota(jnp.int32, (channels, LANES), 0) // HEADDIM
    return (lax.broadcasted_iota(jnp.int32, (channels, LANES), 1) == head).astype(f32).astype(bf16)


def spread(values, marks):
    lane = lax.broadcasted_iota(jnp.int32, values.shape, 1)
    values = jnp.where(lane < 16, values, 0.0)
    high = values.astype(bf16).astype(f32)
    left = values - high
    middle = left.astype(bf16).astype(f32)
    low = (left - middle).astype(bf16).astype(f32)
    three = high + pltpu.roll(middle, 16, 1) + pltpu.roll(low, 32, 1)
    return jnp.dot(three.astype(bf16), marks, preferred_element_type=f32)


def gather_heads(values, marks):
    high = values.astype(bf16)
    low = (values - high.astype(f32)).astype(bf16)
    return jnp.dot(high, marks, preferred_element_type=f32) + jnp.dot(
        low, marks, preferred_element_type=f32
    )


def softplus(x):
    y = jnp.exp(-jnp.abs(x))
    small = y * (1.0 - y * (1.0 / 2 - y * (1.0 / 3 - y * (1.0 / 4 - y * (1.0 / 5)))))
    return jnp.maximum(x, 0.0) + jnp.where(y < 0.03, small, jnp.log(1.0 + y))


def lane_row(ref):
    row = ref[...][None, :]
    return jnp.concatenate([row, jnp.zeros((1, LANES - row.shape[1]), f32)], axis=1)


def long_row(ref, b, length):
    per = length // LANES
    return jnp.concatenate([ref[pl.ds(b * per + i, 1)] for i in range(per)], axis=1)


def spread_row(row, marks):
    return spread(jnp.broadcast_to(row, (8, LANES)), marks)[:1]


def position_masks(docs_row, begin):
    length = docs_row.shape[1]
    column = jnp.broadcast_to(docs_row, (LANES, length)).T
    place = begin + lax.broadcasted_iota(jnp.int32, (length, LANES), 0).astype(f32)
    return column, place


def front_kernel(
    heads,
    tokens_hbm,
    gain_ref,
    value_hbm,
    keyquery_hbm,
    step_ref,
    gate_hbm,
    docs_ref,
    step_bias_ref,
    rate_log_ref,
    skip_ref,
    value_conv_ref,
    value_offset_ref,
    keyquery_conv_ref,
    keyquery_offset_ref,
    norm_gain_ref,
    valid_ref,
    normed_out,
    linear_out,
    conv_out,
    gate_out,
    mixed_out,
    gained_out,
    halo_out,
    state_out,
    steps_out,
    cumulative_out,
    linear_steps_out,
    square_out,
    inverse_out,
    mask_out,
    tokens,
    last_tokens,
    value_weight,
    keyquery_weight,
    gate_weight,
    normed,
    linear,
    conv,
    gate,
    mixed,
    gained,
    tail,
    halo,
    extended,
    heads_in,
    keys,
    queries,
    scores,
    mask_bias,
    locals_,
    state,
    offers,
    offered,
    hand,
    following,
    passed,
    entering,
    load_sem,
    last_sem,
    token_sem,
    store_sem,
    halo_sem,
    chain_send,
    chain_recv,
):
    n = lax.axis_size("seq")
    place = lax.axis_index("seq")
    head = lax.axis_index("head")
    count, length, _ = tokens.shape
    channels = value_weight.shape[1]
    both = channels + 2 * STATE
    lags = value_conv_ref.shape[0]
    begin = (place * length).astype(f32)

    loads = [
        pltpu.make_async_copy(value_hbm, value_weight, load_sem.at[0]),
        pltpu.make_async_copy(keyquery_hbm, keyquery_weight, load_sem.at[1]),
        pltpu.make_async_copy(gate_hbm, gate_weight, load_sem.at[2]),
    ]

    def token_load(b):
        return pltpu.make_async_copy(tokens_hbm.at[b], tokens.at[b], token_sem.at[b])

    def last_load(b):
        return pltpu.make_async_copy(
            tokens_hbm.at[b, length - 16 :], last_tokens.at[b], last_sem.at[b]
        )

    for b in range(count):
        last_load(b).start()
    loads[0].start()
    loads[1].start()
    for b in range(count):
        token_load(b).start()
    loads[2].start()

    stores = [
        (normed, normed_out),
        (linear, linear_out),
        (conv, conv_out),
        (gate, gate_out),
        (mixed, mixed_out),
        (gained, gained_out),
    ]

    def store(i, b):
        source, target = stores[i]
        return pltpu.make_async_copy(source.at[b], target.at[b], store_sem.at[i, b])

    barrier = pltpu.get_barrier_semaphore()

    chain = PairChain(
        place,
        1,
        locals_,
        passed,
        (state, offers, offered, hand, following),
        chain_send,
        chain_recv,
    )
    for k in range(1, n):
        pl.semaphore_signal(
            barrier, inc=1, device_id=(lax.rem(place + k, n), head), device_id_type=MESH
        )

    def normalized(x):
        inverse = lax.rsqrt(jnp.mean(x * x, axis=-1, keepdims=True) + norm_eps)
        return inverse, (x * inverse * gain_ref[...][None, :]).astype(bf16)

    for b in range(count):
        last_load(b).wait()
    last = jnp.concatenate([normalized(last_tokens[b])[1] for b in range(count)], axis=0)
    loads[0].wait()
    loads[1].wait()
    for at, width in blocks(channels):
        tail[:, at : at + width] = jnp.dot(
            last, value_weight[:, at : at + width], preferred_element_type=f32
        ).astype(bf16)
    tail[:, channels:] = jnp.dot(last, keyquery_weight[...], preferred_element_type=f32).astype(bf16)
    pl.semaphore_wait(barrier, n - 1)
    halo_copy = remote(tail, halo, halo_sem.at[0], halo_sem.at[1], (place + 1, head))

    @pl.when(place < n - 1)
    def _():
        halo_copy.start()

    marks = head_spread(channels)
    step_bias = lane_row(step_bias_ref)
    decay_rate = -jnp.exp(lane_row(rate_log_ref))
    skip = spread_row(lane_row(skip_ref), marks)
    triangle = (
        lax.broadcasted_iota(jnp.int32, (length, length), 0)
        >= lax.broadcasted_iota(jnp.int32, (length, length), 1)
    ).astype(f32)

    def norm(b):
        token_load(b).wait()
        inverse, rows = normalized(tokens[b])
        normed[b] = rows
        inverse_out[pl.ds(b, 1)] = jnp.broadcast_to(inverse, (length, LANES)).T[:1]
        store(0, b).start()

    def project_values(b):
        rows = normed[b]
        for at, width in blocks(channels):
            linear[b, :, at : at + width] = jnp.dot(
                rows, value_weight[:, at : at + width], preferred_element_type=f32
            ).astype(bf16)

    def project_rest(b):
        rows = normed[b]
        linear[b, :, channels:] = jnp.dot(
            rows, keyquery_weight[...], preferred_element_type=f32
        ).astype(bf16)
        narrow_steps = dot_nt(rows, step_ref[...])
        linear_steps_out[b] = jnp.concatenate(
            [narrow_steps, jnp.zeros((length, LANES - heads), f32)], axis=1
        )
        store(1, b).start()

    def states(b):
        @pl.when((b == 0) & (place > 0))
        def _():
            halo_copy.wait_recv()

        @pl.when((b == 0) & (place == 0))
        def _():
            halo[...] = jnp.zeros_like(halo)

        column, spot = position_masks(docs_ref[pl.ds(b, 1)].astype(f32), begin)
        extended[0:16] = halo[pl.ds(pl.multiple_of(b * 16, 16), 16)].astype(f32)
        extended[16:] = linear[b].astype(f32)
        usable = [None] + [(spot - lag >= column).astype(f32) for lag in range(1, lags)]
        for at in range(0, both, LANES):
            if at < channels:
                weight, offset, place_at = value_conv_ref, value_offset_ref, at
            else:
                weight, offset, place_at = keyquery_conv_ref, keyquery_offset_ref, at - channels
            lanes = slice(place_at, place_at + LANES)
            value = offset[lanes][None, :] + weight[0:1, lanes] * extended[16:, at : at + LANES]
            for lag in range(1, lags):
                value = value + weight[lag : lag + 1, lanes] * (
                    extended[16 - lag : 16 - lag + length, at : at + LANES] * usable[lag]
                )
            conv[b, :, at : at + LANES] = value
            active = value * jax.nn.sigmoid(value)
            if at < channels:
                heads_in[b, :, at : at + LANES] = active
            elif at < channels + STATE:
                keys[b] = active.astype(bf16)
            else:
                queries[b] = active.astype(bf16)
        store(2, b).start()
        steps = softplus(linear_steps_out[b] + step_bias)
        cumulative = jnp.dot(
            triangle, steps * decay_rate, precision=highest, preferred_element_type=f32
        )
        steps_out[b] = steps
        cumulative_out[b] = cumulative
        kept = (column < begin).astype(f32)
        trailing = (spot >= column[length - 1 :]).astype(f32)
        entering[b] = jnp.exp(cumulative) * kept
        end_weight = jnp.exp(cumulative[length - 1 :] - cumulative) * trailing * steps
        weighted = (heads_in[b] * spread(end_weight, marks)).astype(bf16)
        locals_[b] = dot_tn(keys[b], weighted)
        last_entering = entering[b, length - 8 :]
        passed[b] = spread(last_entering, marks)

    pairs = channels // LANES
    turns = (
        [(b + 1 + k, k, b) for b, k in ((0, 0), (1, 0), (2, 0), (0, 1), (1, 1), (0, 2))]
        + [(5, 0, 3), (5, 1, 2), (5, 2, 1), (5, 3, 0), (7, 1, 3), (7, 2, 2), (7, 3, 1)]
        if n == 8 and count == 4
        else []
    )

    def begin_sequence(b):
        norm(b)
        project_values(b)
        project_rest(b)
        states(b)
        chain.offer(b)
        chain.turn(b, turns)

    loop(count, begin_sequence)
    halo_out[...] = halo[...]
    per_row = 2.0 / (D * jnp.sum(valid_ref[...].astype(f32), keepdims=True))
    here = pl.ds(pl.multiple_of(place * length, length), length)
    for b in range(count):
        row = valid_ref[b : b + 1, here].astype(f32) * per_row
        for i in range(length // LANES):
            at = b * (length // LANES) + i
            mask_out[at : at + 1] = row[:, i * LANES : (i + 1) * LANES]
    first_half = lax.broadcasted_iota(jnp.int32, (length, LANES), 1) < HEADDIM
    loads[2].wait()

    def inside(b):
        column, spot = position_masks(docs_ref[pl.ds(b, 1)].astype(f32), begin)
        wide = jnp.concatenate([column] * (length // LANES), axis=1)
        t = begin + lax.broadcasted_iota(jnp.int32, (length, length), 0).astype(f32)
        u = begin + lax.broadcasted_iota(jnp.int32, (length, length), 1).astype(f32)
        mask_bias[...] = jnp.where((u >= wide) & (u <= t), 0.0, -1e30)
        scores[...] = dot_nt(queries[b], keys[b])
        cumulative = cumulative_out[b]
        across = cumulative.T
        spread_steps = spread(steps_out[b], marks)
        for pair in range(pairs):
            lanes = slice(pair * LANES, (pair + 1) * LANES)
            scaled = heads_in[b, :, lanes] * spread_steps[:, lanes]
            value = jnp.zeros((length, LANES), f32)
            for half in range(2):
                h = 2 * pair + half
                decay = jnp.exp(cumulative[:, h : h + 1] - across[h : h + 1] + mask_bias[...])
                mixing = (decay * scores[...]).astype(bf16)
                mine = jnp.where(first_half if half == 0 else ~first_half, scaled, 0.0).astype(bf16)
                value = value + jnp.dot(mixing, mine, preferred_element_type=f32)
            mixed[b, :, lanes] = value
        rows = normed[b]
        for at, width in blocks(channels):
            gate[b, :, at : at + width] = jnp.dot(
                rows, gate_weight[:, at : at + width], preferred_element_type=f32
            )
        store(3, b).start()
        chain.turn(count + b, turns)

    loop(count, inside)
    chain.rest(turns)

    def close(b):
        chain.ready(b)
        state_out[b] = state[b]
        projected = jnp.dot(queries[b], state[b], preferred_element_type=f32)
        value = mixed[b] + spread(entering[b], marks) * projected + skip * heads_in[b]
        mixed[b] = value
        store(4, b).start()
        linear_gate = gate[b]
        gated = value * (linear_gate * jax.nn.sigmoid(linear_gate))
        gained[b] = (gated * norm_gain_ref[...][None, :]).astype(bf16)
        store(5, b).start()
        squared = rows_of(gated * gated)
        for i in range(length // LANES):
            square_out[pl.ds(b * (length // LANES) + i, 1)] = squared[
                :, i * LANES : (i + 1) * LANES
            ]

    loop(count, close)

    @pl.when(place < n - 1)
    def _():
        halo_copy.wait_send()

    chain.finish()

    for i in range(len(stores)):
        loop(count, lambda b, i=i: store(i, b).wait())


def front(tokens, gain, value_weight, keyquery_weight, step_weight, gate_weight, docs, vectors, conv, norm_gain, valid, cid):
    count, length, _ = tokens.shape
    channels = value_weight.shape[1]
    heads = channels // HEADDIM
    both = channels + 2 * STATE
    dma = pltpu.SemaphoreType.DMA
    hbm = pl.BlockSpec(memory_space=pl.ANY)
    shape = jax.ShapeDtypeStruct
    big = [
        ((count, length, D), bf16),
        ((count, length, both), bf16),
        ((count, length, both), f32),
        ((count, length, channels), f32),
        ((count, length, channels), f32),
        ((count, length, channels), bf16),
    ]
    small = [
        ((count * 16, both), bf16),
        ((count, STATE, channels), bf16),
        ((count, length, LANES), f32),
        ((count, length, LANES), f32),
        ((count, length, LANES), f32),
        ((count * length // LANES, LANES), f32),
        ((count, length), f32),
        ((count * length // LANES, LANES), f32),
    ]
    return pl.pallas_call(
        functools.partial(front_kernel, heads),
        out_shape=[shape(*s) for s in big + small],
        in_specs=[hbm, in_vmem, hbm, hbm, in_vmem, hbm] + [in_vmem] * 10,
        out_specs=[hbm] * len(big) + [in_vmem] * len(small),
        scratch_shapes=[
            pltpu.VMEM((count, length, D), f32),
            pltpu.VMEM((count, 16, D), f32),
            pltpu.VMEM((D, channels), bf16),
            pltpu.VMEM((D, 2 * STATE), bf16),
            pltpu.VMEM((D, channels), bf16),
        ]
        + [pltpu.VMEM(*s) for s in big]
        + [
            pltpu.VMEM((count * 16, both), bf16),
            pltpu.VMEM((count * 16, both), bf16),
            pltpu.VMEM((length + 16, both), f32),
            pltpu.VMEM((count, length, channels), f32),
            pltpu.VMEM((count, length, STATE), bf16),
            pltpu.VMEM((count, length, STATE), bf16),
            pltpu.VMEM((length, length), f32),
            pltpu.VMEM((length, length), f32),
            pltpu.VMEM((count, STATE, channels), f32),
        ]
        + chain_buffers(count, channels)
        + [
            pltpu.VMEM((count, 8, channels), f32),
            pltpu.VMEM((count, length, LANES), f32),
            dma((3,)),
            dma((count,)),
            dma((count,)),
            dma((len(big), count)),
            dma((2,)),
            dma((3, count)),
            dma((3, count)),
        ],
        compiler_params=params(cid),
        name="front",
    )(tokens, gain, value_weight, keyquery_weight, step_weight, gate_weight, docs, *vectors, *conv, norm_gain, valid)


class Doubling:
    def __init__(self, axis, bits, current, table, send_sem, recv_sem):
        self.axis, self.bits, self.current, self.table = axis, list(bits), current, table
        self.send_sem, self.recv_sem = send_sem, recv_sem

    def copy(self, stage):
        bit = 1 << self.bits[stage]
        mine = lax.axis_index(self.axis)
        other = mine + bit - 2 * bit * lax.rem(lax.div(mine, bit), 2)
        if self.axis == "head":
            target = (lax.axis_index("seq"), other)
        else:
            target = (other, lax.axis_index("head"))
        return remote(
            self.current,
            self.table.at[stage],
            self.send_sem.at[stage],
            self.recv_sem.at[stage],
            target,
        )

    def start(self, stage):
        self.copy(stage).start()

    def run(self, first, last=None):
        for stage in range(first, len(self.bits) if last is None else min(last, len(self.bits))):
            self.copy(stage).wait()
            self.current[...] = self.current[...] + self.table[stage]
            if stage + 1 < len(self.bits):
                self.start(stage + 1)


def stages_of(n):
    return n.bit_length() - 1


def tile_place(index, width):
    per = width // LANES
    return index // per, slice(index % per * LANES, index % per * LANES + LANES)


class Tiles:
    def __init__(self, ref):
        self.ref, self.index = ref, 0

    def put(self, row):
        for at in range(0, row.shape[1], LANES):
            r, lanes = tile_place(self.index, self.ref.shape[1])
            self.ref[r : r + 1, lanes] = row[:, at : at + LANES]
            self.index += 1

    def take(self, width):
        found = []
        for _ in range(width // LANES):
            r, lanes = tile_place(self.index, self.ref.shape[1])
            found.append(self.ref[r : r + 1, lanes])
            self.index += 1
        return jnp.concatenate(found, axis=1)


def rear_kernel(names, scoped, heads, *refs):
    r = types.SimpleNamespace(**dict(zip(names, refs)))
    n, heads_n = lax.axis_size("seq"), lax.axis_size("head")
    place = lax.axis_index("seq")
    group = Group(heads_n)
    head = group.me
    ahead = n - 1 - place
    count, length, channels = r.gate_grad.shape
    rows = count * length
    both = channels + 2 * STATE
    lags = r.value_conv.shape[0]
    width = r.mate_in.shape[2]
    begin = (place * length).astype(f32)
    inner_total = NHEADS * HEADDIM
    ring_steps = n - 2
    own = D // n
    quarters = own % 64 == 0
    turns, out_steps, gate_steps = [], [], []
    if n == 8 and count == 4:
        turns = [(3, 0, 0), (4, 0, 1), (5, 0, 2), (7, 0, 3)]
        turns += [(6, 1, 0), (8, 1, 1), (9, 1, 2), (11, 1, 3)]
        turns += [(10, 2, 0), (12, 2, 1), (13, 2, 2), (14, 2, 3)]
        turns += [(13, 3, 0), (15, 3, 1), (16, 3, 2), (17, 3, 3)]
        out_steps = [(8, 0), (11, 1), (14, 2), (17, 3), (19, 4), (22, 5)]
        gate_steps = [(18, 0), (21, 1), (23, 2), (25, 3), (28, 4), (30, 5)]

    barrier = pltpu.get_barrier_semaphore()
    for k in range(1, heads_n):
        pl.semaphore_signal(
            barrier, inc=1, device_id=group.at(group.other(k)), device_id_type=MESH
        )
    for k in range(1, n):
        pl.semaphore_signal(
            barrier, inc=1, device_id=(lax.rem(place + k, n), head), device_id_type=MESH
        )

    normed_load = pltpu.make_async_copy(r.normed_hbm, r.normed, r.load_sem.at[0])
    marks = head_spread(channels)
    collect = head_gather(channels)
    step_bias = lane_row(r.step_bias)
    decay_rate = -jnp.exp(lane_row(r.rate_log))
    skip = spread_row(lane_row(r.skip), marks)
    r.gain_grad[...] = jnp.zeros_like(r.gain_grad)
    r.vector_grad[...] = jnp.zeros_like(r.vector_grad)
    r.conv_grad[...] = jnp.zeros_like(r.conv_grad)
    ring = Ring(r.ring_send, r.ring_recv)
    def matrix(part, slots):
        first = len(ring.streams)
        if quarters:
            ring.add(part, slots[:2], by_rows=True)
            ring.add(part, slots[2:], by_rows=True, first=own // 2)
            return first, first + 2
        ring.add(part, slots[:2])
        return (first,)

    out_halves = matrix(r.out_part, (r.os0, r.os1, r.os2, r.os3))
    gate_halves = matrix(r.gate_part, (r.gs0, r.gs1, r.gs2, r.gs3))

    def pass_on(first, step):
        @pl.when((step >= 0) & (step < ring_steps))
        def _():
            ring.pass_on(first, step)
            ring.pass_on(first + 1, step)

    def weights_turn(here, rounds=1):
        known = range(here, here + 2 * rounds, 2) if isinstance(here, int) else None
        for halves, table in ((out_halves, out_steps), (gate_halves, gate_steps)):
            if known is None or any(place in known for place, _ in table):
                step = step_at(table, here)
                for first in halves:
                    pass_on(first, step)

    def start(first):
        ring.start(first)
        ring.start(first + 1)

    def rest_of_ring(halves, done):
        if ring_steps > done:

            def further(s):
                for first in halves:
                    pass_on(first, done + s)

            loop(ring_steps - done, further)

    def total_of(i, halves, sums, targets):
        for k in [first + way for first in halves for way in range(2)]:
            _, _, (first, lines), columns, _ = ring.streams[k]
            sums[i, first : first + lines, columns] = ring.last(k)
        copy = pltpu.make_async_copy(sums.at[i], targets[i], r.total_sem.at[i])
        copy.start()
        return copy

    def as_wide(ref, b):
        return jnp.broadcast_to(long_row(ref, b, length), (LANES, length)).T

    def widened(column, size):
        return jnp.concatenate([column] * (size // LANES), axis=1)

    def weight_block(target, grads, block):
        sides = jnp.concatenate([r.normed[b, :, block] for b in range(count)], axis=0)
        whole = jnp.concatenate([grads(b) for b in range(count)], axis=0)
        target[block] = dot_tn(sides, whole).astype(target.dtype)

    def phase_one(*locals_one):
        q = types.SimpleNamespace(**dict(zip(scoped[0], locals_one)))
        loads = [
            pltpu.make_async_copy(r.out_weight_hbm, q.weight, r.load_sem.at[1]),
            pltpu.make_async_copy(r.pieces_hbm, q.pieces, r.load_sem.at[2]),
        ]
        for copy in loads:
            copy.start()
        row_arrays = [(r.gate_hbm, q.gate), (r.mixed_hbm, q.mixed), (r.conv_hbm, q.conv)]

        def row_load(i, b):
            source, target = row_arrays[i]
            return pltpu.make_async_copy(source.at[b], target.at[b], r.row_sem.at[i, b])

        def linear_load(b):
            slot = lax.rem(b, 2)
            return pltpu.make_async_copy(r.linear_hbm.at[b], q.linear.at[slot], r.line_load.at[slot])

        for b in range(count):
            for i in range(3):
                row_load(i, b).start()
        normed_load.start()
        linear_load(0).start()
        inner = q.gate
        normed_out = r.values_grad
        chain = PairChain(
            ahead,
            -1,
            q.local,
            q.passed,
            (r.state, q.offer, r.offered, r.hand, q.following),
            r.chain_send,
            r.chain_recv,
        )
        pairs = channels // LANES
        for copy in loads:
            copy.wait()
        pl.semaphore_wait(barrier, heads_n + n - 2)
        groups = q.pieces.shape[0]

        def gated_norm(b):
            for i in range(3):
                row_load(i, b).wait()
            scale = lax.rsqrt(as_wide(r.square, b) * (1.0 / inner_total) + norm_eps)
            pull = scale * scale * as_wide(r.rowdot, b) * (1.0 / inner_total)
            column, _ = position_masks(r.docs[pl.ds(b, 1)].astype(f32), begin)
            entering = spread(jnp.exp(r.cumulative[b]) * (column < begin).astype(f32), marks)
            q.passed[b] = entering[length - 8 :]
            here = pl.ds(pl.multiple_of(b * length, length), length)
            for at, size in blocks(channels):
                lanes = slice(at, at + size)
                grad_rows = jnp.zeros((length, size), f32)
                for j in range(groups):
                    block = (
                        q.weight[lanes, j * width : (j + 1) * width]
                        if len(q.weight.shape) == 2
                        else q.weight[j, lanes]
                    )
                    grad_rows = grad_rows + dot_nt(q.pieces[j, here], block)
                linear_gate = q.gate[b, :, lanes]
                sigmoid_value = jax.nn.sigmoid(linear_gate)
                active = linear_gate * sigmoid_value
                value = q.mixed[b, :, lanes]
                gated = value * active
                norm_gain = r.norm_gain[lanes][None, :]
                scaled = gated * widened(scale, size)
                normed_out[b, :, lanes] = (scaled * norm_gain).astype(bf16)
                r.gain_grad[:, lanes] += jnp.sum(grad_rows * scaled, axis=0, keepdims=True)
                gated_grad = widened(scale, size) * norm_gain * grad_rows - gated * widened(
                    pull, size
                )
                q.heads_grad[b, :, lanes] = gated_grad * active
                slope = sigmoid_value * (1.0 + linear_gate * (1.0 - sigmoid_value))
                r.gate_grad[b, :, lanes] = (gated_grad * value * slope).astype(bf16)
                values = q.conv[b, :, lanes]
                q.heads_in[b, :, lanes] = values * jax.nn.sigmoid(values)
            values = q.conv[b, :, channels : channels + STATE]
            q.keys[b] = (values * jax.nn.sigmoid(values)).astype(bf16)
            values = q.conv[b, :, channels + STATE :]
            q.queries[b] = (values * jax.nn.sigmoid(values)).astype(bf16)
            q.local[b] = dot_tn(q.queries[b], (q.heads_grad[b] * entering).astype(bf16))
            chain.offer(b)

        loop(count, gated_norm)
        chain.turn(3, turns)

        for j in range(groups):
            grads = jnp.concatenate([normed_out[b] for b in range(count)], axis=0)
            r.out_part[j * width : (j + 1) * width] = dot_tn(q.pieces[j], grads).astype(bf16)
            if j == groups // 2 - 1:
                chain.turn(4, turns)
        for first in out_halves:
            start(first)
        chain.turn(5, turns)
        normed_load.wait()

        first_half = lax.broadcasted_iota(jnp.int32, (length, LANES), 1) < HEADDIM

        def inside(b):
            docs_row = r.docs[pl.ds(b, 1)].astype(f32)
            u = begin + lax.broadcasted_iota(jnp.int32, (length, length), 0).astype(f32)
            t = begin + lax.broadcasted_iota(jnp.int32, (length, length), 1).astype(f32)
            q.mask_bias[...] = jnp.where((u >= docs_row) & (u <= t), 0.0, -1e30)
            q.scores[...] = dot_nt(q.keys[b], q.queries[b])
            q.scores_grad[...] = jnp.zeros_like(q.scores_grad)
            cumulative = r.cumulative[b]
            across = cumulative.T
            spread_steps = spread(r.steps[b], marks)
            for pair in range(pairs):
                lanes = slice(pair * LANES, (pair + 1) * LANES)
                scaled = q.heads_in[b, :, lanes] * spread_steps[:, lanes]
                grads = q.heads_grad[b, :, lanes]
                low_grads = grads.astype(bf16)
                value = jnp.zeros((length, LANES), f32)
                for half in range(2):
                    h = 2 * pair + half
                    mine = first_half if half == 0 else ~first_half
                    decay = jnp.exp(
                        across[h : h + 1] - cumulative[:, h : h + 1] + q.mask_bias[...]
                    )
                    mixing = (decay * q.scores[...]).astype(bf16)
                    value = value + jnp.dot(
                        mixing, jnp.where(mine, grads, 0.0).astype(bf16), preferred_element_type=f32
                    )
                    pairwise = dot_nt(jnp.where(mine, scaled, 0.0).astype(bf16), low_grads)
                    q.scores_grad[...] += decay * pairwise
                inner[b, :, lanes] = value
                if pair == (pairs - 1) // 2:
                    weights_turn(6 + 2 * b)
                    chain.turn(6 + 2 * b, turns)
            low = q.scores_grad[...].astype(bf16)
            q.narrow_grad[b, :, :STATE] = jnp.dot(low, q.queries[b], preferred_element_type=f32)
            column, _ = position_masks(docs_row, begin)
            entering = jnp.exp(cumulative) * (column < begin).astype(f32)
            x = q.heads_in[b]
            dy = q.heads_grad[b]
            q.narrow_grad[b, :, STATE:] = dot_tn(low, q.keys[b]) + dot_nt(
                (dy * spread(entering, marks)).astype(bf16), r.state_in[b]
            )
            dot_inner = gather_heads(x * inner[b], collect)
            dot_skip = gather_heads(dy * x, collect)
            q.dot_inner[b] = dot_inner
            q.cum_part[b] = (
                gather_heads(dy * (q.mixed[b] - skip * x), collect) - r.steps[b] * dot_inner
            )
            r.vector_grad[2:3] += jnp.sum(dot_skip, axis=0, keepdims=True)
            inner[b] = skip * dy + spread_steps * inner[b]
            weights_turn(7 + 2 * b)
            chain.turn(7 + 2 * b, turns)

        loop(count, inside)
        chain.rest(turns)

        def gate_block(i):
            block = pl.ds(pl.multiple_of(i * 256, 256), 256)
            weight_block(r.gate_part, lambda b: r.gate_grad[b], block)

        loop(D // 512, gate_block)
        weights_turn(14)
        chain.turn(14, turns)
        loop(D // 512, lambda i: gate_block(i + D // 512))
        for first in gate_halves:
            start(first)
        weights_turn(15)
        chain.turn(15, turns)
        q.around[...] = jnp.zeros_like(q.around)
        q.usable[...] = jnp.zeros_like(q.usable)
        upper = (
            lax.broadcasted_iota(jnp.int32, (length, length), 0)
            <= lax.broadcasted_iota(jnp.int32, (length, length), 1)
        ).astype(f32)
        last_row = lax.broadcasted_iota(jnp.int32, (length, LANES), 0) == length - 1

        def edge_copy(b):
            return remote(
                r.edge.at[b], r.edge_in.at[b], r.edge_send.at[b], r.edge_recv.at[b], (place - 1, head)
            )

        def close(b):
            @pl.when(b + 1 < count)
            def _():
                linear_load(b + 1).start()

            column, spot = position_masks(r.docs[pl.ds(b, 1)].astype(f32), begin)
            cumulative = r.cumulative[b]
            steps = r.steps[b]
            kept = (column < begin).astype(f32)
            trailing = (spot >= column[length - 1 :]).astype(f32)
            entering = jnp.exp(cumulative) * kept
            end_decay = jnp.exp(cumulative[length - 1 :] - cumulative) * trailing
            end_weight = end_decay * steps
            chain.ready(b)
            end_grad = r.state[b]
            x = q.heads_in[b]
            grown = jnp.dot(q.keys[b], end_grad, preferred_element_type=f32)
            spread_end = spread(end_weight, marks)
            q.narrow_grad[b, :, :STATE] += dot_nt((x * spread_end).astype(bf16), end_grad)
            grad = inner[b] + spread_end * grown
            dot_end = gather_heads(x * grown, collect)
            through = jnp.sum(
                end_grad.astype(f32) * r.state_in[b].astype(f32), axis=0, keepdims=True
            )
            passed_grad = gather_heads(jnp.broadcast_to(through, (8, channels)), collect)[:1]
            end_mix = dot_end * end_weight
            last_term = passed_grad * entering[length - 1 :] + jnp.sum(
                end_mix, axis=0, keepdims=True
            )
            cum_grad = q.cum_part[b] - end_mix + jnp.where(last_row, last_term, 0.0)
            rates_grad = jnp.dot(upper, cum_grad, precision=highest, preferred_element_type=f32)
            steps_grad = q.dot_inner[b] + end_decay * dot_end + rates_grad * decay_rate
            linear_grad = steps_grad * jax.nn.sigmoid(r.linear_steps[b] + step_bias)
            r.narrow[b, :, 2 * STATE :] = linear_grad.astype(bf16)
            r.vector_grad[0:1] += jnp.sum(linear_grad, axis=0, keepdims=True)
            r.vector_grad[1:2] += jnp.sum(rates_grad * steps, axis=0, keepdims=True) * decay_rate

            weights_turn(16 + 2 * b)
            chain.turn(16 + 2 * b, turns)
            linear_load(b).wait()
            halo_rows = pl.ds(pl.multiple_of(b * 16, 16), 16)
            line = lax.rem(b, 2)
            middle = slice(16, 16 + length)
            for lag in range(1, lags):
                q.usable[lag - 1, middle] = (spot - lag >= column).astype(f32)
            for at in range(0, both, LANES):
                lanes = slice(at, at + LANES)
                slot = at // LANES % 2
                q.extended[slot, 0:16] = r.halo[halo_rows, lanes].astype(f32)
                q.extended[slot, 16:] = q.linear[line, :, lanes].astype(f32)
                values = q.conv[b, :, lanes]
                sigmoid_value = jax.nn.sigmoid(values)
                slope = sigmoid_value * (1.0 + values * (1.0 - sigmoid_value))
                if at < channels:
                    out_grad = grad[:, lanes]
                    taps, tap = r.value_conv, lanes
                else:
                    place_at = at - channels
                    out_grad = q.narrow_grad[b, :, place_at : place_at + LANES]
                    taps, tap = r.keyquery_conv, slice(place_at, place_at + LANES)
                local = out_grad * slope
                q.around[slot, middle] = local
                input_grad = taps[0:1, tap] * local
                edges = jnp.zeros((8, LANES), f32)
                r.conv_grad[0:1, lanes] += jnp.sum(
                    local * q.extended[slot, middle], axis=0, keepdims=True
                )
                r.conv_grad[lags : lags + 1, lanes] += jnp.sum(local, axis=0, keepdims=True)
                for lag in range(1, lags):
                    mask = q.usable[lag - 1, middle]
                    r.conv_grad[lag : lag + 1, lanes] += jnp.sum(
                        local * mask * q.extended[slot, 16 - lag : 16 - lag + length],
                        axis=0,
                        keepdims=True,
                    )
                    later = slice(16 + lag, 16 + lag + length)
                    input_grad = input_grad + taps[lag : lag + 1, tap] * (
                        q.around[slot, later] * q.usable[lag - 1, later]
                    )
                    first = slice(8 + lag, 16 + lag)
                    edges = edges + taps[lag : lag + 1, tap] * (
                        q.around[slot, first] * q.usable[lag - 1, first]
                    )
                r.edge[b, :, lanes] = edges
                q.tails[b, :, lanes] = input_grad[length - 16 :]
                if at < channels:
                    r.values_grad[b, :, lanes] = input_grad.astype(bf16)
                else:
                    r.narrow[b, :, tap] = input_grad.astype(bf16)

            @pl.when(place > 0)
            def _():
                edge_copy(b).start()

            weights_turn(17 + 2 * b)
            chain.turn(17 + 2 * b, turns)

        loop(count, close)

        @pl.when(place < n - 1)
        def _():
            def join(b):
                edge_copy(b).wait_recv()
                last = slice(length - 16, length)
                q.tails[b, 8:] = q.tails[b, 8:] + r.edge_in[b]
                r.values_grad[b, last] = q.tails[b, :, :channels].astype(bf16)
                r.narrow[b, last, : 2 * STATE] = q.tails[b, :, channels:].astype(bf16)

            loop(count, join)

        @pl.when(place > 0)
        def _():
            loop(count, lambda b: edge_copy(b).wait_send())

        chain.finish()

    pl.run_scoped(phase_one, *scoped[1])

    def phase_two(*locals_two):
        q = types.SimpleNamespace(**dict(zip(scoped[2], locals_two)))
        loads = [
            pltpu.make_async_copy(source, target, r.load_two.at[i])
            for i, (source, target) in enumerate(
                [
                    (r.gate_weight_hbm, q.gate_weight),
                    (r.value_weight_hbm, q.value_weight),
                    (r.keyquery_weight_hbm, q.keyquery_weight),
                    (r.tokens_hbm, q.tokens),
                    (r.output_hbm, q.output),
                    (r.teacher_hbm, q.teacher),
                ]
            )
        ]
        for copy in loads:
            copy.start()
        value_halves = matrix(q.value_part, (r.vs0, r.vs1, r.vs2, r.vs3))
        keyquery_first = len(ring.streams)
        ring.add(q.keyquery_half, (r.ks0, r.ks1), by_rows=True)

        def value_block(i):
            block = pl.ds(pl.multiple_of(i * 256, 256), 256)
            weight_block(q.value_part, lambda b: r.values_grad[b], block)

        loop(D // 512, value_block)
        weights_turn(24)
        loop(D // 512, lambda i: value_block(i + D // 512))
        for first in value_halves:
            start(first)
        weights_turn(25)

        def narrow_block(i):
            block = pl.ds(pl.multiple_of(i * 256, 256), 256)
            for half in range(2):
                lanes = slice(half * STATE, (half + 1) * STATE)
                weight_block(q.keyquery_part.at[half], lambda b: r.narrow[b, :, lanes], block)

        loop(D // 256, narrow_block)
        keyquery_mate = remote(
            q.keyquery_part.at[1 - group.core],
            r.keyquery_in,
            r.small_send.at[0],
            r.small_recv.at[0],
            group.at(group.mate),
        )
        keyquery_mate.start()
        weights_turn(26)
        targets = (r.out_total, r.gate_total, r.value_total)

        def end_ring(i, halves, done):
            rest_of_ring(halves, done)
            return total_of(i, halves, q.sums, targets)

        for copy in loads[:3]:
            copy.wait()
        q.columns[...] = jnp.zeros_like(q.columns)

        def own_columns(row):
            mine = jnp.zeros((1, width), f32)
            for j in range(heads_n):
                mine = mine + jnp.where(head == j, row[:, j * width : (j + 1) * width], 0.0)
            return mine

        gain = own_columns(r.gain[...][None, :])

        def row_block(c):
            return pl.ds(pl.multiple_of(c * length, length), length)

        start_mate, start_chip, total, finish = scatter_phases(
            group,
            row_block,
            q.part,
            r.mate_in,
            q.chip_out,
            r.chip_in,
            (r.mate_send, r.mate_recv, r.chip_send, r.chip_recv),
        )

        def value_turn(s):
            if s < ring_steps:
                for first in value_halves:
                    pass_on(first, s)

        def keyquery_turn(s):
            if s < ring_steps:
                pass_on(keyquery_first, s)

        def product(c):
            row_sum = jnp.zeros((length, LANES), f32)
            for j in range(heads_n):
                lanes = slice(j * width, (j + 1) * width)
                value = dot_nt(r.gate_grad[c], q.gate_weight[lanes])
                value = value + dot_nt(r.values_grad[c], q.value_weight[lanes])
                value = value + dot_nt(r.narrow[c, :, : 2 * STATE], q.keyquery_weight[lanes])
                value = value + jnp.dot(
                    r.narrow[c, :, 2 * STATE : 2 * STATE + heads],
                    r.step_weight[:, lanes],
                    preferred_element_type=f32,
                )
                q.part[j, row_block(c)] = value.astype(bf16)
                scaled = value * r.normed[c, :, lanes].astype(f32)
                q.columns[:, lanes] += jnp.sum(scaled, axis=0, keepdims=True)
                row_sum = row_sum + fold_lanes(scaled)
            r.dot_out[pl.ds(c, 1)] = jnp.sum(row_sum.T, axis=0, keepdims=True)
            start_mate(c)

            @pl.when(c > 0)
            def _():
                start_chip(c - 1)

        product(0)
        keyquery_mate.wait_recv()
        q.keyquery_half[...] = q.keyquery_part[group.core] + r.keyquery_in[...]
        start(keyquery_first)
        total_copies = [end_ring(0, out_halves, len(out_steps))]
        product(1)
        weights_turn(28)
        product(2)
        value_turn(0)
        keyquery_turn(0)
        product(3)
        start_chip(count - 1)
        weights_turn(30)
        share(group, r.dot_out, r.dots, r.rd_send, r.rd_recv)

        group_total = Doubling(
            "head", range(stages_of(heads_n)), r.group_sum, r.group_table, r.group_send, r.group_recv
        )
        line_total = Doubling(
            "seq", range(stages_of(n)), r.line_sum, r.line_table, r.line_send, r.line_recv
        )
        chip_total = Doubling(
            "head",
            range(1, stages_of(heads_n)),
            r.keyquery_sum,
            r.keyquery_table,
            r.kq_send,
            r.kq_recv,
        )
        tiles = Tiles(r.group_sum)
        r.group_sum[...] = jnp.zeros_like(r.group_sum)
        for lag in range(lags + 1):
            tiles.put(r.conv_grad[lag : lag + 1, channels:])
        tiles.put(q.columns[...])
        tiles.put(fold_lanes(r.loss_cols[...]))
        group_total.start(0)
        value_turn(1)
        keyquery_turn(1)

        for at, size in blocks(D):
            whole = jnp.concatenate([r.normed[b, :, at : at + size] for b in range(count)], axis=0)
            grads = jnp.concatenate([r.narrow[b, :, 2 * STATE :] for b in range(count)], axis=0)
            q.step_whole[:, at : at + size] = dot_tn(grads, whole)
        q.step_part[...] = jnp.zeros_like(q.step_part)
        for s in range(n):
            q.step_part[s, :, :own] = q.step_whole[:16, s * own : (s + 1) * own]

        def step_copy(k, index, sender):
            return remote(
                q.step_part.at[index],
                r.step_table.at[sender],
                r.step_send.at[k - 1],
                r.step_recv.at[sender],
                (index, head),
            )

        for k in range(1, n):
            step_copy(k, lax.rem(place + k, n), place).start()
        total_copies.append(end_ring(1, gate_halves, len(gate_steps)))
        value_turn(2)
        keyquery_turn(2)
        group_total.run(0, 1)
        shared(group, r.dot_out, r.dots, r.rd_send, r.rd_recv)
        r.dots[head] = r.dot_out[...]
        for copy in loads[3:]:
            copy.wait()

        def fill_line():
            tiles, summed = Tiles(r.line_sum), Tiles(r.group_sum)
            r.line_sum[...] = jnp.zeros_like(r.line_sum)
            for lag in range(lags + 1):
                tiles.put(r.conv_grad[lag : lag + 1, :channels])
                tiles.put(summed.take(2 * STATE))
            tiles.put(r.gain_grad[...])
            for i in range(3):
                tiles.put(r.vector_grad[i : i + 1])
            tiles.put(summed.take(D))
            tiles.put(summed.take(LANES))

        def grad_store(c):
            return pltpu.make_async_copy(q.tokens_grad.at[c], r.tokens_grad.at[c], r.grad_sem.at[c])

        def rest(c):
            row_sum = r.dots[0, c : c + 1]
            for j in range(1, heads_n):
                row_sum = row_sum + r.dots[j, c : c + 1]
            inverse = r.inverse[c : c + 1]
            out_grad = (q.output[row_block(c)] - q.teacher[c]) * as_column(
                long_row(r.mask, c, length), width
            )
            q.tokens_grad[c] = (
                out_grad
                + as_column(inverse, width) * gain * total(c)
                - q.tokens[c] * as_column(inverse * inverse * row_sum * (1.0 / D), width)
            )
            grad_store(c).start()

        rest(0)
        rest(1)
        value_turn(3)
        keyquery_turn(3)
        group_total.run(1)
        fill_line()
        line_total.start(0)
        rest(2)
        value_turn(4)
        keyquery_turn(4)
        line_total.run(0, 1)
        for c in range(3, count):
            rest(c)
        value_turn(5)
        keyquery_turn(5)
        line_total.run(1, 2)
        if ring_steps > 6:

            def remaining(s):
                for first in value_halves + (keyquery_first,):
                    pass_on(first, s + 6)

            loop(ring_steps - 6, remaining)
        for k in (keyquery_first, keyquery_first + 1):
            _, _, (first, lines), _, _ = ring.streams[k]
            r.keyquery_sum[first : first + lines] = ring.last(k)
        chip_total.start(0)
        total_copies.append(total_of(2, value_halves, q.sums, targets))
        for k in range(1, n):
            sender = lax.rem(place + k, n)
            copy = step_copy(k, sender, sender)
            copy.wait_send()
            copy.wait_recv()
        r.step_table[place] = q.step_part[place]
        step_sum = r.step_table[0]
        for s in range(1, n):
            step_sum = step_sum + r.step_table[s]
        r.step_total[...] = step_sum[:heads, :own]
        line_total.run(2)
        chip_total.run(0)
        keyquery_swap = remote(
            r.keyquery_sum,
            r.keyquery_other,
            r.small_send.at[1],
            r.small_recv.at[1],
            group.at(group.mate),
        )
        keyquery_swap.start()

        tiles = Tiles(r.line_sum)
        for lag in range(lags + 1):
            own_row, shared_row = tiles.take(channels), tiles.take(2 * STATE)
            if lag < lags:
                r.value_conv_total[lag : lag + 1] = own_row
                r.keyquery_conv_total[lag : lag + 1] = shared_row
            else:
                r.value_offset_total[...] = own_row[0]
                r.keyquery_offset_total[...] = shared_row[0]
        r.norm_gain_total[...] = tiles.take(channels)[0]
        for target in (r.step_bias_total, r.rate_log_total, r.skip_total):
            target[...] = tiles.take(LANES)[0, :heads]
        r.input_gain_total[...] = (own_columns(tiles.take(D)) / gain)[0]
        r.loss_total[...] = 0.5 * jnp.sum(tiles.take(LANES), axis=1, keepdims=True)[0]

        loop(count, finish)
        for c in range(count):
            grad_store(c).wait()
        for copy in total_copies:
            copy.wait()
        keyquery_mate.wait_send()
        keyquery_swap.wait()
        mine, other = r.keyquery_sum[...], r.keyquery_other[...]
        r.keyquery_total[:, :STATE] = jnp.where(group.core == 0, mine, other)
        r.keyquery_total[:, STATE:] = jnp.where(group.core == 0, other, mine)
        for i in range(len(ring.streams)):
            ring.finish(i)

    pl.run_scoped(phase_two, *scoped[3])


def rear(inputs, lags, cid):
    heads_n, n = lax.axis_size("head"), lax.axis_size("seq")
    count, length, channels = inputs["gate_hbm"].shape
    pieces = inputs["pieces_hbm"]
    rows, width = pieces.shape[1:]
    heads = channels // HEADDIM
    both = channels + 2 * STATE
    own = D // n
    step_lanes = -(-own // LANES) * LANES
    chips = heads_n // 2
    vmem, dma = pltpu.VMEM, pltpu.SemaphoreType.DMA
    hbm = pl.BlockSpec(memory_space=pl.ANY)
    group_tiles = (lags + 1) * 2 * STATE // LANES + D // LANES + 1
    line_tiles = (lags + 1) * both // LANES + channels // LANES + 3 + D // LANES + 1
    group_shape = (-(-group_tiles * LANES // (8 * 512)) * 8, 512)
    line_shape = (-(-line_tiles * LANES // (8 * both)) * 8, both)
    head_stages, line_stages = stages_of(heads_n), stages_of(n)
    outs = {
        "tokens_grad": (count, length, width),
        "out_total": (own, channels),
        "gate_total": (own, channels),
        "value_total": (own, channels),
        "keyquery_total": (own, 2 * STATE),
        "step_total": (heads, own),
        "value_conv_total": (lags, channels),
        "value_offset_total": (channels,),
        "keyquery_conv_total": (lags, 2 * STATE),
        "keyquery_offset_total": (2 * STATE,),
        "step_bias_total": (heads,),
        "rate_log_total": (heads,),
        "skip_total": (heads,),
        "norm_gain_total": (channels,),
        "input_gain_total": (width,),
        "loss_total": (1,),
    }
    if own % 64 == 0:
        slots = [vmem((n - 1, own // 4, channels), bf16)] * 4
    else:
        slots = ring_slots(n, own, channels, bf16) + [vmem((16, LANES), bf16)] * 2
    chained = chain_buffers(count, channels)
    scratch = {
        "normed": vmem((count, length, D), bf16),
        "gate_grad": vmem((count, length, channels), bf16),
        "values_grad": vmem((count, length, channels), bf16),
        "narrow": vmem((count, length, 2 * STATE + LANES), bf16),
        "out_part": vmem((D, channels), bf16),
        "gate_part": vmem((D, channels), bf16),
        "os0": slots[0],
        "os1": slots[1],
        "os2": slots[2],
        "os3": slots[3],
        "gs0": slots[0],
        "gs1": slots[1],
        "gs2": slots[2],
        "gs3": slots[3],
        "vs0": slots[0],
        "vs1": slots[1],
        "vs2": slots[2],
        "vs3": slots[3],
        "ks0": vmem((n - 1, own // 2, STATE), f32),
        "ks1": vmem((n - 1, own // 2, STATE), f32),
        "state": chained[0],
        "offered": chained[2],
        "hand": chained[3],
        "edge": vmem((count, 8, both), f32),
        "edge_in": vmem((count, 8, both), f32),
        "gain_grad": vmem((1, channels), f32),
        "vector_grad": vmem((8, LANES), f32),
        "conv_grad": vmem((8, both), f32),
        "mate_in": vmem((chips, rows, width), bf16),
        "chip_in": vmem((chips - 1, rows, width), bf16),
        "dots": vmem((heads_n, count, length), f32),
        "dot_out": vmem((count, length), f32),
        "keyquery_in": vmem((D, STATE), f32),
        "keyquery_sum": vmem((own, STATE), f32),
        "keyquery_other": vmem((own, STATE), f32),
        "keyquery_table": vmem((head_stages - 1, own, STATE), f32),
        "step_table": vmem((n, 16, step_lanes), f32),
        "group_sum": vmem(group_shape, f32),
        "group_table": vmem((head_stages,) + group_shape, f32),
        "line_sum": vmem(line_shape, f32),
        "line_table": vmem((line_stages,) + line_shape, f32),
        "load_sem": dma((3,)),
        "row_sem": dma((3, count)),
        "line_load": dma((2,)),
        "load_two": dma((6,)),
        "grad_sem": dma((count,)),
        "total_sem": dma((3,)),
        "edge_send": dma((count,)),
        "edge_recv": dma((count,)),
        "chain_send": dma((3, count)),
        "chain_recv": dma((3, count)),
        "ring_send": dma((14, n - 1)),
        "ring_recv": dma((14, n - 1)),
        "mate_send": dma((chips, count)),
        "mate_recv": dma((chips, count)),
        "chip_send": dma((chips - 1, count)),
        "chip_recv": dma((chips - 1, count)),
        "rd_send": dma((heads_n - 1,)),
        "rd_recv": dma((heads_n,)),
        "small_send": dma((2,)),
        "small_recv": dma((2,)),
        "kq_send": dma((head_stages - 1,)),
        "kq_recv": dma((head_stages - 1,)),
        "group_send": dma((head_stages,)),
        "group_recv": dma((head_stages,)),
        "line_send": dma((line_stages,)),
        "line_recv": dma((line_stages,)),
        "step_send": dma((n - 1,)),
        "step_recv": dma((n,)),
    }
    first = {
        "weight": vmem(inputs["out_weight_hbm"].shape, bf16),
        "pieces": vmem(pieces.shape, bf16),
        "gate": vmem((count, length, channels), f32),
        "mixed": vmem((count, length, channels), f32),
        "conv": vmem((count, length, both), f32),
        "linear": vmem((2, length, both), bf16),
        "heads_in": vmem((count, length, channels), f32),
        "heads_grad": vmem((count, length, channels), f32),
        "keys": vmem((count, length, STATE), bf16),
        "queries": vmem((count, length, STATE), bf16),
        "scores": vmem((length, length), f32),
        "scores_grad": vmem((length, length), f32),
        "mask_bias": vmem((length, length), f32),
        "narrow_grad": vmem((count, length, 2 * STATE), f32),
        "local": vmem((count, STATE, channels), f32),
        "passed": vmem((count, 8, channels), f32),
        "offer": chained[1],
        "following": chained[4],
        "extended": vmem((2, length + 16, LANES), f32),
        "around": vmem((2, length + 32, LANES), f32),
        "usable": vmem((lags - 1, length + 32, LANES), f32),
        "tails": vmem((count, 16, both), f32),
        "dot_inner": vmem((count, length, LANES), f32),
        "cum_part": vmem((count, length, LANES), f32),
    }
    second = {
        "gate_weight": vmem((D, channels), bf16),
        "value_weight": vmem((D, channels), bf16),
        "keyquery_weight": vmem((D, 2 * STATE), bf16),
        "tokens": vmem((count, length, width), f32),
        "output": vmem((rows, width), f32),
        "teacher": vmem((count, length, width), f32),
        "tokens_grad": vmem((count, length, width), f32),
        "value_part": vmem((D, channels), bf16),
        "keyquery_part": vmem((2, D, STATE), f32),
        "keyquery_half": vmem((D, STATE), f32),
        "part": vmem((heads_n, rows, width), bf16),
        "chip_out": vmem((chips - 1, rows, width), bf16),
        "columns": vmem((1, D), f32),
        "step_whole": vmem((LANES, D), f32),
        "step_part": vmem((n, 16, step_lanes), f32),
        "sums": vmem((3, own, channels), f32),
    }
    names = list(inputs) + list(outs) + list(scratch)
    scoped = (list(first), list(first.values()), list(second), list(second.values()))
    in_hbm = [name.endswith("_hbm") for name in inputs]
    found = pl.pallas_call(
        functools.partial(rear_kernel, names, scoped, heads),
        out_shape=[jax.ShapeDtypeStruct(s, f32) for s in outs.values()],
        in_specs=[hbm if there else in_vmem for there in in_hbm],
        out_specs=[hbm] * 4 + [in_vmem] * (len(outs) - 4),
        scratch_shapes=list(scratch.values()),
        compiler_params=params(cid),
        name="rear",
    )(*inputs.values())
    return dict(zip(outs, found))


def deliver_kernel(count, *refs):
    for source, target in zip(refs[:count], refs[count:]):
        target[...] = source[...]


def deliver(arrays):
    return pl.pallas_call(
        functools.partial(deliver_kernel, len(arrays)),
        out_shape=[jax.ShapeDtypeStruct(a.shape, a.dtype) for a in arrays],
        in_specs=[in_vmem] * len(arrays),
        out_specs=[in_vmem] * len(arrays),
        compiler_params=pltpu.CompilerParams(vmem_limit_bytes=VMEM_LIMIT),
        name="deliver",
    )(*arrays)


def body(
    tokens,
    teacher,
    document_start,
    valid_mask,
    input_gain,
    gate_weight,
    value_weight,
    keyquery_weight,
    step_weight,
    value_conv_weight,
    value_conv_bias,
    keyquery_conv_weight,
    keyquery_conv_bias,
    step_bias,
    rate_log,
    skip_gain,
    norm_gain,
    out_weight,
):
    count, length, _ = tokens.shape
    channels = gate_weight.shape[1]
    width = teacher.shape[2]
    rows = count * length
    lags = value_conv_weight.shape[0]
    vectors = (step_bias, rate_log, skip_gain)
    (
        normed,
        linear,
        conv_linear,
        gate_linear,
        mixed,
        gained,
        halo,
        state_in,
        steps,
        cumulative,
        steps_linear,
        square_rows,
        inverse_rows,
        mask_rows,
    ) = front(
        tokens,
        input_gain,
        value_weight,
        keyquery_weight,
        step_weight.T,
        gate_weight,
        document_start,
        vectors,
        (value_conv_weight, value_conv_bias, keyquery_conv_weight, keyquery_conv_bias),
        norm_gain,
        valid_mask,
        1,
    )
    output, pieces, rowdot, square_total, loss_cols, token_cols = out_phase(
        gained.reshape(rows, channels), out_weight, square_rows, tokens, teacher, mask_rows, 2
    )
    totals = rear(
        {
            "pieces_hbm": pieces,
            "out_weight_hbm": blocked(out_weight, pieces.shape[0]),
            "gate_hbm": gate_linear,
            "mixed_hbm": mixed,
            "conv_hbm": conv_linear,
            "linear_hbm": linear,
            "normed_hbm": normed,
            "gate_weight_hbm": gate_weight,
            "value_weight_hbm": value_weight,
            "keyquery_weight_hbm": keyquery_weight,
            "tokens_hbm": token_cols,
            "output_hbm": output,
            "teacher_hbm": teacher,
            "step_weight": step_weight.T,
            "halo": halo,
            "state_in": state_in,
            "steps": steps,
            "cumulative": cumulative,
            "linear_steps": steps_linear,
            "square": square_total,
            "rowdot": rowdot,
            "docs": document_start,
            "step_bias": step_bias,
            "rate_log": rate_log,
            "skip": skip_gain,
            "value_conv": value_conv_weight,
            "keyquery_conv": keyquery_conv_weight,
            "norm_gain": norm_gain,
            "gain": input_gain,
            "mask": mask_rows,
            "inverse": inverse_rows,
            "loss_cols": loss_cols,
        },
        lags,
        3,
    )
    results = deliver(
        (
            output.reshape(count, length, width),
            totals["loss_total"],
            totals["tokens_grad"],
            totals["input_gain_total"],
            totals["gate_total"],
            totals["value_total"],
            totals["keyquery_total"],
            totals["step_total"],
            totals["value_conv_total"],
            totals["value_offset_total"],
            totals["keyquery_conv_total"],
            totals["keyquery_offset_total"],
            totals["step_bias_total"],
            totals["rate_log_total"],
            totals["skip_total"],
            totals["norm_gain_total"],
            totals["out_total"],
        )
    )
    return (
        results[0],
        results[1].reshape(()),
        *results[2:7],
        results[7].T,
        *results[8:16],
        results[16].T,
    )


def solution(mesh):
    placed = (
        P(None, "seq", None),
        P(None, "seq", "head"),
        P(None, "seq"),
        P(),
        P(),
        P(None, "head"),
        P(None, "head"),
        P(),
        P(None, "head"),
        P(None, "head"),
        P("head"),
        P(),
        P(),
        P("head"),
        P("head"),
        P("head"),
        P("head"),
        P("head", None),
    )
    return jax.shard_map(
        body,
        mesh=mesh,
        in_specs=placed,
        out_specs=(
            P(None, "seq", "head"),
            P(),
            P(None, "seq", "head"),
            P("head"),
            P("seq", "head"),
            P("seq", "head"),
            P("seq", None),
            P("seq", "head"),
            P(None, "head"),
            P("head"),
            P(),
            P(),
            P("head"),
            P("head"),
            P("head"),
            P("head"),
            P("head", "seq"),
        ),
        check_vma=False,
    )
```

```python
import functools
import types

import jax
import jax.numpy as jnp
from jax import lax
from jax.experimental import pallas as pl
from jax.experimental.pallas import tpu as pltpu
from jax.sharding import PartitionSpec as P

D = 1536
NHEADS = 48
HEADDIM = 64
STATE = 128
LANES = 128
VMEM_LIMIT = 62 << 20

norm_eps = 1e-05
highest = lax.Precision.HIGHEST
MESH = pl.DeviceIdType.MESH
f32 = jnp.float32
bf16 = jnp.bfloat16
NT = (((1,), (1,)), ((), ()))
TN = (((0,), (0,)), ((), ()))

in_vmem = pl.BlockSpec(memory_space=pltpu.VMEM)
in_smem = pl.BlockSpec(memory_space=pltpu.SMEM)


def params(cid):
    return pltpu.CompilerParams(
        collective_id=cid, has_side_effects=True, vmem_limit_bytes=VMEM_LIMIT
    )


def remote(src, dst, send, recv, target):
    return pltpu.make_async_remote_copy(
        src_ref=src,
        dst_ref=dst,
        send_sem=send,
        recv_sem=recv,
        device_id=target,
        device_id_type=MESH,
    )


def loop(count, fn):
    lax.fori_loop(0, count, lambda i, c: (fn(i), c)[1], 0)


def dot_nt(a, b, precision=None):
    return lax.dot_general(a, b, NT, precision=precision, preferred_element_type=f32)


def dot_tn(a, b, precision=None):
    return lax.dot_general(a, b, TN, precision=precision, preferred_element_type=f32)


def is_true(condition):
    return condition.astype(jnp.int32)


def ring_place(n, index):
    odd, half = lax.rem(index, 2), lax.div(index, 2)
    return half * (1 - odd) + (n - 1 - half) * odd


def ring_index(n, spot):
    late = is_true(2 * spot >= n)
    return 2 * spot + late * (2 * n - 1 - 4 * spot)


def wrapped(n, spot):
    return spot + n * is_true(spot < 0) - n * is_true(spot >= n)


class Ring:
    def __init__(self, send_sem, recv_sem):
        self.n = lax.axis_size("seq")
        self.streams, self.send_sem, self.recv_sem = [], send_sem, recv_sem
        head = lax.axis_index("head")
        self.spot = ring_place(self.n, lax.axis_index("seq"))
        self.after = (ring_index(self.n, wrapped(self.n, self.spot + 1)), head)
        self.before = (ring_index(self.n, wrapped(self.n, self.spot - 1)), head)

    def add(self, part, slots, by_rows=False, first=0):
        rows, width = part.shape[0] // self.n, part.shape[1]
        cut = slots[0].shape[1] if by_rows else slots[0].shape[2]
        if by_rows:
            halves = tuple(((first + way * cut, cut), (0, width)) for way in range(2))
        else:
            halves = (((0, rows), (0, cut)), ((0, rows), (cut, width - cut)))
        for way in range(2):
            lines, columns = halves[way]
            self.streams.append((part, slots[way], lines, pl.ds(*columns), way))

    def piece(self, i, step):
        part, _, (first, count), columns, way = self.streams[i]
        shift = -1 - step if way == 0 else 1 + step
        rows = part.shape[0] // self.n
        index = ring_index(self.n, wrapped(self.n, self.spot + shift))
        tile = 16 if part.dtype == bf16 else 8
        return part.at[pl.ds(pl.multiple_of(index * rows + first, tile), count), columns]

    def copy(self, i, step, source):
        slots, way = self.streams[i][1], self.streams[i][4]
        return remote(
            source,
            slots.at[step],
            self.send_sem.at[i],
            self.recv_sem.at[i, step],
            self.after if way == 0 else self.before,
        )

    def start(self, i):
        self.copy(i, 0, self.piece(i, 0)).start()

    def pass_on(self, i, step):
        slots = self.streams[i][1]
        self.copy(i, step, slots.at[step]).wait_recv()
        total = slots[step].astype(f32) + self.piece(i, step + 1)[...].astype(f32)
        slots[step] = total.astype(slots.dtype)
        self.copy(i, step + 1, slots.at[step]).start()

    def last(self, i):
        slots, step = self.streams[i][1], self.n - 2
        self.copy(i, step, slots.at[step]).wait_recv()
        return slots[step].astype(f32) + self.piece(i, step + 1)[...].astype(f32)

    def finish(self, i):
        slots, way = self.streams[i][1], self.streams[i][4]
        remote(
            slots,
            slots,
            self.send_sem.at[i],
            self.recv_sem.at[i, 0],
            self.after if way == 0 else self.before,
        ).wait_send()


def ring_slots(n, rows, width, kind):
    cut = width // LANES // 2 * LANES
    return [pltpu.VMEM((n - 1, rows, cut), kind), pltpu.VMEM((n - 1, rows, width - cut), kind)]


def step_at(table, here):
    found, here = jnp.int32(-1), jnp.asarray(here, jnp.int32)
    for place, step in table:
        found = found + (step + 1) * (here == place).astype(jnp.int32)
    return found


def sequence_at(table, here, pair):
    found, here = jnp.int32(-1), jnp.asarray(here, jnp.int32)
    for place, owner, b in table:
        found = found + (b + 1) * ((here == place) & (pair == owner)).astype(jnp.int32)
    return found


class PairChain:
    def __init__(self, ahead, by, local, passed, buffers, send_sem, recv_sem):
        self.n = lax.axis_size("seq")
        self.place, self.head = lax.axis_index("seq"), lax.axis_index("head")
        self.by, self.pair, self.second = by, lax.div(ahead, 2), lax.rem(ahead, 2)
        self.local, self.passed = local, passed
        self.state, self.offers, self.offered, self.hand, self.following = buffers
        self.send_sem, self.recv_sem = send_sem, recv_sem
        self.count, _, channels = self.state.shape
        cut = channels // LANES // 2 * LANES
        self.sizes = (channels - cut, cut)
        self.lanes = (pl.ds(cut, channels - cut), pl.ds(0, cut))

    def copy(self, kind, b, source, target, ahead):
        return remote(
            source,
            target,
            self.send_sem.at[kind, b],
            self.recv_sem.at[kind, b],
            (self.place + self.by * ahead, self.head),
        )

    def within(self, buffer, b, second):
        return buffer.at[b, pl.ds(0, buffer.shape[1]), pl.ds(0, self.sizes[second])]

    def offering(self, b, second):
        other = 1 - second
        return self.copy(
            0,
            b,
            self.within(self.offers, b, other),
            self.within(self.offered, b, other),
            1 - 2 * second,
        )

    def handing(self, b, second):
        target = self.state.at[b, pl.ds(0, STATE), self.lanes[second]]
        return self.copy(1, b, self.within(self.hand, b, second), target, 1 - 2 * second)

    def passing(self, b, second):
        if second:
            target = self.within(self.hand, b, second)
        else:
            target = self.state.at[b, pl.ds(0, STATE), self.lanes[second]]
        return self.copy(2, b, self.within(self.following, b, second), target, 2)

    def offer(self, b):
        for second in range(2):

            @pl.when(self.second == second)
            def _():
                other = 1 - second
                lanes, size = self.lanes[other], self.sizes[other]
                self.offers[b, :STATE, :size] = self.local[b, :, lanes].astype(bf16)
                decay = self.passed[b, 7:8, lanes]
                high = decay.astype(bf16).astype(f32)
                row = lax.broadcasted_iota(jnp.int32, (16, size), 0)
                rows = jnp.where(row == 0, high, jnp.where(row == 1, decay - high, 0.0))
                self.offers[b, STATE:, :size] = rows.astype(bf16)
                self.offering(b, second).start()

    def pass_on(self, b):
        more = self.pair < self.n // 2 - 1
        for second in range(2):

            @pl.when(self.second == second)
            def _():
                lanes, size = self.lanes[second], self.sizes[second]
                self.offering(b, 1 - second).wait_recv()

                @pl.when(self.pair > 0)
                def _():
                    self.passing(b, second).wait_recv()

                @pl.when(self.pair == 0)
                def _():
                    zeros = jnp.zeros((STATE, size), bf16)
                    if second:
                        self.hand[b, :, :size] = zeros
                    else:
                        self.state[b, :, lanes] = zeros

                own_decay, own = self.passed[b, 7:8, lanes], self.local[b, :, lanes]
                decay = self.offered[b, STATE:, :size].astype(f32)
                decay = decay[0:1] + decay[1:2]
                offered = self.offered[b, :STATE, :size].astype(f32)
                if second:
                    self.handing(b, second).start()
                    value = decay * self.hand[b, :, :size].astype(f32) + offered
                    self.state[b, :, lanes] = value.astype(bf16)
                    following = own_decay * value + own
                else:
                    value = own_decay * self.state[b, :, lanes].astype(f32) + own
                    self.hand[b, :, :size] = value.astype(bf16)
                    self.handing(b, second).start()
                    following = decay * value + offered

                @pl.when(more)
                def _():
                    self.following[b, :, :size] = following.astype(bf16)
                    self.passing(b, second).start()

    def ready(self, b):
        for second in range(2):

            @pl.when(self.second == second)
            def _():
                self.handing(b, 1 - second).wait_recv()

    def turn(self, here, table):
        b = sequence_at(table, here, self.pair)

        @pl.when(b >= 0)
        def _():
            self.pass_on(b)

    def rest(self, table):
        held = {(pair, b) for _, pair, b in table}
        for pair in range(self.n // 2):
            for b in range(self.count):
                if (pair, b) not in held:

                    @pl.when(self.pair == pair)
                    def _():
                        self.pass_on(b)

    def finish(self):
        for second in range(2):

            @pl.when(self.second == second)
            def _():
                def one(b):
                    self.offering(b, second).wait_send()
                    self.handing(b, second).wait_send()

                    @pl.when(self.pair < self.n // 2 - 1)
                    def _():
                        self.passing(b, second).wait_send()

                loop(self.count, one)


def chain_buffers(count, channels):
    wide = channels - channels // LANES // 2 * LANES
    shapes = [(STATE, channels), (STATE + 16, wide), (STATE + 16, wide), (STATE, wide), (STATE, wide)]
    return [pltpu.VMEM((count,) + s, bf16) for s in shapes]


class Group:
    def __init__(self, n):
        self.n = n
        self.chips = n // 2
        self.seq = lax.axis_index("seq")
        self.me = lax.axis_index("head")
        self.chip = lax.div(self.me, 2)
        self.core = lax.rem(self.me, 2)
        self.mate = self.me + 1 - 2 * self.core

    def at(self, head):
        return (self.seq, head)

    def chip_after(self, k):
        return lax.rem(self.chip + k, self.chips)

    def chip_before(self, k):
        return lax.rem(self.chip + self.chips - k, self.chips)

    def peer(self, k):
        return 2 * self.chip_after(k) + self.core

    def other(self, k):
        return lax.rem(self.me + k, self.n)

    def greet(self):
        barrier = pltpu.get_barrier_semaphore()
        for k in range(1, self.n):
            pl.semaphore_signal(
                barrier, inc=1, device_id=self.at(self.other(k)), device_id_type=MESH
            )
        pl.semaphore_wait(barrier, self.n - 1)


def share(group, source, table, send_sem, recv_sem):
    for k in range(1, group.n):
        remote(
            source,
            table.at[group.me],
            send_sem.at[k - 1],
            recv_sem.at[group.me],
            group.at(group.other(k)),
        ).start()


def shared(group, source, table, send_sem, recv_sem):
    for k in range(1, group.n):
        sender = group.other(k)
        copy = remote(
            source, table.at[sender], send_sem.at[k - 1], recv_sem.at[sender], group.at(sender)
        )
        copy.wait_send()
        copy.wait_recv()


def as_column(row, width):
    tile = jnp.broadcast_to(row, (LANES, row.shape[1])).T
    return jnp.concatenate([tile] * (-(-width // LANES)), axis=1)[:, :width]


def scatter_phases(group, row_block, part, mate_in, chip_out, chip_in, sems):
    mate_send, mate_recv, chip_send, chip_recv = sems

    def mate_copy(c, x):
        return remote(
            part.at[2 * x + 1 - group.core, row_block(c)],
            mate_in.at[x, row_block(c)],
            mate_send.at[x, c],
            mate_recv.at[x, c],
            group.at(group.mate),
        )

    def chip_copy(c, k):
        return remote(
            chip_out.at[k - 1, row_block(c)],
            chip_in.at[k - 1, row_block(c)],
            chip_send.at[k - 1, c],
            chip_recv.at[k - 1, c],
            group.at(group.peer(k)),
        )

    def start_mate(c):
        for x in range(group.chips):
            mate_copy(c, x).start()

    def start_chip(c):
        for x in range(group.chips):
            mate_copy(c, x).wait_recv()
        for k in range(1, group.chips):
            x = group.chip_after(k)
            both = part[2 * x + group.core, row_block(c)].astype(f32) + mate_in[
                x, row_block(c)
            ].astype(f32)
            chip_out[k - 1, row_block(c)] = both.astype(bf16)
            chip_copy(c, k).start()

    def total(c):
        value = part[group.me, row_block(c)].astype(f32) + mate_in[
            group.chip, row_block(c)
        ].astype(f32)
        for k in range(1, group.chips):
            chip_copy(c, k).wait_recv()
            value = value + chip_in[k - 1, row_block(c)].astype(f32)
        return value

    def finish(c):
        for x in range(group.chips):
            mate_copy(c, x).wait_send()
        for k in range(1, group.chips):
            chip_copy(c, k).wait_send()

    return start_mate, start_chip, total, finish


def scatter_scratch(n, rows, width, chunks):
    chips = n // 2
    dma = pltpu.SemaphoreType.DMA
    return [
        pltpu.VMEM((n, rows, width), bf16),
        pltpu.VMEM((chips, rows, width), bf16),
        pltpu.VMEM((chips - 1, rows, width), bf16),
        pltpu.VMEM((chips - 1, rows, width), bf16),
    ], [dma((chips, chunks)), dma((chips, chunks)), dma((chips - 1, chunks)), dma((chips - 1, chunks))]


def blocked(weight, n):
    width = weight.shape[1] // n
    if width % LANES == 0:
        return weight
    return jnp.moveaxis(weight.reshape(weight.shape[0], n, width), 1, 0)


def blocks(width, size=256):
    return [(at, min(size, width - at)) for at in range(0, width, size)]


def fold_lanes(values):
    rows, width = values.shape
    if width % LANES:
        fill = jnp.zeros((rows, LANES - width % LANES), values.dtype)
        values = jnp.concatenate([values, fill], axis=1)
    total = values[:, :LANES]
    for at in range(LANES, width, LANES):
        total = total + values[:, at : at + LANES]
    return total


def rows_of(values):
    return jnp.sum(fold_lanes(values).T, axis=0, keepdims=True)


def head_spread(channels):
    row = lax.broadcasted_iota(jnp.int32, (LANES, channels), 0)
    head = lax.broadcasted_iota(jnp.int32, (LANES, channels), 1) // HEADDIM
    return ((row % 16 == head) & (row < 48)).astype(f32).astype(bf16)


def head_gather(channels):
    head = lax.broadcasted_iota(jnp.int32, (channels, LANES), 0) // HEADDIM
    return (lax.broadcasted_iota(jnp.int32, (channels, LANES), 1) == head).astype(f32).astype(bf16)


def spread(values, marks):
    lane = lax.broadcasted_iota(jnp.int32, values.shape, 1)
    values = jnp.where(lane < 16, values, 0.0)
    high = values.astype(bf16).astype(f32)
    left = values - high
    middle = left.astype(bf16).astype(f32)
    low = (left - middle).astype(bf16).astype(f32)
    three = high + pltpu.roll(middle, 16, 1) + pltpu.roll(low, 32, 1)
    return jnp.dot(three.astype(bf16), marks, preferred_element_type=f32)


def gather_heads(values, marks):
    high = values.astype(bf16)
    low = (values - high.astype(f32)).astype(bf16)
    return jnp.dot(high, marks, preferred_element_type=f32) + jnp.dot(
        low, marks, preferred_element_type=f32
    )


def softplus(x):
    y = jnp.exp(-jnp.abs(x))
    small = y * (1.0 - y * (1.0 / 2 - y * (1.0 / 3 - y * (1.0 / 4 - y * (1.0 / 5)))))
    return jnp.maximum(x, 0.0) + jnp.where(y < 0.03, small, jnp.log(1.0 + y))


def lane_row(ref):
    row = ref[...][None, :]
    return jnp.concatenate([row, jnp.zeros((1, LANES - row.shape[1]), f32)], axis=1)


def long_row(ref, b, length):
    per = length // LANES
    return jnp.concatenate([ref[pl.ds(b * per + i, 1)] for i in range(per)], axis=1)


def put_row(ref, b, row):
    per = row.shape[1] // LANES
    for i in range(per):
        ref[pl.ds(b * per + i, 1)] = row[:, i * LANES : (i + 1) * LANES]


def spread_row(row, marks):
    return spread(jnp.broadcast_to(row, (8, LANES)), marks)[:1]


def position_masks(docs_row, begin):
    length = docs_row.shape[1]
    column = jnp.broadcast_to(docs_row, (LANES, length)).T
    place = begin + lax.broadcasted_iota(jnp.int32, (length, LANES), 0).astype(f32)
    return column, place


def front_kernel(
    heads,
    tokens_hbm,
    gain_ref,
    value_hbm,
    keyquery_hbm,
    step_ref,
    gate_hbm,
    docs_ref,
    step_bias_ref,
    rate_log_ref,
    skip_ref,
    value_conv_ref,
    value_offset_ref,
    keyquery_conv_ref,
    keyquery_offset_ref,
    norm_gain_ref,
    valid_ref,
    out_weight_hbm,
    teacher_hbm,
    normed_out,
    linear_out,
    conv_out,
    gate_out,
    mixed_out,
    output_out,
    pieces_out,
    halo_out,
    state_out,
    steps_out,
    cumulative_out,
    linear_steps_out,
    square_out,
    inverse_out,
    mask_out,
    rowdot_ref,
    squared_ref,
    loss_ref,
    tokens,
    last_tokens,
    value_weight,
    keyquery_weight,
    gate_weight,
    normed,
    linear,
    conv,
    gate,
    mixed,
    gained,
    tail,
    halo,
    extended,
    heads_in,
    keys,
    queries,
    scores,
    mask_bias,
    locals_,
    state,
    offers,
    offered,
    hand,
    following,
    passed,
    entering,
    load_sem,
    last_sem,
    token_sem,
    store_sem,
    halo_sem,
    chain_send,
    chain_recv,
    out_weight,
    teacher,
    output_cols,
    part,
    mate_in,
    chip_out,
    chip_in,
    gathered,
    squares,
    dots,
    dot_out,
    mate_send,
    mate_recv,
    chip_send,
    chip_recv,
    gm_send,
    gm_recv,
    gc_send,
    gc_recv,
    gf_send,
    gf_recv,
    sq_send,
    sq_recv,
    rd_send,
    rd_recv,
    output_sem,
    pieces_sem,
):
    n = lax.axis_size("seq")
    place = lax.axis_index("seq")
    heads_n = lax.axis_size("head")
    group = Group(heads_n)
    head = group.me
    width = teacher.shape[2]
    chunks = tokens.shape[0]
    count, length, _ = tokens.shape
    channels = value_weight.shape[1]
    both = channels + 2 * STATE
    lags = value_conv_ref.shape[0]
    begin = (place * length).astype(f32)

    loads = [
        pltpu.make_async_copy(value_hbm, value_weight, load_sem.at[0]),
        pltpu.make_async_copy(keyquery_hbm, keyquery_weight, load_sem.at[1]),
        pltpu.make_async_copy(gate_hbm, gate_weight, load_sem.at[2]),
        pltpu.make_async_copy(out_weight_hbm, out_weight, load_sem.at[3]),
        pltpu.make_async_copy(teacher_hbm, teacher, load_sem.at[4]),
    ]

    def token_load(b):
        return pltpu.make_async_copy(tokens_hbm.at[b], tokens.at[b], token_sem.at[b])

    def last_load(b):
        return pltpu.make_async_copy(
            tokens_hbm.at[b, length - 16 :], last_tokens.at[b], last_sem.at[b]
        )

    for b in range(count):
        last_load(b).start()
    loads[0].start()
    loads[1].start()
    for b in range(count):
        token_load(b).start()
    for copy in loads[2:]:
        copy.start()

    stores = [
        (normed, normed_out),
        (linear, linear_out),
        (conv, conv_out),
        (gate, gate_out),
        (mixed, mixed_out),
    ]

    def store(i, b):
        source, target = stores[i]
        return pltpu.make_async_copy(source.at[b], target.at[b], store_sem.at[i, b])

    barrier = pltpu.get_barrier_semaphore()

    chain = PairChain(
        place,
        1,
        locals_,
        passed,
        (state, offers, offered, hand, following),
        chain_send,
        chain_recv,
    )
    for k in range(1, heads_n):
        pl.semaphore_signal(
            barrier, inc=1, device_id=group.at(group.other(k)), device_id_type=MESH
        )
    for k in range(1, n):
        pl.semaphore_signal(
            barrier, inc=1, device_id=(lax.rem(place + k, n), head), device_id_type=MESH
        )

    def normalized(x):
        inverse = lax.rsqrt(jnp.mean(x * x, axis=-1, keepdims=True) + norm_eps)
        return inverse, (x * inverse * gain_ref[...][None, :]).astype(bf16)

    for b in range(count):
        last_load(b).wait()
    last = jnp.concatenate([normalized(last_tokens[b])[1] for b in range(count)], axis=0)
    loads[0].wait()
    loads[1].wait()
    for at, size in blocks(channels):
        tail[:, at : at + size] = jnp.dot(
            last, value_weight[:, at : at + size], preferred_element_type=f32
        ).astype(bf16)
    tail[:, channels:] = jnp.dot(last, keyquery_weight[...], preferred_element_type=f32).astype(bf16)
    pl.semaphore_wait(barrier, n + heads_n - 2)
    halo_copy = remote(tail, halo, halo_sem.at[0], halo_sem.at[1], (place + 1, head))

    @pl.when(place < n - 1)
    def _():
        halo_copy.start()

    marks = head_spread(channels)
    step_bias = lane_row(step_bias_ref)
    decay_rate = -jnp.exp(lane_row(rate_log_ref))
    skip = spread_row(lane_row(skip_ref), marks)
    triangle = (
        lax.broadcasted_iota(jnp.int32, (length, length), 0)
        >= lax.broadcasted_iota(jnp.int32, (length, length), 1)
    ).astype(f32)

    def norm(b):
        token_load(b).wait()
        inverse, rows = normalized(tokens[b])
        normed[b] = rows
        inverse_out[pl.ds(b, 1)] = jnp.broadcast_to(inverse, (length, LANES)).T[:1]
        store(0, b).start()

    def project_values(b):
        rows = normed[b]
        for at, size in blocks(channels):
            linear[b, :, at : at + size] = jnp.dot(
                rows, value_weight[:, at : at + size], preferred_element_type=f32
            ).astype(bf16)

    def project_rest(b):
        rows = normed[b]
        linear[b, :, channels:] = jnp.dot(
            rows, keyquery_weight[...], preferred_element_type=f32
        ).astype(bf16)
        narrow_steps = dot_nt(rows, step_ref[...])
        linear_steps_out[b] = jnp.concatenate(
            [narrow_steps, jnp.zeros((length, LANES - heads), f32)], axis=1
        )
        store(1, b).start()

    def states(b):
        @pl.when((b == 0) & (place > 0))
        def _():
            halo_copy.wait_recv()

        @pl.when((b == 0) & (place == 0))
        def _():
            halo[...] = jnp.zeros_like(halo)

        column, spot = position_masks(docs_ref[pl.ds(b, 1)].astype(f32), begin)
        extended[0:16] = halo[pl.ds(pl.multiple_of(b * 16, 16), 16)].astype(f32)
        extended[16:] = linear[b].astype(f32)
        usable = [None] + [(spot - lag >= column).astype(f32) for lag in range(1, lags)]
        for at in range(0, both, LANES):
            if at < channels:
                weight, offset, place_at = value_conv_ref, value_offset_ref, at
            else:
                weight, offset, place_at = keyquery_conv_ref, keyquery_offset_ref, at - channels
            lanes = slice(place_at, place_at + LANES)
            value = offset[lanes][None, :] + weight[0:1, lanes] * extended[16:, at : at + LANES]
            for lag in range(1, lags):
                value = value + weight[lag : lag + 1, lanes] * (
                    extended[16 - lag : 16 - lag + length, at : at + LANES] * usable[lag]
                )
            conv[b, :, at : at + LANES] = value
            active = value * jax.nn.sigmoid(value)
            if at < channels:
                heads_in[b, :, at : at + LANES] = active
            elif at < channels + STATE:
                keys[b] = active.astype(bf16)
            else:
                queries[b] = active.astype(bf16)
        store(2, b).start()
        steps = softplus(linear_steps_out[b] + step_bias)
        cumulative = jnp.dot(
            triangle, steps * decay_rate, precision=highest, preferred_element_type=f32
        )
        steps_out[b] = steps
        cumulative_out[b] = cumulative
        kept = (column < begin).astype(f32)
        trailing = (spot >= column[length - 1 :]).astype(f32)
        entering[b] = jnp.exp(cumulative) * kept
        end_weight = jnp.exp(cumulative[length - 1 :] - cumulative) * trailing * steps
        weighted = (heads_in[b] * spread(end_weight, marks)).astype(bf16)
        locals_[b] = dot_tn(keys[b], weighted)
        last_entering = entering[b, length - 8 :]
        passed[b] = spread(last_entering, marks)

    pairs = channels // LANES
    turns = []
    if n == 8 and count == 4:
        turns = [(1, 0, 0), (2, 0, 1), (3, 0, 2), (5, 0, 3)]
        turns += [(2, 1, 0), (3, 1, 1), (5, 1, 2), (7, 1, 3)]
        turns += [(3, 2, 0), (5, 2, 1), (7, 2, 2), (9, 2, 3)]
        turns += [(5, 3, 0), (7, 3, 1), (9, 3, 2), (10, 3, 3)]

    def begin_sequence(b):
        norm(b)
        project_values(b)
        project_rest(b)
        states(b)
        chain.offer(b)
        chain.turn(b, turns)

    loop(count, begin_sequence)
    halo_out[...] = halo[...]
    per_row = 2.0 / (D * jnp.sum(valid_ref[...].astype(f32), keepdims=True))
    here = pl.ds(pl.multiple_of(place * length, length), length)
    for b in range(count):
        row = valid_ref[b : b + 1, here].astype(f32) * per_row
        for i in range(length // LANES):
            at = b * (length // LANES) + i
            mask_out[at : at + 1] = row[:, i * LANES : (i + 1) * LANES]
    first_half = lax.broadcasted_iota(jnp.int32, (length, LANES), 1) < HEADDIM
    loads[2].wait()

    def inside(b):
        column, spot = position_masks(docs_ref[pl.ds(b, 1)].astype(f32), begin)
        wide = jnp.concatenate([column] * (length // LANES), axis=1)
        t = begin + lax.broadcasted_iota(jnp.int32, (length, length), 0).astype(f32)
        u = begin + lax.broadcasted_iota(jnp.int32, (length, length), 1).astype(f32)
        mask_bias[...] = jnp.where((u >= wide) & (u <= t), 0.0, -1e30)
        scores[...] = dot_nt(queries[b], keys[b])
        cumulative = cumulative_out[b]
        across = cumulative.T
        spread_steps = spread(steps_out[b], marks)
        for pair in range(pairs):
            lanes = slice(pair * LANES, (pair + 1) * LANES)
            scaled = heads_in[b, :, lanes] * spread_steps[:, lanes]
            value = jnp.zeros((length, LANES), f32)
            for half in range(2):
                h = 2 * pair + half
                decay = jnp.exp(cumulative[:, h : h + 1] - across[h : h + 1] + mask_bias[...])
                mixing = (decay * scores[...]).astype(bf16)
                mine = jnp.where(first_half if half == 0 else ~first_half, scaled, 0.0).astype(bf16)
                value = value + jnp.dot(mixing, mine, preferred_element_type=f32)
            mixed[b, :, lanes] = value
        rows = normed[b]
        for at, size in blocks(channels):
            gate[b, :, at : at + size] = jnp.dot(
                rows, gate_weight[:, at : at + size], preferred_element_type=f32
            )
        store(3, b).start()
        chain.turn(count + b, turns)

    loop(count, inside)
    chain.rest(turns)

    def close(b):
        chain.ready(b)
        state_out[b] = state[b]
        projected = jnp.dot(queries[b], state[b], preferred_element_type=f32)
        value = mixed[b] + spread(entering[b], marks) * projected + skip * heads_in[b]
        mixed[b] = value
        store(4, b).start()
        linear_gate = gate[b]
        gated = value * (linear_gate * jax.nn.sigmoid(linear_gate))
        gained[b] = (gated * norm_gain_ref[...][None, :]).astype(bf16)
        put_row(square_out, b, rows_of(gated * gated))

    def row_block(c):
        return pl.ds(pl.multiple_of(c * length, length), length)

    start_mate, start_chip, total, finish = scatter_phases(
        group, row_block, part, mate_in, chip_out, chip_in, (mate_send, mate_recv, chip_send, chip_recv)
    )

    def product(c):
        rows = gained[c]
        for j in range(heads_n):
            block = (
                out_weight[:, j * width : (j + 1) * width] if len(out_weight.shape) == 2 else out_weight[j]
            )
            part[j, row_block(c)] = jnp.dot(rows, block, preferred_element_type=f32).astype(bf16)
        start_mate(c)

    loads[3].wait()

    def close_and_send(b):
        close(b)
        product(b)

        @pl.when(b > 0)
        def _():
            start_chip(b - 1)

        chain.turn(9 + b, turns)

    loop(count, close_and_send)
    start_chip(count - 1)
    share(group, square_out, squares, sq_send, sq_recv)
    shared(group, square_out, squares, sq_send, sq_recv)
    squares[group.me] = square_out[...]
    loss_ref[...] = jnp.zeros_like(loss_ref)

    def to_mate(c):
        block = gathered.at[group.me, row_block(c)]
        return remote(block, block, gm_send.at[c], gm_recv.at[c], group.at(group.mate))

    def to_chip(c, k):
        block = gathered.at[group.me, row_block(c)]
        return remote(
            block, block, gc_send.at[k - 1, c], gc_recv.at[k - 1, c], group.at(group.peer(k))
        )

    def forward(c, k):
        block = gathered.at[2 * group.chip_before(k) + group.core, row_block(c)]
        return remote(
            block, block, gf_send.at[k - 1, c], gf_recv.at[k - 1, c], group.at(group.mate)
        )

    loads[4].wait()

    def own_tokens(c):
        if width % LANES == 0:
            return tokens[c, :, pl.ds(pl.multiple_of(head * width, LANES), width)]
        found = jnp.zeros((length, width), f32)
        for j in range(heads_n):
            mine = tokens[c, :, j * width : (j + 1) * width]
            found = found + jnp.where(head == j, mine, 0.0)
        return found

    def rest(c):
        squared = long_row(squares.at[0], c, length)
        for j in range(1, heads_n):
            squared = squared + long_row(squares.at[j], c, length)
        put_row(squared_ref, c, squared)
        scale = lax.rsqrt(squared * (1.0 / (NHEADS * HEADDIM)) + norm_eps)
        branch = total(c) * as_column(scale, width)
        output = own_tokens(c) + branch
        output_cols[row_block(c)] = output
        difference = output - teacher[c]
        weighted = difference * as_column(long_row(mask_out, c, length), width)
        low = weighted.astype(bf16)
        gathered[group.me, row_block(c)] = low
        to_mate(c).start()
        for k in range(1, group.chips):
            to_chip(c, k).start()
        loss_ref[...] += jnp.sum(weighted * difference, axis=0, keepdims=True)
        put_row(dot_out, c, rows_of(low.astype(f32) * branch))

    loop(chunks, rest)
    output_store = pltpu.make_async_copy(output_cols, output_out, output_sem.at[0])
    output_store.start()
    share(group, dot_out, dots, rd_send, rd_recv)

    def pass_on(c):
        for k in range(1, group.chips):
            to_chip(c, k).wait_recv()
            forward(c, k).start()

    loop(chunks, pass_on)

    def pieces_store(c):
        return pltpu.make_async_copy(
            gathered.at[pl.ds(0, heads_n), row_block(c)],
            pieces_out.at[pl.ds(0, heads_n), row_block(c)],
            pieces_sem.at[c],
        )

    def end(c):
        to_mate(c).wait()
        for k in range(1, group.chips):
            to_chip(c, k).wait_send()
            forward(c, k).wait()
        finish(c)
        pieces_store(c).start()

    loop(chunks, end)
    shared(group, dot_out, dots, rd_send, rd_recv)
    row_sum = dot_out[...]
    for k in range(1, heads_n):
        row_sum = row_sum + dots[group.other(k)]
    rowdot_ref[...] = row_sum
    output_store.wait()
    loop(chunks, lambda c: pieces_store(c).wait())

    @pl.when(place < n - 1)
    def _():
        halo_copy.wait_send()

    chain.finish()

    for i in range(len(stores)):
        loop(count, lambda b, i=i: store(i, b).wait())


def front(tokens, gain, value_weight, keyquery_weight, step_weight, gate_weight, docs, vectors, conv, norm_gain, valid, out_weight, teacher, cid):
    count, length, _ = tokens.shape
    channels = value_weight.shape[1]
    heads = channels // HEADDIM
    both = channels + 2 * STATE
    dma = pltpu.SemaphoreType.DMA
    hbm = pl.BlockSpec(memory_space=pl.ANY)
    shape = jax.ShapeDtypeStruct
    heads_n, width = lax.axis_size("head"), teacher.shape[2]
    rows, chips = count * length, heads_n // 2
    chunks, lines = count, rows // LANES
    out_weight = blocked(out_weight, heads_n)
    buffers, sems = scatter_scratch(heads_n, rows, width, chunks)
    big = [
        ((count, length, D), bf16),
        ((count, length, both), bf16),
        ((count, length, both), f32),
        ((count, length, channels), f32),
        ((count, length, channels), f32),
    ]
    results = [((rows, width), f32), ((heads_n, rows, width), bf16)]
    small = [
        ((count * 16, both), bf16),
        ((count, STATE, channels), bf16),
        ((count, length, LANES), f32),
        ((count, length, LANES), f32),
        ((count, length, LANES), f32),
        ((count * length // LANES, LANES), f32),
        ((count, length), f32),
        ((count * length // LANES, LANES), f32),
        ((lines, LANES), f32),
        ((lines, LANES), f32),
        ((1, width), f32),
    ]
    return pl.pallas_call(
        functools.partial(front_kernel, heads),
        out_shape=[shape(*s) for s in big + results + small],
        in_specs=[hbm, in_vmem, hbm, hbm, in_vmem, hbm] + [in_vmem] * 10 + [hbm] * 2,
        out_specs=[hbm] * (len(big) + 2) + [in_vmem] * len(small),
        scratch_shapes=[
            pltpu.VMEM((count, length, D), f32),
            pltpu.VMEM((count, 16, D), f32),
            pltpu.VMEM((D, channels), bf16),
            pltpu.VMEM((D, 2 * STATE), bf16),
            pltpu.VMEM((D, channels), bf16),
        ]
        + [pltpu.VMEM(*s) for s in big]
        + [
            pltpu.VMEM((count, length, channels), bf16),
            pltpu.VMEM((count * 16, both), bf16),
            pltpu.VMEM((count * 16, both), bf16),
            pltpu.VMEM((length + 16, both), f32),
            pltpu.VMEM((count, length, channels), f32),
            pltpu.VMEM((count, length, STATE), bf16),
            pltpu.VMEM((count, length, STATE), bf16),
            pltpu.VMEM((length, length), f32),
            pltpu.VMEM((length, length), f32),
            pltpu.VMEM((count, STATE, channels), f32),
        ]
        + chain_buffers(count, channels)
        + [
            pltpu.VMEM((count, 8, channels), f32),
            pltpu.VMEM((count, length, LANES), f32),
            dma((5,)),
            dma((count,)),
            dma((count,)),
            dma((len(big), count)),
            dma((2,)),
            dma((3, count)),
            dma((3, count)),
            pltpu.VMEM(out_weight.shape, bf16),
            pltpu.VMEM((count, length, width), f32),
            pltpu.VMEM((rows, width), f32),
        ]
        + buffers
        + [
            pltpu.VMEM((heads_n, rows, width), bf16),
            pltpu.VMEM((heads_n, lines, LANES), f32),
            pltpu.VMEM((heads_n, lines, LANES), f32),
            pltpu.VMEM((lines, LANES), f32),
        ]
        + sems
        + [
            dma((chunks,)),
            dma((chunks,)),
            dma((chips - 1, chunks)),
            dma((chips - 1, chunks)),
            dma((chips - 1, chunks)),
            dma((chips - 1, chunks)),
            dma((heads_n - 1,)),
            dma((heads_n,)),
            dma((heads_n - 1,)),
            dma((heads_n,)),
            dma((1,)),
            dma((chunks,)),
        ],
        compiler_params=params(cid),
        name="front",
    )(tokens, gain, value_weight, keyquery_weight, step_weight, gate_weight, docs, *vectors, *conv, norm_gain, valid, out_weight, teacher)


class Doubling:
    def __init__(self, axis, bits, current, table, send_sem, recv_sem):
        self.axis, self.bits, self.current, self.table = axis, list(bits), current, table
        self.send_sem, self.recv_sem = send_sem, recv_sem

    def copy(self, stage):
        bit = 1 << self.bits[stage]
        mine = lax.axis_index(self.axis)
        other = mine + bit - 2 * bit * lax.rem(lax.div(mine, bit), 2)
        if self.axis == "head":
            target = (lax.axis_index("seq"), other)
        else:
            target = (other, lax.axis_index("head"))
        return remote(
            self.current,
            self.table.at[stage],
            self.send_sem.at[stage],
            self.recv_sem.at[stage],
            target,
        )

    def start(self, stage):
        self.copy(stage).start()

    def run(self, first, last=None):
        for stage in range(first, len(self.bits) if last is None else min(last, len(self.bits))):
            self.copy(stage).wait()
            self.current[...] = self.current[...] + self.table[stage]
            if stage + 1 < len(self.bits):
                self.start(stage + 1)


def stages_of(n):
    return n.bit_length() - 1


def tile_place(index, width):
    per = width // LANES
    return index // per, slice(index % per * LANES, index % per * LANES + LANES)


class Tiles:
    def __init__(self, ref):
        self.ref, self.index = ref, 0

    def put(self, row):
        for at in range(0, row.shape[1], LANES):
            r, lanes = tile_place(self.index, self.ref.shape[1])
            self.ref[r : r + 1, lanes] = row[:, at : at + LANES]
            self.index += 1

    def take(self, width):
        found = []
        for _ in range(width // LANES):
            r, lanes = tile_place(self.index, self.ref.shape[1])
            found.append(self.ref[r : r + 1, lanes])
            self.index += 1
        return jnp.concatenate(found, axis=1)


def rear_kernel(names, scoped, heads, *refs):
    r = types.SimpleNamespace(**dict(zip(names, refs)))
    n, heads_n = lax.axis_size("seq"), lax.axis_size("head")
    place = lax.axis_index("seq")
    group = Group(heads_n)
    head = group.me
    ahead = n - 1 - place
    count, length, channels = r.gate_grad.shape
    rows = count * length
    both = channels + 2 * STATE
    lags = r.value_conv.shape[0]
    width = r.mate_in.shape[2]
    begin = (place * length).astype(f32)
    inner_total = NHEADS * HEADDIM
    ring_steps = n - 2
    own = D // n
    quarters = own % 64 == 0
    turns, out_steps, gate_steps = [], [], []
    if n == 8 and count == 4:
        turns = [(3, 0, 0), (4, 0, 1), (5, 0, 2), (7, 0, 3)]
        turns += [(6, 1, 0), (8, 1, 1), (9, 1, 2), (11, 1, 3)]
        turns += [(10, 2, 0), (12, 2, 1), (13, 2, 2), (14, 2, 3)]
        turns += [(13, 3, 0), (15, 3, 1), (16, 3, 2), (17, 3, 3)]
        out_steps = [(8, 0), (11, 1), (14, 2), (17, 3), (19, 4), (22, 5)]
        gate_steps = [(18, 0), (21, 1), (23, 2), (25, 3), (28, 4), (30, 5)]

    barrier = pltpu.get_barrier_semaphore()
    for k in range(1, heads_n):
        pl.semaphore_signal(
            barrier, inc=1, device_id=group.at(group.other(k)), device_id_type=MESH
        )
    for k in range(1, n):
        pl.semaphore_signal(
            barrier, inc=1, device_id=(lax.rem(place + k, n), head), device_id_type=MESH
        )

    normed_load = pltpu.make_async_copy(r.normed_hbm, r.normed, r.load_sem.at[0])
    marks = head_spread(channels)
    collect = head_gather(channels)
    step_bias = lane_row(r.step_bias)
    decay_rate = -jnp.exp(lane_row(r.rate_log))
    skip = spread_row(lane_row(r.skip), marks)
    r.gain_grad[...] = jnp.zeros_like(r.gain_grad)
    r.vector_grad[...] = jnp.zeros_like(r.vector_grad)
    r.conv_grad[...] = jnp.zeros_like(r.conv_grad)
    ring = Ring(r.ring_send, r.ring_recv)
    def matrix(part, slots, cut):
        first = len(ring.streams)
        if not quarters:
            ring.add(part, slots[:2])
            return (first,)
        ring.add(part, slots[:2], by_rows=True)
        if not cut:
            return (first,)
        ring.add(part, slots[2:], by_rows=True, first=own // 2)
        return first, first + 2

    out_halves = matrix(r.out_part, (r.os0, r.os1), False)
    gate_halves = matrix(r.gate_part, (r.gs0, r.gs1), False)

    def pass_on(first, step):
        @pl.when((step >= 0) & (step < ring_steps))
        def _():
            ring.pass_on(first, step)
            ring.pass_on(first + 1, step)

    def weights_turn(here, rounds=1):
        known = range(here, here + 2 * rounds, 2) if isinstance(here, int) else None
        for halves, table in ((out_halves, out_steps), (gate_halves, gate_steps)):
            if known is None or any(place in known for place, _ in table):
                step = step_at(table, here)
                for first in halves:
                    pass_on(first, step)

    def start(first):
        ring.start(first)
        ring.start(first + 1)

    def rest_of_ring(halves, done):
        if ring_steps > done:

            def further(s):
                for first in halves:
                    pass_on(first, done + s)

            loop(ring_steps - done, further)

    def total_of(i, halves, sums, targets):
        for k in [first + way for first in halves for way in range(2)]:
            _, _, (first, lines), columns, _ = ring.streams[k]
            sums[i, first : first + lines, columns] = ring.last(k)
        copy = pltpu.make_async_copy(sums.at[i], targets[i], r.total_sem.at[i])
        copy.start()
        return copy

    def as_wide(ref, b):
        return jnp.broadcast_to(long_row(ref, b, length), (LANES, length)).T

    def widened(column, size):
        return jnp.concatenate([column] * (size // LANES), axis=1)

    def weight_block(target, grads, block):
        sides = jnp.concatenate([r.normed[b, :, block] for b in range(count)], axis=0)
        whole = jnp.concatenate([grads(b) for b in range(count)], axis=0)
        target[block] = dot_tn(sides, whole).astype(target.dtype)

    def phase_one(*locals_one):
        q = types.SimpleNamespace(**dict(zip(scoped[0], locals_one)))
        loads = [
            pltpu.make_async_copy(r.out_weight_hbm, q.weight, r.load_sem.at[1]),
            pltpu.make_async_copy(r.pieces_hbm, q.pieces, r.load_sem.at[2]),
        ]
        for copy in loads:
            copy.start()
        row_arrays = [(r.gate_hbm, q.gate), (r.mixed_hbm, q.mixed), (r.conv_hbm, q.conv)]

        def row_load(i, b):
            source, target = row_arrays[i]
            return pltpu.make_async_copy(source.at[b], target.at[b], r.row_sem.at[i, b])

        def linear_load(b):
            slot = lax.rem(b, 2)
            return pltpu.make_async_copy(r.linear_hbm.at[b], q.linear.at[slot], r.line_load.at[slot])

        for b in range(count):
            for i in range(3):
                row_load(i, b).start()
        normed_load.start()
        linear_load(0).start()
        inner = q.gate
        normed_out = r.values_grad
        chain = PairChain(
            ahead,
            -1,
            q.local,
            q.passed,
            (r.state, q.offer, r.offered, r.hand, q.following),
            r.chain_send,
            r.chain_recv,
        )
        pairs = channels // LANES
        for copy in loads:
            copy.wait()
        pl.semaphore_wait(barrier, heads_n + n - 2)
        groups = q.pieces.shape[0]

        def gated_norm(b):
            for i in range(3):
                row_load(i, b).wait()
            scale = lax.rsqrt(as_wide(r.square, b) * (1.0 / inner_total) + norm_eps)
            pull = scale * scale * as_wide(r.rowdot, b) * (1.0 / inner_total)
            column, _ = position_masks(r.docs[pl.ds(b, 1)].astype(f32), begin)
            entering = spread(jnp.exp(r.cumulative[b]) * (column < begin).astype(f32), marks)
            q.passed[b] = entering[length - 8 :]
            here = pl.ds(pl.multiple_of(b * length, length), length)
            for at, size in blocks(channels):
                lanes = slice(at, at + size)
                grad_rows = jnp.zeros((length, size), f32)
                for j in range(groups):
                    block = (
                        q.weight[lanes, j * width : (j + 1) * width]
                        if len(q.weight.shape) == 2
                        else q.weight[j, lanes]
                    )
                    grad_rows = grad_rows + dot_nt(q.pieces[j, here], block)
                linear_gate = q.gate[b, :, lanes]
                sigmoid_value = jax.nn.sigmoid(linear_gate)
                active = linear_gate * sigmoid_value
                value = q.mixed[b, :, lanes]
                gated = value * active
                norm_gain = r.norm_gain[lanes][None, :]
                scaled = gated * widened(scale, size)
                normed_out[b, :, lanes] = (scaled * norm_gain).astype(bf16)
                r.gain_grad[:, lanes] += jnp.sum(grad_rows * scaled, axis=0, keepdims=True)
                gated_grad = widened(scale, size) * norm_gain * grad_rows - gated * widened(
                    pull, size
                )
                q.heads_grad[b, :, lanes] = gated_grad * active
                slope = sigmoid_value * (1.0 + linear_gate * (1.0 - sigmoid_value))
                r.gate_grad[b, :, lanes] = (gated_grad * value * slope).astype(bf16)
                values = q.conv[b, :, lanes]
                q.heads_in[b, :, lanes] = values * jax.nn.sigmoid(values)
            values = q.conv[b, :, channels : channels + STATE]
            q.keys[b] = (values * jax.nn.sigmoid(values)).astype(bf16)
            values = q.conv[b, :, channels + STATE :]
            q.queries[b] = (values * jax.nn.sigmoid(values)).astype(bf16)
            q.local[b] = dot_tn(q.queries[b], (q.heads_grad[b] * entering).astype(bf16))
            chain.offer(b)

        loop(count, gated_norm)
        chain.turn(3, turns)

        for j in range(groups):
            grads = jnp.concatenate([normed_out[b] for b in range(count)], axis=0)
            r.out_part[j * width : (j + 1) * width] = dot_tn(q.pieces[j], grads).astype(bf16)
            if j == groups // 2 - 1:
                chain.turn(4, turns)
        for first in out_halves:
            start(first)
        chain.turn(5, turns)
        normed_load.wait()

        first_half = lax.broadcasted_iota(jnp.int32, (length, LANES), 1) < HEADDIM

        def inside(b):
            docs_row = r.docs[pl.ds(b, 1)].astype(f32)
            u = begin + lax.broadcasted_iota(jnp.int32, (length, length), 0).astype(f32)
            t = begin + lax.broadcasted_iota(jnp.int32, (length, length), 1).astype(f32)
            q.mask_bias[...] = jnp.where((u >= docs_row) & (u <= t), 0.0, -1e30)
            q.scores[...] = dot_nt(q.keys[b], q.queries[b])
            q.scores_grad[...] = jnp.zeros_like(q.scores_grad)
            cumulative = r.cumulative[b]
            across = cumulative.T
            spread_steps = spread(r.steps[b], marks)
            for pair in range(pairs):
                lanes = slice(pair * LANES, (pair + 1) * LANES)
                scaled = q.heads_in[b, :, lanes] * spread_steps[:, lanes]
                grads = q.heads_grad[b, :, lanes]
                low_grads = grads.astype(bf16)
                value = jnp.zeros((length, LANES), f32)
                for half in range(2):
                    h = 2 * pair + half
                    mine = first_half if half == 0 else ~first_half
                    decay = jnp.exp(
                        across[h : h + 1] - cumulative[:, h : h + 1] + q.mask_bias[...]
                    )
                    mixing = (decay * q.scores[...]).astype(bf16)
                    value = value + jnp.dot(
                        mixing, jnp.where(mine, grads, 0.0).astype(bf16), preferred_element_type=f32
                    )
                    pairwise = dot_nt(jnp.where(mine, scaled, 0.0).astype(bf16), low_grads)
                    q.scores_grad[...] += decay * pairwise
                inner[b, :, lanes] = value
                if pair == (pairs - 1) // 2:
                    weights_turn(6 + 2 * b)
                    chain.turn(6 + 2 * b, turns)
            low = q.scores_grad[...].astype(bf16)
            q.narrow_grad[b, :, :STATE] = jnp.dot(low, q.queries[b], preferred_element_type=f32)
            column, _ = position_masks(docs_row, begin)
            entering = jnp.exp(cumulative) * (column < begin).astype(f32)
            x = q.heads_in[b]
            dy = q.heads_grad[b]
            q.narrow_grad[b, :, STATE:] = dot_tn(low, q.keys[b]) + dot_nt(
                (dy * spread(entering, marks)).astype(bf16), r.state_in[b]
            )
            dot_inner = gather_heads(x * inner[b], collect)
            dot_skip = gather_heads(dy * x, collect)
            q.dot_inner[b] = dot_inner
            q.cum_part[b] = (
                gather_heads(dy * (q.mixed[b] - skip * x), collect) - r.steps[b] * dot_inner
            )
            r.vector_grad[2:3] += jnp.sum(dot_skip, axis=0, keepdims=True)
            inner[b] = skip * dy + spread_steps * inner[b]
            weights_turn(7 + 2 * b)
            chain.turn(7 + 2 * b, turns)

        loop(count, inside)
        chain.rest(turns)

        def gate_block(i):
            block = pl.ds(pl.multiple_of(i * 256, 256), 256)
            weight_block(r.gate_part, lambda b: r.gate_grad[b], block)

        loop(D // 512, gate_block)
        weights_turn(14)
        chain.turn(14, turns)
        loop(D // 512, lambda i: gate_block(i + D // 512))
        for first in gate_halves:
            start(first)
        weights_turn(15)
        chain.turn(15, turns)
        q.around[...] = jnp.zeros_like(q.around)
        q.usable[...] = jnp.zeros_like(q.usable)
        upper = (
            lax.broadcasted_iota(jnp.int32, (length, length), 0)
            <= lax.broadcasted_iota(jnp.int32, (length, length), 1)
        ).astype(f32)
        last_row = lax.broadcasted_iota(jnp.int32, (length, LANES), 0) == length - 1

        def edge_copy(b):
            return remote(
                r.edge.at[b], r.edge_in.at[b], r.edge_send.at[b], r.edge_recv.at[b], (place - 1, head)
            )

        def close(b):
            @pl.when(b + 1 < count)
            def _():
                linear_load(b + 1).start()

            column, spot = position_masks(r.docs[pl.ds(b, 1)].astype(f32), begin)
            cumulative = r.cumulative[b]
            steps = r.steps[b]
            kept = (column < begin).astype(f32)
            trailing = (spot >= column[length - 1 :]).astype(f32)
            entering = jnp.exp(cumulative) * kept
            end_decay = jnp.exp(cumulative[length - 1 :] - cumulative) * trailing
            end_weight = end_decay * steps
            chain.ready(b)
            end_grad = r.state[b]
            x = q.heads_in[b]
            grown = jnp.dot(q.keys[b], end_grad, preferred_element_type=f32)
            spread_end = spread(end_weight, marks)
            q.narrow_grad[b, :, :STATE] += dot_nt((x * spread_end).astype(bf16), end_grad)
            grad = inner[b] + spread_end * grown
            dot_end = gather_heads(x * grown, collect)
            through = jnp.sum(
                end_grad.astype(f32) * r.state_in[b].astype(f32), axis=0, keepdims=True
            )
            passed_grad = gather_heads(jnp.broadcast_to(through, (8, channels)), collect)[:1]
            end_mix = dot_end * end_weight
            last_term = passed_grad * entering[length - 1 :] + jnp.sum(
                end_mix, axis=0, keepdims=True
            )
            cum_grad = q.cum_part[b] - end_mix + jnp.where(last_row, last_term, 0.0)
            rates_grad = jnp.dot(upper, cum_grad, precision=highest, preferred_element_type=f32)
            steps_grad = q.dot_inner[b] + end_decay * dot_end + rates_grad * decay_rate
            linear_grad = steps_grad * jax.nn.sigmoid(r.linear_steps[b] + step_bias)
            r.narrow[b, :, 2 * STATE :] = linear_grad.astype(bf16)
            r.vector_grad[0:1] += jnp.sum(linear_grad, axis=0, keepdims=True)
            r.vector_grad[1:2] += jnp.sum(rates_grad * steps, axis=0, keepdims=True) * decay_rate

            weights_turn(16 + 2 * b)
            chain.turn(16 + 2 * b, turns)
            linear_load(b).wait()
            halo_rows = pl.ds(pl.multiple_of(b * 16, 16), 16)
            line = lax.rem(b, 2)
            middle = slice(16, 16 + length)
            for lag in range(1, lags):
                q.usable[lag - 1, middle] = (spot - lag >= column).astype(f32)
            for at in range(0, both, LANES):
                lanes = slice(at, at + LANES)
                slot = at // LANES % 2
                q.extended[slot, 0:16] = r.halo[halo_rows, lanes].astype(f32)
                q.extended[slot, 16:] = q.linear[line, :, lanes].astype(f32)
                values = q.conv[b, :, lanes]
                sigmoid_value = jax.nn.sigmoid(values)
                slope = sigmoid_value * (1.0 + values * (1.0 - sigmoid_value))
                if at < channels:
                    out_grad = grad[:, lanes]
                    taps, tap = r.value_conv, lanes
                else:
                    place_at = at - channels
                    out_grad = q.narrow_grad[b, :, place_at : place_at + LANES]
                    taps, tap = r.keyquery_conv, slice(place_at, place_at + LANES)
                local = out_grad * slope
                q.around[slot, middle] = local
                input_grad = taps[0:1, tap] * local
                edges = jnp.zeros((8, LANES), f32)
                r.conv_grad[0:1, lanes] += jnp.sum(
                    local * q.extended[slot, middle], axis=0, keepdims=True
                )
                r.conv_grad[lags : lags + 1, lanes] += jnp.sum(local, axis=0, keepdims=True)
                for lag in range(1, lags):
                    mask = q.usable[lag - 1, middle]
                    r.conv_grad[lag : lag + 1, lanes] += jnp.sum(
                        local * mask * q.extended[slot, 16 - lag : 16 - lag + length],
                        axis=0,
                        keepdims=True,
                    )
                    later = slice(16 + lag, 16 + lag + length)
                    input_grad = input_grad + taps[lag : lag + 1, tap] * (
                        q.around[slot, later] * q.usable[lag - 1, later]
                    )
                    first = slice(8 + lag, 16 + lag)
                    edges = edges + taps[lag : lag + 1, tap] * (
                        q.around[slot, first] * q.usable[lag - 1, first]
                    )
                r.edge[b, :, lanes] = edges
                q.tails[b, :, lanes] = input_grad[length - 16 :]
                if at < channels:
                    r.values_grad[b, :, lanes] = input_grad.astype(bf16)
                else:
                    r.narrow[b, :, tap] = input_grad.astype(bf16)

            @pl.when(place > 0)
            def _():
                edge_copy(b).start()

            weights_turn(17 + 2 * b)
            chain.turn(17 + 2 * b, turns)

        loop(count, close)

        @pl.when(place < n - 1)
        def _():
            def join(b):
                edge_copy(b).wait_recv()
                last = slice(length - 16, length)
                q.tails[b, 8:] = q.tails[b, 8:] + r.edge_in[b]
                r.values_grad[b, last] = q.tails[b, :, :channels].astype(bf16)
                r.narrow[b, last, : 2 * STATE] = q.tails[b, :, channels:].astype(bf16)

            loop(count, join)

        @pl.when(place > 0)
        def _():
            loop(count, lambda b: edge_copy(b).wait_send())

        chain.finish()

    pl.run_scoped(phase_one, *scoped[1])

    def phase_two(*locals_two):
        q = types.SimpleNamespace(**dict(zip(scoped[2], locals_two)))
        token_columns = r.tokens_hbm
        if token_columns.shape[2] != width:
            first_column = pl.multiple_of(head * width, LANES)
            token_columns = token_columns.at[:, :, pl.ds(first_column, width)]
        loads = [
            pltpu.make_async_copy(source, target, r.load_two.at[i])
            for i, (source, target) in enumerate(
                [
                    (r.gate_weight_hbm, q.gate_weight),
                    (r.value_weight_hbm, q.value_weight),
                    (r.keyquery_weight_hbm, q.keyquery_weight),
                    (token_columns, q.tokens),
                    (r.output_hbm, q.output),
                    (r.teacher_hbm, q.teacher),
                ]
            )
        ]
        for copy in loads:
            copy.start()
        value_halves = matrix(q.value_part, (r.vs0, r.vs1, r.vs2, r.vs3), True)
        keyquery_first = len(ring.streams)
        ring.add(q.keyquery_half, (r.ks0, r.ks1), by_rows=True)

        def value_block(i):
            block = pl.ds(pl.multiple_of(i * 256, 256), 256)
            weight_block(q.value_part, lambda b: r.values_grad[b], block)

        loop(D // 512, value_block)
        weights_turn(24)
        loop(D // 512, lambda i: value_block(i + D // 512))
        for first in value_halves:
            start(first)
        weights_turn(25)

        def narrow_block(i):
            block = pl.ds(pl.multiple_of(i * 256, 256), 256)
            for half in range(2):
                lanes = slice(half * STATE, (half + 1) * STATE)
                weight_block(q.keyquery_part.at[half], lambda b: r.narrow[b, :, lanes], block)

        loop(D // 256, narrow_block)
        keyquery_mate = remote(
            q.keyquery_part.at[1 - group.core],
            r.keyquery_in,
            r.small_send.at[0],
            r.small_recv.at[0],
            group.at(group.mate),
        )
        keyquery_mate.start()
        weights_turn(26)
        targets = (r.out_total, r.gate_total, r.value_total)

        def end_ring(i, halves, done):
            rest_of_ring(halves, done)
            return total_of(i, halves, q.sums, targets)

        for copy in loads[:3]:
            copy.wait()
        q.columns[...] = jnp.zeros_like(q.columns)

        def own_columns(row):
            mine = jnp.zeros((1, width), f32)
            for j in range(heads_n):
                mine = mine + jnp.where(head == j, row[:, j * width : (j + 1) * width], 0.0)
            return mine

        gain = own_columns(r.gain[...][None, :])

        def row_block(c):
            return pl.ds(pl.multiple_of(c * length, length), length)

        start_mate, start_chip, total, finish = scatter_phases(
            group,
            row_block,
            q.part,
            r.mate_in,
            q.chip_out,
            r.chip_in,
            (r.mate_send, r.mate_recv, r.chip_send, r.chip_recv),
        )

        def value_turn(s):
            if s < ring_steps:
                for first in value_halves:
                    pass_on(first, s)

        def keyquery_turn(s):
            if s < ring_steps:
                pass_on(keyquery_first, s)

        def product(c):
            row_sum = jnp.zeros((length, LANES), f32)
            for j in range(heads_n):
                lanes = slice(j * width, (j + 1) * width)
                value = dot_nt(r.gate_grad[c], q.gate_weight[lanes])
                value = value + dot_nt(r.values_grad[c], q.value_weight[lanes])
                value = value + dot_nt(r.narrow[c, :, : 2 * STATE], q.keyquery_weight[lanes])
                value = value + jnp.dot(
                    r.narrow[c, :, 2 * STATE : 2 * STATE + heads],
                    r.step_weight[:, lanes],
                    preferred_element_type=f32,
                )
                q.part[j, row_block(c)] = value.astype(bf16)
                scaled = value * r.normed[c, :, lanes].astype(f32)
                q.columns[:, lanes] += jnp.sum(scaled, axis=0, keepdims=True)
                row_sum = row_sum + fold_lanes(scaled)
            r.dot_out[pl.ds(c, 1)] = jnp.sum(row_sum.T, axis=0, keepdims=True)
            start_mate(c)

            @pl.when(c > 0)
            def _():
                start_chip(c - 1)

        product(0)
        keyquery_mate.wait_recv()
        q.keyquery_half[...] = q.keyquery_part[group.core] + r.keyquery_in[...]
        start(keyquery_first)
        total_copies = [end_ring(0, out_halves, len(out_steps))]
        product(1)
        weights_turn(28)
        product(2)
        value_turn(0)
        keyquery_turn(0)
        product(3)
        start_chip(count - 1)
        weights_turn(30)
        share(group, r.dot_out, r.dots, r.rd_send, r.rd_recv)

        group_total = Doubling(
            "head", range(stages_of(heads_n)), r.group_sum, r.group_table, r.group_send, r.group_recv
        )
        line_total = Doubling(
            "seq", range(stages_of(n)), r.line_sum, r.line_table, r.line_send, r.line_recv
        )
        chip_total = Doubling(
            "head",
            range(1, stages_of(heads_n)),
            r.keyquery_sum,
            r.keyquery_table,
            r.kq_send,
            r.kq_recv,
        )
        tiles = Tiles(r.group_sum)
        r.group_sum[...] = jnp.zeros_like(r.group_sum)
        for lag in range(lags + 1):
            tiles.put(r.conv_grad[lag : lag + 1, channels:])
        tiles.put(q.columns[...])
        tiles.put(fold_lanes(r.loss_cols[...]))
        group_total.start(0)
        value_turn(1)
        keyquery_turn(1)

        for at, size in blocks(D):
            whole = jnp.concatenate([r.normed[b, :, at : at + size] for b in range(count)], axis=0)
            grads = jnp.concatenate([r.narrow[b, :, 2 * STATE :] for b in range(count)], axis=0)
            q.step_whole[:, at : at + size] = dot_tn(grads, whole)
        q.step_part[...] = jnp.zeros_like(q.step_part)
        for s in range(n):
            q.step_part[s, :, :own] = q.step_whole[:16, s * own : (s + 1) * own]

        def step_copy(k, index, sender):
            return remote(
                q.step_part.at[index],
                r.step_table.at[sender],
                r.step_send.at[k - 1],
                r.step_recv.at[sender],
                (index, head),
            )

        for k in range(1, n):
            step_copy(k, lax.rem(place + k, n), place).start()
        total_copies.append(end_ring(1, gate_halves, len(gate_steps)))
        value_turn(2)
        keyquery_turn(2)
        group_total.run(0, 1)
        shared(group, r.dot_out, r.dots, r.rd_send, r.rd_recv)
        r.dots[head] = r.dot_out[...]
        for copy in loads[3:]:
            copy.wait()

        def fill_line():
            tiles, summed = Tiles(r.line_sum), Tiles(r.group_sum)
            r.line_sum[...] = jnp.zeros_like(r.line_sum)
            for lag in range(lags + 1):
                tiles.put(r.conv_grad[lag : lag + 1, :channels])
                tiles.put(summed.take(2 * STATE))
            tiles.put(r.gain_grad[...])
            for i in range(3):
                tiles.put(r.vector_grad[i : i + 1])
            tiles.put(summed.take(D))
            tiles.put(summed.take(LANES))

        def grad_store(c):
            return pltpu.make_async_copy(q.tokens_grad.at[c], r.tokens_grad.at[c], r.grad_sem.at[c])

        def rest(c):
            row_sum = r.dots[0, c : c + 1]
            for j in range(1, heads_n):
                row_sum = row_sum + r.dots[j, c : c + 1]
            inverse = r.inverse[c : c + 1]
            out_grad = (q.output[row_block(c)] - q.teacher[c]) * as_column(
                long_row(r.mask, c, length), width
            )
            q.tokens_grad[c] = (
                out_grad
                + as_column(inverse, width) * gain * total(c)
                - q.tokens[c] * as_column(inverse * inverse * row_sum * (1.0 / D), width)
            )
            grad_store(c).start()

        rest(0)
        rest(1)
        value_turn(3)
        keyquery_turn(3)
        group_total.run(1)
        fill_line()
        line_total.start(0)
        rest(2)
        value_turn(4)
        keyquery_turn(4)
        line_total.run(0, 1)
        for c in range(3, count):
            rest(c)
        value_turn(5)
        keyquery_turn(5)
        line_total.run(1, 2)
        if ring_steps > 6:

            def remaining(s):
                for first in value_halves + (keyquery_first,):
                    pass_on(first, s + 6)

            loop(ring_steps - 6, remaining)
        for k in (keyquery_first, keyquery_first + 1):
            _, _, (first, lines), _, _ = ring.streams[k]
            r.keyquery_sum[first : first + lines] = ring.last(k)
        chip_total.start(0)
        total_copies.append(total_of(2, value_halves, q.sums, targets))
        for k in range(1, n):
            sender = lax.rem(place + k, n)
            copy = step_copy(k, sender, sender)
            copy.wait_send()
            copy.wait_recv()
        r.step_table[place] = q.step_part[place]
        step_sum = r.step_table[0]
        for s in range(1, n):
            step_sum = step_sum + r.step_table[s]
        r.step_total[...] = step_sum[:heads, :own]
        line_total.run(2)
        chip_total.run(0)
        keyquery_swap = remote(
            r.keyquery_sum,
            r.keyquery_other,
            r.small_send.at[1],
            r.small_recv.at[1],
            group.at(group.mate),
        )
        keyquery_swap.start()

        tiles = Tiles(r.line_sum)
        for lag in range(lags + 1):
            own_row, shared_row = tiles.take(channels), tiles.take(2 * STATE)
            if lag < lags:
                r.value_conv_total[lag : lag + 1] = own_row
                r.keyquery_conv_total[lag : lag + 1] = shared_row
            else:
                r.value_offset_total[...] = own_row[0]
                r.keyquery_offset_total[...] = shared_row[0]
        r.norm_gain_total[...] = tiles.take(channels)[0]
        for target in (r.step_bias_total, r.rate_log_total, r.skip_total):
            target[...] = tiles.take(LANES)[0, :heads]
        r.input_gain_total[...] = (own_columns(tiles.take(D)) / gain)[0]
        r.loss_total[...] = 0.5 * jnp.sum(tiles.take(LANES), axis=1, keepdims=True)[0]

        loop(count, finish)
        for c in range(count):
            grad_store(c).wait()
        for copy in total_copies:
            copy.wait()
        keyquery_mate.wait_send()
        keyquery_swap.wait()
        mine, other = r.keyquery_sum[...], r.keyquery_other[...]
        r.keyquery_total[:, :STATE] = jnp.where(group.core == 0, mine, other)
        r.keyquery_total[:, STATE:] = jnp.where(group.core == 0, other, mine)
        for i in range(len(ring.streams)):
            ring.finish(i)

    pl.run_scoped(phase_two, *scoped[3])


def rear(inputs, lags, cid):
    heads_n, n = lax.axis_size("head"), lax.axis_size("seq")
    count, length, channels = inputs["gate_hbm"].shape
    pieces = inputs["pieces_hbm"]
    rows, width = pieces.shape[1:]
    heads = channels // HEADDIM
    both = channels + 2 * STATE
    own = D // n
    step_lanes = -(-own // LANES) * LANES
    chips = heads_n // 2
    vmem, dma = pltpu.VMEM, pltpu.SemaphoreType.DMA
    hbm = pl.BlockSpec(memory_space=pl.ANY)
    group_tiles = (lags + 1) * 2 * STATE // LANES + D // LANES + 1
    line_tiles = (lags + 1) * both // LANES + channels // LANES + 3 + D // LANES + 1
    group_shape = (-(-group_tiles * LANES // (8 * 512)) * 8, 512)
    line_shape = (-(-line_tiles * LANES // (8 * both)) * 8, both)
    head_stages, line_stages = stages_of(heads_n), stages_of(n)
    outs = {
        "tokens_grad": (count, length, width),
        "out_total": (own, channels),
        "gate_total": (own, channels),
        "value_total": (own, channels),
        "keyquery_total": (own, 2 * STATE),
        "step_total": (heads, own),
        "value_conv_total": (lags, channels),
        "value_offset_total": (channels,),
        "keyquery_conv_total": (lags, 2 * STATE),
        "keyquery_offset_total": (2 * STATE,),
        "step_bias_total": (heads,),
        "rate_log_total": (heads,),
        "skip_total": (heads,),
        "norm_gain_total": (channels,),
        "input_gain_total": (width,),
        "loss_total": (1,),
    }
    if own % 64 == 0:
        wide_slots = [vmem((n - 1, own // 2, channels), bf16)] * 2
        slots = [vmem((n - 1, own // 4, channels), bf16)] * 4
    else:
        wide_slots = ring_slots(n, own, channels, bf16)
        slots = wide_slots + [vmem((16, LANES), bf16)] * 2
    chained = chain_buffers(count, channels)
    scratch = {
        "normed": vmem((count, length, D), bf16),
        "gate_grad": vmem((count, length, channels), bf16),
        "values_grad": vmem((count, length, channels), bf16),
        "narrow": vmem((count, length, 2 * STATE + LANES), bf16),
        "out_part": vmem((D, channels), bf16),
        "gate_part": vmem((D, channels), bf16),
        "os0": wide_slots[0],
        "os1": wide_slots[1],
        "gs0": wide_slots[0],
        "gs1": wide_slots[1],
        "vs0": slots[0],
        "vs1": slots[1],
        "vs2": slots[2],
        "vs3": slots[3],
        "ks0": vmem((n - 1, own // 2, STATE), f32),
        "ks1": vmem((n - 1, own // 2, STATE), f32),
        "state": chained[0],
        "offered": chained[2],
        "hand": chained[3],
        "edge": vmem((count, 8, both), f32),
        "edge_in": vmem((count, 8, both), f32),
        "gain_grad": vmem((1, channels), f32),
        "vector_grad": vmem((8, LANES), f32),
        "conv_grad": vmem((8, both), f32),
        "mate_in": vmem((chips, rows, width), bf16),
        "chip_in": vmem((chips - 1, rows, width), bf16),
        "dots": vmem((heads_n, count, length), f32),
        "dot_out": vmem((count, length), f32),
        "keyquery_in": vmem((D, STATE), f32),
        "keyquery_sum": vmem((own, STATE), f32),
        "keyquery_other": vmem((own, STATE), f32),
        "keyquery_table": vmem((head_stages - 1, own, STATE), f32),
        "step_table": vmem((n, 16, step_lanes), f32),
        "group_sum": vmem(group_shape, f32),
        "group_table": vmem((head_stages,) + group_shape, f32),
        "line_sum": vmem(line_shape, f32),
        "line_table": vmem((line_stages,) + line_shape, f32),
        "load_sem": dma((3,)),
        "row_sem": dma((3, count)),
        "line_load": dma((2,)),
        "load_two": dma((6,)),
        "grad_sem": dma((count,)),
        "total_sem": dma((3,)),
        "edge_send": dma((count,)),
        "edge_recv": dma((count,)),
        "chain_send": dma((3, count)),
        "chain_recv": dma((3, count)),
        "ring_send": dma((10,)),
        "ring_recv": dma((10, n - 1)),
        "mate_send": dma((chips, count)),
        "mate_recv": dma((chips, count)),
        "chip_send": dma((chips - 1, count)),
        "chip_recv": dma((chips - 1, count)),
        "rd_send": dma((heads_n - 1,)),
        "rd_recv": dma((heads_n,)),
        "small_send": dma((2,)),
        "small_recv": dma((2,)),
        "kq_send": dma((head_stages - 1,)),
        "kq_recv": dma((head_stages - 1,)),
        "group_send": dma((head_stages,)),
        "group_recv": dma((head_stages,)),
        "line_send": dma((line_stages,)),
        "line_recv": dma((line_stages,)),
        "step_send": dma((n - 1,)),
        "step_recv": dma((n,)),
    }
    first = {
        "weight": vmem(inputs["out_weight_hbm"].shape, bf16),
        "pieces": vmem(pieces.shape, bf16),
        "gate": vmem((count, length, channels), f32),
        "mixed": vmem((count, length, channels), f32),
        "conv": vmem((count, length, both), f32),
        "linear": vmem((2, length, both), bf16),
        "heads_in": vmem((count, length, channels), f32),
        "heads_grad": vmem((count, length, channels), f32),
        "keys": vmem((count, length, STATE), bf16),
        "queries": vmem((count, length, STATE), bf16),
        "scores": vmem((length, length), f32),
        "scores_grad": vmem((length, length), f32),
        "mask_bias": vmem((length, length), f32),
        "narrow_grad": vmem((count, length, 2 * STATE), f32),
        "local": vmem((count, STATE, channels), f32),
        "passed": vmem((count, 8, channels), f32),
        "offer": chained[1],
        "following": chained[4],
        "extended": vmem((2, length + 16, LANES), f32),
        "around": vmem((2, length + 32, LANES), f32),
        "usable": vmem((lags - 1, length + 32, LANES), f32),
        "tails": vmem((count, 16, both), f32),
        "dot_inner": vmem((count, length, LANES), f32),
        "cum_part": vmem((count, length, LANES), f32),
    }
    second = {
        "gate_weight": vmem((D, channels), bf16),
        "value_weight": vmem((D, channels), bf16),
        "keyquery_weight": vmem((D, 2 * STATE), bf16),
        "tokens": vmem((count, length, width), f32),
        "output": vmem((rows, width), f32),
        "teacher": vmem((count, length, width), f32),
        "tokens_grad": vmem((count, length, width), f32),
        "value_part": vmem((D, channels), bf16),
        "keyquery_part": vmem((2, D, STATE), f32),
        "keyquery_half": vmem((D, STATE), f32),
        "part": vmem((heads_n, rows, width), bf16),
        "chip_out": vmem((chips - 1, rows, width), bf16),
        "columns": vmem((1, D), f32),
        "step_whole": vmem((LANES, D), f32),
        "step_part": vmem((n, 16, step_lanes), f32),
        "sums": vmem((3, own, channels), f32),
    }
    names = list(inputs) + list(outs) + list(scratch)
    scoped = (list(first), list(first.values()), list(second), list(second.values()))
    in_hbm = [name.endswith("_hbm") for name in inputs]
    found = pl.pallas_call(
        functools.partial(rear_kernel, names, scoped, heads),
        out_shape=[jax.ShapeDtypeStruct(s, f32) for s in outs.values()],
        in_specs=[hbm if there else in_vmem for there in in_hbm],
        out_specs=[hbm] * 4 + [in_vmem] * (len(outs) - 4),
        scratch_shapes=list(scratch.values()),
        compiler_params=params(cid),
        name="rear",
    )(*inputs.values())
    return dict(zip(outs, found))


def deliver_kernel(count, *refs):
    for source, target in zip(refs[:count], refs[count:]):
        target[...] = source[...]


def deliver(arrays):
    return pl.pallas_call(
        functools.partial(deliver_kernel, len(arrays)),
        out_shape=[jax.ShapeDtypeStruct(a.shape, a.dtype) for a in arrays],
        in_specs=[in_vmem] * len(arrays),
        out_specs=[in_vmem] * len(arrays),
        compiler_params=pltpu.CompilerParams(vmem_limit_bytes=VMEM_LIMIT),
        name="deliver",
    )(*arrays)


def body(
    tokens,
    teacher,
    document_start,
    valid_mask,
    input_gain,
    gate_weight,
    value_weight,
    keyquery_weight,
    step_weight,
    value_conv_weight,
    value_conv_bias,
    keyquery_conv_weight,
    keyquery_conv_bias,
    step_bias,
    rate_log,
    skip_gain,
    norm_gain,
    out_weight,
):
    count, length, _ = tokens.shape
    channels = gate_weight.shape[1]
    width = teacher.shape[2]
    rows = count * length
    lags = value_conv_weight.shape[0]
    vectors = (step_bias, rate_log, skip_gain)
    (
        normed,
        linear,
        conv_linear,
        gate_linear,
        mixed,
        output,
        pieces,
        halo,
        state_in,
        steps,
        cumulative,
        steps_linear,
        square_rows,
        inverse_rows,
        mask_rows,
        rowdot,
        square_total,
        loss_cols,
    ) = front(
        tokens,
        input_gain,
        value_weight,
        keyquery_weight,
        step_weight.T,
        gate_weight,
        document_start,
        vectors,
        (value_conv_weight, value_conv_bias, keyquery_conv_weight, keyquery_conv_bias),
        norm_gain,
        valid_mask,
        out_weight,
        teacher,
        1,
    )
    token_cols = tokens
    if width % LANES:
        token_cols = lax.dynamic_slice_in_dim(tokens, lax.axis_index("head") * width, width, 2)
    totals = rear(
        {
            "pieces_hbm": pieces,
            "out_weight_hbm": blocked(out_weight, pieces.shape[0]),
            "gate_hbm": gate_linear,
            "mixed_hbm": mixed,
            "conv_hbm": conv_linear,
            "linear_hbm": linear,
            "normed_hbm": normed,
            "gate_weight_hbm": gate_weight,
            "value_weight_hbm": value_weight,
            "keyquery_weight_hbm": keyquery_weight,
            "tokens_hbm": token_cols,
            "output_hbm": output,
            "teacher_hbm": teacher,
            "step_weight": step_weight.T,
            "halo": halo,
            "state_in": state_in,
            "steps": steps,
            "cumulative": cumulative,
            "linear_steps": steps_linear,
            "square": square_total,
            "rowdot": rowdot,
            "docs": document_start,
            "step_bias": step_bias,
            "rate_log": rate_log,
            "skip": skip_gain,
            "value_conv": value_conv_weight,
            "keyquery_conv": keyquery_conv_weight,
            "norm_gain": norm_gain,
            "gain": input_gain,
            "mask": mask_rows,
            "inverse": inverse_rows,
            "loss_cols": loss_cols,
        },
        lags,
        3,
    )
    results = deliver(
        (
            output.reshape(count, length, width),
            totals["loss_total"],
            totals["tokens_grad"],
            totals["input_gain_total"],
            totals["gate_total"],
            totals["value_total"],
            totals["keyquery_total"],
            totals["step_total"],
            totals["value_conv_total"],
            totals["value_offset_total"],
            totals["keyquery_conv_total"],
            totals["keyquery_offset_total"],
            totals["step_bias_total"],
            totals["rate_log_total"],
            totals["skip_total"],
            totals["norm_gain_total"],
            totals["out_total"],
        )
    )
    return (
        results[0],
        results[1].reshape(()),
        *results[2:7],
        results[7].T,
        *results[8:16],
        results[16].T,
    )


def solution(mesh):
    placed = (
        P(None, "seq", None),
        P(None, "seq", "head"),
        P(None, "seq"),
        P(),
        P(),
        P(None, "head"),
        P(None, "head"),
        P(),
        P(None, "head"),
        P(None, "head"),
        P("head"),
        P(),
        P(),
        P("head"),
        P("head"),
        P("head"),
        P("head"),
        P("head", None),
    )
    return jax.shard_map(
        body,
        mesh=mesh,
        in_specs=placed,
        out_specs=(
            P(None, "seq", "head"),
            P(),
            P(None, "seq", "head"),
            P("head"),
            P("seq", "head"),
            P("seq", "head"),
            P("seq", None),
            P("seq", "head"),
            P(None, "head"),
            P("head"),
            P(),
            P(),
            P("head"),
            P("head"),
            P("head"),
            P("head"),
            P("head", "seq"),
        ),
        check_vma=False,
    )
```

```python
import functools
import types

import jax
import jax.numpy as jnp
from jax import lax
from jax.experimental import pallas as pl
from jax.experimental.pallas import tpu as pltpu
from jax.sharding import PartitionSpec as P

D = 1536
NHEADS = 48
HEADDIM = 64
STATE = 128
LANES = 128
VMEM_LIMIT = 62 << 20

norm_eps = 1e-05
highest = lax.Precision.HIGHEST
MESH = pl.DeviceIdType.MESH
f32 = jnp.float32
bf16 = jnp.bfloat16
NT = (((1,), (1,)), ((), ()))
TN = (((0,), (0,)), ((), ()))

in_vmem = pl.BlockSpec(memory_space=pltpu.VMEM)
in_smem = pl.BlockSpec(memory_space=pltpu.SMEM)


def params(cid):
    return pltpu.CompilerParams(
        collective_id=cid, has_side_effects=True, vmem_limit_bytes=VMEM_LIMIT
    )


def remote(src, dst, send, recv, target):
    return pltpu.make_async_remote_copy(
        src_ref=src,
        dst_ref=dst,
        send_sem=send,
        recv_sem=recv,
        device_id=target,
        device_id_type=MESH,
    )


def loop(count, fn):
    lax.fori_loop(0, count, lambda i, c: (fn(i), c)[1], 0)


def dot_nt(a, b, precision=None):
    return lax.dot_general(a, b, NT, precision=precision, preferred_element_type=f32)


def dot_tn(a, b, precision=None):
    return lax.dot_general(a, b, TN, precision=precision, preferred_element_type=f32)


def is_true(condition):
    return condition.astype(jnp.int32)


def ring_place(n, index):
    odd, half = lax.rem(index, 2), lax.div(index, 2)
    return half * (1 - odd) + (n - 1 - half) * odd


def ring_index(n, spot):
    late = is_true(2 * spot >= n)
    return 2 * spot + late * (2 * n - 1 - 4 * spot)


def wrapped(n, spot):
    return spot + n * is_true(spot < 0) - n * is_true(spot >= n)


class Ring:
    def __init__(self, send_sem, recv_sem):
        self.n = lax.axis_size("seq")
        self.streams, self.send_sem, self.recv_sem = [], send_sem, recv_sem
        head = lax.axis_index("head")
        self.spot = ring_place(self.n, lax.axis_index("seq"))
        self.after = (ring_index(self.n, wrapped(self.n, self.spot + 1)), head)
        self.before = (ring_index(self.n, wrapped(self.n, self.spot - 1)), head)

    def add(self, part, slots, by_rows=False, first=0):
        rows, width = part.shape[0] // self.n, part.shape[1]
        cut = slots[0].shape[1] if by_rows else slots[0].shape[2]
        if by_rows:
            halves = tuple(((first + way * cut, cut), (0, width)) for way in range(2))
        else:
            halves = (((0, rows), (0, cut)), ((0, rows), (cut, width - cut)))
        for way in range(2):
            lines, columns = halves[way]
            self.streams.append((part, slots[way], lines, pl.ds(*columns), way))

    def piece(self, i, step):
        part, _, (first, count), columns, way = self.streams[i]
        shift = -1 - step if way == 0 else 1 + step
        rows = part.shape[0] // self.n
        index = ring_index(self.n, wrapped(self.n, self.spot + shift))
        tile = 16 if part.dtype == bf16 else 8
        return part.at[pl.ds(pl.multiple_of(index * rows + first, tile), count), columns]

    def copy(self, i, step, source):
        slots, way = self.streams[i][1], self.streams[i][4]
        return remote(
            source,
            slots.at[step],
            self.send_sem.at[i],
            self.recv_sem.at[i, step],
            self.after if way == 0 else self.before,
        )

    def start(self, i):
        self.copy(i, 0, self.piece(i, 0)).start()

    def pass_on(self, i, step):
        slots = self.streams[i][1]
        self.copy(i, step, slots.at[step]).wait_recv()
        total = slots[step].astype(f32) + self.piece(i, step + 1)[...].astype(f32)
        slots[step] = total.astype(slots.dtype)
        self.copy(i, step + 1, slots.at[step]).start()

    def last(self, i):
        slots, step = self.streams[i][1], self.n - 2
        self.copy(i, step, slots.at[step]).wait_recv()
        return slots[step].astype(f32) + self.piece(i, step + 1)[...].astype(f32)

    def finish(self, i):
        slots, way = self.streams[i][1], self.streams[i][4]
        remote(
            slots,
            slots,
            self.send_sem.at[i],
            self.recv_sem.at[i, 0],
            self.after if way == 0 else self.before,
        ).wait_send()


def ring_slots(n, rows, width, kind):
    cut = width // LANES // 2 * LANES
    return [pltpu.VMEM((n - 1, rows, cut), kind), pltpu.VMEM((n - 1, rows, width - cut), kind)]


def step_at(table, here):
    found, here = jnp.int32(-1), jnp.asarray(here, jnp.int32)
    for place, step in table:
        found = found + (step + 1) * (here == place).astype(jnp.int32)
    return found


def sequence_at(table, here, pair):
    found, here = jnp.int32(-1), jnp.asarray(here, jnp.int32)
    for place, owner, b in table:
        found = found + (b + 1) * ((here == place) & (pair == owner)).astype(jnp.int32)
    return found


class PairChain:
    def __init__(self, ahead, by, local, passed, buffers, send_sem, recv_sem):
        self.n = lax.axis_size("seq")
        self.place, self.head = lax.axis_index("seq"), lax.axis_index("head")
        self.by, self.pair, self.second = by, lax.div(ahead, 2), lax.rem(ahead, 2)
        self.local, self.passed = local, passed
        self.state, self.offers, self.offered, self.hand, self.following = buffers
        self.send_sem, self.recv_sem = send_sem, recv_sem
        self.count, _, channels = self.state.shape
        cut = channels // LANES // 2 * LANES
        self.sizes = (channels - cut, cut)
        self.lanes = (pl.ds(cut, channels - cut), pl.ds(0, cut))

    def copy(self, kind, b, source, target, ahead):
        return remote(
            source,
            target,
            self.send_sem.at[kind, b],
            self.recv_sem.at[kind, b],
            (self.place + self.by * ahead, self.head),
        )

    def within(self, buffer, b, second):
        return buffer.at[b, pl.ds(0, buffer.shape[1]), pl.ds(0, self.sizes[second])]

    def offering(self, b, second):
        other = 1 - second
        return self.copy(
            0,
            b,
            self.within(self.offers, b, other),
            self.within(self.offered, b, other),
            1 - 2 * second,
        )

    def handing(self, b, second):
        target = self.state.at[b, pl.ds(0, STATE), self.lanes[second]]
        return self.copy(1, b, self.within(self.hand, b, second), target, 1 - 2 * second)

    def passing(self, b, second):
        if second:
            target = self.within(self.hand, b, second)
        else:
            target = self.state.at[b, pl.ds(0, STATE), self.lanes[second]]
        return self.copy(2, b, self.within(self.following, b, second), target, 2)

    def offer(self, b):
        for second in range(2):

            @pl.when(self.second == second)
            def _():
                other = 1 - second
                lanes, size = self.lanes[other], self.sizes[other]
                self.offers[b, :STATE, :size] = self.local[b, :, lanes].astype(bf16)
                decay = self.passed[b, 7:8, lanes]
                high = decay.astype(bf16).astype(f32)
                row = lax.broadcasted_iota(jnp.int32, (16, size), 0)
                rows = jnp.where(row == 0, high, jnp.where(row == 1, decay - high, 0.0))
                self.offers[b, STATE:, :size] = rows.astype(bf16)
                self.offering(b, second).start()

    def pass_on(self, b):
        more = self.pair < self.n // 2 - 1
        for second in range(2):

            @pl.when(self.second == second)
            def _():
                lanes, size = self.lanes[second], self.sizes[second]
                self.offering(b, 1 - second).wait_recv()

                @pl.when(self.pair > 0)
                def _():
                    self.passing(b, second).wait_recv()

                @pl.when(self.pair == 0)
                def _():
                    zeros = jnp.zeros((STATE, size), bf16)
                    if second:
                        self.hand[b, :, :size] = zeros
                    else:
                        self.state[b, :, lanes] = zeros

                own_decay, own = self.passed[b, 7:8, lanes], self.local[b, :, lanes]
                decay = self.offered[b, STATE:, :size].astype(f32)
                decay = decay[0:1] + decay[1:2]
                offered = self.offered[b, :STATE, :size].astype(f32)
                if second:
                    self.handing(b, second).start()
                    value = decay * self.hand[b, :, :size].astype(f32) + offered
                    self.state[b, :, lanes] = value.astype(bf16)
                    following = own_decay * value + own
                else:
                    value = own_decay * self.state[b, :, lanes].astype(f32) + own
                    self.hand[b, :, :size] = value.astype(bf16)
                    self.handing(b, second).start()
                    following = decay * value + offered

                @pl.when(more)
                def _():
                    self.following[b, :, :size] = following.astype(bf16)
                    self.passing(b, second).start()

    def ready(self, b):
        for second in range(2):

            @pl.when(self.second == second)
            def _():
                self.handing(b, 1 - second).wait_recv()

    def turn(self, here, table):
        b = sequence_at(table, here, self.pair)

        @pl.when(b >= 0)
        def _():
            self.pass_on(b)

    def rest(self, table):
        held = {(pair, b) for _, pair, b in table}
        for pair in range(self.n // 2):
            for b in range(self.count):
                if (pair, b) not in held:

                    @pl.when(self.pair == pair)
                    def _():
                        self.pass_on(b)

    def finish(self):
        for second in range(2):

            @pl.when(self.second == second)
            def _():
                def one(b):
                    self.offering(b, second).wait_send()
                    self.handing(b, second).wait_send()

                    @pl.when(self.pair < self.n // 2 - 1)
                    def _():
                        self.passing(b, second).wait_send()

                loop(self.count, one)


def chain_buffers(count, channels):
    wide = channels - channels // LANES // 2 * LANES
    shapes = [(STATE, channels), (STATE + 16, wide), (STATE + 16, wide), (STATE, wide), (STATE, wide)]
    return [pltpu.VMEM((count,) + s, bf16) for s in shapes]


class Group:
    def __init__(self, n):
        self.n = n
        self.chips = n // 2
        self.seq = lax.axis_index("seq")
        self.me = lax.axis_index("head")
        self.chip = lax.div(self.me, 2)
        self.core = lax.rem(self.me, 2)
        self.mate = self.me + 1 - 2 * self.core

    def at(self, head):
        return (self.seq, head)

    def chip_after(self, k):
        return lax.rem(self.chip + k, self.chips)

    def chip_before(self, k):
        return lax.rem(self.chip + self.chips - k, self.chips)

    def peer(self, k):
        return 2 * self.chip_after(k) + self.core

    def other(self, k):
        return lax.rem(self.me + k, self.n)

    def greet(self):
        barrier = pltpu.get_barrier_semaphore()
        for k in range(1, self.n):
            pl.semaphore_signal(
                barrier, inc=1, device_id=self.at(self.other(k)), device_id_type=MESH
            )
        pl.semaphore_wait(barrier, self.n - 1)


def share(group, source, table, send_sem, recv_sem):
    for k in range(1, group.n):
        remote(
            source,
            table.at[group.me],
            send_sem.at[k - 1],
            recv_sem.at[group.me],
            group.at(group.other(k)),
        ).start()


def shared(group, source, table, send_sem, recv_sem):
    for k in range(1, group.n):
        sender = group.other(k)
        copy = remote(
            source, table.at[sender], send_sem.at[k - 1], recv_sem.at[sender], group.at(sender)
        )
        copy.wait_send()
        copy.wait_recv()


def as_column(row, width):
    tile = jnp.broadcast_to(row, (LANES, row.shape[1])).T
    return jnp.concatenate([tile] * (-(-width // LANES)), axis=1)[:, :width]


def scatter_phases(group, row_block, part, mate_in, chip_out, chip_in, sems):
    mate_send, mate_recv, chip_send, chip_recv = sems

    def mate_copy(c, x):
        return remote(
            part.at[2 * x + 1 - group.core, row_block(c)],
            mate_in.at[x, row_block(c)],
            mate_send.at[x, c],
            mate_recv.at[x, c],
            group.at(group.mate),
        )

    def chip_copy(c, k):
        return remote(
            chip_out.at[k - 1, row_block(c)],
            chip_in.at[k - 1, row_block(c)],
            chip_send.at[k - 1, c],
            chip_recv.at[k - 1, c],
            group.at(group.peer(k)),
        )

    def start_mate(c):
        for x in range(group.chips):
            mate_copy(c, x).start()

    def start_chip(c):
        for x in range(group.chips):
            mate_copy(c, x).wait_recv()
        for k in range(1, group.chips):
            x = group.chip_after(k)
            both = part[2 * x + group.core, row_block(c)].astype(f32) + mate_in[
                x, row_block(c)
            ].astype(f32)
            chip_out[k - 1, row_block(c)] = both.astype(bf16)
            chip_copy(c, k).start()

    def total(c):
        value = part[group.me, row_block(c)].astype(f32) + mate_in[
            group.chip, row_block(c)
        ].astype(f32)
        for k in range(1, group.chips):
            chip_copy(c, k).wait_recv()
            value = value + chip_in[k - 1, row_block(c)].astype(f32)
        return value

    def finish(c):
        for x in range(group.chips):
            mate_copy(c, x).wait_send()
        for k in range(1, group.chips):
            chip_copy(c, k).wait_send()

    return start_mate, start_chip, total, finish


def scatter_scratch(n, rows, width, chunks):
    chips = n // 2
    dma = pltpu.SemaphoreType.DMA
    return [
        pltpu.VMEM((n, rows, width), bf16),
        pltpu.VMEM((chips, rows, width), bf16),
        pltpu.VMEM((chips - 1, rows, width), bf16),
        pltpu.VMEM((chips - 1, rows, width), bf16),
    ], [dma((chips, chunks)), dma((chips, chunks)), dma((chips - 1, chunks)), dma((chips - 1, chunks))]


def blocked(weight, n):
    width = weight.shape[1] // n
    if width % LANES == 0:
        return weight
    return jnp.moveaxis(weight.reshape(weight.shape[0], n, width), 1, 0)


def blocks(width, size=256):
    return [(at, min(size, width - at)) for at in range(0, width, size)]


def fold_lanes(values):
    rows, width = values.shape
    if width % LANES:
        fill = jnp.zeros((rows, LANES - width % LANES), values.dtype)
        values = jnp.concatenate([values, fill], axis=1)
    total = values[:, :LANES]
    for at in range(LANES, width, LANES):
        total = total + values[:, at : at + LANES]
    return total


def rows_of(values):
    return jnp.sum(fold_lanes(values).T, axis=0, keepdims=True)


def head_spread(channels):
    row = lax.broadcasted_iota(jnp.int32, (LANES, channels), 0)
    head = lax.broadcasted_iota(jnp.int32, (LANES, channels), 1) // HEADDIM
    return ((row % 16 == head) & (row < 48)).astype(f32).astype(bf16)


def head_gather(channels):
    head = lax.broadcasted_iota(jnp.int32, (channels, LANES), 0) // HEADDIM
    return (lax.broadcasted_iota(jnp.int32, (channels, LANES), 1) == head).astype(f32).astype(bf16)


def spread(values, marks):
    lane = lax.broadcasted_iota(jnp.int32, values.shape, 1)
    values = jnp.where(lane < 16, values, 0.0)
    high = values.astype(bf16).astype(f32)
    left = values - high
    middle = left.astype(bf16).astype(f32)
    low = (left - middle).astype(bf16).astype(f32)
    three = high + pltpu.roll(middle, 16, 1) + pltpu.roll(low, 32, 1)
    return jnp.dot(three.astype(bf16), marks, preferred_element_type=f32)


def gather_heads(values, marks):
    high = values.astype(bf16)
    low = (values - high.astype(f32)).astype(bf16)
    return jnp.dot(high, marks, preferred_element_type=f32) + jnp.dot(
        low, marks, preferred_element_type=f32
    )


def softplus(x):
    y = jnp.exp(-jnp.abs(x))
    small = y * (1.0 - y * (1.0 / 2 - y * (1.0 / 3 - y * (1.0 / 4 - y * (1.0 / 5)))))
    return jnp.maximum(x, 0.0) + jnp.where(y < 0.03, small, jnp.log(1.0 + y))


def lane_row(ref):
    row = ref[...][None, :]
    return jnp.concatenate([row, jnp.zeros((1, LANES - row.shape[1]), f32)], axis=1)


def long_row(ref, b, length):
    per = length // LANES
    return jnp.concatenate([ref[pl.ds(b * per + i, 1)] for i in range(per)], axis=1)


def put_row(ref, b, row):
    per = row.shape[1] // LANES
    for i in range(per):
        ref[pl.ds(b * per + i, 1)] = row[:, i * LANES : (i + 1) * LANES]


def spread_row(row, marks):
    return spread(jnp.broadcast_to(row, (8, LANES)), marks)[:1]


def position_masks(docs_row, begin):
    length = docs_row.shape[1]
    column = jnp.broadcast_to(docs_row, (LANES, length)).T
    place = begin + lax.broadcasted_iota(jnp.int32, (length, LANES), 0).astype(f32)
    return column, place


def front_kernel(
    heads,
    tokens_hbm,
    gain_ref,
    value_hbm,
    keyquery_hbm,
    step_ref,
    gate_hbm,
    docs_ref,
    step_bias_ref,
    rate_log_ref,
    skip_ref,
    value_conv_ref,
    value_offset_ref,
    keyquery_conv_ref,
    keyquery_offset_ref,
    norm_gain_ref,
    valid_ref,
    out_weight_hbm,
    teacher_hbm,
    normed_out,
    linear_out,
    conv_out,
    gate_out,
    mixed_out,
    output_out,
    pieces_out,
    halo_out,
    state_out,
    steps_out,
    cumulative_out,
    linear_steps_out,
    square_out,
    inverse_out,
    mask_out,
    rowdot_ref,
    squared_ref,
    loss_ref,
    tokens,
    last_tokens,
    value_weight,
    keyquery_weight,
    gate_weight,
    normed,
    linear,
    conv,
    gate,
    mixed,
    gained,
    tail,
    halo,
    extended,
    heads_in,
    keys,
    queries,
    scores,
    mask_bias,
    locals_,
    state,
    offers,
    offered,
    hand,
    following,
    passed,
    entering,
    load_sem,
    last_sem,
    token_sem,
    store_sem,
    halo_sem,
    chain_send,
    chain_recv,
    out_weight,
    teacher,
    output_cols,
    part,
    mate_in,
    chip_out,
    chip_in,
    gathered,
    squares,
    dots,
    dot_out,
    mate_send,
    mate_recv,
    chip_send,
    chip_recv,
    gm_send,
    gm_recv,
    gc_send,
    gc_recv,
    gf_send,
    gf_recv,
    sq_send,
    sq_recv,
    rd_send,
    rd_recv,
    output_sem,
    pieces_sem,
):
    n = lax.axis_size("seq")
    place = lax.axis_index("seq")
    heads_n = lax.axis_size("head")
    group = Group(heads_n)
    head = group.me
    width = teacher.shape[2]
    chunks = tokens.shape[0]
    count, length, _ = tokens.shape
    channels = value_weight.shape[1]
    both = channels + 2 * STATE
    lags = value_conv_ref.shape[0]
    begin = (place * length).astype(f32)

    loads = [
        pltpu.make_async_copy(value_hbm, value_weight, load_sem.at[0]),
        pltpu.make_async_copy(keyquery_hbm, keyquery_weight, load_sem.at[1]),
        pltpu.make_async_copy(gate_hbm, gate_weight, load_sem.at[2]),
        pltpu.make_async_copy(out_weight_hbm, out_weight, load_sem.at[3]),
        pltpu.make_async_copy(teacher_hbm, teacher, load_sem.at[4]),
    ]

    def token_load(b):
        return pltpu.make_async_copy(tokens_hbm.at[b], tokens.at[b], token_sem.at[b])

    def last_load(b):
        return pltpu.make_async_copy(
            tokens_hbm.at[b, length - 16 :], last_tokens.at[b], last_sem.at[b]
        )

    for b in range(count):
        last_load(b).start()
    loads[0].start()
    loads[1].start()
    for b in range(count):
        token_load(b).start()
    for copy in loads[2:]:
        copy.start()

    stores = [
        (normed, normed_out),
        (linear, linear_out),
        (conv, conv_out),
        (gate, gate_out),
        (mixed, mixed_out),
    ]

    def store(i, b):
        source, target = stores[i]
        return pltpu.make_async_copy(source.at[b], target.at[b], store_sem.at[i, b])

    barrier = pltpu.get_barrier_semaphore()

    chain = PairChain(
        place,
        1,
        locals_,
        passed,
        (state, offers, offered, hand, following),
        chain_send,
        chain_recv,
    )
    for k in range(1, heads_n):
        pl.semaphore_signal(
            barrier, inc=1, device_id=group.at(group.other(k)), device_id_type=MESH
        )
    for k in range(1, n):
        pl.semaphore_signal(
            barrier, inc=1, device_id=(lax.rem(place + k, n), head), device_id_type=MESH
        )

    def normalized(x):
        inverse = lax.rsqrt(jnp.mean(x * x, axis=-1, keepdims=True) + norm_eps)
        return inverse, (x * inverse * gain_ref[...][None, :]).astype(bf16)

    for b in range(count):
        last_load(b).wait()
    last = jnp.concatenate([normalized(last_tokens[b])[1] for b in range(count)], axis=0)
    loads[0].wait()
    loads[1].wait()
    for at, size in blocks(channels):
        tail[:, at : at + size] = jnp.dot(
            last, value_weight[:, at : at + size], preferred_element_type=f32
        ).astype(bf16)
    tail[:, channels:] = jnp.dot(last, keyquery_weight[...], preferred_element_type=f32).astype(bf16)
    pl.semaphore_wait(barrier, n + heads_n - 2)
    halo_copy = remote(tail, halo, halo_sem.at[0], halo_sem.at[1], (place + 1, head))

    @pl.when(place < n - 1)
    def _():
        halo_copy.start()

    marks = head_spread(channels)
    step_bias = lane_row(step_bias_ref)
    decay_rate = -jnp.exp(lane_row(rate_log_ref))
    skip = spread_row(lane_row(skip_ref), marks)
    triangle = (
        lax.broadcasted_iota(jnp.int32, (length, length), 0)
        >= lax.broadcasted_iota(jnp.int32, (length, length), 1)
    ).astype(f32)

    def norm(b):
        token_load(b).wait()
        inverse, rows = normalized(tokens[b])
        normed[b] = rows
        inverse_out[pl.ds(b, 1)] = jnp.broadcast_to(inverse, (length, LANES)).T[:1]
        store(0, b).start()

    def project_values(b):
        rows = normed[b]
        for at, size in blocks(channels):
            linear[b, :, at : at + size] = jnp.dot(
                rows, value_weight[:, at : at + size], preferred_element_type=f32
            ).astype(bf16)

    def project_rest(b):
        rows = normed[b]
        linear[b, :, channels:] = jnp.dot(
            rows, keyquery_weight[...], preferred_element_type=f32
        ).astype(bf16)
        narrow_steps = dot_nt(rows, step_ref[...])
        linear_steps_out[b] = jnp.concatenate(
            [narrow_steps, jnp.zeros((length, LANES - heads), f32)], axis=1
        )
        store(1, b).start()

    def states(b):
        @pl.when((b == 0) & (place > 0))
        def _():
            halo_copy.wait_recv()

        @pl.when((b == 0) & (place == 0))
        def _():
            halo[...] = jnp.zeros_like(halo)

        column, spot = position_masks(docs_ref[pl.ds(b, 1)].astype(f32), begin)
        extended[0:16] = halo[pl.ds(pl.multiple_of(b * 16, 16), 16)].astype(f32)
        extended[16:] = linear[b].astype(f32)
        usable = [None] + [(spot - lag >= column).astype(f32) for lag in range(1, lags)]
        for at in range(0, both, LANES):
            if at < channels:
                weight, offset, place_at = value_conv_ref, value_offset_ref, at
            else:
                weight, offset, place_at = keyquery_conv_ref, keyquery_offset_ref, at - channels
            lanes = slice(place_at, place_at + LANES)
            value = offset[lanes][None, :] + weight[0:1, lanes] * extended[16:, at : at + LANES]
            for lag in range(1, lags):
                value = value + weight[lag : lag + 1, lanes] * (
                    extended[16 - lag : 16 - lag + length, at : at + LANES] * usable[lag]
                )
            conv[b, :, at : at + LANES] = value
            active = value * jax.nn.sigmoid(value)
            if at < channels:
                heads_in[b, :, at : at + LANES] = active
            elif at < channels + STATE:
                keys[b] = active.astype(bf16)
            else:
                queries[b] = active.astype(bf16)
        store(2, b).start()
        steps = softplus(linear_steps_out[b] + step_bias)
        cumulative = jnp.dot(
            triangle, steps * decay_rate, precision=highest, preferred_element_type=f32
        )
        steps_out[b] = steps
        cumulative_out[b] = cumulative
        kept = (column < begin).astype(f32)
        trailing = (spot >= column[length - 1 :]).astype(f32)
        entering[b] = jnp.exp(cumulative) * kept
        end_weight = jnp.exp(cumulative[length - 1 :] - cumulative) * trailing * steps
        weighted = (heads_in[b] * spread(end_weight, marks)).astype(bf16)
        locals_[b] = dot_tn(keys[b], weighted)
        last_entering = entering[b, length - 8 :]
        passed[b] = spread(last_entering, marks)

    pairs = channels // LANES
    turns = []
    if n == 8 and count == 4:
        turns = [(1, 0, 0), (2, 0, 1), (3, 0, 2), (5, 0, 3)]
        turns += [(2, 1, 0), (3, 1, 1), (5, 1, 2), (7, 1, 3)]
        turns += [(3, 2, 0), (5, 2, 1), (7, 2, 2), (9, 2, 3)]
        turns += [(5, 3, 0), (7, 3, 1), (9, 3, 2), (10, 3, 3)]

    def begin_sequence(b):
        norm(b)
        project_values(b)
        project_rest(b)
        states(b)
        chain.offer(b)
        chain.turn(b, turns)

    loop(count, begin_sequence)
    halo_out[...] = halo[...]
    per_row = 2.0 / (D * jnp.sum(valid_ref[...].astype(f32), keepdims=True))
    here = pl.ds(pl.multiple_of(place * length, length), length)
    for b in range(count):
        row = valid_ref[b : b + 1, here].astype(f32) * per_row
        for i in range(length // LANES):
            at = b * (length // LANES) + i
            mask_out[at : at + 1] = row[:, i * LANES : (i + 1) * LANES]
    first_half = lax.broadcasted_iota(jnp.int32, (length, LANES), 1) < HEADDIM
    loads[2].wait()

    def inside(b):
        column, spot = position_masks(docs_ref[pl.ds(b, 1)].astype(f32), begin)
        wide = jnp.concatenate([column] * (length // LANES), axis=1)
        t = begin + lax.broadcasted_iota(jnp.int32, (length, length), 0).astype(f32)
        u = begin + lax.broadcasted_iota(jnp.int32, (length, length), 1).astype(f32)
        mask_bias[...] = jnp.where((u >= wide) & (u <= t), 0.0, -1e30)
        scores[...] = dot_nt(queries[b], keys[b])
        cumulative = cumulative_out[b]
        across = cumulative.T
        spread_steps = spread(steps_out[b], marks)
        for pair in range(pairs):
            lanes = slice(pair * LANES, (pair + 1) * LANES)
            scaled = heads_in[b, :, lanes] * spread_steps[:, lanes]
            value = jnp.zeros((length, LANES), f32)
            for half in range(2):
                h = 2 * pair + half
                decay = jnp.exp(cumulative[:, h : h + 1] - across[h : h + 1] + mask_bias[...])
                mixing = (decay * scores[...]).astype(bf16)
                mine = jnp.where(first_half if half == 0 else ~first_half, scaled, 0.0).astype(bf16)
                value = value + jnp.dot(mixing, mine, preferred_element_type=f32)
            mixed[b, :, lanes] = value
        rows = normed[b]
        for at, size in blocks(channels):
            gate[b, :, at : at + size] = jnp.dot(
                rows, gate_weight[:, at : at + size], preferred_element_type=f32
            )
        store(3, b).start()
        chain.turn(count + b, turns)

    loop(count, inside)
    chain.rest(turns)

    def close(b):
        chain.ready(b)
        state_out[b] = state[b]
        projected = jnp.dot(queries[b], state[b], preferred_element_type=f32)
        value = mixed[b] + spread(entering[b], marks) * projected + skip * heads_in[b]
        mixed[b] = value
        store(4, b).start()
        linear_gate = gate[b]
        gated = value * (linear_gate * jax.nn.sigmoid(linear_gate))
        gained[b] = (gated * norm_gain_ref[...][None, :]).astype(bf16)
        put_row(square_out, b, rows_of(gated * gated))

    def row_block(c):
        return pl.ds(pl.multiple_of(c * length, length), length)

    start_mate, start_chip, total, finish = scatter_phases(
        group, row_block, part, mate_in, chip_out, chip_in, (mate_send, mate_recv, chip_send, chip_recv)
    )

    def product(c):
        rows = gained[c]
        for j in range(heads_n):
            block = (
                out_weight[:, j * width : (j + 1) * width] if len(out_weight.shape) == 2 else out_weight[j]
            )
            part[j, row_block(c)] = jnp.dot(rows, block, preferred_element_type=f32).astype(bf16)
        start_mate(c)

    loads[3].wait()

    def close_and_send(b):
        close(b)
        product(b)

        @pl.when(b > 0)
        def _():
            start_chip(b - 1)

        chain.turn(9 + b, turns)

    loop(count, close_and_send)
    start_chip(count - 1)
    share(group, square_out, squares, sq_send, sq_recv)
    shared(group, square_out, squares, sq_send, sq_recv)
    squares[group.me] = square_out[...]
    loss_ref[...] = jnp.zeros_like(loss_ref)

    def to_mate(c):
        block = gathered.at[group.me, row_block(c)]
        return remote(block, block, gm_send.at[c], gm_recv.at[c], group.at(group.mate))

    def to_chip(c, k):
        block = gathered.at[group.me, row_block(c)]
        return remote(
            block, block, gc_send.at[k - 1, c], gc_recv.at[k - 1, c], group.at(group.peer(k))
        )

    def forward(c, k):
        block = gathered.at[2 * group.chip_before(k) + group.core, row_block(c)]
        return remote(
            block, block, gf_send.at[k - 1, c], gf_recv.at[k - 1, c], group.at(group.mate)
        )

    loads[4].wait()

    def own_tokens(c):
        if width % LANES == 0:
            return tokens[c, :, pl.ds(pl.multiple_of(head * width, LANES), width)]
        found = jnp.zeros((length, width), f32)
        for j in range(heads_n):
            mine = tokens[c, :, j * width : (j + 1) * width]
            found = found + jnp.where(head == j, mine, 0.0)
        return found

    def rest(c):
        squared = long_row(squares.at[0], c, length)
        for j in range(1, heads_n):
            squared = squared + long_row(squares.at[j], c, length)
        put_row(squared_ref, c, squared)
        scale = lax.rsqrt(squared * (1.0 / (NHEADS * HEADDIM)) + norm_eps)
        branch = total(c) * as_column(scale, width)
        output = own_tokens(c) + branch
        output_cols[row_block(c)] = output
        difference = output - teacher[c]
        weighted = difference * as_column(long_row(mask_out, c, length), width)
        low = weighted.astype(bf16)
        gathered[group.me, row_block(c)] = low
        to_mate(c).start()
        for k in range(1, group.chips):
            to_chip(c, k).start()
        loss_ref[...] += jnp.sum(weighted * difference, axis=0, keepdims=True)
        put_row(dot_out, c, rows_of(low.astype(f32) * branch))

    loop(chunks, rest)
    output_store = pltpu.make_async_copy(output_cols, output_out, output_sem.at[0])
    output_store.start()
    share(group, dot_out, dots, rd_send, rd_recv)

    def pass_on(c):
        for k in range(1, group.chips):
            to_chip(c, k).wait_recv()
            forward(c, k).start()

    loop(chunks, pass_on)

    def pieces_store(c):
        return pltpu.make_async_copy(
            gathered.at[pl.ds(0, heads_n), row_block(c)],
            pieces_out.at[pl.ds(0, heads_n), row_block(c)],
            pieces_sem.at[c],
        )

    def end(c):
        to_mate(c).wait()
        for k in range(1, group.chips):
            to_chip(c, k).wait_send()
            forward(c, k).wait()
        finish(c)
        pieces_store(c).start()

    loop(chunks, end)
    shared(group, dot_out, dots, rd_send, rd_recv)
    row_sum = dot_out[...]
    for k in range(1, heads_n):
        row_sum = row_sum + dots[group.other(k)]
    rowdot_ref[...] = row_sum
    output_store.wait()
    loop(chunks, lambda c: pieces_store(c).wait())

    @pl.when(place < n - 1)
    def _():
        halo_copy.wait_send()

    chain.finish()

    for i in range(len(stores)):
        loop(count, lambda b, i=i: store(i, b).wait())


def front(tokens, gain, value_weight, keyquery_weight, step_weight, gate_weight, docs, vectors, conv, norm_gain, valid, out_weight, teacher, cid):
    count, length, _ = tokens.shape
    channels = value_weight.shape[1]
    heads = channels // HEADDIM
    both = channels + 2 * STATE
    dma = pltpu.SemaphoreType.DMA
    hbm = pl.BlockSpec(memory_space=pl.ANY)
    shape = jax.ShapeDtypeStruct
    heads_n, width = lax.axis_size("head"), teacher.shape[2]
    rows, chips = count * length, heads_n // 2
    chunks, lines = count, rows // LANES
    out_weight = blocked(out_weight, heads_n)
    buffers, sems = scatter_scratch(heads_n, rows, width, chunks)
    big = [
        ((count, length, D), bf16),
        ((count, length, both), bf16),
        ((count, length, both), f32),
        ((count, length, channels), f32),
        ((count, length, channels), f32),
    ]
    results = [((rows, width), f32), ((heads_n, rows, width), bf16)]
    small = [
        ((count * 16, both), bf16),
        ((count, STATE, channels), bf16),
        ((count, length, LANES), f32),
        ((count, length, LANES), f32),
        ((count, length, LANES), f32),
        ((count * length // LANES, LANES), f32),
        ((count, length), f32),
        ((count * length // LANES, LANES), f32),
        ((lines, LANES), f32),
        ((lines, LANES), f32),
        ((1, width), f32),
    ]
    return pl.pallas_call(
        functools.partial(front_kernel, heads),
        out_shape=[shape(*s) for s in big + results + small],
        in_specs=[hbm, in_vmem, hbm, hbm, in_vmem, hbm] + [in_vmem] * 10 + [hbm] * 2,
        out_specs=[hbm] * (len(big) + 2) + [in_vmem] * len(small),
        scratch_shapes=[
            pltpu.VMEM((count, length, D), f32),
            pltpu.VMEM((count, 16, D), f32),
            pltpu.VMEM((D, channels), bf16),
            pltpu.VMEM((D, 2 * STATE), bf16),
            pltpu.VMEM((D, channels), bf16),
        ]
        + [pltpu.VMEM(*s) for s in big]
        + [
            pltpu.VMEM((count, length, channels), bf16),
            pltpu.VMEM((count * 16, both), bf16),
            pltpu.VMEM((count * 16, both), bf16),
            pltpu.VMEM((length + 16, both), f32),
            pltpu.VMEM((count, length, channels), f32),
            pltpu.VMEM((count, length, STATE), bf16),
            pltpu.VMEM((count, length, STATE), bf16),
            pltpu.VMEM((length, length), f32),
            pltpu.VMEM((length, length), f32),
            pltpu.VMEM((count, STATE, channels), f32),
        ]
        + chain_buffers(count, channels)
        + [
            pltpu.VMEM((count, 8, channels), f32),
            pltpu.VMEM((count, length, LANES), f32),
            dma((5,)),
            dma((count,)),
            dma((count,)),
            dma((len(big), count)),
            dma((2,)),
            dma((3, count)),
            dma((3, count)),
            pltpu.VMEM(out_weight.shape, bf16),
            pltpu.VMEM((count, length, width), f32),
            pltpu.VMEM((rows, width), f32),
        ]
        + buffers
        + [
            pltpu.VMEM((heads_n, rows, width), bf16),
            pltpu.VMEM((heads_n, lines, LANES), f32),
            pltpu.VMEM((heads_n, lines, LANES), f32),
            pltpu.VMEM((lines, LANES), f32),
        ]
        + sems
        + [
            dma((chunks,)),
            dma((chunks,)),
            dma((chips - 1, chunks)),
            dma((chips - 1, chunks)),
            dma((chips - 1, chunks)),
            dma((chips - 1, chunks)),
            dma((heads_n - 1,)),
            dma((heads_n,)),
            dma((heads_n - 1,)),
            dma((heads_n,)),
            dma((1,)),
            dma((chunks,)),
        ],
        compiler_params=params(cid),
        name="front",
    )(tokens, gain, value_weight, keyquery_weight, step_weight, gate_weight, docs, *vectors, *conv, norm_gain, valid, out_weight, teacher)


class Doubling:
    def __init__(self, axis, bits, current, table, send_sem, recv_sem):
        self.axis, self.bits, self.current, self.table = axis, list(bits), current, table
        self.send_sem, self.recv_sem = send_sem, recv_sem

    def copy(self, stage):
        bit = 1 << self.bits[stage]
        mine = lax.axis_index(self.axis)
        other = mine + bit - 2 * bit * lax.rem(lax.div(mine, bit), 2)
        if self.axis == "head":
            target = (lax.axis_index("seq"), other)
        else:
            target = (other, lax.axis_index("head"))
        return remote(
            self.current,
            self.table.at[stage],
            self.send_sem.at[stage],
            self.recv_sem.at[stage],
            target,
        )

    def start(self, stage):
        self.copy(stage).start()

    def run(self, first, last=None):
        for stage in range(first, len(self.bits) if last is None else min(last, len(self.bits))):
            self.copy(stage).wait()
            self.current[...] = self.current[...] + self.table[stage]
            if stage + 1 < len(self.bits):
                self.start(stage + 1)


def stages_of(n):
    return n.bit_length() - 1


def tile_place(index, width):
    per = width // LANES
    return index // per, slice(index % per * LANES, index % per * LANES + LANES)


class Tiles:
    def __init__(self, ref):
        self.ref, self.index = ref, 0

    def put(self, row):
        for at in range(0, row.shape[1], LANES):
            r, lanes = tile_place(self.index, self.ref.shape[1])
            self.ref[r : r + 1, lanes] = row[:, at : at + LANES]
            self.index += 1

    def take(self, width):
        found = []
        for _ in range(width // LANES):
            r, lanes = tile_place(self.index, self.ref.shape[1])
            found.append(self.ref[r : r + 1, lanes])
            self.index += 1
        return jnp.concatenate(found, axis=1)


def rear_kernel(names, scoped, heads, *refs):
    r = types.SimpleNamespace(**dict(zip(names, refs)))
    n, heads_n = lax.axis_size("seq"), lax.axis_size("head")
    place = lax.axis_index("seq")
    group = Group(heads_n)
    head = group.me
    ahead = n - 1 - place
    count, length, channels = r.gate_grad.shape
    rows = count * length
    both = channels + 2 * STATE
    lags = r.value_conv.shape[0]
    width = r.mate_in.shape[2]
    begin = (place * length).astype(f32)
    inner_total = NHEADS * HEADDIM
    ring_steps = n - 2
    own = D // n
    quarters = own % 64 == 0
    turns, out_steps, gate_steps = [], [], []
    if n == 8 and count == 4:
        turns = [(3, 0, 0), (4, 0, 1), (5, 0, 2), (7, 0, 3)]
        turns += [(6, 1, 0), (8, 1, 1), (9, 1, 2), (11, 1, 3)]
        turns += [(10, 2, 0), (12, 2, 1), (13, 2, 2), (14, 2, 3)]
        turns += [(13, 3, 0), (15, 3, 1), (16, 3, 2), (17, 3, 3)]
        out_steps = [(8, 0), (11, 1), (14, 2), (17, 3), (19, 4), (22, 5)]
        gate_steps = [(18, 0), (21, 1), (23, 2), (25, 3), (28, 4), (30, 5)]

    barrier = pltpu.get_barrier_semaphore()
    for k in range(1, heads_n):
        pl.semaphore_signal(
            barrier, inc=1, device_id=group.at(group.other(k)), device_id_type=MESH
        )
    for k in range(1, n):
        pl.semaphore_signal(
            barrier, inc=1, device_id=(lax.rem(place + k, n), head), device_id_type=MESH
        )

    normed_load = pltpu.make_async_copy(r.normed_hbm, r.normed, r.load_sem.at[0])
    marks = head_spread(channels)
    collect = head_gather(channels)
    step_bias = lane_row(r.step_bias)
    decay_rate = -jnp.exp(lane_row(r.rate_log))
    skip = spread_row(lane_row(r.skip), marks)
    r.gain_grad[...] = jnp.zeros_like(r.gain_grad)
    r.vector_grad[...] = jnp.zeros_like(r.vector_grad)
    r.conv_grad[...] = jnp.zeros_like(r.conv_grad)
    ring = Ring(r.ring_send, r.ring_recv)
    def matrix(part, slots, cut):
        first = len(ring.streams)
        if not quarters:
            ring.add(part, slots[:2])
            return (first,)
        ring.add(part, slots[:2], by_rows=True)
        if not cut:
            return (first,)
        ring.add(part, slots[2:], by_rows=True, first=own // 2)
        return first, first + 2

    out_halves = matrix(r.out_part, (r.os0, r.os1), False)
    gate_halves = matrix(r.gate_part, (r.gs0, r.gs1), False)

    def pass_on(first, step):
        @pl.when((step >= 0) & (step < ring_steps))
        def _():
            ring.pass_on(first, step)
            ring.pass_on(first + 1, step)

    def weights_turn(here, rounds=1):
        known = range(here, here + 2 * rounds, 2) if isinstance(here, int) else None
        for halves, table in ((out_halves, out_steps), (gate_halves, gate_steps)):
            if known is None or any(place in known for place, _ in table):
                step = step_at(table, here)
                for first in halves:
                    pass_on(first, step)

    def start(first):
        ring.start(first)
        ring.start(first + 1)

    def rest_of_ring(halves, done):
        if ring_steps > done:

            def further(s):
                for first in halves:
                    pass_on(first, done + s)

            loop(ring_steps - done, further)

    def total_of(i, halves, sums, targets):
        for k in [first + way for first in halves for way in range(2)]:
            _, _, (first, lines), columns, _ = ring.streams[k]
            sums[i, first : first + lines, columns] = ring.last(k)
        copy = pltpu.make_async_copy(sums.at[i], targets[i], r.total_sem.at[i])
        copy.start()
        return copy

    def as_wide(ref, b):
        return jnp.broadcast_to(long_row(ref, b, length), (LANES, length)).T

    def widened(column, size):
        return jnp.concatenate([column] * (size // LANES), axis=1)

    def weight_block(target, grads, block):
        sides = jnp.concatenate([r.normed[b, :, block] for b in range(count)], axis=0)
        whole = jnp.concatenate([grads(b) for b in range(count)], axis=0)
        target[block] = dot_tn(sides, whole).astype(target.dtype)

    def phase_one(*locals_one):
        q = types.SimpleNamespace(**dict(zip(scoped[0], locals_one)))
        loads = [
            pltpu.make_async_copy(r.out_weight_hbm, q.weight, r.load_sem.at[1]),
            pltpu.make_async_copy(r.pieces_hbm, q.pieces, r.load_sem.at[2]),
        ]
        for copy in loads:
            copy.start()
        row_arrays = [(r.gate_hbm, q.gate), (r.mixed_hbm, q.mixed), (r.conv_hbm, q.conv)]

        def row_load(i, b):
            source, target = row_arrays[i]
            return pltpu.make_async_copy(source.at[b], target.at[b], r.row_sem.at[i, b])

        def linear_load(b):
            slot = lax.rem(b, 2)
            return pltpu.make_async_copy(r.linear_hbm.at[b], q.linear.at[slot], r.line_load.at[slot])

        for b in range(count):
            for i in range(3):
                row_load(i, b).start()
        normed_load.start()
        linear_load(0).start()
        inner = q.gate
        normed_out = r.values_grad
        chain = PairChain(
            ahead,
            -1,
            q.local,
            q.passed,
            (r.state, q.offer, r.offered, r.hand, q.following),
            r.chain_send,
            r.chain_recv,
        )
        pairs = channels // LANES
        for copy in loads:
            copy.wait()
        pl.semaphore_wait(barrier, heads_n + n - 2)
        groups = q.pieces.shape[0]

        def gated_norm(b):
            for i in range(3):
                row_load(i, b).wait()
            scale = lax.rsqrt(as_wide(r.square, b) * (1.0 / inner_total) + norm_eps)
            pull = scale * scale * as_wide(r.rowdot, b) * (1.0 / inner_total)
            column, _ = position_masks(r.docs[pl.ds(b, 1)].astype(f32), begin)
            entering = spread(jnp.exp(r.cumulative[b]) * (column < begin).astype(f32), marks)
            q.passed[b] = entering[length - 8 :]
            here = pl.ds(pl.multiple_of(b * length, length), length)
            for at, size in blocks(channels):
                lanes = slice(at, at + size)
                grad_rows = jnp.zeros((length, size), f32)
                for j in range(groups):
                    block = (
                        q.weight[lanes, j * width : (j + 1) * width]
                        if len(q.weight.shape) == 2
                        else q.weight[j, lanes]
                    )
                    grad_rows = grad_rows + dot_nt(q.pieces[j, here], block)
                linear_gate = q.gate[b, :, lanes]
                sigmoid_value = jax.nn.sigmoid(linear_gate)
                active = linear_gate * sigmoid_value
                value = q.mixed[b, :, lanes]
                gated = value * active
                norm_gain = r.norm_gain[lanes][None, :]
                scaled = gated * widened(scale, size)
                normed_out[b, :, lanes] = (scaled * norm_gain).astype(bf16)
                r.gain_grad[:, lanes] += jnp.sum(grad_rows * scaled, axis=0, keepdims=True)
                gated_grad = widened(scale, size) * norm_gain * grad_rows - gated * widened(
                    pull, size
                )
                q.heads_grad[b, :, lanes] = gated_grad * active
                slope = sigmoid_value * (1.0 + linear_gate * (1.0 - sigmoid_value))
                r.gate_grad[b, :, lanes] = (gated_grad * value * slope).astype(bf16)
                values = q.conv[b, :, lanes]
                q.heads_in[b, :, lanes] = values * jax.nn.sigmoid(values)
            values = q.conv[b, :, channels : channels + STATE]
            q.keys[b] = (values * jax.nn.sigmoid(values)).astype(bf16)
            values = q.conv[b, :, channels + STATE :]
            q.queries[b] = (values * jax.nn.sigmoid(values)).astype(bf16)
            q.local[b] = dot_tn(q.queries[b], (q.heads_grad[b] * entering).astype(bf16))
            chain.offer(b)

        loop(count, gated_norm)
        chain.turn(3, turns)

        for j in range(groups):
            grads = jnp.concatenate([normed_out[b] for b in range(count)], axis=0)
            r.out_part[j * width : (j + 1) * width] = dot_tn(q.pieces[j], grads).astype(bf16)
            if j == groups // 2 - 1:
                chain.turn(4, turns)
        for first in out_halves:
            start(first)
        chain.turn(5, turns)
        normed_load.wait()

        first_half = lax.broadcasted_iota(jnp.int32, (length, LANES), 1) < HEADDIM

        def inside(b):
            docs_row = r.docs[pl.ds(b, 1)].astype(f32)
            u = begin + lax.broadcasted_iota(jnp.int32, (length, length), 0).astype(f32)
            t = begin + lax.broadcasted_iota(jnp.int32, (length, length), 1).astype(f32)
            q.mask_bias[...] = jnp.where((u >= docs_row) & (u <= t), 0.0, -1e30)
            q.scores[...] = dot_nt(q.keys[b], q.queries[b])
            q.scores_grad[...] = jnp.zeros_like(q.scores_grad)
            cumulative = r.cumulative[b]
            across = cumulative.T
            spread_steps = spread(r.steps[b], marks)
            for pair in range(pairs):
                lanes = slice(pair * LANES, (pair + 1) * LANES)
                scaled = q.heads_in[b, :, lanes] * spread_steps[:, lanes]
                grads = q.heads_grad[b, :, lanes]
                low_grads = grads.astype(bf16)
                value = jnp.zeros((length, LANES), f32)
                for half in range(2):
                    h = 2 * pair + half
                    mine = first_half if half == 0 else ~first_half
                    decay = jnp.exp(
                        across[h : h + 1] - cumulative[:, h : h + 1] + q.mask_bias[...]
                    )
                    mixing = (decay * q.scores[...]).astype(bf16)
                    value = value + jnp.dot(
                        mixing, jnp.where(mine, grads, 0.0).astype(bf16), preferred_element_type=f32
                    )
                    pairwise = dot_nt(jnp.where(mine, scaled, 0.0).astype(bf16), low_grads)
                    q.scores_grad[...] += decay * pairwise
                inner[b, :, lanes] = value
                if pair == (pairs - 1) // 2:
                    weights_turn(6 + 2 * b)
                    chain.turn(6 + 2 * b, turns)
            low = q.scores_grad[...].astype(bf16)
            q.narrow_grad[b, :, :STATE] = jnp.dot(low, q.queries[b], preferred_element_type=f32)
            column, _ = position_masks(docs_row, begin)
            entering = jnp.exp(cumulative) * (column < begin).astype(f32)
            x = q.heads_in[b]
            dy = q.heads_grad[b]
            q.narrow_grad[b, :, STATE:] = dot_tn(low, q.keys[b]) + dot_nt(
                (dy * spread(entering, marks)).astype(bf16), r.state_in[b]
            )
            dot_inner = gather_heads(x * inner[b], collect)
            dot_skip = gather_heads(dy * x, collect)
            q.dot_inner[b] = dot_inner
            q.cum_part[b] = (
                gather_heads(dy * (q.mixed[b] - skip * x), collect) - r.steps[b] * dot_inner
            )
            r.vector_grad[2:3] += jnp.sum(dot_skip, axis=0, keepdims=True)
            inner[b] = skip * dy + spread_steps * inner[b]
            weights_turn(7 + 2 * b)
            chain.turn(7 + 2 * b, turns)

        loop(count, inside)
        chain.rest(turns)

        def gate_block(i):
            block = pl.ds(pl.multiple_of(i * 256, 256), 256)
            weight_block(r.gate_part, lambda b: r.gate_grad[b], block)

        loop(D // 512, gate_block)
        weights_turn(14)
        chain.turn(14, turns)
        loop(D // 512, lambda i: gate_block(i + D // 512))
        for first in gate_halves:
            start(first)
        weights_turn(15)
        chain.turn(15, turns)
        q.around[...] = jnp.zeros_like(q.around)
        q.usable[...] = jnp.zeros_like(q.usable)
        upper = (
            lax.broadcasted_iota(jnp.int32, (length, length), 0)
            <= lax.broadcasted_iota(jnp.int32, (length, length), 1)
        ).astype(f32)
        last_row = lax.broadcasted_iota(jnp.int32, (length, LANES), 0) == length - 1

        def edge_copy(b):
            return remote(
                r.edge.at[b], r.edge_in.at[b], r.edge_send.at[b], r.edge_recv.at[b], (place - 1, head)
            )

        def close(b):
            @pl.when(b + 1 < count)
            def _():
                linear_load(b + 1).start()

            column, spot = position_masks(r.docs[pl.ds(b, 1)].astype(f32), begin)
            cumulative = r.cumulative[b]
            steps = r.steps[b]
            kept = (column < begin).astype(f32)
            trailing = (spot >= column[length - 1 :]).astype(f32)
            entering = jnp.exp(cumulative) * kept
            end_decay = jnp.exp(cumulative[length - 1 :] - cumulative) * trailing
            end_weight = end_decay * steps
            chain.ready(b)
            end_grad = r.state[b]
            x = q.heads_in[b]
            grown = jnp.dot(q.keys[b], end_grad, preferred_element_type=f32)
            spread_end = spread(end_weight, marks)
            q.narrow_grad[b, :, :STATE] += dot_nt((x * spread_end).astype(bf16), end_grad)
            grad = inner[b] + spread_end * grown
            dot_end = gather_heads(x * grown, collect)
            through = jnp.sum(
                end_grad.astype(f32) * r.state_in[b].astype(f32), axis=0, keepdims=True
            )
            passed_grad = gather_heads(jnp.broadcast_to(through, (8, channels)), collect)[:1]
            end_mix = dot_end * end_weight
            last_term = passed_grad * entering[length - 1 :] + jnp.sum(
                end_mix, axis=0, keepdims=True
            )
            cum_grad = q.cum_part[b] - end_mix + jnp.where(last_row, last_term, 0.0)
            rates_grad = jnp.dot(upper, cum_grad, precision=highest, preferred_element_type=f32)
            steps_grad = q.dot_inner[b] + end_decay * dot_end + rates_grad * decay_rate
            linear_grad = steps_grad * jax.nn.sigmoid(r.linear_steps[b] + step_bias)
            r.narrow[b, :, 2 * STATE :] = linear_grad.astype(bf16)
            r.vector_grad[0:1] += jnp.sum(linear_grad, axis=0, keepdims=True)
            r.vector_grad[1:2] += jnp.sum(rates_grad * steps, axis=0, keepdims=True) * decay_rate

            weights_turn(16 + 2 * b)
            chain.turn(16 + 2 * b, turns)
            linear_load(b).wait()
            halo_rows = pl.ds(pl.multiple_of(b * 16, 16), 16)
            line = lax.rem(b, 2)
            middle = slice(16, 16 + length)
            for lag in range(1, lags):
                q.usable[lag - 1, middle] = (spot - lag >= column).astype(f32)
            for at in range(0, both, LANES):
                lanes = slice(at, at + LANES)
                slot = at // LANES % 2
                q.extended[slot, 0:16] = r.halo[halo_rows, lanes].astype(f32)
                q.extended[slot, 16:] = q.linear[line, :, lanes].astype(f32)
                values = q.conv[b, :, lanes]
                sigmoid_value = jax.nn.sigmoid(values)
                slope = sigmoid_value * (1.0 + values * (1.0 - sigmoid_value))
                if at < channels:
                    out_grad = grad[:, lanes]
                    taps, tap = r.value_conv, lanes
                else:
                    place_at = at - channels
                    out_grad = q.narrow_grad[b, :, place_at : place_at + LANES]
                    taps, tap = r.keyquery_conv, slice(place_at, place_at + LANES)
                local = out_grad * slope
                q.around[slot, middle] = local
                input_grad = taps[0:1, tap] * local
                edges = jnp.zeros((8, LANES), f32)
                r.conv_grad[0:1, lanes] += jnp.sum(
                    local * q.extended[slot, middle], axis=0, keepdims=True
                )
                r.conv_grad[lags : lags + 1, lanes] += jnp.sum(local, axis=0, keepdims=True)
                for lag in range(1, lags):
                    mask = q.usable[lag - 1, middle]
                    r.conv_grad[lag : lag + 1, lanes] += jnp.sum(
                        local * mask * q.extended[slot, 16 - lag : 16 - lag + length],
                        axis=0,
                        keepdims=True,
                    )
                    later = slice(16 + lag, 16 + lag + length)
                    input_grad = input_grad + taps[lag : lag + 1, tap] * (
                        q.around[slot, later] * q.usable[lag - 1, later]
                    )
                    first = slice(8 + lag, 16 + lag)
                    edges = edges + taps[lag : lag + 1, tap] * (
                        q.around[slot, first] * q.usable[lag - 1, first]
                    )
                r.edge[b, :, lanes] = edges
                q.tails[b, :, lanes] = input_grad[length - 16 :]
                if at < channels:
                    r.values_grad[b, :, lanes] = input_grad.astype(bf16)
                else:
                    r.narrow[b, :, tap] = input_grad.astype(bf16)

            @pl.when(place > 0)
            def _():
                edge_copy(b).start()

            weights_turn(17 + 2 * b)
            chain.turn(17 + 2 * b, turns)

        loop(count, close)

        @pl.when(place < n - 1)
        def _():
            def join(b):
                edge_copy(b).wait_recv()
                last = slice(length - 16, length)
                q.tails[b, 8:] = q.tails[b, 8:] + r.edge_in[b]
                r.values_grad[b, last] = q.tails[b, :, :channels].astype(bf16)
                r.narrow[b, last, : 2 * STATE] = q.tails[b, :, channels:].astype(bf16)

            loop(count, join)

        @pl.when(place > 0)
        def _():
            loop(count, lambda b: edge_copy(b).wait_send())

        chain.finish()

    pl.run_scoped(phase_one, *scoped[1])

    def phase_two(*locals_two):
        q = types.SimpleNamespace(**dict(zip(scoped[2], locals_two)))
        token_columns = r.tokens_hbm
        if token_columns.shape[2] != width:
            first_column = pl.multiple_of(head * width, LANES)
            token_columns = token_columns.at[:, :, pl.ds(first_column, width)]
        loads = [
            pltpu.make_async_copy(source, target, r.load_two.at[i])
            for i, (source, target) in enumerate(
                [
                    (r.gate_weight_hbm, q.gate_weight),
                    (r.value_weight_hbm, q.value_weight),
                    (r.keyquery_weight_hbm, q.keyquery_weight),
                    (token_columns, q.tokens),
                    (r.output_hbm, q.output),
                    (r.teacher_hbm, q.teacher),
                ]
            )
        ]
        for copy in loads:
            copy.start()
        value_halves = matrix(q.value_part, (r.vs0, r.vs1, r.vs2, r.vs3), True)
        keyquery_first = len(ring.streams)
        ring.add(q.keyquery_half, (r.ks0, r.ks1), by_rows=True)

        def value_block(i):
            block = pl.ds(pl.multiple_of(i * 256, 256), 256)
            weight_block(q.value_part, lambda b: r.values_grad[b], block)

        loop(D // 512, value_block)
        weights_turn(24)
        loop(D // 512, lambda i: value_block(i + D // 512))
        for first in value_halves:
            start(first)
        weights_turn(25)

        def narrow_block(i):
            block = pl.ds(pl.multiple_of(i * 256, 256), 256)
            for half in range(2):
                lanes = slice(half * STATE, (half + 1) * STATE)
                weight_block(q.keyquery_part.at[half], lambda b: r.narrow[b, :, lanes], block)

        loop(D // 256, narrow_block)
        keyquery_mate = remote(
            q.keyquery_part.at[1 - group.core],
            r.keyquery_in,
            r.small_send.at[0],
            r.small_recv.at[0],
            group.at(group.mate),
        )
        keyquery_mate.start()
        weights_turn(26)
        targets = (r.out_total, r.gate_total, r.value_total)

        def end_ring(i, halves, done):
            rest_of_ring(halves, done)
            return total_of(i, halves, q.sums, targets)

        for copy in loads[:3]:
            copy.wait()
        q.columns[...] = jnp.zeros_like(q.columns)

        def own_columns(row):
            mine = jnp.zeros((1, width), f32)
            for j in range(heads_n):
                mine = mine + jnp.where(head == j, row[:, j * width : (j + 1) * width], 0.0)
            return mine

        gain = own_columns(r.gain[...][None, :])

        def row_block(c):
            return pl.ds(pl.multiple_of(c * length, length), length)

        start_mate, start_chip, total, finish = scatter_phases(
            group,
            row_block,
            q.part,
            r.mate_in,
            q.chip_out,
            r.chip_in,
            (r.mate_send, r.mate_recv, r.chip_send, r.chip_recv),
        )

        def value_turn(s):
            if s < ring_steps:
                for first in value_halves:
                    pass_on(first, s)

        def keyquery_turn(s):
            if s < ring_steps:
                pass_on(keyquery_first, s)

        def product(c):
            row_sum = jnp.zeros((length, LANES), f32)
            for j in range(heads_n):
                lanes = slice(j * width, (j + 1) * width)
                value = dot_nt(r.gate_grad[c], q.gate_weight[lanes])
                value = value + dot_nt(r.values_grad[c], q.value_weight[lanes])
                value = value + dot_nt(r.narrow[c, :, : 2 * STATE], q.keyquery_weight[lanes])
                value = value + jnp.dot(
                    r.narrow[c, :, 2 * STATE : 2 * STATE + heads],
                    r.step_weight[:, lanes],
                    preferred_element_type=f32,
                )
                q.part[j, row_block(c)] = value.astype(bf16)
                scaled = value * r.normed[c, :, lanes].astype(f32)
                q.columns[:, lanes] += jnp.sum(scaled, axis=0, keepdims=True)
                row_sum = row_sum + fold_lanes(scaled)
            r.dot_out[pl.ds(c, 1)] = jnp.sum(row_sum.T, axis=0, keepdims=True)
            start_mate(c)

            @pl.when(c > 0)
            def _():
                start_chip(c - 1)

        product(0)
        keyquery_mate.wait_recv()
        q.keyquery_half[...] = q.keyquery_part[group.core] + r.keyquery_in[...]
        start(keyquery_first)
        total_copies = [end_ring(0, out_halves, len(out_steps))]
        product(1)
        weights_turn(28)
        keyquery_turn(0)
        product(2)
        value_turn(0)
        keyquery_turn(1)
        product(3)
        start_chip(count - 1)
        keyquery_turn(2)
        weights_turn(30)
        share(group, r.dot_out, r.dots, r.rd_send, r.rd_recv)

        group_total = Doubling(
            "head", range(stages_of(heads_n)), r.group_sum, r.group_table, r.group_send, r.group_recv
        )
        line_total = Doubling(
            "seq", range(stages_of(n)), r.line_sum, r.line_table, r.line_send, r.line_recv
        )
        chip_total = Doubling(
            "head",
            range(1, stages_of(heads_n)),
            r.keyquery_sum,
            r.keyquery_table,
            r.kq_send,
            r.kq_recv,
        )
        tiles = Tiles(r.group_sum)
        r.group_sum[...] = jnp.zeros_like(r.group_sum)
        for lag in range(lags + 1):
            tiles.put(r.conv_grad[lag : lag + 1, channels:])
        tiles.put(q.columns[...])
        tiles.put(fold_lanes(r.loss_cols[...]))
        group_total.start(0)
        value_turn(1)
        keyquery_turn(3)

        for at, size in blocks(D):
            whole = jnp.concatenate([r.normed[b, :, at : at + size] for b in range(count)], axis=0)
            grads = jnp.concatenate([r.narrow[b, :, 2 * STATE :] for b in range(count)], axis=0)
            q.step_whole[:, at : at + size] = dot_tn(grads, whole)
        q.step_part[...] = jnp.zeros_like(q.step_part)
        for s in range(n):
            q.step_part[s, :, :own] = q.step_whole[:16, s * own : (s + 1) * own]

        def step_copy(k, index, sender):
            return remote(
                q.step_part.at[index],
                r.step_table.at[sender],
                r.step_send.at[k - 1],
                r.step_recv.at[sender],
                (index, head),
            )

        for k in range(1, n):
            step_copy(k, lax.rem(place + k, n), place).start()
        total_copies.append(end_ring(1, gate_halves, len(gate_steps)))
        value_turn(2)
        keyquery_turn(4)
        group_total.run(0, 1)
        shared(group, r.dot_out, r.dots, r.rd_send, r.rd_recv)
        r.dots[head] = r.dot_out[...]
        for copy in loads[3:]:
            copy.wait()

        def fill_line():
            tiles, summed = Tiles(r.line_sum), Tiles(r.group_sum)
            r.line_sum[...] = jnp.zeros_like(r.line_sum)
            for lag in range(lags + 1):
                tiles.put(r.conv_grad[lag : lag + 1, :channels])
                tiles.put(summed.take(2 * STATE))
            tiles.put(r.gain_grad[...])
            for i in range(3):
                tiles.put(r.vector_grad[i : i + 1])
            tiles.put(summed.take(D))
            tiles.put(summed.take(LANES))

        def grad_store(c):
            return pltpu.make_async_copy(q.tokens_grad.at[c], r.tokens_grad.at[c], r.grad_sem.at[c])

        def rest(c):
            row_sum = r.dots[0, c : c + 1]
            for j in range(1, heads_n):
                row_sum = row_sum + r.dots[j, c : c + 1]
            inverse = r.inverse[c : c + 1]
            out_grad = (q.output[row_block(c)] - q.teacher[c]) * as_column(
                long_row(r.mask, c, length), width
            )
            q.tokens_grad[c] = (
                out_grad
                + as_column(inverse, width) * gain * total(c)
                - q.tokens[c] * as_column(inverse * inverse * row_sum * (1.0 / D), width)
            )
            grad_store(c).start()

        rest(0)
        rest(1)
        value_turn(3)
        keyquery_turn(5)
        group_total.run(1)
        fill_line()
        line_total.start(0)
        rest(2)
        if ring_steps > 6:
            loop(ring_steps - 6, lambda s: pass_on(keyquery_first, s + 6))
        value_turn(4)
        line_total.run(0, 1)
        for c in range(3, count):
            rest(c)
        for k in (keyquery_first, keyquery_first + 1):
            _, _, (first, lines), _, _ = ring.streams[k]
            r.keyquery_sum[first : first + lines] = ring.last(k)
        chip_total.start(0)
        value_turn(5)
        line_total.run(1, 2)
        chip_total.run(0)
        keyquery_swap = remote(
            r.keyquery_sum,
            r.keyquery_other,
            r.small_send.at[1],
            r.small_recv.at[1],
            group.at(group.mate),
        )
        keyquery_swap.start()
        if ring_steps > 6:

            def remaining(s):
                for first in value_halves:
                    pass_on(first, s + 6)

            loop(ring_steps - 6, remaining)
        total_copies.append(total_of(2, value_halves, q.sums, targets))
        for k in range(1, n):
            sender = lax.rem(place + k, n)
            copy = step_copy(k, sender, sender)
            copy.wait_send()
            copy.wait_recv()
        r.step_table[place] = q.step_part[place]
        step_sum = r.step_table[0]
        for s in range(1, n):
            step_sum = step_sum + r.step_table[s]
        r.step_total[...] = step_sum[:heads, :own]
        line_total.run(2)

        tiles = Tiles(r.line_sum)
        for lag in range(lags + 1):
            own_row, shared_row = tiles.take(channels), tiles.take(2 * STATE)
            if lag < lags:
                r.value_conv_total[lag : lag + 1] = own_row
                r.keyquery_conv_total[lag : lag + 1] = shared_row
            else:
                r.value_offset_total[...] = own_row[0]
                r.keyquery_offset_total[...] = shared_row[0]
        r.norm_gain_total[...] = tiles.take(channels)[0]
        for target in (r.step_bias_total, r.rate_log_total, r.skip_total):
            target[...] = tiles.take(LANES)[0, :heads]
        r.input_gain_total[...] = (own_columns(tiles.take(D)) / gain)[0]
        r.loss_total[...] = 0.5 * jnp.sum(tiles.take(LANES), axis=1, keepdims=True)[0]

        loop(count, finish)
        for c in range(count):
            grad_store(c).wait()
        for copy in total_copies:
            copy.wait()
        keyquery_mate.wait_send()
        keyquery_swap.wait()
        mine, other = r.keyquery_sum[...], r.keyquery_other[...]
        r.keyquery_total[:, :STATE] = jnp.where(group.core == 0, mine, other)
        r.keyquery_total[:, STATE:] = jnp.where(group.core == 0, other, mine)
        for i in range(len(ring.streams)):
            ring.finish(i)

    pl.run_scoped(phase_two, *scoped[3])


def rear(inputs, lags, cid):
    heads_n, n = lax.axis_size("head"), lax.axis_size("seq")
    count, length, channels = inputs["gate_hbm"].shape
    pieces = inputs["pieces_hbm"]
    rows, width = pieces.shape[1:]
    heads = channels // HEADDIM
    both = channels + 2 * STATE
    own = D // n
    step_lanes = -(-own // LANES) * LANES
    chips = heads_n // 2
    vmem, dma = pltpu.VMEM, pltpu.SemaphoreType.DMA
    hbm = pl.BlockSpec(memory_space=pl.ANY)
    group_tiles = (lags + 1) * 2 * STATE // LANES + D // LANES + 1
    line_tiles = (lags + 1) * both // LANES + channels // LANES + 3 + D // LANES + 1
    group_shape = (-(-group_tiles * LANES // (8 * 512)) * 8, 512)
    line_shape = (-(-line_tiles * LANES // (8 * both)) * 8, both)
    head_stages, line_stages = stages_of(heads_n), stages_of(n)
    outs = {
        "tokens_grad": (count, length, width),
        "out_total": (own, channels),
        "gate_total": (own, channels),
        "value_total": (own, channels),
        "keyquery_total": (own, 2 * STATE),
        "step_total": (heads, own),
        "value_conv_total": (lags, channels),
        "value_offset_total": (channels,),
        "keyquery_conv_total": (lags, 2 * STATE),
        "keyquery_offset_total": (2 * STATE,),
        "step_bias_total": (heads,),
        "rate_log_total": (heads,),
        "skip_total": (heads,),
        "norm_gain_total": (channels,),
        "input_gain_total": (width,),
        "loss_total": (1,),
    }
    if own % 64 == 0:
        wide_slots = [vmem((n - 1, own // 2, channels), bf16)] * 2
        slots = [vmem((n - 1, own // 4, channels), bf16)] * 4
    else:
        wide_slots = ring_slots(n, own, channels, bf16)
        slots = wide_slots + [vmem((16, LANES), bf16)] * 2
    chained = chain_buffers(count, channels)
    scratch = {
        "normed": vmem((count, length, D), bf16),
        "gate_grad": vmem((count, length, channels), bf16),
        "values_grad": vmem((count, length, channels), bf16),
        "narrow": vmem((count, length, 2 * STATE + LANES), bf16),
        "out_part": vmem((D, channels), bf16),
        "gate_part": vmem((D, channels), bf16),
        "os0": wide_slots[0],
        "os1": wide_slots[1],
        "gs0": wide_slots[0],
        "gs1": wide_slots[1],
        "vs0": slots[0],
        "vs1": slots[1],
        "vs2": slots[2],
        "vs3": slots[3],
        "ks0": vmem((n - 1, own // 2, STATE), f32),
        "ks1": vmem((n - 1, own // 2, STATE), f32),
        "state": chained[0],
        "offered": chained[2],
        "hand": chained[3],
        "edge": vmem((count, 8, both), f32),
        "edge_in": vmem((count, 8, both), f32),
        "gain_grad": vmem((1, channels), f32),
        "vector_grad": vmem((8, LANES), f32),
        "conv_grad": vmem((8, both), f32),
        "mate_in": vmem((chips, rows, width), bf16),
        "chip_in": vmem((chips - 1, rows, width), bf16),
        "dots": vmem((heads_n, count, length), f32),
        "dot_out": vmem((count, length), f32),
        "keyquery_in": vmem((D, STATE), f32),
        "keyquery_sum": vmem((own, STATE), f32),
        "keyquery_other": vmem((own, STATE), f32),
        "keyquery_table": vmem((head_stages - 1, own, STATE), f32),
        "step_table": vmem((n, 16, step_lanes), f32),
        "group_sum": vmem(group_shape, f32),
        "group_table": vmem((head_stages,) + group_shape, f32),
        "line_sum": vmem(line_shape, f32),
        "line_table": vmem((line_stages,) + line_shape, f32),
        "load_sem": dma((3,)),
        "row_sem": dma((3, count)),
        "line_load": dma((2,)),
        "load_two": dma((6,)),
        "grad_sem": dma((count,)),
        "total_sem": dma((3,)),
        "edge_send": dma((count,)),
        "edge_recv": dma((count,)),
        "chain_send": dma((3, count)),
        "chain_recv": dma((3, count)),
        "ring_send": dma((10,)),
        "ring_recv": dma((10, n - 1)),
        "mate_send": dma((chips, count)),
        "mate_recv": dma((chips, count)),
        "chip_send": dma((chips - 1, count)),
        "chip_recv": dma((chips - 1, count)),
        "rd_send": dma((heads_n - 1,)),
        "rd_recv": dma((heads_n,)),
        "small_send": dma((2,)),
        "small_recv": dma((2,)),
        "kq_send": dma((head_stages - 1,)),
        "kq_recv": dma((head_stages - 1,)),
        "group_send": dma((head_stages,)),
        "group_recv": dma((head_stages,)),
        "line_send": dma((line_stages,)),
        "line_recv": dma((line_stages,)),
        "step_send": dma((n - 1,)),
        "step_recv": dma((n,)),
    }
    first = {
        "weight": vmem(inputs["out_weight_hbm"].shape, bf16),
        "pieces": vmem(pieces.shape, bf16),
        "gate": vmem((count, length, channels), f32),
        "mixed": vmem((count, length, channels), f32),
        "conv": vmem((count, length, both), f32),
        "linear": vmem((2, length, both), bf16),
        "heads_in": vmem((count, length, channels), f32),
        "heads_grad": vmem((count, length, channels), f32),
        "keys": vmem((count, length, STATE), bf16),
        "queries": vmem((count, length, STATE), bf16),
        "scores": vmem((length, length), f32),
        "scores_grad": vmem((length, length), f32),
        "mask_bias": vmem((length, length), f32),
        "narrow_grad": vmem((count, length, 2 * STATE), f32),
        "local": vmem((count, STATE, channels), f32),
        "passed": vmem((count, 8, channels), f32),
        "offer": chained[1],
        "following": chained[4],
        "extended": vmem((2, length + 16, LANES), f32),
        "around": vmem((2, length + 32, LANES), f32),
        "usable": vmem((lags - 1, length + 32, LANES), f32),
        "tails": vmem((count, 16, both), f32),
        "dot_inner": vmem((count, length, LANES), f32),
        "cum_part": vmem((count, length, LANES), f32),
    }
    second = {
        "gate_weight": vmem((D, channels), bf16),
        "value_weight": vmem((D, channels), bf16),
        "keyquery_weight": vmem((D, 2 * STATE), bf16),
        "tokens": vmem((count, length, width), f32),
        "output": vmem((rows, width), f32),
        "teacher": vmem((count, length, width), f32),
        "tokens_grad": vmem((count, length, width), f32),
        "value_part": vmem((D, channels), bf16),
        "keyquery_part": vmem((2, D, STATE), f32),
        "keyquery_half": vmem((D, STATE), f32),
        "part": vmem((heads_n, rows, width), bf16),
        "chip_out": vmem((chips - 1, rows, width), bf16),
        "columns": vmem((1, D), f32),
        "step_whole": vmem((LANES, D), f32),
        "step_part": vmem((n, 16, step_lanes), f32),
        "sums": vmem((3, own, channels), f32),
    }
    names = list(inputs) + list(outs) + list(scratch)
    scoped = (list(first), list(first.values()), list(second), list(second.values()))
    in_hbm = [name.endswith("_hbm") for name in inputs]
    found = pl.pallas_call(
        functools.partial(rear_kernel, names, scoped, heads),
        out_shape=[jax.ShapeDtypeStruct(s, f32) for s in outs.values()],
        in_specs=[hbm if there else in_vmem for there in in_hbm],
        out_specs=[hbm] * 4 + [in_vmem] * (len(outs) - 4),
        scratch_shapes=list(scratch.values()),
        compiler_params=params(cid),
        name="rear",
    )(*inputs.values())
    return dict(zip(outs, found))


def deliver_kernel(count, *refs):
    sources, targets, held = refs[:count], refs[count : 2 * count], refs[2 * count : 3 * count]
    sem = refs[3 * count]
    loads = [pltpu.make_async_copy(a, b, sem.at[0, i]) for i, (a, b) in enumerate(zip(sources, held))]
    stores = [pltpu.make_async_copy(a, b, sem.at[1, i]) for i, (a, b) in enumerate(zip(held, targets))]
    for copy in loads:
        copy.start()
    for load, store in zip(loads, stores):
        load.wait()
        store.start()
    for copy in stores:
        copy.wait()


def deliver(arrays):
    hbm = pl.BlockSpec(memory_space=pl.ANY)
    count = len(arrays)
    return pl.pallas_call(
        functools.partial(deliver_kernel, count),
        out_shape=[jax.ShapeDtypeStruct(a.shape, a.dtype) for a in arrays],
        in_specs=[hbm] * count,
        out_specs=[hbm] * count,
        scratch_shapes=[pltpu.VMEM(a.shape, a.dtype) for a in arrays]
        + [pltpu.SemaphoreType.DMA((2, count))],
        compiler_params=pltpu.CompilerParams(vmem_limit_bytes=VMEM_LIMIT),
        name="deliver",
    )(*arrays)


def body(
    tokens,
    teacher,
    document_start,
    valid_mask,
    input_gain,
    gate_weight,
    value_weight,
    keyquery_weight,
    step_weight,
    value_conv_weight,
    value_conv_bias,
    keyquery_conv_weight,
    keyquery_conv_bias,
    step_bias,
    rate_log,
    skip_gain,
    norm_gain,
    out_weight,
):
    count, length, _ = tokens.shape
    channels = gate_weight.shape[1]
    width = teacher.shape[2]
    rows = count * length
    lags = value_conv_weight.shape[0]
    vectors = (step_bias, rate_log, skip_gain)
    (
        normed,
        linear,
        conv_linear,
        gate_linear,
        mixed,
        output,
        pieces,
        halo,
        state_in,
        steps,
        cumulative,
        steps_linear,
        square_rows,
        inverse_rows,
        mask_rows,
        rowdot,
        square_total,
        loss_cols,
    ) = front(
        tokens,
        input_gain,
        value_weight,
        keyquery_weight,
        step_weight.T,
        gate_weight,
        document_start,
        vectors,
        (value_conv_weight, value_conv_bias, keyquery_conv_weight, keyquery_conv_bias),
        norm_gain,
        valid_mask,
        out_weight,
        teacher,
        1,
    )
    token_cols = tokens
    if width % LANES:
        token_cols = lax.dynamic_slice_in_dim(tokens, lax.axis_index("head") * width, width, 2)
    totals = rear(
        {
            "pieces_hbm": pieces,
            "out_weight_hbm": blocked(out_weight, pieces.shape[0]),
            "gate_hbm": gate_linear,
            "mixed_hbm": mixed,
            "conv_hbm": conv_linear,
            "linear_hbm": linear,
            "normed_hbm": normed,
            "gate_weight_hbm": gate_weight,
            "value_weight_hbm": value_weight,
            "keyquery_weight_hbm": keyquery_weight,
            "tokens_hbm": token_cols,
            "output_hbm": output,
            "teacher_hbm": teacher,
            "step_weight": step_weight.T,
            "halo": halo,
            "state_in": state_in,
            "steps": steps,
            "cumulative": cumulative,
            "linear_steps": steps_linear,
            "square": square_total,
            "rowdot": rowdot,
            "docs": document_start,
            "step_bias": step_bias,
            "rate_log": rate_log,
            "skip": skip_gain,
            "value_conv": value_conv_weight,
            "keyquery_conv": keyquery_conv_weight,
            "norm_gain": norm_gain,
            "gain": input_gain,
            "mask": mask_rows,
            "inverse": inverse_rows,
            "loss_cols": loss_cols,
        },
        lags,
        3,
    )
    results = deliver(
        (
            output.reshape(count, length, width),
            totals["loss_total"],
            totals["tokens_grad"],
            totals["input_gain_total"],
            totals["gate_total"],
            totals["value_total"],
            totals["keyquery_total"],
            totals["step_total"],
            totals["value_conv_total"],
            totals["value_offset_total"],
            totals["keyquery_conv_total"],
            totals["keyquery_offset_total"],
            totals["step_bias_total"],
            totals["rate_log_total"],
            totals["skip_total"],
            totals["norm_gain_total"],
            totals["out_total"],
        )
    )
    return (
        results[0],
        results[1].reshape(()),
        *results[2:7],
        results[7].T,
        *results[8:16],
        results[16].T,
    )


def solution(mesh):
    placed = (
        P(None, "seq", None),
        P(None, "seq", "head"),
        P(None, "seq"),
        P(),
        P(),
        P(None, "head"),
        P(None, "head"),
        P(),
        P(None, "head"),
        P(None, "head"),
        P("head"),
        P(),
        P(),
        P("head"),
        P("head"),
        P("head"),
        P("head"),
        P("head", None),
    )
    return jax.shard_map(
        body,
        mesh=mesh,
        in_specs=placed,
        out_specs=(
            P(None, "seq", "head"),
            P(),
            P(None, "seq", "head"),
            P("head"),
            P("seq", "head"),
            P("seq", "head"),
            P("seq", None),
            P("seq", "head"),
            P(None, "head"),
            P("head"),
            P(),
            P(),
            P("head"),
            P("head"),
            P("head"),
            P("head"),
            P("head", "seq"),
        ),
        check_vma=False,
    )
```

```python
import functools
import types

import jax
import jax.numpy as jnp
from jax import lax
from jax.experimental import pallas as pl
from jax.experimental.pallas import tpu as pltpu
from jax.sharding import PartitionSpec as P

D = 1536
NHEADS = 48
HEADDIM = 64
STATE = 128
LANES = 128
VMEM_LIMIT = 62 << 20

norm_eps = 1e-05
highest = lax.Precision.HIGHEST
MESH = pl.DeviceIdType.MESH
f32 = jnp.float32
bf16 = jnp.bfloat16
NT = (((1,), (1,)), ((), ()))
TN = (((0,), (0,)), ((), ()))

in_vmem = pl.BlockSpec(memory_space=pltpu.VMEM)
in_smem = pl.BlockSpec(memory_space=pltpu.SMEM)


def params(cid):
    return pltpu.CompilerParams(
        collective_id=cid, has_side_effects=True, vmem_limit_bytes=VMEM_LIMIT
    )


def remote(src, dst, send, recv, target):
    return pltpu.make_async_remote_copy(
        src_ref=src,
        dst_ref=dst,
        send_sem=send,
        recv_sem=recv,
        device_id=target,
        device_id_type=MESH,
    )


def loop(count, fn):
    lax.fori_loop(0, count, lambda i, c: (fn(i), c)[1], 0)


def dot_nt(a, b, precision=None):
    return lax.dot_general(a, b, NT, precision=precision, preferred_element_type=f32)


def dot_tn(a, b, precision=None):
    return lax.dot_general(a, b, TN, precision=precision, preferred_element_type=f32)


def is_true(condition):
    return condition.astype(jnp.int32)


def ring_place(n, index):
    odd, half = lax.rem(index, 2), lax.div(index, 2)
    return half * (1 - odd) + (n - 1 - half) * odd


def ring_index(n, spot):
    late = is_true(2 * spot >= n)
    return 2 * spot + late * (2 * n - 1 - 4 * spot)


def wrapped(n, spot):
    return spot + n * is_true(spot < 0) - n * is_true(spot >= n)


class Ring:
    def __init__(self, send_sem, recv_sem):
        self.n = lax.axis_size("seq")
        self.streams, self.send_sem, self.recv_sem = [], send_sem, recv_sem
        head = lax.axis_index("head")
        self.spot = ring_place(self.n, lax.axis_index("seq"))
        self.after = (ring_index(self.n, wrapped(self.n, self.spot + 1)), head)
        self.before = (ring_index(self.n, wrapped(self.n, self.spot - 1)), head)

    def add(self, part, slots, by_rows=False, first=0):
        rows, width = part.shape[0] // self.n, part.shape[1]
        cut = slots[0].shape[1] if by_rows else slots[0].shape[2]
        if by_rows:
            halves = tuple(((first + way * cut, cut), (0, width)) for way in range(2))
        else:
            halves = (((0, rows), (0, cut)), ((0, rows), (cut, width - cut)))
        for way in range(2):
            lines, columns = halves[way]
            self.streams.append((part, slots[way], lines, pl.ds(*columns), way))

    def piece(self, i, step):
        part, _, (first, count), columns, way = self.streams[i]
        shift = -1 - step if way == 0 else 1 + step
        rows = part.shape[0] // self.n
        index = ring_index(self.n, wrapped(self.n, self.spot + shift))
        tile = 16 if part.dtype == bf16 else 8
        return part.at[pl.ds(pl.multiple_of(index * rows + first, tile), count), columns]

    def copy(self, i, step, source):
        slots, way = self.streams[i][1], self.streams[i][4]
        return remote(
            source,
            slots.at[step],
            self.send_sem.at[i],
            self.recv_sem.at[i, step],
            self.after if way == 0 else self.before,
        )

    def start(self, i):
        self.copy(i, 0, self.piece(i, 0)).start()

    def pass_on(self, i, step):
        slots = self.streams[i][1]
        self.copy(i, step, slots.at[step]).wait_recv()
        total = slots[step].astype(f32) + self.piece(i, step + 1)[...].astype(f32)
        slots[step] = total.astype(slots.dtype)
        self.copy(i, step + 1, slots.at[step]).start()

    def last(self, i):
        slots, step = self.streams[i][1], self.n - 2
        self.copy(i, step, slots.at[step]).wait_recv()
        return slots[step].astype(f32) + self.piece(i, step + 1)[...].astype(f32)

    def finish(self, i):
        slots, way = self.streams[i][1], self.streams[i][4]
        remote(
            slots,
            slots,
            self.send_sem.at[i],
            self.recv_sem.at[i, 0],
            self.after if way == 0 else self.before,
        ).wait_send()


def ring_slots(n, rows, width, kind):
    cut = width // LANES // 2 * LANES
    return [pltpu.VMEM((n - 1, rows, cut), kind), pltpu.VMEM((n - 1, rows, width - cut), kind)]


def step_at(table, here):
    found, here = jnp.int32(-1), jnp.asarray(here, jnp.int32)
    for place, step in table:
        found = found + (step + 1) * (here == place).astype(jnp.int32)
    return found


def sequence_at(table, here, pair):
    found, here = jnp.int32(-1), jnp.asarray(here, jnp.int32)
    for place, owner, b in table:
        found = found + (b + 1) * ((here == place) & (pair == owner)).astype(jnp.int32)
    return found


class PairChain:
    def __init__(self, ahead, by, local, passed, buffers, send_sem, recv_sem):
        self.n = lax.axis_size("seq")
        self.place, self.head = lax.axis_index("seq"), lax.axis_index("head")
        self.by, self.pair, self.second = by, lax.div(ahead, 2), lax.rem(ahead, 2)
        self.local, self.passed = local, passed
        self.state, self.offers, self.offered, self.hand, self.following = buffers
        self.send_sem, self.recv_sem = send_sem, recv_sem
        self.count, _, channels = self.state.shape
        cut = channels // LANES // 2 * LANES
        self.sizes = (channels - cut, cut)
        self.lanes = (pl.ds(cut, channels - cut), pl.ds(0, cut))

    def copy(self, kind, b, source, target, ahead):
        return remote(
            source,
            target,
            self.send_sem.at[kind, b],
            self.recv_sem.at[kind, b],
            (self.place + self.by * ahead, self.head),
        )

    def within(self, buffer, b, second):
        return buffer.at[b, pl.ds(0, buffer.shape[1]), pl.ds(0, self.sizes[second])]

    def offering(self, b, second):
        other = 1 - second
        return self.copy(
            0,
            b,
            self.within(self.offers, b, other),
            self.within(self.offered, b, other),
            1 - 2 * second,
        )

    def handing(self, b, second):
        target = self.state.at[b, pl.ds(0, STATE), self.lanes[second]]
        return self.copy(1, b, self.within(self.hand, b, second), target, 1 - 2 * second)

    def passing(self, b, second):
        if second:
            target = self.within(self.hand, b, second)
        else:
            target = self.state.at[b, pl.ds(0, STATE), self.lanes[second]]
        return self.copy(2, b, self.within(self.following, b, second), target, 2)

    def offer(self, b):
        for second in range(2):

            @pl.when(self.second == second)
            def _():
                other = 1 - second
                lanes, size = self.lanes[other], self.sizes[other]
                self.offers[b, :STATE, :size] = self.local[b, :, lanes].astype(bf16)
                decay = self.passed[b, 7:8, lanes]
                high = decay.astype(bf16).astype(f32)
                row = lax.broadcasted_iota(jnp.int32, (16, size), 0)
                rows = jnp.where(row == 0, high, jnp.where(row == 1, decay - high, 0.0))
                self.offers[b, STATE:, :size] = rows.astype(bf16)
                self.offering(b, second).start()

    def pass_on(self, b):
        more = self.pair < self.n // 2 - 1
        for second in range(2):

            @pl.when(self.second == second)
            def _():
                lanes, size = self.lanes[second], self.sizes[second]
                self.offering(b, 1 - second).wait_recv()

                @pl.when(self.pair > 0)
                def _():
                    self.passing(b, second).wait_recv()

                @pl.when(self.pair == 0)
                def _():
                    zeros = jnp.zeros((STATE, size), bf16)
                    if second:
                        self.hand[b, :, :size] = zeros
                    else:
                        self.state[b, :, lanes] = zeros

                own_decay, own = self.passed[b, 7:8, lanes], self.local[b, :, lanes]
                decay = self.offered[b, STATE:, :size].astype(f32)
                decay = decay[0:1] + decay[1:2]
                offered = self.offered[b, :STATE, :size].astype(f32)
                if second:
                    self.handing(b, second).start()
                    value = decay * self.hand[b, :, :size].astype(f32) + offered
                    self.state[b, :, lanes] = value.astype(bf16)
                    following = own_decay * value + own
                else:
                    value = own_decay * self.state[b, :, lanes].astype(f32) + own
                    self.hand[b, :, :size] = value.astype(bf16)
                    self.handing(b, second).start()
                    following = decay * value + offered

                @pl.when(more)
                def _():
                    self.following[b, :, :size] = following.astype(bf16)
                    self.passing(b, second).start()

    def ready(self, b):
        for second in range(2):

            @pl.when(self.second == second)
            def _():
                self.handing(b, 1 - second).wait_recv()

    def turn(self, here, table):
        b = sequence_at(table, here, self.pair)

        @pl.when(b >= 0)
        def _():
            self.pass_on(b)

    def rest(self, table):
        held = {(pair, b) for _, pair, b in table}
        for pair in range(self.n // 2):
            for b in range(self.count):
                if (pair, b) not in held:

                    @pl.when(self.pair == pair)
                    def _():
                        self.pass_on(b)

    def finish(self):
        for second in range(2):

            @pl.when(self.second == second)
            def _():
                def one(b):
                    self.offering(b, second).wait_send()
                    self.handing(b, second).wait_send()

                    @pl.when(self.pair < self.n // 2 - 1)
                    def _():
                        self.passing(b, second).wait_send()

                loop(self.count, one)


def chain_buffers(count, channels):
    wide = channels - channels // LANES // 2 * LANES
    shapes = [(STATE, channels), (STATE + 16, wide), (STATE + 16, wide), (STATE, wide), (STATE, wide)]
    return [pltpu.VMEM((count,) + s, bf16) for s in shapes]


class Group:
    def __init__(self, n):
        self.n = n
        self.chips = n // 2
        self.seq = lax.axis_index("seq")
        self.me = lax.axis_index("head")
        self.chip = lax.div(self.me, 2)
        self.core = lax.rem(self.me, 2)
        self.mate = self.me + 1 - 2 * self.core

    def at(self, head):
        return (self.seq, head)

    def chip_after(self, k):
        return lax.rem(self.chip + k, self.chips)

    def chip_before(self, k):
        return lax.rem(self.chip + self.chips - k, self.chips)

    def peer(self, k):
        return 2 * self.chip_after(k) + self.core

    def other(self, k):
        return lax.rem(self.me + k, self.n)

    def greet(self):
        barrier = pltpu.get_barrier_semaphore()
        for k in range(1, self.n):
            pl.semaphore_signal(
                barrier, inc=1, device_id=self.at(self.other(k)), device_id_type=MESH
            )
        pl.semaphore_wait(barrier, self.n - 1)


def share(group, source, table, send_sem, recv_sem):
    for k in range(1, group.n):
        remote(
            source,
            table.at[group.me],
            send_sem.at[k - 1],
            recv_sem.at[group.me],
            group.at(group.other(k)),
        ).start()


def shared(group, source, table, send_sem, recv_sem):
    for k in range(1, group.n):
        sender = group.other(k)
        copy = remote(
            source, table.at[sender], send_sem.at[k - 1], recv_sem.at[sender], group.at(sender)
        )
        copy.wait_send()
        copy.wait_recv()


def as_column(row, width):
    tile = jnp.broadcast_to(row, (LANES, row.shape[1])).T
    return jnp.concatenate([tile] * (-(-width // LANES)), axis=1)[:, :width]


def scatter_phases(group, row_block, part, mate_in, chip_out, chip_in, sems):
    mate_send, mate_recv, chip_send, chip_recv = sems

    def mate_copy(c, x):
        return remote(
            part.at[2 * x + 1 - group.core, row_block(c)],
            mate_in.at[x, row_block(c)],
            mate_send.at[x, c],
            mate_recv.at[x, c],
            group.at(group.mate),
        )

    def chip_copy(c, k):
        return remote(
            chip_out.at[k - 1, row_block(c)],
            chip_in.at[k - 1, row_block(c)],
            chip_send.at[k - 1, c],
            chip_recv.at[k - 1, c],
            group.at(group.peer(k)),
        )

    def start_mate(c):
        for x in range(group.chips):
            mate_copy(c, x).start()

    def start_chip(c):
        for x in range(group.chips):
            mate_copy(c, x).wait_recv()
        for k in range(1, group.chips):
            x = group.chip_after(k)
            both = part[2 * x + group.core, row_block(c)].astype(f32) + mate_in[
                x, row_block(c)
            ].astype(f32)
            chip_out[k - 1, row_block(c)] = both.astype(bf16)
            chip_copy(c, k).start()

    def total(c):
        value = part[group.me, row_block(c)].astype(f32) + mate_in[
            group.chip, row_block(c)
        ].astype(f32)
        for k in range(1, group.chips):
            chip_copy(c, k).wait_recv()
            value = value + chip_in[k - 1, row_block(c)].astype(f32)
        return value

    def finish(c):
        for x in range(group.chips):
            mate_copy(c, x).wait_send()
        for k in range(1, group.chips):
            chip_copy(c, k).wait_send()

    return start_mate, start_chip, total, finish


def scatter_scratch(n, rows, width, chunks):
    chips = n // 2
    dma = pltpu.SemaphoreType.DMA
    return [
        pltpu.VMEM((n, rows, width), bf16),
        pltpu.VMEM((chips, rows, width), bf16),
        pltpu.VMEM((chips - 1, rows, width), bf16),
        pltpu.VMEM((chips - 1, rows, width), bf16),
    ], [dma((chips, chunks)), dma((chips, chunks)), dma((chips - 1, chunks)), dma((chips - 1, chunks))]


def blocked(weight, n):
    width = weight.shape[1] // n
    if width % LANES == 0:
        return weight
    return jnp.moveaxis(weight.reshape(weight.shape[0], n, width), 1, 0)


def blocks(width, size=256):
    return [(at, min(size, width - at)) for at in range(0, width, size)]


def fold_lanes(values):
    rows, width = values.shape
    if width % LANES:
        fill = jnp.zeros((rows, LANES - width % LANES), values.dtype)
        values = jnp.concatenate([values, fill], axis=1)
    total = values[:, :LANES]
    for at in range(LANES, width, LANES):
        total = total + values[:, at : at + LANES]
    return total


def rows_of(values):
    return jnp.sum(fold_lanes(values).T, axis=0, keepdims=True)


def head_spread(channels):
    row = lax.broadcasted_iota(jnp.int32, (LANES, channels), 0)
    head = lax.broadcasted_iota(jnp.int32, (LANES, channels), 1) // HEADDIM
    return ((row % 16 == head) & (row < 48)).astype(f32).astype(bf16)


def head_gather(channels):
    head = lax.broadcasted_iota(jnp.int32, (channels, LANES), 0) // HEADDIM
    return (lax.broadcasted_iota(jnp.int32, (channels, LANES), 1) == head).astype(f32).astype(bf16)


def spread(values, marks):
    lane = lax.broadcasted_iota(jnp.int32, values.shape, 1)
    values = jnp.where(lane < 16, values, 0.0)
    high = values.astype(bf16).astype(f32)
    left = values - high
    middle = left.astype(bf16).astype(f32)
    low = (left - middle).astype(bf16).astype(f32)
    three = high + pltpu.roll(middle, 16, 1) + pltpu.roll(low, 32, 1)
    return jnp.dot(three.astype(bf16), marks, preferred_element_type=f32)


def gather_heads(values, marks):
    high = values.astype(bf16)
    low = (values - high.astype(f32)).astype(bf16)
    return jnp.dot(high, marks, preferred_element_type=f32) + jnp.dot(
        low, marks, preferred_element_type=f32
    )


def softplus(x):
    y = jnp.exp(-jnp.abs(x))
    small = y * (1.0 - y * (1.0 / 2 - y * (1.0 / 3 - y * (1.0 / 4 - y * (1.0 / 5)))))
    return jnp.maximum(x, 0.0) + jnp.where(y < 0.03, small, jnp.log(1.0 + y))


def lane_row(ref):
    row = ref[...][None, :]
    return jnp.concatenate([row, jnp.zeros((1, LANES - row.shape[1]), f32)], axis=1)


def long_row(ref, b, length):
    per = length // LANES
    return jnp.concatenate([ref[pl.ds(b * per + i, 1)] for i in range(per)], axis=1)


def put_row(ref, b, row):
    per = row.shape[1] // LANES
    for i in range(per):
        ref[pl.ds(b * per + i, 1)] = row[:, i * LANES : (i + 1) * LANES]


def spread_row(row, marks):
    return spread(jnp.broadcast_to(row, (8, LANES)), marks)[:1]


def position_masks(docs_row, begin):
    length = docs_row.shape[1]
    column = jnp.broadcast_to(docs_row, (LANES, length)).T
    place = begin + lax.broadcasted_iota(jnp.int32, (length, LANES), 0).astype(f32)
    return column, place


def front_kernel(
    heads,
    tokens_hbm,
    gain_ref,
    value_hbm,
    keyquery_hbm,
    step_ref,
    gate_hbm,
    docs_ref,
    step_bias_ref,
    rate_log_ref,
    skip_ref,
    value_conv_ref,
    value_offset_ref,
    keyquery_conv_ref,
    keyquery_offset_ref,
    norm_gain_ref,
    valid_ref,
    out_weight_hbm,
    teacher_hbm,
    normed_out,
    linear_out,
    conv_out,
    gate_out,
    mixed_out,
    output_out,
    pieces_out,
    halo_out,
    state_out,
    steps_out,
    cumulative_out,
    linear_steps_out,
    square_out,
    inverse_out,
    mask_out,
    rowdot_ref,
    squared_ref,
    loss_ref,
    tokens,
    last_tokens,
    value_weight,
    keyquery_weight,
    gate_weight,
    normed,
    linear,
    conv,
    gate,
    mixed,
    gained,
    tail,
    halo,
    extended,
    heads_in,
    keys,
    queries,
    scores,
    mask_bias,
    locals_,
    state,
    offers,
    offered,
    hand,
    following,
    passed,
    entering,
    load_sem,
    last_sem,
    token_sem,
    store_sem,
    halo_sem,
    chain_send,
    chain_recv,
    out_weight,
    teacher,
    output_cols,
    part,
    mate_in,
    chip_out,
    chip_in,
    gathered,
    squares,
    dots,
    dot_out,
    mate_send,
    mate_recv,
    chip_send,
    chip_recv,
    gm_send,
    gm_recv,
    gc_send,
    gc_recv,
    gf_send,
    gf_recv,
    sq_send,
    sq_recv,
    rd_send,
    rd_recv,
    output_sem,
    pieces_sem,
):
    n = lax.axis_size("seq")
    place = lax.axis_index("seq")
    heads_n = lax.axis_size("head")
    group = Group(heads_n)
    head = group.me
    width = teacher.shape[2]
    chunks = tokens.shape[0]
    count, length, _ = tokens.shape
    channels = value_weight.shape[1]
    both = channels + 2 * STATE
    lags = value_conv_ref.shape[0]
    begin = (place * length).astype(f32)

    loads = [
        pltpu.make_async_copy(value_hbm, value_weight, load_sem.at[0]),
        pltpu.make_async_copy(keyquery_hbm, keyquery_weight, load_sem.at[1]),
        pltpu.make_async_copy(gate_hbm, gate_weight, load_sem.at[2]),
        pltpu.make_async_copy(out_weight_hbm, out_weight, load_sem.at[3]),
        pltpu.make_async_copy(teacher_hbm, teacher, load_sem.at[4]),
    ]

    def token_load(b):
        return pltpu.make_async_copy(tokens_hbm.at[b], tokens.at[b], token_sem.at[b])

    def last_load(b):
        return pltpu.make_async_copy(
            tokens_hbm.at[b, length - 16 :], last_tokens.at[b], last_sem.at[b]
        )

    for b in range(count):
        last_load(b).start()
    loads[0].start()
    loads[1].start()
    for b in range(count):
        token_load(b).start()
    for copy in loads[2:]:
        copy.start()

    stores = [
        (normed, normed_out),
        (linear, linear_out),
        (conv, conv_out),
        (gate, gate_out),
        (mixed, mixed_out),
    ]

    def store(i, b):
        source, target = stores[i]
        return pltpu.make_async_copy(source.at[b], target.at[b], store_sem.at[i, b])

    barrier = pltpu.get_barrier_semaphore()

    chain = PairChain(
        place,
        1,
        locals_,
        passed,
        (state, offers, offered, hand, following),
        chain_send,
        chain_recv,
    )
    for k in range(1, heads_n):
        pl.semaphore_signal(
            barrier, inc=1, device_id=group.at(group.other(k)), device_id_type=MESH
        )
    for k in range(1, n):
        pl.semaphore_signal(
            barrier, inc=1, device_id=(lax.rem(place + k, n), head), device_id_type=MESH
        )

    def normalized(x):
        inverse = lax.rsqrt(jnp.mean(x * x, axis=-1, keepdims=True) + norm_eps)
        return inverse, (x * inverse * gain_ref[...][None, :]).astype(bf16)

    for b in range(count):
        last_load(b).wait()
    last = jnp.concatenate([normalized(last_tokens[b])[1] for b in range(count)], axis=0)
    loads[0].wait()
    loads[1].wait()
    for at, size in blocks(channels):
        tail[:, at : at + size] = jnp.dot(
            last, value_weight[:, at : at + size], preferred_element_type=f32
        ).astype(bf16)
    tail[:, channels:] = jnp.dot(last, keyquery_weight[...], preferred_element_type=f32).astype(bf16)
    pl.semaphore_wait(barrier, n + heads_n - 2)
    halo_copy = remote(tail, halo, halo_sem.at[0], halo_sem.at[1], (place + 1, head))

    @pl.when(place < n - 1)
    def _():
        halo_copy.start()

    marks = head_spread(channels)
    step_bias = lane_row(step_bias_ref)
    decay_rate = -jnp.exp(lane_row(rate_log_ref))
    skip = spread_row(lane_row(skip_ref), marks)
    triangle = (
        lax.broadcasted_iota(jnp.int32, (length, length), 0)
        >= lax.broadcasted_iota(jnp.int32, (length, length), 1)
    ).astype(f32)

    def norm(b):
        token_load(b).wait()
        inverse, rows = normalized(tokens[b])
        normed[b] = rows
        inverse_out[pl.ds(b, 1)] = jnp.broadcast_to(inverse, (length, LANES)).T[:1]
        store(0, b).start()

    def project_values(b):
        rows = normed[b]
        for at, size in blocks(channels):
            linear[b, :, at : at + size] = jnp.dot(
                rows, value_weight[:, at : at + size], preferred_element_type=f32
            ).astype(bf16)

    def project_rest(b):
        rows = normed[b]
        linear[b, :, channels:] = jnp.dot(
            rows, keyquery_weight[...], preferred_element_type=f32
        ).astype(bf16)
        narrow_steps = dot_nt(rows, step_ref[...])
        linear_steps_out[b] = jnp.concatenate(
            [narrow_steps, jnp.zeros((length, LANES - heads), f32)], axis=1
        )
        store(1, b).start()

    def states(b):
        @pl.when((b == 0) & (place > 0))
        def _():
            halo_copy.wait_recv()

        @pl.when((b == 0) & (place == 0))
        def _():
            halo[...] = jnp.zeros_like(halo)

        column, spot = position_masks(docs_ref[pl.ds(b, 1)].astype(f32), begin)
        extended[0:16] = halo[pl.ds(pl.multiple_of(b * 16, 16), 16)].astype(f32)
        extended[16:] = linear[b].astype(f32)
        usable = [None] + [(spot - lag >= column).astype(f32) for lag in range(1, lags)]
        for at in range(0, both, LANES):
            if at < channels:
                weight, offset, place_at = value_conv_ref, value_offset_ref, at
            else:
                weight, offset, place_at = keyquery_conv_ref, keyquery_offset_ref, at - channels
            lanes = slice(place_at, place_at + LANES)
            value = offset[lanes][None, :] + weight[0:1, lanes] * extended[16:, at : at + LANES]
            for lag in range(1, lags):
                value = value + weight[lag : lag + 1, lanes] * (
                    extended[16 - lag : 16 - lag + length, at : at + LANES] * usable[lag]
                )
            conv[b, :, at : at + LANES] = value
            active = value * jax.nn.sigmoid(value)
            if at < channels:
                heads_in[b, :, at : at + LANES] = active
            elif at < channels + STATE:
                keys[b] = active.astype(bf16)
            else:
                queries[b] = active.astype(bf16)
        store(2, b).start()
        steps = softplus(linear_steps_out[b] + step_bias)
        cumulative = jnp.dot(
            triangle, steps * decay_rate, precision=highest, preferred_element_type=f32
        )
        steps_out[b] = steps
        cumulative_out[b] = cumulative
        kept = (column < begin).astype(f32)
        trailing = (spot >= column[length - 1 :]).astype(f32)
        entering[b] = jnp.exp(cumulative) * kept
        end_weight = jnp.exp(cumulative[length - 1 :] - cumulative) * trailing * steps
        weighted = (heads_in[b] * spread(end_weight, marks)).astype(bf16)
        locals_[b] = dot_tn(keys[b], weighted)
        last_entering = entering[b, length - 8 :]
        passed[b] = spread(last_entering, marks)

    pairs = channels // LANES
    turns = []
    if n == 8 and count == 4:
        turns = [(1, 0, 0), (2, 0, 1), (3, 0, 2), (5, 0, 3)]
        turns += [(2, 1, 0), (3, 1, 1), (5, 1, 2), (7, 1, 3)]
        turns += [(3, 2, 0), (5, 2, 1), (7, 2, 2), (9, 2, 3)]
        turns += [(5, 3, 0), (7, 3, 1), (9, 3, 2), (10, 3, 3)]

    def begin_sequence(b):
        norm(b)
        project_values(b)
        project_rest(b)
        states(b)
        chain.offer(b)
        chain.turn(b, turns)

    loop(count, begin_sequence)
    halo_out[...] = halo[...]
    per_row = 2.0 / (D * jnp.sum(valid_ref[...].astype(f32), keepdims=True))
    here = pl.ds(pl.multiple_of(place * length, length), length)
    for b in range(count):
        row = valid_ref[b : b + 1, here].astype(f32) * per_row
        for i in range(length // LANES):
            at = b * (length // LANES) + i
            mask_out[at : at + 1] = row[:, i * LANES : (i + 1) * LANES]
    first_half = lax.broadcasted_iota(jnp.int32, (length, LANES), 1) < HEADDIM
    loads[2].wait()

    def inside(b):
        column, spot = position_masks(docs_ref[pl.ds(b, 1)].astype(f32), begin)
        wide = jnp.concatenate([column] * (length // LANES), axis=1)
        t = begin + lax.broadcasted_iota(jnp.int32, (length, length), 0).astype(f32)
        u = begin + lax.broadcasted_iota(jnp.int32, (length, length), 1).astype(f32)
        mask_bias[...] = jnp.where((u >= wide) & (u <= t), 0.0, -1e30)
        scores[...] = dot_nt(queries[b], keys[b])
        cumulative = cumulative_out[b]
        across = cumulative.T
        spread_steps = spread(steps_out[b], marks)
        for pair in range(pairs):
            lanes = slice(pair * LANES, (pair + 1) * LANES)
            scaled = heads_in[b, :, lanes] * spread_steps[:, lanes]
            value = jnp.zeros((length, LANES), f32)
            for half in range(2):
                h = 2 * pair + half
                decay = jnp.exp(cumulative[:, h : h + 1] - across[h : h + 1] + mask_bias[...])
                mixing = (decay * scores[...]).astype(bf16)
                mine = jnp.where(first_half if half == 0 else ~first_half, scaled, 0.0).astype(bf16)
                value = value + jnp.dot(mixing, mine, preferred_element_type=f32)
            mixed[b, :, lanes] = value
        rows = normed[b]
        for at, size in blocks(channels):
            gate[b, :, at : at + size] = jnp.dot(
                rows, gate_weight[:, at : at + size], preferred_element_type=f32
            )
        store(3, b).start()
        chain.turn(count + b, turns)

    loop(count, inside)
    chain.rest(turns)

    def close(b):
        chain.ready(b)
        state_out[b] = state[b]
        projected = jnp.dot(queries[b], state[b], preferred_element_type=f32)
        value = mixed[b] + spread(entering[b], marks) * projected + skip * heads_in[b]
        mixed[b] = value
        store(4, b).start()
        linear_gate = gate[b]
        gated = value * (linear_gate * jax.nn.sigmoid(linear_gate))
        gained[b] = (gated * norm_gain_ref[...][None, :]).astype(bf16)
        put_row(square_out, b, rows_of(gated * gated))

    def row_block(c):
        return pl.ds(pl.multiple_of(c * length, length), length)

    start_mate, start_chip, total, finish = scatter_phases(
        group, row_block, part, mate_in, chip_out, chip_in, (mate_send, mate_recv, chip_send, chip_recv)
    )

    def product(c):
        rows = gained[c]
        for j in range(heads_n):
            block = (
                out_weight[:, j * width : (j + 1) * width] if len(out_weight.shape) == 2 else out_weight[j]
            )
            part[j, row_block(c)] = jnp.dot(rows, block, preferred_element_type=f32).astype(bf16)
        start_mate(c)

    loads[3].wait()

    def close_and_send(b):
        close(b)
        product(b)

        @pl.when(b > 0)
        def _():
            start_chip(b - 1)

        chain.turn(9 + b, turns)

    loop(count, close_and_send)
    start_chip(count - 1)
    share(group, square_out, squares, sq_send, sq_recv)
    shared(group, square_out, squares, sq_send, sq_recv)
    squares[group.me] = square_out[...]
    loss_ref[...] = jnp.zeros_like(loss_ref)

    def to_mate(c):
        block = gathered.at[group.me, row_block(c)]
        return remote(block, block, gm_send.at[c], gm_recv.at[c], group.at(group.mate))

    def to_chip(c, k):
        block = gathered.at[group.me, row_block(c)]
        return remote(
            block, block, gc_send.at[k - 1, c], gc_recv.at[k - 1, c], group.at(group.peer(k))
        )

    def forward(c, k):
        block = gathered.at[2 * group.chip_before(k) + group.core, row_block(c)]
        return remote(
            block, block, gf_send.at[k - 1, c], gf_recv.at[k - 1, c], group.at(group.mate)
        )

    loads[4].wait()

    def own_tokens(c):
        if width % LANES == 0:
            return tokens[c, :, pl.ds(pl.multiple_of(head * width, LANES), width)]
        found = jnp.zeros((length, width), f32)
        for j in range(heads_n):
            mine = tokens[c, :, j * width : (j + 1) * width]
            found = found + jnp.where(head == j, mine, 0.0)
        return found

    def rest(c):
        squared = long_row(squares.at[0], c, length)
        for j in range(1, heads_n):
            squared = squared + long_row(squares.at[j], c, length)
        put_row(squared_ref, c, squared)
        scale = lax.rsqrt(squared * (1.0 / (NHEADS * HEADDIM)) + norm_eps)
        branch = total(c) * as_column(scale, width)
        output = own_tokens(c) + branch
        output_cols[row_block(c)] = output
        difference = output - teacher[c]
        weighted = difference * as_column(long_row(mask_out, c, length), width)
        low = weighted.astype(bf16)
        gathered[group.me, row_block(c)] = low
        to_mate(c).start()
        for k in range(1, group.chips):
            to_chip(c, k).start()
        loss_ref[...] += jnp.sum(weighted * difference, axis=0, keepdims=True)
        put_row(dot_out, c, rows_of(low.astype(f32) * branch))

    loop(chunks, rest)
    output_store = pltpu.make_async_copy(output_cols, output_out, output_sem.at[0])
    output_store.start()
    share(group, dot_out, dots, rd_send, rd_recv)

    def pass_on(c):
        for k in range(1, group.chips):
            to_chip(c, k).wait_recv()
            forward(c, k).start()

    loop(chunks, pass_on)

    def pieces_store(c):
        return pltpu.make_async_copy(
            gathered.at[pl.ds(0, heads_n), row_block(c)],
            pieces_out.at[pl.ds(0, heads_n), row_block(c)],
            pieces_sem.at[c],
        )

    def end(c):
        to_mate(c).wait()
        for k in range(1, group.chips):
            to_chip(c, k).wait_send()
            forward(c, k).wait()
        finish(c)
        pieces_store(c).start()

    loop(chunks, end)
    shared(group, dot_out, dots, rd_send, rd_recv)
    row_sum = dot_out[...]
    for k in range(1, heads_n):
        row_sum = row_sum + dots[group.other(k)]
    rowdot_ref[...] = row_sum
    output_store.wait()
    loop(chunks, lambda c: pieces_store(c).wait())

    @pl.when(place < n - 1)
    def _():
        halo_copy.wait_send()

    chain.finish()

    for i in range(len(stores)):
        loop(count, lambda b, i=i: store(i, b).wait())


def front(tokens, gain, value_weight, keyquery_weight, step_weight, gate_weight, docs, vectors, conv, norm_gain, valid, out_weight, teacher, cid):
    count, length, _ = tokens.shape
    channels = value_weight.shape[1]
    heads = channels // HEADDIM
    both = channels + 2 * STATE
    dma = pltpu.SemaphoreType.DMA
    hbm = pl.BlockSpec(memory_space=pl.ANY)
    shape = jax.ShapeDtypeStruct
    heads_n, width = lax.axis_size("head"), teacher.shape[2]
    rows, chips = count * length, heads_n // 2
    chunks, lines = count, rows // LANES
    out_weight = blocked(out_weight, heads_n)
    buffers, sems = scatter_scratch(heads_n, rows, width, chunks)
    big = [
        ((count, length, D), bf16),
        ((count, length, both), bf16),
        ((count, length, both), f32),
        ((count, length, channels), f32),
        ((count, length, channels), f32),
    ]
    results = [((rows, width), f32), ((heads_n, rows, width), bf16)]
    small = [
        ((count * 16, both), bf16),
        ((count, STATE, channels), bf16),
        ((count, length, LANES), f32),
        ((count, length, LANES), f32),
        ((count, length, LANES), f32),
        ((count * length // LANES, LANES), f32),
        ((count, length), f32),
        ((count * length // LANES, LANES), f32),
        ((lines, LANES), f32),
        ((lines, LANES), f32),
        ((1, width), f32),
    ]
    return pl.pallas_call(
        functools.partial(front_kernel, heads),
        out_shape=[shape(*s) for s in big + results + small],
        in_specs=[hbm, in_vmem, hbm, hbm, in_vmem, hbm] + [in_vmem] * 10 + [hbm] * 2,
        out_specs=[hbm] * (len(big) + 2) + [in_vmem] * len(small),
        scratch_shapes=[
            pltpu.VMEM((count, length, D), f32),
            pltpu.VMEM((count, 16, D), f32),
            pltpu.VMEM((D, channels), bf16),
            pltpu.VMEM((D, 2 * STATE), bf16),
            pltpu.VMEM((D, channels), bf16),
        ]
        + [pltpu.VMEM(*s) for s in big]
        + [
            pltpu.VMEM((count, length, channels), bf16),
            pltpu.VMEM((count * 16, both), bf16),
            pltpu.VMEM((count * 16, both), bf16),
            pltpu.VMEM((length + 16, both), f32),
            pltpu.VMEM((count, length, channels), f32),
            pltpu.VMEM((count, length, STATE), bf16),
            pltpu.VMEM((count, length, STATE), bf16),
            pltpu.VMEM((length, length), f32),
            pltpu.VMEM((length, length), f32),
            pltpu.VMEM((count, STATE, channels), f32),
        ]
        + chain_buffers(count, channels)
        + [
            pltpu.VMEM((count, 8, channels), f32),
            pltpu.VMEM((count, length, LANES), f32),
            dma((5,)),
            dma((count,)),
            dma((count,)),
            dma((len(big), count)),
            dma((2,)),
            dma((3, count)),
            dma((3, count)),
            pltpu.VMEM(out_weight.shape, bf16),
            pltpu.VMEM((count, length, width), f32),
            pltpu.VMEM((rows, width), f32),
        ]
        + buffers
        + [
            pltpu.VMEM((heads_n, rows, width), bf16),
            pltpu.VMEM((heads_n, lines, LANES), f32),
            pltpu.VMEM((heads_n, lines, LANES), f32),
            pltpu.VMEM((lines, LANES), f32),
        ]
        + sems
        + [
            dma((chunks,)),
            dma((chunks,)),
            dma((chips - 1, chunks)),
            dma((chips - 1, chunks)),
            dma((chips - 1, chunks)),
            dma((chips - 1, chunks)),
            dma((heads_n - 1,)),
            dma((heads_n,)),
            dma((heads_n - 1,)),
            dma((heads_n,)),
            dma((1,)),
            dma((chunks,)),
        ],
        compiler_params=params(cid),
        name="front",
    )(tokens, gain, value_weight, keyquery_weight, step_weight, gate_weight, docs, *vectors, *conv, norm_gain, valid, out_weight, teacher)


class Doubling:
    def __init__(self, axis, bits, current, table, send_sem, recv_sem):
        self.axis, self.bits, self.current, self.table = axis, list(bits), current, table
        self.send_sem, self.recv_sem = send_sem, recv_sem

    def copy(self, stage):
        bit = 1 << self.bits[stage]
        mine = lax.axis_index(self.axis)
        other = mine + bit - 2 * bit * lax.rem(lax.div(mine, bit), 2)
        if self.axis == "head":
            target = (lax.axis_index("seq"), other)
        else:
            target = (other, lax.axis_index("head"))
        return remote(
            self.current,
            self.table.at[stage],
            self.send_sem.at[stage],
            self.recv_sem.at[stage],
            target,
        )

    def start(self, stage):
        self.copy(stage).start()

    def run(self, first, last=None):
        for stage in range(first, len(self.bits) if last is None else min(last, len(self.bits))):
            self.copy(stage).wait()
            self.current[...] = self.current[...] + self.table[stage]
            if stage + 1 < len(self.bits):
                self.start(stage + 1)


def stages_of(n):
    return n.bit_length() - 1


def tile_place(index, width):
    per = width // LANES
    return index // per, slice(index % per * LANES, index % per * LANES + LANES)


class Tiles:
    def __init__(self, ref):
        self.ref, self.index = ref, 0

    def put(self, row):
        for at in range(0, row.shape[1], LANES):
            r, lanes = tile_place(self.index, self.ref.shape[1])
            self.ref[r : r + 1, lanes] = row[:, at : at + LANES]
            self.index += 1

    def take(self, width):
        found = []
        for _ in range(width // LANES):
            r, lanes = tile_place(self.index, self.ref.shape[1])
            found.append(self.ref[r : r + 1, lanes])
            self.index += 1
        return jnp.concatenate(found, axis=1)


def rear_kernel(names, scoped, heads, *refs):
    r = types.SimpleNamespace(**dict(zip(names, refs)))
    n, heads_n = lax.axis_size("seq"), lax.axis_size("head")
    place = lax.axis_index("seq")
    group = Group(heads_n)
    head = group.me
    ahead = n - 1 - place
    count, length, channels = r.gate_grad.shape
    rows = count * length
    both = channels + 2 * STATE
    lags = r.value_conv.shape[0]
    width = r.mate_in.shape[2]
    begin = (place * length).astype(f32)
    inner_total = NHEADS * HEADDIM
    ring_steps = n - 2
    own = D // n
    quarters = own % 64 == 0
    turns, out_steps, gate_steps = [], [], []
    if n == 8 and count == 4:
        turns = [(3, 0, 0), (4, 0, 1), (5, 0, 2), (7, 0, 3)]
        turns += [(6, 1, 0), (8, 1, 1), (9, 1, 2), (11, 1, 3)]
        turns += [(10, 2, 0), (12, 2, 1), (13, 2, 2), (14, 2, 3)]
        turns += [(13, 3, 0), (15, 3, 1), (16, 3, 2), (17, 3, 3)]
        out_steps = [(8, 0), (11, 1), (14, 2), (17, 3), (19, 4), (22, 5)]
        gate_steps = [(18, 0), (21, 1), (23, 2), (25, 3), (28, 4), (30, 5)]

    barrier = pltpu.get_barrier_semaphore()
    for k in range(1, heads_n):
        pl.semaphore_signal(
            barrier, inc=1, device_id=group.at(group.other(k)), device_id_type=MESH
        )
    for k in range(1, n):
        pl.semaphore_signal(
            barrier, inc=1, device_id=(lax.rem(place + k, n), head), device_id_type=MESH
        )

    normed_load = pltpu.make_async_copy(r.normed_hbm, r.normed, r.load_sem.at[0])
    marks = head_spread(channels)
    collect = head_gather(channels)
    step_bias = lane_row(r.step_bias)
    decay_rate = -jnp.exp(lane_row(r.rate_log))
    skip = spread_row(lane_row(r.skip), marks)
    r.gain_grad[...] = jnp.zeros_like(r.gain_grad)
    r.vector_grad[...] = jnp.zeros_like(r.vector_grad)
    r.conv_grad[...] = jnp.zeros_like(r.conv_grad)
    ring = Ring(r.ring_send, r.ring_recv)
    def matrix(part, slots, cut):
        first = len(ring.streams)
        if not quarters:
            ring.add(part, slots[:2])
            return (first,)
        ring.add(part, slots[:2], by_rows=True)
        if not cut:
            return (first,)
        ring.add(part, slots[2:], by_rows=True, first=own // 2)
        return first, first + 2

    out_halves = matrix(r.out_part, (r.os0, r.os1), False)
    gate_halves = matrix(r.gate_part, (r.gs0, r.gs1), False)

    def pass_on(first, step):
        @pl.when((step >= 0) & (step < ring_steps))
        def _():
            ring.pass_on(first, step)
            ring.pass_on(first + 1, step)

    def weights_turn(here, rounds=1):
        known = range(here, here + 2 * rounds, 2) if isinstance(here, int) else None
        for halves, table in ((out_halves, out_steps), (gate_halves, gate_steps)):
            if known is None or any(place in known for place, _ in table):
                step = step_at(table, here)
                for first in halves:
                    pass_on(first, step)

    def start(first):
        ring.start(first)
        ring.start(first + 1)

    def rest_of_ring(halves, done):
        if ring_steps > done:

            def further(s):
                for first in halves:
                    pass_on(first, done + s)

            loop(ring_steps - done, further)

    def total_of(i, halves, sums, targets):
        for k in [first + way for first in halves for way in range(2)]:
            _, _, (first, lines), columns, _ = ring.streams[k]
            sums[i, first : first + lines, columns] = ring.last(k)
        copy = pltpu.make_async_copy(sums.at[i], targets[i], r.total_sem.at[i])
        copy.start()
        return copy

    def as_wide(ref, b):
        return jnp.broadcast_to(long_row(ref, b, length), (LANES, length)).T

    def widened(column, size):
        return jnp.concatenate([column] * (size // LANES), axis=1)

    def weight_block(target, grads, block):
        sides = jnp.concatenate([r.normed[b, :, block] for b in range(count)], axis=0)
        whole = jnp.concatenate([grads(b) for b in range(count)], axis=0)
        target[block] = dot_tn(sides, whole).astype(target.dtype)

    def phase_one(*locals_one):
        q = types.SimpleNamespace(**dict(zip(scoped[0], locals_one)))
        loads = [
            pltpu.make_async_copy(r.out_weight_hbm, q.weight, r.load_sem.at[1]),
            pltpu.make_async_copy(r.pieces_hbm, q.pieces, r.load_sem.at[2]),
        ]
        for copy in loads:
            copy.start()
        row_arrays = [(r.gate_hbm, q.gate), (r.mixed_hbm, q.mixed), (r.conv_hbm, q.conv)]

        def row_load(i, b):
            source, target = row_arrays[i]
            return pltpu.make_async_copy(source.at[b], target.at[b], r.row_sem.at[i, b])

        def linear_load(b):
            slot = lax.rem(b, 2)
            return pltpu.make_async_copy(r.linear_hbm.at[b], q.linear.at[slot], r.line_load.at[slot])

        for i in range(3):
            row_load(i, 0).start()
        inner = q.gate
        normed_out = r.values_grad
        chain = PairChain(
            ahead,
            -1,
            q.local,
            q.passed,
            (r.state, q.offer, r.offered, r.hand, q.following),
            r.chain_send,
            r.chain_recv,
        )
        pairs = channels // LANES
        for copy in loads:
            copy.wait()
        for b in range(1, count):
            for i in range(3):
                row_load(i, b).start()
        normed_load.start()
        linear_load(0).start()
        pl.semaphore_wait(barrier, heads_n + n - 2)
        groups = q.pieces.shape[0]

        def gated_norm(b):
            for i in range(3):
                row_load(i, b).wait()
            scale = lax.rsqrt(as_wide(r.square, b) * (1.0 / inner_total) + norm_eps)
            pull = scale * scale * as_wide(r.rowdot, b) * (1.0 / inner_total)
            column, _ = position_masks(r.docs[pl.ds(b, 1)].astype(f32), begin)
            entering = spread(jnp.exp(r.cumulative[b]) * (column < begin).astype(f32), marks)
            q.passed[b] = entering[length - 8 :]
            here = pl.ds(pl.multiple_of(b * length, length), length)
            for at, size in blocks(channels):
                lanes = slice(at, at + size)
                grad_rows = jnp.zeros((length, size), f32)
                for j in range(groups):
                    block = (
                        q.weight[lanes, j * width : (j + 1) * width]
                        if len(q.weight.shape) == 2
                        else q.weight[j, lanes]
                    )
                    grad_rows = grad_rows + dot_nt(q.pieces[j, here], block)
                linear_gate = q.gate[b, :, lanes]
                sigmoid_value = jax.nn.sigmoid(linear_gate)
                active = linear_gate * sigmoid_value
                value = q.mixed[b, :, lanes]
                gated = value * active
                norm_gain = r.norm_gain[lanes][None, :]
                scaled = gated * widened(scale, size)
                normed_out[b, :, lanes] = (scaled * norm_gain).astype(bf16)
                r.gain_grad[:, lanes] += jnp.sum(grad_rows * scaled, axis=0, keepdims=True)
                gated_grad = widened(scale, size) * norm_gain * grad_rows - gated * widened(
                    pull, size
                )
                q.heads_grad[b, :, lanes] = gated_grad * active
                slope = sigmoid_value * (1.0 + linear_gate * (1.0 - sigmoid_value))
                r.gate_grad[b, :, lanes] = (gated_grad * value * slope).astype(bf16)
                values = q.conv[b, :, lanes]
                q.heads_in[b, :, lanes] = values * jax.nn.sigmoid(values)
            values = q.conv[b, :, channels : channels + STATE]
            q.keys[b] = (values * jax.nn.sigmoid(values)).astype(bf16)
            values = q.conv[b, :, channels + STATE :]
            q.queries[b] = (values * jax.nn.sigmoid(values)).astype(bf16)
            q.local[b] = dot_tn(q.queries[b], (q.heads_grad[b] * entering).astype(bf16))
            chain.offer(b)

        loop(count, gated_norm)
        chain.turn(3, turns)

        for j in range(groups):
            grads = jnp.concatenate([normed_out[b] for b in range(count)], axis=0)
            r.out_part[j * width : (j + 1) * width] = dot_tn(q.pieces[j], grads).astype(bf16)
            if j == groups // 2 - 1:
                chain.turn(4, turns)
        for first in out_halves:
            start(first)
        chain.turn(5, turns)
        normed_load.wait()

        first_half = lax.broadcasted_iota(jnp.int32, (length, LANES), 1) < HEADDIM

        def inside(b):
            docs_row = r.docs[pl.ds(b, 1)].astype(f32)
            u = begin + lax.broadcasted_iota(jnp.int32, (length, length), 0).astype(f32)
            t = begin + lax.broadcasted_iota(jnp.int32, (length, length), 1).astype(f32)
            q.mask_bias[...] = jnp.where((u >= docs_row) & (u <= t), 0.0, -1e30)
            q.scores[...] = dot_nt(q.keys[b], q.queries[b])
            q.scores_grad[...] = jnp.zeros_like(q.scores_grad)
            cumulative = r.cumulative[b]
            across = cumulative.T
            spread_steps = spread(r.steps[b], marks)
            for pair in range(pairs):
                lanes = slice(pair * LANES, (pair + 1) * LANES)
                scaled = q.heads_in[b, :, lanes] * spread_steps[:, lanes]
                grads = q.heads_grad[b, :, lanes]
                low_grads = grads.astype(bf16)
                value = jnp.zeros((length, LANES), f32)
                for half in range(2):
                    h = 2 * pair + half
                    mine = first_half if half == 0 else ~first_half
                    decay = jnp.exp(
                        across[h : h + 1] - cumulative[:, h : h + 1] + q.mask_bias[...]
                    )
                    mixing = (decay * q.scores[...]).astype(bf16)
                    value = value + jnp.dot(
                        mixing, jnp.where(mine, grads, 0.0).astype(bf16), preferred_element_type=f32
                    )
                    pairwise = dot_nt(jnp.where(mine, scaled, 0.0).astype(bf16), low_grads)
                    q.scores_grad[...] += decay * pairwise
                inner[b, :, lanes] = value
                if pair == (pairs - 1) // 2:
                    weights_turn(6 + 2 * b)
                    chain.turn(6 + 2 * b, turns)
            low = q.scores_grad[...].astype(bf16)
            q.narrow_grad[b, :, :STATE] = jnp.dot(low, q.queries[b], preferred_element_type=f32)
            column, _ = position_masks(docs_row, begin)
            entering = jnp.exp(cumulative) * (column < begin).astype(f32)
            x = q.heads_in[b]
            dy = q.heads_grad[b]
            q.narrow_grad[b, :, STATE:] = dot_tn(low, q.keys[b]) + dot_nt(
                (dy * spread(entering, marks)).astype(bf16), r.state_in[b]
            )
            dot_inner = gather_heads(x * inner[b], collect)
            dot_skip = gather_heads(dy * x, collect)
            q.dot_inner[b] = dot_inner
            q.cum_part[b] = (
                gather_heads(dy * (q.mixed[b] - skip * x), collect) - r.steps[b] * dot_inner
            )
            r.vector_grad[2:3] += jnp.sum(dot_skip, axis=0, keepdims=True)
            inner[b] = skip * dy + spread_steps * inner[b]
            weights_turn(7 + 2 * b)
            chain.turn(7 + 2 * b, turns)

        loop(count, inside)
        chain.rest(turns)

        def gate_block(i):
            block = pl.ds(pl.multiple_of(i * 256, 256), 256)
            weight_block(r.gate_part, lambda b: r.gate_grad[b], block)

        loop(D // 512, gate_block)
        weights_turn(14)
        chain.turn(14, turns)
        loop(D // 512, lambda i: gate_block(i + D // 512))
        for first in gate_halves:
            start(first)
        weights_turn(15)
        chain.turn(15, turns)
        q.around[...] = jnp.zeros_like(q.around)
        q.usable[...] = jnp.zeros_like(q.usable)
        upper = (
            lax.broadcasted_iota(jnp.int32, (length, length), 0)
            <= lax.broadcasted_iota(jnp.int32, (length, length), 1)
        ).astype(f32)
        last_row = lax.broadcasted_iota(jnp.int32, (length, LANES), 0) == length - 1

        def edge_copy(b):
            return remote(
                r.edge.at[b], r.edge_in.at[b], r.edge_send.at[b], r.edge_recv.at[b], (place - 1, head)
            )

        def close(b):
            @pl.when(b + 1 < count)
            def _():
                linear_load(b + 1).start()

            column, spot = position_masks(r.docs[pl.ds(b, 1)].astype(f32), begin)
            cumulative = r.cumulative[b]
            steps = r.steps[b]
            kept = (column < begin).astype(f32)
            trailing = (spot >= column[length - 1 :]).astype(f32)
            entering = jnp.exp(cumulative) * kept
            end_decay = jnp.exp(cumulative[length - 1 :] - cumulative) * trailing
            end_weight = end_decay * steps
            chain.ready(b)
            end_grad = r.state[b]
            x = q.heads_in[b]
            grown = jnp.dot(q.keys[b], end_grad, preferred_element_type=f32)
            spread_end = spread(end_weight, marks)
            q.narrow_grad[b, :, :STATE] += dot_nt((x * spread_end).astype(bf16), end_grad)
            grad = inner[b] + spread_end * grown
            dot_end = gather_heads(x * grown, collect)
            through = jnp.sum(
                end_grad.astype(f32) * r.state_in[b].astype(f32), axis=0, keepdims=True
            )
            passed_grad = gather_heads(jnp.broadcast_to(through, (8, channels)), collect)[:1]
            end_mix = dot_end * end_weight
            last_term = passed_grad * entering[length - 1 :] + jnp.sum(
                end_mix, axis=0, keepdims=True
            )
            cum_grad = q.cum_part[b] - end_mix + jnp.where(last_row, last_term, 0.0)
            rates_grad = jnp.dot(upper, cum_grad, precision=highest, preferred_element_type=f32)
            steps_grad = q.dot_inner[b] + end_decay * dot_end + rates_grad * decay_rate
            linear_grad = steps_grad * jax.nn.sigmoid(r.linear_steps[b] + step_bias)
            r.narrow[b, :, 2 * STATE :] = linear_grad.astype(bf16)
            r.vector_grad[0:1] += jnp.sum(linear_grad, axis=0, keepdims=True)
            r.vector_grad[1:2] += jnp.sum(rates_grad * steps, axis=0, keepdims=True) * decay_rate

            weights_turn(16 + 2 * b)
            chain.turn(16 + 2 * b, turns)
            linear_load(b).wait()
            halo_rows = pl.ds(pl.multiple_of(b * 16, 16), 16)
            line = lax.rem(b, 2)
            middle = slice(16, 16 + length)
            for lag in range(1, lags):
                q.usable[lag - 1, middle] = (spot - lag >= column).astype(f32)
            for at in range(0, both, LANES):
                lanes = slice(at, at + LANES)
                slot = at // LANES % 2
                q.extended[slot, 0:16] = r.halo[halo_rows, lanes].astype(f32)
                q.extended[slot, 16:] = q.linear[line, :, lanes].astype(f32)
                values = q.conv[b, :, lanes]
                sigmoid_value = jax.nn.sigmoid(values)
                slope = sigmoid_value * (1.0 + values * (1.0 - sigmoid_value))
                if at < channels:
                    out_grad = grad[:, lanes]
                    taps, tap = r.value_conv, lanes
                else:
                    place_at = at - channels
                    out_grad = q.narrow_grad[b, :, place_at : place_at + LANES]
                    taps, tap = r.keyquery_conv, slice(place_at, place_at + LANES)
                local = out_grad * slope
                q.around[slot, middle] = local
                input_grad = taps[0:1, tap] * local
                edges = jnp.zeros((8, LANES), f32)
                r.conv_grad[0:1, lanes] += jnp.sum(
                    local * q.extended[slot, middle], axis=0, keepdims=True
                )
                r.conv_grad[lags : lags + 1, lanes] += jnp.sum(local, axis=0, keepdims=True)
                for lag in range(1, lags):
                    mask = q.usable[lag - 1, middle]
                    r.conv_grad[lag : lag + 1, lanes] += jnp.sum(
                        local * mask * q.extended[slot, 16 - lag : 16 - lag + length],
                        axis=0,
                        keepdims=True,
                    )
                    later = slice(16 + lag, 16 + lag + length)
                    input_grad = input_grad + taps[lag : lag + 1, tap] * (
                        q.around[slot, later] * q.usable[lag - 1, later]
                    )
                    first = slice(8 + lag, 16 + lag)
                    edges = edges + taps[lag : lag + 1, tap] * (
                        q.around[slot, first] * q.usable[lag - 1, first]
                    )
                r.edge[b, :, lanes] = edges
                q.tails[b, :, lanes] = input_grad[length - 16 :]
                if at < channels:
                    r.values_grad[b, :, lanes] = input_grad.astype(bf16)
                else:
                    r.narrow[b, :, tap] = input_grad.astype(bf16)

            @pl.when(place > 0)
            def _():
                edge_copy(b).start()

            weights_turn(17 + 2 * b)
            chain.turn(17 + 2 * b, turns)

        loop(count, close)

        @pl.when(place < n - 1)
        def _():
            def join(b):
                edge_copy(b).wait_recv()
                last = slice(length - 16, length)
                q.tails[b, 8:] = q.tails[b, 8:] + r.edge_in[b]
                r.values_grad[b, last] = q.tails[b, :, :channels].astype(bf16)
                r.narrow[b, last, : 2 * STATE] = q.tails[b, :, channels:].astype(bf16)

            loop(count, join)

        @pl.when(place > 0)
        def _():
            loop(count, lambda b: edge_copy(b).wait_send())

        chain.finish()

    pl.run_scoped(phase_one, *scoped[1])

    def phase_two(*locals_two):
        q = types.SimpleNamespace(**dict(zip(scoped[2], locals_two)))
        token_columns = r.tokens_hbm
        if token_columns.shape[2] != width:
            first_column = pl.multiple_of(head * width, LANES)
            token_columns = token_columns.at[:, :, pl.ds(first_column, width)]
        loads = [
            pltpu.make_async_copy(source, target, r.load_two.at[i])
            for i, (source, target) in enumerate(
                [
                    (r.gate_weight_hbm, q.gate_weight),
                    (r.value_weight_hbm, q.value_weight),
                    (r.keyquery_weight_hbm, q.keyquery_weight),
                    (token_columns, q.tokens),
                    (r.output_hbm, q.output),
                    (r.teacher_hbm, q.teacher),
                ]
            )
        ]
        for copy in loads:
            copy.start()
        value_halves = matrix(q.value_part, (r.vs0, r.vs1, r.vs2, r.vs3), True)
        keyquery_first = len(ring.streams)
        ring.add(q.keyquery_half, (r.ks0, r.ks1), by_rows=True)

        def value_block(i):
            block = pl.ds(pl.multiple_of(i * 256, 256), 256)
            weight_block(q.value_part, lambda b: r.values_grad[b], block)

        loop(D // 512, value_block)
        weights_turn(24)
        loop(D // 512, lambda i: value_block(i + D // 512))
        for first in value_halves:
            start(first)
        weights_turn(25)

        def narrow_block(i):
            block = pl.ds(pl.multiple_of(i * 256, 256), 256)
            for half in range(2):
                lanes = slice(half * STATE, (half + 1) * STATE)
                weight_block(q.keyquery_part.at[half], lambda b: r.narrow[b, :, lanes], block)

        loop(D // 256, narrow_block)
        keyquery_mate = remote(
            q.keyquery_part.at[1 - group.core],
            r.keyquery_in,
            r.small_send.at[0],
            r.small_recv.at[0],
            group.at(group.mate),
        )
        keyquery_mate.start()
        weights_turn(26)
        targets = (r.out_total, r.gate_total, r.value_total)

        def end_ring(i, halves, done):
            rest_of_ring(halves, done)
            return total_of(i, halves, q.sums, targets)

        for copy in loads[:3]:
            copy.wait()
        q.columns[...] = jnp.zeros_like(q.columns)

        def own_columns(row):
            mine = jnp.zeros((1, width), f32)
            for j in range(heads_n):
                mine = mine + jnp.where(head == j, row[:, j * width : (j + 1) * width], 0.0)
            return mine

        gain = own_columns(r.gain[...][None, :])

        def row_block(c):
            return pl.ds(pl.multiple_of(c * length, length), length)

        start_mate, start_chip, total, finish = scatter_phases(
            group,
            row_block,
            q.part,
            r.mate_in,
            q.chip_out,
            r.chip_in,
            (r.mate_send, r.mate_recv, r.chip_send, r.chip_recv),
        )

        def value_turn(s):
            if s < ring_steps:
                for first in value_halves:
                    pass_on(first, s)

        def keyquery_turn(s):
            if s < ring_steps:
                pass_on(keyquery_first, s)

        def product(c):
            row_sum = jnp.zeros((length, LANES), f32)
            for j in range(heads_n):
                lanes = slice(j * width, (j + 1) * width)
                value = dot_nt(r.gate_grad[c], q.gate_weight[lanes])
                value = value + dot_nt(r.values_grad[c], q.value_weight[lanes])
                value = value + dot_nt(r.narrow[c, :, : 2 * STATE], q.keyquery_weight[lanes])
                value = value + jnp.dot(
                    r.narrow[c, :, 2 * STATE : 2 * STATE + heads],
                    r.step_weight[:, lanes],
                    preferred_element_type=f32,
                )
                q.part[j, row_block(c)] = value.astype(bf16)
                scaled = value * r.normed[c, :, lanes].astype(f32)
                q.columns[:, lanes] += jnp.sum(scaled, axis=0, keepdims=True)
                row_sum = row_sum + fold_lanes(scaled)
            r.dot_out[pl.ds(c, 1)] = jnp.sum(row_sum.T, axis=0, keepdims=True)
            start_mate(c)

            @pl.when(c > 0)
            def _():
                start_chip(c - 1)

        product(0)
        keyquery_mate.wait_recv()
        q.keyquery_half[...] = q.keyquery_part[group.core] + r.keyquery_in[...]
        start(keyquery_first)
        total_copies = [end_ring(0, out_halves, len(out_steps))]
        product(1)
        weights_turn(28)
        keyquery_turn(0)
        product(2)
        value_turn(0)
        keyquery_turn(1)
        product(3)
        start_chip(count - 1)
        keyquery_turn(2)
        weights_turn(30)
        share(group, r.dot_out, r.dots, r.rd_send, r.rd_recv)

        group_total = Doubling(
            "head", range(stages_of(heads_n)), r.group_sum, r.group_table, r.group_send, r.group_recv
        )
        line_total = Doubling(
            "seq", range(stages_of(n)), r.line_sum, r.line_table, r.line_send, r.line_recv
        )
        chip_total = Doubling(
            "head",
            range(1, stages_of(heads_n)),
            r.keyquery_sum,
            r.keyquery_table,
            r.kq_send,
            r.kq_recv,
        )
        tiles = Tiles(r.group_sum)
        r.group_sum[...] = jnp.zeros_like(r.group_sum)
        for lag in range(lags + 1):
            tiles.put(r.conv_grad[lag : lag + 1, channels:])
        tiles.put(q.columns[...])
        tiles.put(fold_lanes(r.loss_cols[...]))
        group_total.start(0)
        value_turn(1)
        keyquery_turn(3)

        for at, size in blocks(D):
            whole = jnp.concatenate([r.normed[b, :, at : at + size] for b in range(count)], axis=0)
            grads = jnp.concatenate([r.narrow[b, :, 2 * STATE :] for b in range(count)], axis=0)
            q.step_whole[:, at : at + size] = dot_tn(grads, whole)
        q.step_part[...] = jnp.zeros_like(q.step_part)
        for s in range(n):
            q.step_part[s, :, :own] = q.step_whole[:16, s * own : (s + 1) * own]

        def step_copy(k, index, sender):
            return remote(
                q.step_part.at[index],
                r.step_table.at[sender],
                r.step_send.at[k - 1],
                r.step_recv.at[sender],
                (index, head),
            )

        for k in range(1, n):
            step_copy(k, lax.rem(place + k, n), place).start()
        total_copies.append(end_ring(1, gate_halves, len(gate_steps)))
        value_turn(2)
        keyquery_turn(4)
        group_total.run(0, 1)
        shared(group, r.dot_out, r.dots, r.rd_send, r.rd_recv)
        r.dots[head] = r.dot_out[...]
        for copy in loads[3:]:
            copy.wait()

        def fill_line():
            tiles, summed = Tiles(r.line_sum), Tiles(r.group_sum)
            r.line_sum[...] = jnp.zeros_like(r.line_sum)
            for lag in range(lags + 1):
                tiles.put(r.conv_grad[lag : lag + 1, :channels])
                tiles.put(summed.take(2 * STATE))
            tiles.put(r.gain_grad[...])
            for i in range(3):
                tiles.put(r.vector_grad[i : i + 1])
            tiles.put(summed.take(D))
            tiles.put(summed.take(LANES))

        def grad_store(c):
            return pltpu.make_async_copy(q.tokens_grad.at[c], r.tokens_grad.at[c], r.grad_sem.at[c])

        def rest(c):
            row_sum = r.dots[0, c : c + 1]
            for j in range(1, heads_n):
                row_sum = row_sum + r.dots[j, c : c + 1]
            inverse = r.inverse[c : c + 1]
            out_grad = (q.output[row_block(c)] - q.teacher[c]) * as_column(
                long_row(r.mask, c, length), width
            )
            q.tokens_grad[c] = (
                out_grad
                + as_column(inverse, width) * gain * total(c)
                - q.tokens[c] * as_column(inverse * inverse * row_sum * (1.0 / D), width)
            )
            grad_store(c).start()

        rest(0)
        rest(1)
        value_turn(3)
        keyquery_turn(5)
        group_total.run(1)
        fill_line()
        line_total.start(0)
        rest(2)
        if ring_steps > 6:
            loop(ring_steps - 6, lambda s: pass_on(keyquery_first, s + 6))
        value_turn(4)
        line_total.run(0, 1)
        for c in range(3, count):
            rest(c)
        for k in (keyquery_first, keyquery_first + 1):
            _, _, (first, lines), _, _ = ring.streams[k]
            r.keyquery_sum[first : first + lines] = ring.last(k)
        chip_total.start(0)
        value_turn(5)
        line_total.run(1, 2)
        chip_total.run(0)
        keyquery_swap = remote(
            r.keyquery_sum,
            r.keyquery_other,
            r.small_send.at[1],
            r.small_recv.at[1],
            group.at(group.mate),
        )
        keyquery_swap.start()
        if ring_steps > 6:

            def remaining(s):
                for first in value_halves:
                    pass_on(first, s + 6)

            loop(ring_steps - 6, remaining)
        total_copies.append(total_of(2, value_halves, q.sums, targets))
        for k in range(1, n):
            sender = lax.rem(place + k, n)
            copy = step_copy(k, sender, sender)
            copy.wait_send()
            copy.wait_recv()
        r.step_table[place] = q.step_part[place]
        step_sum = r.step_table[0]
        for s in range(1, n):
            step_sum = step_sum + r.step_table[s]
        r.step_total[...] = step_sum[:heads, :own]
        line_total.run(2)

        tiles = Tiles(r.line_sum)
        for lag in range(lags + 1):
            own_row, shared_row = tiles.take(channels), tiles.take(2 * STATE)
            if lag < lags:
                r.value_conv_total[lag : lag + 1] = own_row
                r.keyquery_conv_total[lag : lag + 1] = shared_row
            else:
                r.value_offset_total[...] = own_row[0]
                r.keyquery_offset_total[...] = shared_row[0]
        r.norm_gain_total[...] = tiles.take(channels)[0]
        for target in (r.step_bias_total, r.rate_log_total, r.skip_total):
            target[...] = tiles.take(LANES)[0, :heads]
        r.input_gain_total[...] = (own_columns(tiles.take(D)) / gain)[0]
        r.loss_total[...] = 0.5 * jnp.sum(tiles.take(LANES), axis=1, keepdims=True)[0]

        loop(count, finish)
        for c in range(count):
            grad_store(c).wait()
        for copy in total_copies:
            copy.wait()
        keyquery_mate.wait_send()
        keyquery_swap.wait()
        mine, other = r.keyquery_sum[...], r.keyquery_other[...]
        r.keyquery_total[:, :STATE] = jnp.where(group.core == 0, mine, other)
        r.keyquery_total[:, STATE:] = jnp.where(group.core == 0, other, mine)
        for i in range(len(ring.streams)):
            ring.finish(i)

    pl.run_scoped(phase_two, *scoped[3])


def rear(inputs, lags, cid):
    heads_n, n = lax.axis_size("head"), lax.axis_size("seq")
    count, length, channels = inputs["gate_hbm"].shape
    pieces = inputs["pieces_hbm"]
    rows, width = pieces.shape[1:]
    heads = channels // HEADDIM
    both = channels + 2 * STATE
    own = D // n
    step_lanes = -(-own // LANES) * LANES
    chips = heads_n // 2
    vmem, dma = pltpu.VMEM, pltpu.SemaphoreType.DMA
    hbm = pl.BlockSpec(memory_space=pl.ANY)
    group_tiles = (lags + 1) * 2 * STATE // LANES + D // LANES + 1
    line_tiles = (lags + 1) * both // LANES + channels // LANES + 3 + D // LANES + 1
    group_shape = (-(-group_tiles * LANES // (8 * 512)) * 8, 512)
    line_shape = (-(-line_tiles * LANES // (8 * both)) * 8, both)
    head_stages, line_stages = stages_of(heads_n), stages_of(n)
    outs = {
        "tokens_grad": (count, length, width),
        "out_total": (own, channels),
        "gate_total": (own, channels),
        "value_total": (own, channels),
        "keyquery_total": (own, 2 * STATE),
        "step_total": (heads, own),
        "value_conv_total": (lags, channels),
        "value_offset_total": (channels,),
        "keyquery_conv_total": (lags, 2 * STATE),
        "keyquery_offset_total": (2 * STATE,),
        "step_bias_total": (heads,),
        "rate_log_total": (heads,),
        "skip_total": (heads,),
        "norm_gain_total": (channels,),
        "input_gain_total": (width,),
        "loss_total": (1,),
    }
    if own % 64 == 0:
        wide_slots = [vmem((n - 1, own // 2, channels), bf16)] * 2
        slots = [vmem((n - 1, own // 4, channels), bf16)] * 4
    else:
        wide_slots = ring_slots(n, own, channels, bf16)
        slots = wide_slots + [vmem((16, LANES), bf16)] * 2
    chained = chain_buffers(count, channels)
    scratch = {
        "normed": vmem((count, length, D), bf16),
        "gate_grad": vmem((count, length, channels), bf16),
        "values_grad": vmem((count, length, channels), bf16),
        "narrow": vmem((count, length, 2 * STATE + LANES), bf16),
        "out_part": vmem((D, channels), bf16),
        "gate_part": vmem((D, channels), bf16),
        "os0": wide_slots[0],
        "os1": wide_slots[1],
        "gs0": wide_slots[0],
        "gs1": wide_slots[1],
        "vs0": slots[0],
        "vs1": slots[1],
        "vs2": slots[2],
        "vs3": slots[3],
        "ks0": vmem((n - 1, own // 2, STATE), f32),
        "ks1": vmem((n - 1, own // 2, STATE), f32),
        "state": chained[0],
        "offered": chained[2],
        "hand": chained[3],
        "edge": vmem((count, 8, both), f32),
        "edge_in": vmem((count, 8, both), f32),
        "gain_grad": vmem((1, channels), f32),
        "vector_grad": vmem((8, LANES), f32),
        "conv_grad": vmem((8, both), f32),
        "mate_in": vmem((chips, rows, width), bf16),
        "chip_in": vmem((chips - 1, rows, width), bf16),
        "dots": vmem((heads_n, count, length), f32),
        "dot_out": vmem((count, length), f32),
        "keyquery_in": vmem((D, STATE), f32),
        "keyquery_sum": vmem((own, STATE), f32),
        "keyquery_other": vmem((own, STATE), f32),
        "keyquery_table": vmem((head_stages - 1, own, STATE), f32),
        "step_table": vmem((n, 16, step_lanes), f32),
        "group_sum": vmem(group_shape, f32),
        "group_table": vmem((head_stages,) + group_shape, f32),
        "line_sum": vmem(line_shape, f32),
        "line_table": vmem((line_stages,) + line_shape, f32),
        "load_sem": dma((3,)),
        "row_sem": dma((3, count)),
        "line_load": dma((2,)),
        "load_two": dma((6,)),
        "grad_sem": dma((count,)),
        "total_sem": dma((3,)),
        "edge_send": dma((count,)),
        "edge_recv": dma((count,)),
        "chain_send": dma((3, count)),
        "chain_recv": dma((3, count)),
        "ring_send": dma((10,)),
        "ring_recv": dma((10, n - 1)),
        "mate_send": dma((chips, count)),
        "mate_recv": dma((chips, count)),
        "chip_send": dma((chips - 1, count)),
        "chip_recv": dma((chips - 1, count)),
        "rd_send": dma((heads_n - 1,)),
        "rd_recv": dma((heads_n,)),
        "small_send": dma((2,)),
        "small_recv": dma((2,)),
        "kq_send": dma((head_stages - 1,)),
        "kq_recv": dma((head_stages - 1,)),
        "group_send": dma((head_stages,)),
        "group_recv": dma((head_stages,)),
        "line_send": dma((line_stages,)),
        "line_recv": dma((line_stages,)),
        "step_send": dma((n - 1,)),
        "step_recv": dma((n,)),
    }
    first = {
        "weight": vmem(inputs["out_weight_hbm"].shape, bf16),
        "pieces": vmem(pieces.shape, bf16),
        "gate": vmem((count, length, channels), f32),
        "mixed": vmem((count, length, channels), f32),
        "conv": vmem((count, length, both), f32),
        "linear": vmem((2, length, both), bf16),
        "heads_in": vmem((count, length, channels), f32),
        "heads_grad": vmem((count, length, channels), f32),
        "keys": vmem((count, length, STATE), bf16),
        "queries": vmem((count, length, STATE), bf16),
        "scores": vmem((length, length), f32),
        "scores_grad": vmem((length, length), f32),
        "mask_bias": vmem((length, length), f32),
        "narrow_grad": vmem((count, length, 2 * STATE), f32),
        "local": vmem((count, STATE, channels), f32),
        "passed": vmem((count, 8, channels), f32),
        "offer": chained[1],
        "following": chained[4],
        "extended": vmem((2, length + 16, LANES), f32),
        "around": vmem((2, length + 32, LANES), f32),
        "usable": vmem((lags - 1, length + 32, LANES), f32),
        "tails": vmem((count, 16, both), f32),
        "dot_inner": vmem((count, length, LANES), f32),
        "cum_part": vmem((count, length, LANES), f32),
    }
    second = {
        "gate_weight": vmem((D, channels), bf16),
        "value_weight": vmem((D, channels), bf16),
        "keyquery_weight": vmem((D, 2 * STATE), bf16),
        "tokens": vmem((count, length, width), f32),
        "output": vmem((rows, width), f32),
        "teacher": vmem((count, length, width), f32),
        "tokens_grad": vmem((count, length, width), f32),
        "value_part": vmem((D, channels), bf16),
        "keyquery_part": vmem((2, D, STATE), f32),
        "keyquery_half": vmem((D, STATE), f32),
        "part": vmem((heads_n, rows, width), bf16),
        "chip_out": vmem((chips - 1, rows, width), bf16),
        "columns": vmem((1, D), f32),
        "step_whole": vmem((LANES, D), f32),
        "step_part": vmem((n, 16, step_lanes), f32),
        "sums": vmem((3, own, channels), f32),
    }
    names = list(inputs) + list(outs) + list(scratch)
    scoped = (list(first), list(first.values()), list(second), list(second.values()))
    in_hbm = [name.endswith("_hbm") for name in inputs]
    found = pl.pallas_call(
        functools.partial(rear_kernel, names, scoped, heads),
        out_shape=[jax.ShapeDtypeStruct(s, f32) for s in outs.values()],
        in_specs=[hbm if there else in_vmem for there in in_hbm],
        out_specs=[hbm] * 4 + [in_vmem] * (len(outs) - 4),
        scratch_shapes=list(scratch.values()),
        compiler_params=params(cid),
        name="rear",
    )(*inputs.values())
    return dict(zip(outs, found))


def deliver_kernel(count, *refs):
    sources, targets, held = refs[:count], refs[count : 2 * count], refs[2 * count : 3 * count]
    sem = refs[3 * count]
    loads = [pltpu.make_async_copy(a, b, sem.at[0, i]) for i, (a, b) in enumerate(zip(sources, held))]
    stores = [pltpu.make_async_copy(a, b, sem.at[1, i]) for i, (a, b) in enumerate(zip(held, targets))]
    for copy in loads:
        copy.start()
    for load, store in zip(loads, stores):
        load.wait()
        store.start()
    for copy in stores:
        copy.wait()


def deliver(arrays):
    hbm = pl.BlockSpec(memory_space=pl.ANY)
    count = len(arrays)
    return pl.pallas_call(
        functools.partial(deliver_kernel, count),
        out_shape=[jax.ShapeDtypeStruct(a.shape, a.dtype) for a in arrays],
        in_specs=[hbm] * count,
        out_specs=[hbm] * count,
        scratch_shapes=[pltpu.VMEM(a.shape, a.dtype) for a in arrays]
        + [pltpu.SemaphoreType.DMA((2, count))],
        compiler_params=pltpu.CompilerParams(vmem_limit_bytes=VMEM_LIMIT),
        name="deliver",
    )(*arrays)


def body(
    tokens,
    teacher,
    document_start,
    valid_mask,
    input_gain,
    gate_weight,
    value_weight,
    keyquery_weight,
    step_weight,
    value_conv_weight,
    value_conv_bias,
    keyquery_conv_weight,
    keyquery_conv_bias,
    step_bias,
    rate_log,
    skip_gain,
    norm_gain,
    out_weight,
):
    count, length, _ = tokens.shape
    channels = gate_weight.shape[1]
    width = teacher.shape[2]
    rows = count * length
    lags = value_conv_weight.shape[0]
    vectors = (step_bias, rate_log, skip_gain)
    (
        normed,
        linear,
        conv_linear,
        gate_linear,
        mixed,
        output,
        pieces,
        halo,
        state_in,
        steps,
        cumulative,
        steps_linear,
        square_rows,
        inverse_rows,
        mask_rows,
        rowdot,
        square_total,
        loss_cols,
    ) = front(
        tokens,
        input_gain,
        value_weight,
        keyquery_weight,
        step_weight.T,
        gate_weight,
        document_start,
        vectors,
        (value_conv_weight, value_conv_bias, keyquery_conv_weight, keyquery_conv_bias),
        norm_gain,
        valid_mask,
        out_weight,
        teacher,
        1,
    )
    token_cols = tokens
    if width % LANES:
        token_cols = lax.dynamic_slice_in_dim(tokens, lax.axis_index("head") * width, width, 2)
    totals = rear(
        {
            "pieces_hbm": pieces,
            "out_weight_hbm": blocked(out_weight, pieces.shape[0]),
            "gate_hbm": gate_linear,
            "mixed_hbm": mixed,
            "conv_hbm": conv_linear,
            "linear_hbm": linear,
            "normed_hbm": normed,
            "gate_weight_hbm": gate_weight,
            "value_weight_hbm": value_weight,
            "keyquery_weight_hbm": keyquery_weight,
            "tokens_hbm": token_cols,
            "output_hbm": output,
            "teacher_hbm": teacher,
            "step_weight": step_weight.T,
            "halo": halo,
            "state_in": state_in,
            "steps": steps,
            "cumulative": cumulative,
            "linear_steps": steps_linear,
            "square": square_total,
            "rowdot": rowdot,
            "docs": document_start,
            "step_bias": step_bias,
            "rate_log": rate_log,
            "skip": skip_gain,
            "value_conv": value_conv_weight,
            "keyquery_conv": keyquery_conv_weight,
            "norm_gain": norm_gain,
            "gain": input_gain,
            "mask": mask_rows,
            "inverse": inverse_rows,
            "loss_cols": loss_cols,
        },
        lags,
        3,
    )
    results = deliver(
        (
            output.reshape(count, length, width),
            totals["loss_total"],
            totals["tokens_grad"],
            totals["input_gain_total"],
            totals["gate_total"],
            totals["value_total"],
            totals["keyquery_total"],
            totals["step_total"],
            totals["value_conv_total"],
            totals["value_offset_total"],
            totals["keyquery_conv_total"],
            totals["keyquery_offset_total"],
            totals["step_bias_total"],
            totals["rate_log_total"],
            totals["skip_total"],
            totals["norm_gain_total"],
            totals["out_total"],
        )
    )
    return (
        results[0],
        results[1].reshape(()),
        *results[2:7],
        results[7].T,
        *results[8:16],
        results[16].T,
    )


def solution(mesh):
    placed = (
        P(None, "seq", None),
        P(None, "seq", "head"),
        P(None, "seq"),
        P(),
        P(),
        P(None, "head"),
        P(None, "head"),
        P(),
        P(None, "head"),
        P(None, "head"),
        P("head"),
        P(),
        P(),
        P("head"),
        P("head"),
        P("head"),
        P("head"),
        P("head", None),
    )
    return jax.shard_map(
        body,
        mesh=mesh,
        in_specs=placed,
        out_specs=(
            P(None, "seq", "head"),
            P(),
            P(None, "seq", "head"),
            P("head"),
            P("seq", "head"),
            P("seq", "head"),
            P("seq", None),
            P("seq", "head"),
            P(None, "head"),
            P("head"),
            P(),
            P(),
            P("head"),
            P("head"),
            P("head"),
            P("head"),
            P("head", "seq"),
        ),
        check_vma=False,
    )
```
